32 devices in a mesh: band: 8 (over z, y), batch: 4 (over x, core).
Axes of the slice: x: 2, y: 2, z: 4, core: 2. Of those that a mesh axis runs over, the one named last changes fastest.
Arguments:
- activations: bfloat16 [64, 1, 1024, 384], P('band', None, 'batch'), may hold values from -6 to 6
- cotangent: bfloat16 [64, 1, 1024, 384], P('band', None, 'batch'), may hold values from -6 to 6
- frame_counts: int32 [1], replicated, may hold values from 896 to 1024, as said below
- slot_bands: int32 [64], replicated, may hold values from -1 to 61, as said below
- time_prenorm: bfloat16 [384], replicated, may hold values from 0.5 to 1.5
- time_project: bfloat16 [384, 1536], replicated, may hold values from -0.3125 to 0.3125
- time_gating: bfloat16 [384, 8], replicated, may hold values from -0.3125 to 0.3125
- time_output: bfloat16 [512, 384], replicated, may hold values from -6 to 6
- time_midnorm: bfloat16 [384], replicated, may hold values from 0.5 to 1.5
- time_expand: bfloat16 [384, 1536], replicated, may hold values from -0.3125 to 0.3125
- time_shrink: bfloat16 [1536, 384], replicated, may hold values from -0.15625 to 0.15625
- band_prenorm: bfloat16 [384], replicated, may hold values from 0.5 to 1.5
- band_project: bfloat16 [384, 1536], replicated, may hold values from -0.3125 to 0.3125
- band_gating: bfloat16 [384, 8], replicated, may hold values from -0.3125 to 0.3125
- band_output: bfloat16 [512, 384], replicated, may hold values from -3 to 3
- band_midnorm: bfloat16 [384], replicated, may hold values from 0.5 to 1.5
- band_expand: bfloat16 [384, 1536], replicated, may hold values from -0.3125 to 0.3125
- band_shrink: bfloat16 [1536, 384], replicated, may hold values from -0.15625 to 0.15625
Outputs:
- layer_output: bfloat16 [64, 1, 1024, 384], P('band', None, 'batch')
- input_grad: float32 [64, 1, 1024, 384], P('band', None, 'batch')
- time_prenorm_grad: float32 [384], replicated
- time_project_grad: float32 [384, 1536], replicated
- time_gating_grad: float32 [384, 8], replicated
- time_output_grad: float32 [512, 384], replicated
- time_midnorm_grad: float32 [384], replicated
- time_expand_grad: float32 [384, 1536], replicated
- time_shrink_grad: float32 [1536, 384], replicated
- band_prenorm_grad: float32 [384], replicated
- band_project_grad: float32 [384, 1536], replicated
- band_gating_grad: float32 [384, 8], replicated
- band_output_grad: float32 [512, 384], replicated
- band_midnorm_grad: float32 [384], replicated
- band_expand_grad: float32 [384, 1536], replicated
- band_shrink_grad: float32 [1536, 384], replicated
The draws below stay inside these ranges and needn't reach their ends.
Inputs may be any that keep to these rules, and one draw needn't show every extreme that they name: `frame_counts`: real frames come first. `slot_bands`: each band 0 to 61 stands in exactly one slot; the other 2 slots hold -1.
All inputs are finite; a program needn't handle non-finite values.
Results may differ from the reference program's by a relative error of at most 0.03.
Values may be sent and summed in bfloat16 or wider, within the bound.
A program may use at most 448 MiB of HBM per device.

```python
import math
import jax
import jax.numpy as jnp
from jax import lax

D = 384
HEADS = 8
HEAD = 64
FF = 1536
BANDS = 62
SLOTS = 64
FRAMES = 1024
CLIPS = 1


def draw_frame_counts(key, part):
    key = jax.random.fold_in(key, 11)
    first_key, second_key = jax.random.split(key)
    counts = jax.random.randint(first_key, (CLIPS,), FRAMES - FRAMES // 8, FRAMES + 1)
    chosen = jax.random.randint(second_key, (), 0, CLIPS)
    return jnp.where(jnp.arange(CLIPS) == chosen, FRAMES, counts).astype(jnp.int32)


def draw_slot_bands(key, part):
    key = jax.random.fold_in(key, 23)
    order = jax.random.permutation(key, SLOTS)
    return jnp.where(order < BANDS, order, -1).astype(jnp.int32)


def levels(key, extent, cuts, least, high):
    loudness = 1.0
    for axis_at, blocks in cuts:
        heights = jax.random.uniform(jax.random.fold_in(jax.random.fold_in(key, 6), axis_at), (blocks,), jnp.float32, least / len(cuts), high / len(cuts))
        loudness = loudness * jnp.repeat(jnp.exp(heights), extent[axis_at] // blocks).reshape((-1,) + (1,) * (len(extent) - 1 - axis_at))
    return loudness


def bell_draw(own_key, shape, width, bound, cuts=(), kind=jnp.bfloat16):
    drawn = jax.random.normal(own_key, shape, jnp.float32) * width
    if len(cuts) > 0:
        drawn = levels(own_key, shape, cuts, -0.22, 0.18) * drawn
    return jnp.clip(drawn, min=-bound, max=bound).astype(kind)


def setup_inputs(seed: int = 0) -> dict:
    splits = jax.random.split(jax.random.key(seed), 19)
    activations = bell_draw(splits[0], (SLOTS, CLIPS, FRAMES, D), 1.0, 6.0, ((0, 8), (2, 4)))
    cotangent = bell_draw(splits[1], (SLOTS, CLIPS, FRAMES, D), 1.0, 6.0, ((0, 8), (2, 4)))
    frame_counts = draw_frame_counts(jax.random.fold_in(splits[18], 71), 0)
    slot_bands = draw_slot_bands(jax.random.fold_in(splits[18], 71), 0)
    time_prenorm = jnp.clip(1.0 + 0.1 * jax.random.normal(splits[4], (D,), jnp.float32), 0.5, 1.5).astype(jnp.bfloat16)
    time_project = bell_draw(splits[5], (D, 3 * HEADS * HEAD), D ** -0.5, 0.3125)
    time_gating = bell_draw(splits[6], (D, HEADS), D ** -0.5, 0.3125)
    time_output = bell_draw(splits[7], (HEADS * HEAD, D), 1 ** -0.5, 6.0)
    time_midnorm = jnp.clip(1.0 + 0.1 * jax.random.normal(splits[8], (D,), jnp.float32), 0.5, 1.5).astype(jnp.bfloat16)
    time_expand = bell_draw(splits[9], (D, FF), D ** -0.5, 0.3125)
    time_shrink = bell_draw(splits[10], (FF, D), FF ** -0.5, 0.15625)
    band_prenorm = jnp.clip(1.0 + 0.1 * jax.random.normal(splits[11], (D,), jnp.float32), 0.5, 1.5).astype(jnp.bfloat16)
    band_project = bell_draw(splits[12], (D, 3 * HEADS * HEAD), D ** -0.5, 0.3125)
    band_gating = bell_draw(splits[13], (D, HEADS), D ** -0.5, 0.3125)
    band_output = bell_draw(splits[14], (HEADS * HEAD, D), 4 ** -0.5, 3.0)
    band_midnorm = jnp.clip(1.0 + 0.1 * jax.random.normal(splits[15], (D,), jnp.float32), 0.5, 1.5).astype(jnp.bfloat16)
    band_expand = bell_draw(splits[16], (D, FF), D ** -0.5, 0.3125)
    band_shrink = bell_draw(splits[17], (FF, D), FF ** -0.5, 0.15625)
    return {"activations": activations, "cotangent": cotangent, "frame_counts": frame_counts, "slot_bands": slot_bands, "time_prenorm": time_prenorm, "time_project": time_project, "time_gating": time_gating, "time_output": time_output, "time_midnorm": time_midnorm, "time_expand": time_expand, "time_shrink": time_shrink, "band_prenorm": band_prenorm, "band_project": band_project, "band_gating": band_gating, "band_output": band_output, "band_midnorm": band_midnorm, "band_expand": band_expand, "band_shrink": band_shrink}


EPSILON = 1e-05
NEG_FILL = -1000000000.0
TIME_LAYOUT = ('bqhe', 'bkhe')
BAND_LAYOUT = ('qbhe', 'kbhe')

@jax.custom_vjp
def low(v):
    return lax.optimization_barrier(v.astype(jnp.bfloat16)).astype(jnp.float32)

@jax.custom_vjp
def low_back(v):
    return v

def low_keep(v):
    return (low(v), None)

def low_pass(kept, grad):
    return (grad,)

def back_keep(v):
    return (v, None)

def back_low(kept, grad):
    return (low(grad),)
low.defvjp(low_keep, low_pass)
low_back.defvjp(back_keep, back_low)

def rms_scale(residual, gain):
    return residual * lax.rsqrt(lax.optimization_barrier(jnp.mean(residual * residual, axis=-1, keepdims=True)) + EPSILON) * gain

def product(left, right):
    return jnp.matmul(left, right, precision=lax.Precision.HIGHEST)

def gelu_exact(values):
    return jax.nn.gelu(values, approximate=False)

def rotary_tables(positions, head_size):
    half_size = head_size // 2
    rates = jnp.exp(-math.log(10000.0) * jnp.arange(half_size, dtype=jnp.float32) / half_size)
    angles = positions[:, None] * rates[None, :]
    return (jnp.cos(angles), jnp.sin(angles))

def rotate(vectors, cos_table, sin_table):
    half_size = vectors.shape[-1] // 2
    first = vectors[..., :half_size]
    second = vectors[..., half_size:]
    return jnp.concatenate([first * cos_table - second * sin_table, first * sin_table + second * cos_table], axis=-1)

def attend(queries, key_rows, value_rows, key_valid, layout):
    query_form, key_form = layout
    scores = low_back(jnp.einsum(query_form + ',' + key_form + '->bhqk', queries, key_rows, precision=lax.Precision.HIGHEST) * 0.125)
    scores = jnp.where(key_valid[:, None, None, :], scores, NEG_FILL)
    soft_weights = jax.nn.softmax(scores, axis=-1)
    return low_back(jnp.einsum('bhqk,' + key_form + '->' + query_form, low(soft_weights), value_rows, precision=lax.Precision.HIGHEST))

def layer(residual, params, cos_table, sin_table, key_valid, layout):
    prenorm, project, gating, output_weight, midnorm, expand, shrink = params
    normed = low(rms_scale(residual, prenorm))
    projected = low_back(product(normed, project))
    gate_logits = low_back(product(normed, gating))
    inner_width = output_weight.shape[0]
    head_count = gating.shape[1]
    head_shape = residual.shape[:-1] + (head_count, inner_width // head_count)
    queries = low(rotate(projected[..., :inner_width].reshape(head_shape), cos_table, sin_table))
    key_rows = low(rotate(projected[..., inner_width:2 * inner_width].reshape(head_shape), cos_table, sin_table))
    value_rows = low(projected[..., 2 * inner_width:].reshape(head_shape))
    attended = attend(queries, key_rows, value_rows, key_valid, layout)
    gate_values = jax.nn.sigmoid(gate_logits)
    mixed_heads = low((attended * gate_values[..., None]).reshape(residual.shape[:-1] + (inner_width,)))
    middle = residual + low_back(product(mixed_heads, output_weight))
    normed_ffn = low(rms_scale(middle, midnorm))
    hidden = low_back(product(normed_ffn, expand))
    active = low(gelu_exact(hidden))
    return middle + low_back(product(active, shrink))

def reference(activations, cotangent, frame_counts, slot_bands, time_prenorm, time_project, time_gating, time_output, time_midnorm, time_expand, time_shrink, band_prenorm, band_project, band_gating, band_output, band_midnorm, band_expand, band_shrink):
    slot_count, clip_count, frames, model_width = activations.shape
    head_size = time_output.shape[0] // time_gating.shape[1]
    frame_valid = jnp.arange(frames, dtype=jnp.int32)[None, :] < frame_counts[:, None]
    row_valid = (slot_bands >= 0)[:, None, None] & frame_valid[None]
    time_cos, time_sin = rotary_tables(jnp.arange(frames, dtype=jnp.float32), head_size)
    time_cos = time_cos[None, :, None, :]
    time_sin = time_sin[None, :, None, :]
    band_cos, band_sin = rotary_tables(jnp.maximum(slot_bands, 0).astype(jnp.float32), head_size)
    band_cos = band_cos[:, None, None, :]
    band_sin = band_sin[:, None, None, :]
    block_frames = 64
    band_valid = jnp.broadcast_to((slot_bands >= 0)[None, :], (block_frames, slot_count))
    sequence_valid = jnp.tile(frame_valid, (slot_count, 1))

    def forward(inputs, time_params, band_params):
        sequences = inputs.reshape(slot_count * clip_count, 1, frames, model_width)

        def time_layer(sequence_pair):
            return layer(sequence_pair[0], time_params, time_cos, time_sin, sequence_pair[1][None], TIME_LAYOUT)
        middle = lax.map(jax.checkpoint(time_layer), (sequences, sequence_valid))
        block_count = clip_count * frames // block_frames
        blocks = middle.reshape(slot_count, block_count, block_frames, model_width).transpose(1, 0, 2, 3)

        def band_layer(block_rows):
            return layer(block_rows, band_params, band_cos, band_sin, band_valid, BAND_LAYOUT)
        band_out = lax.map(jax.checkpoint(band_layer), blocks)
        result = band_out.transpose(1, 0, 2, 3).reshape(slot_count, clip_count, frames, model_width)
        return jnp.where(row_valid[..., None], result, 0.0)
    time_params = (time_prenorm.astype(jnp.float32), time_project.astype(jnp.float32), time_gating.astype(jnp.float32), time_output.astype(jnp.float32), time_midnorm.astype(jnp.float32), time_expand.astype(jnp.float32), time_shrink.astype(jnp.float32))
    band_params = (band_prenorm.astype(jnp.float32), band_project.astype(jnp.float32), band_gating.astype(jnp.float32), band_output.astype(jnp.float32), band_midnorm.astype(jnp.float32), band_expand.astype(jnp.float32), band_shrink.astype(jnp.float32))
    output, pullback = jax.vjp(forward, activations.astype(jnp.float32), time_params, band_params)
    input_grad, time_grads, band_grads = pullback(cotangent.astype(jnp.float32))
    return (output.astype(jnp.bfloat16), input_grad, time_grads[0], time_grads[1], time_grads[2], time_grads[3], time_grads[4], time_grads[5], time_grads[6], band_grads[0], band_grads[1], band_grads[2], band_grads[3], band_grads[4], band_grads[5], band_grads[6])
```

```python
import math

import jax
import jax.numpy as jnp
from jax import lax
from jax.experimental import pallas as pl
from jax.experimental.pallas import tpu as pltpu
from jax.sharding import PartitionSpec as P

EPSILON = 1e-05
NEG_FILL = -1000000000.0
TIME_LAYOUT = ("bqhe", "bkhe")
BAND_LAYOUT = ("qbhe", "kbhe")


def rms_scale(residual, gain):
    return (
        residual * lax.rsqrt(jnp.mean(residual * residual, axis=-1, keepdims=True) + EPSILON) * gain
    )


def gelu_exact(values):
    return jax.nn.gelu(values, approximate=False)


def rotary_tables(positions, head_size):
    half_size = head_size // 2
    rates = jnp.exp(-math.log(10000.0) * jnp.arange(half_size, dtype=jnp.float32) / half_size)
    angles = positions[:, None] * rates[None, :]
    return (jnp.cos(angles), jnp.sin(angles))


def rotate(vectors, cos_table, sin_table):
    half_size = vectors.shape[-1] // 2
    first = vectors[..., :half_size]
    second = vectors[..., half_size:]
    return jnp.concatenate(
        [first * cos_table - second * sin_table, first * sin_table + second * cos_table], axis=-1
    )


def token_sum(left, right):
    return lax.dot_general(
        left.reshape(-1, left.shape[-1]),
        right.reshape(-1, right.shape[-1]),
        (((0,), (0,)), ((), ())),
        preferred_element_type=jnp.float32,
    )


def back_dot(gradient, weight):
    return lax.dot_general(
        gradient,
        weight,
        (((gradient.ndim - 1,), (1,)), ((), ())),
        preferred_element_type=jnp.float32,
    )


def block_forward(queries, key_rows, value_rows, key_valid, layout):
    query_form, key_form = layout
    scores = (
        jnp.einsum(
            query_form + "," + key_form + "->bhqk",
            queries,
            key_rows,
            preferred_element_type=jnp.float32,
        )
        * 0.125
    )
    scores = jnp.where(key_valid[:, None, None, :], scores, NEG_FILL)
    highest = jnp.max(scores, axis=-1, keepdims=True)
    exponents = jnp.exp(scores - highest)
    totals = jnp.sum(exponents, axis=-1, keepdims=True)
    soft_weights = (exponents / totals).astype(jnp.bfloat16)
    output = jnp.einsum(
        "bhqk," + key_form + "->" + query_form,
        soft_weights,
        value_rows,
        preferred_element_type=jnp.float32,
    )
    return (output, highest + jnp.log(totals))


def block_backward(queries, key_rows, value_rows, key_valid, log_totals, out_grad, layout):
    query_form, key_form = layout
    scores = (
        jnp.einsum(
            query_form + "," + key_form + "->bhqk",
            queries,
            key_rows,
            preferred_element_type=jnp.float32,
        )
        * 0.125
    )
    soft_weights = jnp.where(key_valid[:, None, None, :], jnp.exp(scores - log_totals), 0.0)
    weight_grad = jnp.einsum(
        query_form + "," + key_form + "->bhqk",
        out_grad,
        value_rows,
        preferred_element_type=jnp.float32,
    )
    score_grad = (
        soft_weights * (weight_grad - jnp.sum(soft_weights * weight_grad, axis=-1, keepdims=True))
    ).astype(jnp.bfloat16)
    query_grad = (
        jnp.einsum(
            "bhqk," + key_form + "->" + query_form,
            score_grad,
            key_rows,
            preferred_element_type=jnp.float32,
        )
        * 0.125
    )
    key_grad = (
        jnp.einsum(
            "bhqk," + query_form + "->" + key_form,
            score_grad,
            queries,
            preferred_element_type=jnp.float32,
        )
        * 0.125
    )
    value_grad = jnp.einsum(
        "bhqk," + query_form + "->" + key_form,
        soft_weights.astype(jnp.bfloat16),
        out_grad,
        preferred_element_type=jnp.float32,
    )
    return (query_grad, key_grad, value_grad)


def time_attend(queries, key_rows, value_rows, key_valid):
    keys_full, values_full = (
        lax.all_gather(key_rows, "batch", axis=1, tiled=True),
        lax.all_gather(value_rows, "batch", axis=1, tiled=True),
    )
    output, log_totals = block_forward(queries, keys_full, values_full, key_valid, TIME_LAYOUT)
    return (output, (log_totals, keys_full, values_full))


def time_attend_back(queries, key_rows, value_rows, key_valid, attn_kept, out_grad):
    log_totals, keys_full, values_full = attn_kept
    query_grad, key_full_grad, value_full_grad = block_backward(
        queries, keys_full, values_full, key_valid, log_totals, out_grad, TIME_LAYOUT
    )
    key_grad, value_grad = (
        lax.psum_scatter(
            key_full_grad.astype(jnp.bfloat16), "batch", scatter_dimension=1, tiled=True
        ).astype(jnp.float32),
        lax.psum_scatter(
            value_full_grad.astype(jnp.bfloat16), "batch", scatter_dimension=1, tiled=True
        ).astype(jnp.float32),
    )
    return (query_grad, key_grad, value_grad)


def band_attend(queries, key_rows, value_rows, key_valid):
    return block_forward(queries, key_rows, value_rows, key_valid, BAND_LAYOUT)


def band_attend_back(queries, key_rows, value_rows, key_valid, attn_kept, out_grad):
    return block_backward(
        queries, key_rows, value_rows, key_valid, attn_kept, out_grad, BAND_LAYOUT
    )


def layer_forward(residual, params, tables, key_valid, attend):
    prenorm, project, gating, output_weight, midnorm, expand, shrink = params
    cos_table, sin_table = tables
    normed = rms_scale(residual, prenorm.astype(jnp.float32)).astype(jnp.bfloat16)
    projected = jnp.dot(normed, project, preferred_element_type=jnp.float32)
    gate_logits = jnp.dot(normed, gating, preferred_element_type=jnp.float32)
    inner_width = output_weight.shape[0]
    head_count = gating.shape[1]
    head_shape = residual.shape[:-1] + (head_count, inner_width // head_count)
    queries = rotate(projected[..., :inner_width].reshape(head_shape), cos_table, sin_table).astype(
        jnp.bfloat16
    )
    key_rows = rotate(
        projected[..., inner_width : 2 * inner_width].reshape(head_shape), cos_table, sin_table
    ).astype(jnp.bfloat16)
    value_rows = projected[..., 2 * inner_width :].reshape(head_shape).astype(jnp.bfloat16)
    attended, attn_kept = attend(queries, key_rows, value_rows, key_valid)
    gate_values = jax.nn.sigmoid(gate_logits)
    mixed_heads = (
        (attended * gate_values[..., None])
        .reshape(residual.shape[:-1] + (inner_width,))
        .astype(jnp.bfloat16)
    )
    middle = residual + jnp.dot(mixed_heads, output_weight, preferred_element_type=jnp.float32)
    normed_ffn = rms_scale(middle, midnorm.astype(jnp.float32)).astype(jnp.bfloat16)
    hidden = jnp.dot(normed_ffn, expand, preferred_element_type=jnp.float32)
    active = gelu_exact(hidden).astype(jnp.bfloat16)
    result = middle + jnp.dot(active, shrink, preferred_element_type=jnp.float32)
    kept_values = (
        residual,
        normed,
        gate_logits,
        queries,
        key_rows,
        value_rows,
        attn_kept,
        attended,
        mixed_heads,
        middle,
        normed_ffn,
        hidden,
        active,
    )
    return (result, kept_values)


def layer_backward(result_grad, params, kept_values, tables, key_valid, attend_back):
    prenorm, project, gating, output_weight, midnorm, expand, shrink = params
    (
        residual,
        normed,
        gate_logits,
        queries,
        key_rows,
        value_rows,
        attn_kept,
        attended,
        mixed_heads,
        middle,
        normed_ffn,
        hidden,
        active,
    ) = kept_values
    cos_table, sin_table = tables
    branch_grad = result_grad.astype(jnp.bfloat16)
    shrink_grad = token_sum(active, branch_grad)
    active_grad = back_dot(branch_grad, shrink)
    hidden_grad = jax.vjp(gelu_exact, hidden)[1](active_grad)[0].astype(jnp.bfloat16)
    expand_grad = token_sum(normed_ffn, hidden_grad)
    normed_ffn_grad = back_dot(hidden_grad, expand)
    middle_norm_grad, midnorm_grad = jax.vjp(rms_scale, middle, midnorm.astype(jnp.float32))[1](
        normed_ffn_grad
    )
    middle_grad = result_grad + middle_norm_grad
    attn_branch = middle_grad.astype(jnp.bfloat16)
    output_grad = token_sum(mixed_heads, attn_branch)
    mixed_grad = back_dot(attn_branch, output_weight).reshape(attended.shape)
    gate_values = jax.nn.sigmoid(gate_logits)
    attended_grad = (mixed_grad * gate_values[..., None]).astype(jnp.bfloat16)
    logit_grad = (
        jnp.sum(mixed_grad * attended, axis=-1) * gate_values * (1.0 - gate_values)
    ).astype(jnp.bfloat16)
    query_grad, key_grad, value_grad = attend_back(
        queries, key_rows, value_rows, key_valid, attn_kept, attended_grad
    )
    flat_shape = residual.shape[:-1] + (-1,)
    projected_grad = jnp.concatenate(
        [
            rotate(query_grad, cos_table, -sin_table).reshape(flat_shape),
            rotate(key_grad, cos_table, -sin_table).reshape(flat_shape),
            value_grad.reshape(flat_shape),
        ],
        axis=-1,
    ).astype(jnp.bfloat16)
    project_grad = token_sum(normed, projected_grad)
    gating_grad = token_sum(normed, logit_grad)
    normed_grad = back_dot(projected_grad, project) + back_dot(logit_grad, gating)
    residual_norm_grad, prenorm_grad = jax.vjp(rms_scale, residual, prenorm.astype(jnp.float32))[1](
        normed_grad
    )
    return (
        middle_grad + residual_norm_grad,
        (
            prenorm_grad,
            project_grad,
            gating_grad,
            output_grad,
            midnorm_grad,
            expand_grad,
            shrink_grad,
        ),
    )


def generic_shards(
    activations,
    cotangent,
    frame_counts,
    slot_bands,
    time_prenorm,
    time_project,
    time_gating,
    time_output,
    time_midnorm,
    time_expand,
    time_shrink,
    band_prenorm,
    band_project,
    band_gating,
    band_output,
    band_midnorm,
    band_expand,
    band_shrink,
):
    slot_dev, clip_count, frame_dev, model_width = activations.shape
    slot_count = slot_bands.shape[0]
    frames_all = frame_dev * lax.axis_size("batch")
    head_size = time_output.shape[0] // time_gating.shape[1]
    time_params = (
        time_prenorm,
        time_project,
        time_gating,
        time_output,
        time_midnorm,
        time_expand,
        time_shrink,
    )
    band_params = (
        band_prenorm,
        band_project,
        band_gating,
        band_output,
        band_midnorm,
        band_expand,
        band_shrink,
    )
    own_bands = lax.dynamic_slice_in_dim(slot_bands, lax.axis_index("band") * slot_dev, slot_dev)
    frame_start = lax.axis_index("batch") * frame_dev
    own_frames = frame_start + jnp.arange(frame_dev, dtype=jnp.int32)
    frame_valid = own_frames[None, :] < frame_counts[:, None]
    row_valid = (own_bands >= 0)[:, None, None] & frame_valid[None]
    full_valid = jnp.arange(frames_all, dtype=jnp.int32)[None, :] < frame_counts[:, None]
    time_valid = jnp.broadcast_to(full_valid[None], (slot_dev, clip_count, frames_all)).reshape(
        slot_dev * clip_count, frames_all
    )
    time_cos, time_sin = rotary_tables(own_frames.astype(jnp.float32), head_size)
    time_tables = (time_cos[None, :, None, :], time_sin[None, :, None, :])
    band_cos, band_sin = rotary_tables(jnp.maximum(slot_bands, 0).astype(jnp.float32), head_size)
    band_tables = (band_cos[:, None, None, :], band_sin[:, None, None, :])
    residual = activations.astype(jnp.float32).reshape(
        slot_dev * clip_count, frame_dev, model_width
    )
    time_result, time_kept = layer_forward(
        residual, time_params, time_tables, time_valid, time_attend
    )
    masked_cot = jnp.where(row_valid[..., None], cotangent, jnp.zeros((), jnp.bfloat16)).reshape(
        slot_dev, clip_count * frame_dev, model_width
    )
    frame_rows = lax.all_to_all(
        time_result.astype(jnp.bfloat16), "band", split_axis=1, concat_axis=0, tiled=True
    ).astype(time_result.dtype)
    band_valid = jnp.broadcast_to((slot_bands >= 0)[None, :], (frame_rows.shape[1], slot_count))
    band_result, band_kept = layer_forward(
        frame_rows, band_params, band_tables, band_valid, band_attend
    )
    back_rows = lax.all_to_all(
        band_result.astype(jnp.bfloat16), "band", split_axis=0, concat_axis=1, tiled=True
    ).astype(band_result.dtype)
    layer_output = jnp.where(
        row_valid[..., None], back_rows.reshape(activations.shape), 0.0
    ).astype(jnp.bfloat16)
    frame_cot = lax.all_to_all(masked_cot, "band", split_axis=1, concat_axis=0, tiled=True)
    frame_grad, band_grads = layer_backward(
        frame_cot.astype(jnp.float32),
        band_params,
        band_kept,
        band_tables,
        band_valid,
        band_attend_back,
    )
    slot_grad = lax.all_to_all(
        frame_grad.astype(jnp.bfloat16), "band", split_axis=0, concat_axis=1, tiled=True
    ).astype(frame_grad.dtype)
    input_grad, time_grads = layer_backward(
        slot_grad, time_params, time_kept, time_tables, time_valid, time_attend_back
    )
    input_grad = input_grad.reshape(activations.shape)
    all_grads = lax.psum(
        (
            time_grads[0],
            time_grads[1],
            time_grads[2],
            time_grads[3],
            time_grads[4],
            time_grads[5],
            time_grads[6],
            band_grads[0],
            band_grads[1],
            band_grads[2],
            band_grads[3],
            band_grads[4],
            band_grads[5],
            band_grads[6],
        ),
        ("band", "batch"),
    )
    return (
        layer_output,
        input_grad,
        all_grads[0],
        all_grads[1],
        all_grads[2],
        all_grads[3],
        all_grads[4],
        all_grads[5],
        all_grads[6],
        all_grads[7],
        all_grads[8],
        all_grads[9],
        all_grads[10],
        all_grads[11],
        all_grads[12],
        all_grads[13],
    )


BLOCK = 256
LOG2E = 1.4426950408889634
F32 = jnp.float32
BF16 = jnp.bfloat16
NN = (((1,), (0,)), ((), ()))
NT = (((1,), (1,)), ((), ()))
TN = (((0,), (0,)), ((), ()))
VMEM_BYTES = 60 * 2**20


def dg(left, right, dims):
    return lax.dot_general(left, right, dims, preferred_element_type=F32)


def norm_forward(rows, gain):
    scale = lax.rsqrt(jnp.mean(rows * rows, axis=0, keepdims=True) + EPSILON)
    return (rows * scale * gain).astype(BF16)


def norm_backward(rows, gain, grad):
    scale = lax.rsqrt(jnp.mean(rows * rows, axis=0, keepdims=True) + EPSILON)
    unit = rows * scale
    scaled = grad * gain
    inner = jnp.mean(scaled * unit, axis=0, keepdims=True)
    return scale * (scaled - unit * inner), grad * unit


def gelu_pair(values):
    size = jnp.abs(values)
    denominator = 1.0 + (0.3275911 * math.sqrt(0.5)) * size
    t = pl.reciprocal(denominator, approx=True)
    t = t * (2.0 - denominator * t)
    bell = jnp.exp2(values * values * (-0.5 * LOG2E))
    poly = 0.5 * 1.061405429
    for coefficient in (-1.453152027, 1.421413741, -0.284496736, 0.254829592):
        poly = poly * t + 0.5 * coefficient
    tail = poly * t * bell
    upper = jnp.where(values < 0.0, tail, 1.0 - tail)
    slope = upper + values * bell * (1.0 / math.sqrt(2.0 * math.pi))
    return values * upper, slope


def turn(vectors, cos, sin):
    half = cos.shape[0]
    split = vectors.reshape(-1, 2 * half, vectors.shape[-1])
    first = split[:, :half]
    second = split[:, half:]
    turned = jnp.concatenate([first * cos - second * sin, first * sin + second * cos], axis=1)
    return turned.reshape(vectors.shape)


def three_parts(values):
    top = values.astype(BF16).astype(F32)
    rest = values - top
    middle = rest.astype(BF16).astype(F32)
    return top, middle, rest - middle


def extra_rows(rows, width):
    tile = jnp.concatenate(rows + [jnp.zeros((8 - len(rows), width), F32)], axis=0)
    return jnp.concatenate([tile, jnp.zeros((8, width), F32)], axis=0).astype(BF16)


def project_block(normed, wpt_ref, cos, sin, inner, scale):
    queries = turn(dg(wpt_ref[0:inner, :], normed, NN), cos, sin) * scale
    keys = turn(dg(wpt_ref[inner : 2 * inner, :], normed, NN), cos, sin)
    values = dg(wpt_ref[2 * inner : 3 * inner, :], normed, NN)
    return queries.astype(BF16), keys.astype(BF16), values.astype(BF16)


def time_forward_kernel(
    heads,
    x_ref,
    bias_ref,
    cos_ref,
    sin_ref,
    g1_ref,
    g2_ref,
    wpt_ref,
    wgt_ref,
    wot_ref,
    w1t_ref,
    w2t_ref,
    result_ref,
    n_ref,
    q_ref,
    k_ref,
    v_ref,
    p_ref,
    linv_ref,
    gate_ref,
    att_ref,
    mixed_ref,
    mid_ref,
    nf_ref,
    act_ref,
    slope_ref,
    xt_ref,
):
    head = pl.program_id(1)
    frames, model = x_ref.shape[1:]
    inner = q_ref.shape[1]
    size = inner // heads

    @pl.when(head == 0)
    def before():
        def block(i, carry):
            at = pl.ds(pl.multiple_of(i * BLOCK, BLOCK), BLOCK)
            rows = x_ref[0, at, :].astype(F32).T
            xt_ref[:, at] = rows
            normed = norm_forward(rows, g1_ref[...])
            n_ref[0, :, at] = normed
            queries, keys, values = project_block(
                normed, wpt_ref, cos_ref[:, at], sin_ref[:, at], inner, LOG2E * size**-0.5
            )
            q_ref[0, :, at] = queries
            k_ref[0, :, at] = keys
            v_ref[0, :, at] = values
            gate_ref[0, :, at] = dg(wgt_ref[...], normed, NN)
            return carry

        lax.fori_loop(0, frames // BLOCK, block, 0)

    at_head = pl.ds(pl.multiple_of(head * size, size), size)
    ones = jnp.ones((1, frames), F32)
    queries = jnp.concatenate([q_ref[0, at_head, :], extra_rows([ones], frames)], axis=0)
    keys = jnp.concatenate([k_ref[0, at_head, :], extra_rows([bias_ref[...]], frames)], axis=0)
    values = jnp.concatenate([v_ref[0, at_head, :], extra_rows([ones], frames)], axis=0)
    scores = dg(keys, queries, TN)
    weights = jnp.exp2(scores - jnp.max(scores, axis=0, keepdims=True)).astype(BF16)
    p_ref[0, 0] = weights
    sums = dg(values, weights, NN)
    inverse = 1.0 / sums[size : size + 1]
    attended = sums[:size] * inverse
    linv_ref[0, pl.ds(head, 1), :] = inverse
    att_ref[0, at_head, :] = attended
    gate = jax.nn.sigmoid(gate_ref[0, pl.ds(head, 1), :])
    mixed_ref[0, at_head, :] = (attended * gate).astype(BF16)

    @pl.when(head == heads - 1)
    def after():
        def block(i, carry):
            at = pl.ds(pl.multiple_of(i * BLOCK, BLOCK), BLOCK)
            middle = xt_ref[:, at] + dg(wot_ref[...], mixed_ref[0, :, at], NN)
            mid_ref[0, :, at] = middle
            normed = norm_forward(middle, g2_ref[...])
            nf_ref[0, :, at] = normed
            active, slope = gelu_pair(dg(w1t_ref[...], normed, NN))
            active = active.astype(BF16)
            act_ref[0, :, at] = active
            slope_ref[0, :, at] = slope.astype(BF16)
            result = middle + dg(w2t_ref[...], active, NN)
            result_ref[0, at, :] = result.T.astype(BF16)
            return carry

        lax.fori_loop(0, frames // BLOCK, block, 0)


def whole_spec(array):
    nd = array.ndim
    return pl.BlockSpec(array.shape, lambda *ids: (0,) * nd, pipeline_mode=pl.Buffered(1))


def time_forward(rows, bias, cos, sin, g1, g2, wpt, wgt, wot, w1t, w2t):
    slots, frames, model = rows.shape
    heads = wgt.shape[0]
    inner = wot.shape[1]
    hidden = w1t.shape[0]

    def per_slot(*shape):
        return pl.BlockSpec((1,) + shape, lambda s, h: (s,) + (0,) * len(shape))

    outs = [
        ((frames, model), BF16),
        ((model, frames), BF16),
        ((inner, frames), BF16),
        ((inner, frames), BF16),
        ((inner, frames), BF16),
        None,
        ((heads, frames), F32),
        ((heads, frames), F32),
        ((inner, frames), F32),
        ((inner, frames), BF16),
        ((model, frames), F32),
        ((model, frames), BF16),
        ((hidden, frames), BF16),
        ((hidden, frames), BF16),
    ]
    shapes, specs = [], []
    for entry in outs:
        if entry is None:
            shapes.append(jax.ShapeDtypeStruct((slots, heads, frames, frames), BF16))
            specs.append(pl.BlockSpec((1, 1, frames, frames), lambda s, h: (s, h, 0, 0)))
        else:
            shapes.append(jax.ShapeDtypeStruct((slots,) + entry[0], entry[1]))
            specs.append(per_slot(*entry[0]))
    consts = (bias, cos, sin, g1, g2, wpt, wgt, wot, w1t, w2t)
    return pl.pallas_call(
        lambda *refs: time_forward_kernel(heads, *refs),
        grid=(slots, heads),
        out_shape=shapes,
        in_specs=[per_slot(frames, model)] + [whole_spec(c) for c in consts],
        out_specs=specs,
        scratch_shapes=[pltpu.VMEM((model, frames), F32)],
        compiler_params=pltpu.CompilerParams(vmem_limit_bytes=VMEM_BYTES),
        name="time_forward",
    )(rows, *consts)


def ffn_backward(grad, act, slope, normed, middle, gain, w1_ref, w2_ref, dw1_ref, dw2t_ref, dg2_ref):
    branch = grad.astype(BF16)
    d_hidden = (dg(w2_ref[...], branch, NN) * slope.astype(F32)).astype(BF16)
    dw2t_ref[...] += dg(branch, act, NT)
    dw1_ref[...] += dg(normed, d_hidden, NT)
    d_normed = dg(w1_ref[...], d_hidden, NN)
    d_rows, terms = norm_backward(middle, gain, d_normed)
    dg2_ref[...] += jnp.sum(terms, axis=1, keepdims=True)
    return grad + d_rows


def head_backward(d_mixed, attended, gate_logit, inverse):
    gate = jax.nn.sigmoid(gate_logit)
    d_logit = jnp.sum(d_mixed * attended, axis=0, keepdims=True) * gate * (1.0 - gate)
    d_att = (d_mixed * (gate * inverse)).astype(BF16)
    minus = -jnp.sum(d_att.astype(F32) * attended, axis=0, keepdims=True)
    return d_att, minus, d_logit


def scores_backward(queries, keys, values, weights, d_att, minus, cos, sin, scale):
    width = queries.shape[1]
    ones = jnp.ones((1, width), F32)
    d_weights = dg(
        jnp.concatenate([values, extra_rows([ones, ones, ones], width)], axis=0),
        jnp.concatenate([d_att, extra_rows(list(three_parts(minus)), width)], axis=0),
        TN,
    )
    d_scores = (weights.astype(F32) * d_weights).astype(BF16)
    d_values = dg(d_att, weights, NT)
    d_queries = dg(keys, d_scores, NN) * scale
    d_keys = dg(queries, d_scores, NT) * (1.0 / LOG2E)
    return turn(d_queries, cos, -sin), turn(d_keys, cos, -sin), d_values


def time_ffn_backward_kernel(
    heads,
    grad_ref,
    act_ref,
    slope_ref,
    nf_ref,
    mid_ref,
    mixed_ref,
    att_ref,
    gate_ref,
    linv_ref,
    g2_ref,
    w1_ref,
    w2_ref,
    wo_ref,
    dmid_ref,
    datt_ref,
    minus_ref,
    dlogit_ref,
    sums_ref,
    dw1_ref,
    dw2t_ref,
    dwot_ref,
    dg2_ref,
):
    step = pl.program_id(0) * pl.num_programs(1) + pl.program_id(1)
    last = pl.num_programs(0) * pl.num_programs(1) - 1
    size = wo_ref.shape[0] // heads

    @pl.when(step == 0)
    def clear():
        for ref in (dw1_ref, dw2t_ref, dwot_ref, dg2_ref):
            ref[...] = jnp.zeros_like(ref)

    grad = grad_ref[0].astype(F32).T
    d_middle = ffn_backward(
        grad, act_ref[0], slope_ref[0], nf_ref[0], mid_ref[0], g2_ref[...], w1_ref, w2_ref, dw1_ref, dw2t_ref, dg2_ref
    )
    dmid_ref[0] = d_middle
    branch = d_middle.astype(BF16)
    dwot_ref[...] += dg(branch, mixed_ref[0], NT)
    d_mixed = dg(wo_ref[...], branch, NN)
    logits, minuses = [], []
    for head in range(heads):
        at = slice(head * size, (head + 1) * size)
        d_att, minus, d_logit = head_backward(
            d_mixed[at], att_ref[0, at], gate_ref[0, head : head + 1], linv_ref[0, head : head + 1]
        )
        datt_ref[0, at] = d_att
        minuses.append(minus)
        logits.append(d_logit)
    minus_ref[0] = jnp.concatenate(minuses, axis=0)
    dlogit_ref[0] = jnp.concatenate(logits, axis=0)

    @pl.when(step == last)
    def finish():
        pack_sums(sums_ref, (dw1_ref, dw2t_ref, dwot_ref, dg2_ref))


def pack_sums(sums_ref, parts):
    at = 0
    narrow = []
    for ref in parts:
        width = ref.shape[1]
        if width % 128 == 0:
            sums_ref[:, at : at + width] = ref[...].astype(BF16)
            at += width
        else:
            narrow.append(ref[...])
    used = sum(part.shape[1] for part in narrow)
    narrow.append(jnp.zeros((sums_ref.shape[0], 128 - used), F32))
    sums_ref[:, at : at + 128] = jnp.concatenate(narrow, axis=1).astype(BF16)


def time_ffn_backward(grad, act, slope, nf, mid, mixed, att, gate, linv, g2, w1, w2, wo):
    slots, frames, model = grad.shape
    heads = gate.shape[1]
    inner, hidden = wo.shape[0], w1.shape[1]
    tokens = min(frames, 512)

    def cut(rows):
        return pl.BlockSpec((1, rows, tokens), lambda s, c: (s, 0, c))

    consts = (g2, w1, w2, wo)
    width = 2 * hidden + inner + 128
    return pl.pallas_call(
        lambda *refs: time_ffn_backward_kernel(heads, *refs),
        grid=(slots, frames // tokens),
        out_shape=[
            jax.ShapeDtypeStruct((slots, model, frames), F32),
            jax.ShapeDtypeStruct((slots, inner, frames), BF16),
            jax.ShapeDtypeStruct((slots, heads, frames), F32),
            jax.ShapeDtypeStruct((slots, heads, frames), F32),
            jax.ShapeDtypeStruct((model, width), BF16),
        ],
        in_specs=[pl.BlockSpec((1, tokens, model), lambda s, c: (s, c, 0))]
        + [cut(a.shape[1]) for a in (act, slope, nf, mid, mixed, att, gate, linv)]
        + [whole_spec(c) for c in consts],
        out_specs=[cut(model), cut(inner), cut(heads), cut(heads), pl.BlockSpec((model, width), lambda s, c: (0, 0))],
        scratch_shapes=[
            pltpu.VMEM((model, hidden), F32),
            pltpu.VMEM((model, hidden), F32),
            pltpu.VMEM((model, inner), F32),
            pltpu.VMEM((model, 1), F32),
        ],
        compiler_params=pltpu.CompilerParams(vmem_limit_bytes=VMEM_BYTES),
        name="time_ffn_backward",
    )(grad, act, slope, nf, mid, mixed, att, gate, linv, *consts)


def time_attention_backward_kernel(
    heads,
    p_ref,
    q_ref,
    k_ref,
    v_ref,
    datt_ref,
    minus_ref,
    dlogit_ref,
    n_ref,
    x_ref,
    dmid_ref,
    cos_ref,
    sin_ref,
    g1_ref,
    wp_ref,
    wg_ref,
    out_ref,
    sums_ref,
    dproj_ref,
    dwp_ref,
    dwg_ref,
    dg1_ref,
):
    slot, head = pl.program_id(0), pl.program_id(1)
    inner = q_ref.shape[1]
    size = inner // heads
    frames = q_ref.shape[2]

    @pl.when((slot == 0) & (head == 0))
    def clear():
        for ref in (dwp_ref, dwg_ref, dg1_ref):
            ref[...] = jnp.zeros_like(ref)

    start = pl.multiple_of(head * size, size)
    at = pl.ds(start, size)
    d_queries, d_keys, d_values = scores_backward(
        q_ref[0, at, :],
        k_ref[0, at, :],
        v_ref[0, at, :],
        p_ref[0, 0],
        datt_ref[0, at, :],
        minus_ref[0, pl.ds(head, 1), :],
        cos_ref[...],
        sin_ref[...],
        size**-0.5,
    )
    dproj_ref[at, :] = d_queries.astype(BF16)
    dproj_ref[pl.ds(inner + start, size), :] = d_keys.astype(BF16)
    dproj_ref[pl.ds(2 * inner + start, size), :] = d_values.astype(BF16)

    @pl.when(head == heads - 1)
    def after():
        d_logit = jnp.concatenate([dlogit_ref[0], jnp.zeros_like(dlogit_ref[0])], axis=0).astype(BF16)
        dwp_ref[...] += dg(n_ref[0], dproj_ref[...], NT)
        dwg_ref[...] += dg(n_ref[0], d_logit, NT)[:, :heads]

        def block(i, carry):
            at = pl.ds(pl.multiple_of(i * BLOCK, BLOCK), BLOCK)
            logit = dlogit_ref[0, :, at].astype(BF16)
            d_normed = dg(wp_ref[...], dproj_ref[:, at], NN) + dg(wg_ref[...], logit, NN)
            d_rows, terms = norm_backward(x_ref[0, at, :].astype(F32).T, g1_ref[...], d_normed)
            dg1_ref[...] += jnp.sum(terms, axis=1, keepdims=True)
            out_ref[0, at, :] = (dmid_ref[0, :, at] + d_rows).T.astype(BF16)
            return carry

        lax.fori_loop(0, frames // BLOCK, block, 0)

    @pl.when((slot == pl.num_programs(0) - 1) & (head == heads - 1))
    def finish():
        pack_sums(sums_ref, (dwp_ref, dwg_ref, dg1_ref))


def time_attention_backward(p, q, k, v, datt, minus, dlogit, n, x, dmid, cos, sin, g1, wp, wg):
    slots, inner, frames = q.shape
    heads = minus.shape[1]
    model = n.shape[1]

    def per_slot(array):
        return pl.BlockSpec((1,) + array.shape[1:], lambda s, h: (s, 0, 0))

    consts = (cos, sin, g1, wp, wg)
    width = 3 * inner + 128
    return pl.pallas_call(
        lambda *refs: time_attention_backward_kernel(heads, *refs),
        grid=(slots, heads),
        out_shape=[
            jax.ShapeDtypeStruct((slots, frames, model), BF16),
            jax.ShapeDtypeStruct((model, width), BF16),
        ],
        in_specs=[pl.BlockSpec((1, 1, frames, frames), lambda s, h: (s, h, 0, 0))]
        + [per_slot(a) for a in (q, k, v, datt, minus, dlogit, n, x, dmid)]
        + [whole_spec(c) for c in consts],
        out_specs=[
            pl.BlockSpec((1, frames, model), lambda s, h: (s, 0, 0)),
            pl.BlockSpec((model, width), lambda s, h: (0, 0)),
        ],
        scratch_shapes=[
            pltpu.VMEM((3 * inner, frames), BF16),
            pltpu.VMEM((model, 3 * inner), F32),
            pltpu.VMEM((model, heads), F32),
            pltpu.VMEM((model, 1), F32),
        ],
        compiler_params=pltpu.CompilerParams(vmem_limit_bytes=VMEM_BYTES),
        name="time_attention_backward",
    )(p, q, k, v, datt, minus, dlogit, n, x, dmid, *consts)


def band_kernel(
    heads,
    x_ref,
    cot_ref,
    mask_ref,
    bias_ref,
    cos_ref,
    sin_ref,
    g1_ref,
    g2_ref,
    wpt_ref,
    wgt_ref,
    wot_ref,
    w1t_ref,
    w2t_ref,
    wp_ref,
    wg_ref,
    wo_ref,
    w1_ref,
    w2_ref,
    y_ref,
    dx_ref,
    sums_ref,
    q_ref,
    k_ref,
    v_ref,
    p_ref,
    gate_ref,
    linv_ref,
    att_ref,
    mixed_ref,
    act_ref,
    slope_ref,
    datt_ref,
    dmixed_ref,
    dlogit_ref,
    dproj_ref,
    dwp_ref,
    dw1_ref,
    dw2t_ref,
    dwot_ref,
    dwg_ref,
    dg1_ref,
    dg2_ref,
):
    step = pl.program_id(0)
    tokens, model = x_ref.shape
    inner = q_ref.shape[0]
    size = inner // heads
    groups = tokens // BLOCK

    @pl.when(step == 0)
    def clear():
        for ref in (dwp_ref, dw1_ref, dw2t_ref, dwot_ref, dwg_ref, dg1_ref, dg2_ref):
            ref[...] = jnp.zeros_like(ref)

    rows = x_ref[...].astype(F32).T
    normed = norm_forward(rows, g1_ref[...])
    q_ref[...], k_ref[...], v_ref[...] = project_block(
        normed, wpt_ref, cos_ref[...], sin_ref[...], inner, LOG2E * size**-0.5
    )
    gate_ref[...] = dg(wgt_ref[...], normed, NN)
    ones = extra_rows([jnp.ones((1, BLOCK), F32)], BLOCK)

    def attend(head, carry):
        at = pl.ds(pl.multiple_of(head * size, size), size)
        row = pl.ds(head, 1)
        for group in range(groups):
            lanes = slice(group * BLOCK, (group + 1) * BLOCK)
            scores = dg(k_ref[at, lanes], q_ref[at, lanes], TN) + bias_ref[...]
            weights = jnp.exp2(scores - jnp.max(scores, axis=0, keepdims=True)).astype(BF16)
            p_ref[head * groups + group] = weights
            sums = dg(jnp.concatenate([v_ref[at, lanes], ones], axis=0), weights, NN)
            inverse = 1.0 / sums[size : size + 1]
            attended = sums[:size] * inverse
            linv_ref[row, lanes] = inverse
            att_ref[at, lanes] = attended
            gate = jax.nn.sigmoid(gate_ref[row, lanes])
            mixed_ref[at, lanes] = (attended * gate).astype(BF16)
        return carry

    lax.fori_loop(0, heads, attend, 0)
    middle = rows + dg(wot_ref[...], mixed_ref[...], NN)
    normed_ffn = norm_forward(middle, g2_ref[...])

    hidden = w1t_ref.shape[0]
    part = hidden // 4

    def expand(i, carry):
        at = pl.ds(pl.multiple_of(i * part, part), part)
        active, slope = gelu_pair(dg(w1t_ref[at, :], normed_ffn, NN))
        act_ref[at, :] = active.astype(BF16)
        slope_ref[at, :] = slope.astype(BF16)
        return carry

    lax.fori_loop(0, 4, expand, 0)
    mask = mask_ref[0]
    result = (middle + dg(w2t_ref[...], act_ref[...], NN)) * mask
    y_ref[...] = result.T.astype(BF16)

    grad = cot_ref[...].astype(F32).T * mask
    d_middle = ffn_backward(
        grad, act_ref[...], slope_ref[...], normed_ffn, middle, g2_ref[...], w1_ref, w2_ref, dw1_ref, dw2t_ref, dg2_ref
    )
    branch = d_middle.astype(BF16)
    dwot_ref[...] += dg(branch, mixed_ref[...], NT)
    dmixed_ref[...] = dg(wo_ref[...], branch, NN)

    def attend_back(head, carry):
        start = pl.multiple_of(head * size, size)
        at = pl.ds(start, size)
        row = pl.ds(head, 1)
        d_att, minus, d_logit = head_backward(dmixed_ref[at, :], att_ref[at, :], gate_ref[row, :], linv_ref[row, :])
        dlogit_ref[row, :] = d_logit
        for group in range(groups):
            lanes = slice(group * BLOCK, (group + 1) * BLOCK)
            d_queries, d_keys, d_values = scores_backward(
                q_ref[at, lanes],
                k_ref[at, lanes],
                v_ref[at, lanes],
                p_ref[head * groups + group],
                d_att[:, lanes],
                minus[:, lanes],
                cos_ref[:, lanes],
                sin_ref[:, lanes],
                size**-0.5,
            )
            dproj_ref[at, lanes] = d_queries.astype(BF16)
            dproj_ref[pl.ds(inner + start, size), lanes] = d_keys.astype(BF16)
            dproj_ref[pl.ds(2 * inner + start, size), lanes] = d_values.astype(BF16)
        return carry

    lax.fori_loop(0, heads, attend_back, 0)
    d_logit = jnp.concatenate([dlogit_ref[...], jnp.zeros_like(dlogit_ref)], axis=0).astype(BF16)
    dwp_ref[...] += dg(normed, dproj_ref[...], NT)
    dwg_ref[...] += dg(normed, d_logit, NT)[:, :heads]
    d_normed = dg(wp_ref[...], dproj_ref[...], NN) + dg(wg_ref[...], dlogit_ref[...].astype(BF16), NN)
    d_rows, terms = norm_backward(rows, g1_ref[...], d_normed)
    dg1_ref[...] += jnp.sum(terms, axis=1, keepdims=True)
    dx_ref[...] = (d_middle + d_rows).T.astype(BF16)

    @pl.when(step == pl.num_programs(0) - 1)
    def finish():
        pack_sums(sums_ref, (dwp_ref, dw1_ref, dw2t_ref, dwot_ref, dwg_ref, dg1_ref, dg2_ref))


def band_layer(x, cot, mask, bias, cos, sin, params, turned):
    prenorm, project, gating, output_weight, midnorm, expand, shrink = params
    wpt, wgt, wot, w1t, w2t, g1, g2 = turned
    total, model = x.shape
    steps, _, tokens = mask.shape
    heads, inner, hidden = gating.shape[1], output_weight.shape[0], expand.shape[1]
    groups = tokens // BLOCK
    consts = (bias, cos, sin, g1, g2, wpt, wgt, wot, w1t, w2t, project, gating, output_weight, expand, shrink)
    width = 3 * inner + 2 * hidden + inner + 128
    rows = pl.BlockSpec((tokens, model), lambda i: (i, 0))
    return pl.pallas_call(
        lambda *refs: band_kernel(heads, *refs),
        grid=(steps,),
        out_shape=[
            jax.ShapeDtypeStruct((total, model), BF16),
            jax.ShapeDtypeStruct((total, model), BF16),
            jax.ShapeDtypeStruct((model, width), BF16),
        ],
        in_specs=[rows, rows, pl.BlockSpec((1, 1, tokens), lambda i: (i, 0, 0))] + [whole_spec(c) for c in consts],
        out_specs=[rows, rows, pl.BlockSpec((model, width), lambda i: (0, 0))],
        scratch_shapes=[
            pltpu.VMEM((inner, tokens), BF16),
            pltpu.VMEM((inner, tokens), BF16),
            pltpu.VMEM((inner, tokens), BF16),
            pltpu.VMEM((heads * groups, BLOCK, BLOCK), BF16),
            pltpu.VMEM((heads, tokens), F32),
            pltpu.VMEM((heads, tokens), F32),
            pltpu.VMEM((inner, tokens), F32),
            pltpu.VMEM((inner, tokens), BF16),
            pltpu.VMEM((hidden, tokens), BF16),
            pltpu.VMEM((hidden, tokens), BF16),
            pltpu.VMEM((inner, tokens), BF16),
            pltpu.VMEM((inner, tokens), F32),
            pltpu.VMEM((heads, tokens), F32),
            pltpu.VMEM((3 * inner, tokens), BF16),
            pltpu.VMEM((model, 3 * inner), F32),
            pltpu.VMEM((model, hidden), F32),
            pltpu.VMEM((model, hidden), F32),
            pltpu.VMEM((model, inner), F32),
            pltpu.VMEM((model, heads), F32),
            pltpu.VMEM((model, 1), F32),
            pltpu.VMEM((model, 1), F32),
        ],
        compiler_params=pltpu.CompilerParams(vmem_limit_bytes=VMEM_BYTES),
        name="band_layer",
    )(x, cot, mask, *consts)


def turned_params(params):
    prenorm, project, gating, output_weight, midnorm, expand, shrink = params
    return (
        project.T,
        gating.T,
        output_weight.T,
        expand.T,
        shrink.T,
        prenorm.astype(F32)[:, None],
        midnorm.astype(F32)[:, None],
    )


def slot_shards(activations, cotangent, frame_counts, slot_bands, *weights):
    slot_dev, _, frame_dev, model = activations.shape
    slot_count = slot_bands.shape[0]
    batch, band = lax.axis_size("batch"), lax.axis_size("band")
    frames = frame_dev * batch
    piece = frame_dev // band
    slots = slot_dev // batch
    time_params, band_params = weights[:7], weights[7:]
    heads, inner, hidden = time_params[2].shape[1], time_params[3].shape[0], time_params[5].shape[1]
    size = inner // heads

    positions = jnp.arange(frames, dtype=jnp.int32)
    time_cos, time_sin = rotary_tables(positions.astype(F32), size)
    time_bias = jnp.where(positions[None, :] < frame_counts[:, None], 0.0, NEG_FILL).astype(F32)
    band_cos, band_sin = rotary_tables(jnp.maximum(slot_bands, 0).astype(F32), size)
    tokens = min(2 * BLOCK, piece * slot_count)
    copies = tokens // slot_count
    slot_valid = slot_bands >= 0
    index = jnp.arange(BLOCK, dtype=jnp.int32)
    together = (index[:, None] // slot_count == index[None, :] // slot_count) & jnp.tile(
        slot_valid, BLOCK // slot_count
    )[:, None]
    band_bias = jnp.where(together, 0.0, NEG_FILL).astype(F32)
    own_start = lax.axis_index("batch") * frame_dev + lax.axis_index("band") * piece
    own_frames = own_start + jnp.arange(piece, dtype=jnp.int32)
    mask = ((own_frames < frame_counts[0])[:, None] & slot_valid[None, :]).astype(F32)
    mask = mask.reshape(piece * slot_count // tokens, 1, tokens)

    time_turned = turned_params(time_params)
    band_turned = turned_params(band_params)
    rows = lax.all_to_all(
        activations.reshape(slot_dev, frame_dev, model), "batch", split_axis=0, concat_axis=1, tiled=True
    )
    cot_rows = lax.all_to_all(
        cotangent.reshape(slot_dev, frame_dev, model), "band", split_axis=1, concat_axis=0, tiled=True
    )
    cot_rows = cot_rows.transpose(1, 0, 2).reshape(piece * slot_count, model)
    wpt, wgt, wot, w1t, w2t, g1, g2 = time_turned
    result, n, q, k, v, p, linv, gate, att, mixed, mid, nf, act, slope = time_forward(
        rows, time_bias, time_cos.T, time_sin.T, g1, g2, wpt, wgt, wot, w1t, w2t
    )
    result = result.reshape(slots, batch, band, piece, model).transpose(0, 2, 1, 3, 4)
    frame_rows = lax.all_to_all(
        result.reshape(slots, frames, model), ("band", "batch"), split_axis=1, concat_axis=0, tiled=True
    )
    frame_rows = frame_rows.transpose(1, 0, 2).reshape(piece * slot_count, model)
    y, dx, band_sums = band_layer(
        frame_rows,
        cot_rows,
        mask,
        band_bias,
        jnp.tile(band_cos.T, (1, copies)),
        jnp.tile(band_sin.T, (1, copies)),
        band_params,
        band_turned,
    )
    band_sums = lax.psum(band_sums, ("band", "batch"))
    dx = dx.reshape(piece, slot_count, model).transpose(1, 0, 2)
    slot_grad = lax.all_to_all(dx, ("band", "batch"), split_axis=0, concat_axis=1, tiled=True)
    slot_grad = slot_grad.reshape(slots, band, batch, piece, model).transpose(0, 2, 1, 3, 4)
    slot_grad = slot_grad.reshape(slots, frames, model)
    y = y.reshape(piece, slot_count, model).transpose(1, 0, 2)
    layer_output = lax.all_to_all(y, "band", split_axis=0, concat_axis=1, tiled=True)
    dmid, datt, minus, dlogit, ffn_sums = time_ffn_backward(
        slot_grad, act, slope, nf, mid, mixed, att, gate, linv, g2, time_params[5], time_params[6], time_params[3]
    )
    ffn_sums = lax.psum(ffn_sums, ("band", "batch"))
    grads, attn_sums = time_attention_backward(
        p, q, k, v, datt, minus, dlogit, n, rows, dmid, time_cos.T, time_sin.T, g1, time_params[1], time_params[2]
    )
    input_grad = lax.all_to_all(grads, "batch", split_axis=1, concat_axis=0, tiled=True)
    attn_sums = lax.psum(attn_sums, ("band", "batch"))

    def cut(sums, widths):
        parts, at = [], 0
        for width in widths:
            parts.append(sums[:, at : at + width].astype(F32))
            at += width
        return parts

    dwp, dwg, dg1 = cut(attn_sums, (3 * inner, heads, 1))
    dw1, dw2t, dwot, dg2 = cut(ffn_sums, (hidden, hidden, inner, 1))
    bwp, bw1, bw2t, bwot, bwg, bg1, bg2 = cut(band_sums, (3 * inner, hidden, hidden, inner, heads, 1, 1))
    return (
        layer_output.reshape(activations.shape),
        input_grad.astype(F32).reshape(activations.shape),
        dg1[:, 0],
        dwp,
        dwg,
        dwot.T,
        dg2[:, 0],
        dw1,
        dw2t.T,
        bg1[:, 0],
        bwp,
        bwg,
        bwot.T,
        bg2[:, 0],
        bw1,
        bw2t.T,
    )


def shards(activations, cotangent, frame_counts, slot_bands, *weights):
    slot_dev, clips, frame_dev, _ = activations.shape
    batch, band = lax.axis_size("batch"), lax.axis_size("band")
    fits = (
        clips == 1
        and slot_dev % batch == 0
        and frame_dev % band == 0
        and (frame_dev * batch) % (2 * BLOCK) == 0
        and BLOCK % slot_bands.shape[0] == 0
        and (frame_dev // band * slot_bands.shape[0]) % (2 * BLOCK) == 0
        and weights[2].shape[1] == 8
    )
    form = slot_shards if fits else generic_shards
    return form(activations, cotangent, frame_counts, slot_bands, *weights)


def solution(mesh):
    return jax.shard_map(
        shards,
        mesh=mesh,
        in_specs=(
            P("band", None, "batch", None),
            P("band", None, "batch", None),
            P(),
            P(),
            P(),
            P(),
            P(),
            P(),
            P(),
            P(),
            P(),
            P(),
            P(),
            P(),
            P(),
            P(),
            P(),
            P(),
        ),
        out_specs=(
            P("band", None, "batch", None),
            P("band", None, "batch", None),
            P(),
            P(),
            P(),
            P(),
            P(),
            P(),
            P(),
            P(),
            P(),
            P(),
            P(),
            P(),
            P(),
            P(),
        ),
        check_vma=False,
    )
```

```python
import math

import jax
import jax.numpy as jnp
from jax import lax
from jax.experimental import pallas as pl
from jax.experimental.pallas import tpu as pltpu
from jax.sharding import PartitionSpec as P

EPSILON = 1e-05
NEG_FILL = -1000000000.0
TIME_LAYOUT = ("bqhe", "bkhe")
BAND_LAYOUT = ("qbhe", "kbhe")


def rms_scale(residual, gain):
    return (
        residual * lax.rsqrt(jnp.mean(residual * residual, axis=-1, keepdims=True) + EPSILON) * gain
    )


def gelu_exact(values):
    return jax.nn.gelu(values, approximate=False)


def rotary_tables(positions, head_size):
    half_size = head_size // 2
    rates = jnp.exp(-math.log(10000.0) * jnp.arange(half_size, dtype=jnp.float32) / half_size)
    angles = positions[:, None] * rates[None, :]
    return (jnp.cos(angles), jnp.sin(angles))


def rotate(vectors, cos_table, sin_table):
    half_size = vectors.shape[-1] // 2
    first = vectors[..., :half_size]
    second = vectors[..., half_size:]
    return jnp.concatenate(
        [first * cos_table - second * sin_table, first * sin_table + second * cos_table], axis=-1
    )


def token_sum(left, right):
    return lax.dot_general(
        left.reshape(-1, left.shape[-1]),
        right.reshape(-1, right.shape[-1]),
        (((0,), (0,)), ((), ())),
        preferred_element_type=jnp.float32,
    )


def back_dot(gradient, weight):
    return lax.dot_general(
        gradient,
        weight,
        (((gradient.ndim - 1,), (1,)), ((), ())),
        preferred_element_type=jnp.float32,
    )


def block_forward(queries, key_rows, value_rows, key_valid, layout):
    query_form, key_form = layout
    scores = (
        jnp.einsum(
            query_form + "," + key_form + "->bhqk",
            queries,
            key_rows,
            preferred_element_type=jnp.float32,
        )
        * 0.125
    )
    scores = jnp.where(key_valid[:, None, None, :], scores, NEG_FILL)
    highest = jnp.max(scores, axis=-1, keepdims=True)
    exponents = jnp.exp(scores - highest)
    totals = jnp.sum(exponents, axis=-1, keepdims=True)
    soft_weights = (exponents / totals).astype(jnp.bfloat16)
    output = jnp.einsum(
        "bhqk," + key_form + "->" + query_form,
        soft_weights,
        value_rows,
        preferred_element_type=jnp.float32,
    )
    return (output, highest + jnp.log(totals))


def block_backward(queries, key_rows, value_rows, key_valid, log_totals, out_grad, layout):
    query_form, key_form = layout
    scores = (
        jnp.einsum(
            query_form + "," + key_form + "->bhqk",
            queries,
            key_rows,
            preferred_element_type=jnp.float32,
        )
        * 0.125
    )
    soft_weights = jnp.where(key_valid[:, None, None, :], jnp.exp(scores - log_totals), 0.0)
    weight_grad = jnp.einsum(
        query_form + "," + key_form + "->bhqk",
        out_grad,
        value_rows,
        preferred_element_type=jnp.float32,
    )
    score_grad = (
        soft_weights * (weight_grad - jnp.sum(soft_weights * weight_grad, axis=-1, keepdims=True))
    ).astype(jnp.bfloat16)
    query_grad = (
        jnp.einsum(
            "bhqk," + key_form + "->" + query_form,
            score_grad,
            key_rows,
            preferred_element_type=jnp.float32,
        )
        * 0.125
    )
    key_grad = (
        jnp.einsum(
            "bhqk," + query_form + "->" + key_form,
            score_grad,
            queries,
            preferred_element_type=jnp.float32,
        )
        * 0.125
    )
    value_grad = jnp.einsum(
        "bhqk," + query_form + "->" + key_form,
        soft_weights.astype(jnp.bfloat16),
        out_grad,
        preferred_element_type=jnp.float32,
    )
    return (query_grad, key_grad, value_grad)


def time_attend(queries, key_rows, value_rows, key_valid):
    keys_full, values_full = (
        lax.all_gather(key_rows, "batch", axis=1, tiled=True),
        lax.all_gather(value_rows, "batch", axis=1, tiled=True),
    )
    output, log_totals = block_forward(queries, keys_full, values_full, key_valid, TIME_LAYOUT)
    return (output, (log_totals, keys_full, values_full))


def time_attend_back(queries, key_rows, value_rows, key_valid, attn_kept, out_grad):
    log_totals, keys_full, values_full = attn_kept
    query_grad, key_full_grad, value_full_grad = block_backward(
        queries, keys_full, values_full, key_valid, log_totals, out_grad, TIME_LAYOUT
    )
    key_grad, value_grad = (
        lax.psum_scatter(
            key_full_grad.astype(jnp.bfloat16), "batch", scatter_dimension=1, tiled=True
        ).astype(jnp.float32),
        lax.psum_scatter(
            value_full_grad.astype(jnp.bfloat16), "batch", scatter_dimension=1, tiled=True
        ).astype(jnp.float32),
    )
    return (query_grad, key_grad, value_grad)


def band_attend(queries, key_rows, value_rows, key_valid):
    return block_forward(queries, key_rows, value_rows, key_valid, BAND_LAYOUT)


def band_attend_back(queries, key_rows, value_rows, key_valid, attn_kept, out_grad):
    return block_backward(
        queries, key_rows, value_rows, key_valid, attn_kept, out_grad, BAND_LAYOUT
    )


def layer_forward(residual, params, tables, key_valid, attend):
    prenorm, project, gating, output_weight, midnorm, expand, shrink = params
    cos_table, sin_table = tables
    normed = rms_scale(residual, prenorm.astype(jnp.float32)).astype(jnp.bfloat16)
    projected = jnp.dot(normed, project, preferred_element_type=jnp.float32)
    gate_logits = jnp.dot(normed, gating, preferred_element_type=jnp.float32)
    inner_width = output_weight.shape[0]
    head_count = gating.shape[1]
    head_shape = residual.shape[:-1] + (head_count, inner_width // head_count)
    queries = rotate(projected[..., :inner_width].reshape(head_shape), cos_table, sin_table).astype(
        jnp.bfloat16
    )
    key_rows = rotate(
        projected[..., inner_width : 2 * inner_width].reshape(head_shape), cos_table, sin_table
    ).astype(jnp.bfloat16)
    value_rows = projected[..., 2 * inner_width :].reshape(head_shape).astype(jnp.bfloat16)
    attended, attn_kept = attend(queries, key_rows, value_rows, key_valid)
    gate_values = jax.nn.sigmoid(gate_logits)
    mixed_heads = (
        (attended * gate_values[..., None])
        .reshape(residual.shape[:-1] + (inner_width,))
        .astype(jnp.bfloat16)
    )
    middle = residual + jnp.dot(mixed_heads, output_weight, preferred_element_type=jnp.float32)
    normed_ffn = rms_scale(middle, midnorm.astype(jnp.float32)).astype(jnp.bfloat16)
    hidden = jnp.dot(normed_ffn, expand, preferred_element_type=jnp.float32)
    active = gelu_exact(hidden).astype(jnp.bfloat16)
    result = middle + jnp.dot(active, shrink, preferred_element_type=jnp.float32)
    kept_values = (
        residual,
        normed,
        gate_logits,
        queries,
        key_rows,
        value_rows,
        attn_kept,
        attended,
        mixed_heads,
        middle,
        normed_ffn,
        hidden,
        active,
    )
    return (result, kept_values)


def layer_backward(result_grad, params, kept_values, tables, key_valid, attend_back):
    prenorm, project, gating, output_weight, midnorm, expand, shrink = params
    (
        residual,
        normed,
        gate_logits,
        queries,
        key_rows,
        value_rows,
        attn_kept,
        attended,
        mixed_heads,
        middle,
        normed_ffn,
        hidden,
        active,
    ) = kept_values
    cos_table, sin_table = tables
    branch_grad = result_grad.astype(jnp.bfloat16)
    shrink_grad = token_sum(active, branch_grad)
    active_grad = back_dot(branch_grad, shrink)
    hidden_grad = jax.vjp(gelu_exact, hidden)[1](active_grad)[0].astype(jnp.bfloat16)
    expand_grad = token_sum(normed_ffn, hidden_grad)
    normed_ffn_grad = back_dot(hidden_grad, expand)
    middle_norm_grad, midnorm_grad = jax.vjp(rms_scale, middle, midnorm.astype(jnp.float32))[1](
        normed_ffn_grad
    )
    middle_grad = result_grad + middle_norm_grad
    attn_branch = middle_grad.astype(jnp.bfloat16)
    output_grad = token_sum(mixed_heads, attn_branch)
    mixed_grad = back_dot(attn_branch, output_weight).reshape(attended.shape)
    gate_values = jax.nn.sigmoid(gate_logits)
    attended_grad = (mixed_grad * gate_values[..., None]).astype(jnp.bfloat16)
    logit_grad = (
        jnp.sum(mixed_grad * attended, axis=-1) * gate_values * (1.0 - gate_values)
    ).astype(jnp.bfloat16)
    query_grad, key_grad, value_grad = attend_back(
        queries, key_rows, value_rows, key_valid, attn_kept, attended_grad
    )
    flat_shape = residual.shape[:-1] + (-1,)
    projected_grad = jnp.concatenate(
        [
            rotate(query_grad, cos_table, -sin_table).reshape(flat_shape),
            rotate(key_grad, cos_table, -sin_table).reshape(flat_shape),
            value_grad.reshape(flat_shape),
        ],
        axis=-1,
    ).astype(jnp.bfloat16)
    project_grad = token_sum(normed, projected_grad)
    gating_grad = token_sum(normed, logit_grad)
    normed_grad = back_dot(projected_grad, project) + back_dot(logit_grad, gating)
    residual_norm_grad, prenorm_grad = jax.vjp(rms_scale, residual, prenorm.astype(jnp.float32))[1](
        normed_grad
    )
    return (
        middle_grad + residual_norm_grad,
        (
            prenorm_grad,
            project_grad,
            gating_grad,
            output_grad,
            midnorm_grad,
            expand_grad,
            shrink_grad,
        ),
    )


def generic_shards(
    activations,
    cotangent,
    frame_counts,
    slot_bands,
    time_prenorm,
    time_project,
    time_gating,
    time_output,
    time_midnorm,
    time_expand,
    time_shrink,
    band_prenorm,
    band_project,
    band_gating,
    band_output,
    band_midnorm,
    band_expand,
    band_shrink,
):
    slot_dev, clip_count, frame_dev, model_width = activations.shape
    slot_count = slot_bands.shape[0]
    frames_all = frame_dev * lax.axis_size("batch")
    head_size = time_output.shape[0] // time_gating.shape[1]
    time_params = (
        time_prenorm,
        time_project,
        time_gating,
        time_output,
        time_midnorm,
        time_expand,
        time_shrink,
    )
    band_params = (
        band_prenorm,
        band_project,
        band_gating,
        band_output,
        band_midnorm,
        band_expand,
        band_shrink,
    )
    own_bands = lax.dynamic_slice_in_dim(slot_bands, lax.axis_index("band") * slot_dev, slot_dev)
    frame_start = lax.axis_index("batch") * frame_dev
    own_frames = frame_start + jnp.arange(frame_dev, dtype=jnp.int32)
    frame_valid = own_frames[None, :] < frame_counts[:, None]
    row_valid = (own_bands >= 0)[:, None, None] & frame_valid[None]
    full_valid = jnp.arange(frames_all, dtype=jnp.int32)[None, :] < frame_counts[:, None]
    time_valid = jnp.broadcast_to(full_valid[None], (slot_dev, clip_count, frames_all)).reshape(
        slot_dev * clip_count, frames_all
    )
    time_cos, time_sin = rotary_tables(own_frames.astype(jnp.float32), head_size)
    time_tables = (time_cos[None, :, None, :], time_sin[None, :, None, :])
    band_cos, band_sin = rotary_tables(jnp.maximum(slot_bands, 0).astype(jnp.float32), head_size)
    band_tables = (band_cos[:, None, None, :], band_sin[:, None, None, :])
    residual = activations.astype(jnp.float32).reshape(
        slot_dev * clip_count, frame_dev, model_width
    )
    time_result, time_kept = layer_forward(
        residual, time_params, time_tables, time_valid, time_attend
    )
    masked_cot = jnp.where(row_valid[..., None], cotangent, jnp.zeros((), jnp.bfloat16)).reshape(
        slot_dev, clip_count * frame_dev, model_width
    )
    frame_rows = lax.all_to_all(
        time_result.astype(jnp.bfloat16), "band", split_axis=1, concat_axis=0, tiled=True
    ).astype(time_result.dtype)
    band_valid = jnp.broadcast_to((slot_bands >= 0)[None, :], (frame_rows.shape[1], slot_count))
    band_result, band_kept = layer_forward(
        frame_rows, band_params, band_tables, band_valid, band_attend
    )
    back_rows = lax.all_to_all(
        band_result.astype(jnp.bfloat16), "band", split_axis=0, concat_axis=1, tiled=True
    ).astype(band_result.dtype)
    layer_output = jnp.where(
        row_valid[..., None], back_rows.reshape(activations.shape), 0.0
    ).astype(jnp.bfloat16)
    frame_cot = lax.all_to_all(masked_cot, "band", split_axis=1, concat_axis=0, tiled=True)
    frame_grad, band_grads = layer_backward(
        frame_cot.astype(jnp.float32),
        band_params,
        band_kept,
        band_tables,
        band_valid,
        band_attend_back,
    )
    slot_grad = lax.all_to_all(
        frame_grad.astype(jnp.bfloat16), "band", split_axis=0, concat_axis=1, tiled=True
    ).astype(frame_grad.dtype)
    input_grad, time_grads = layer_backward(
        slot_grad, time_params, time_kept, time_tables, time_valid, time_attend_back
    )
    input_grad = input_grad.reshape(activations.shape)
    all_grads = lax.psum(
        (
            time_grads[0],
            time_grads[1],
            time_grads[2],
            time_grads[3],
            time_grads[4],
            time_grads[5],
            time_grads[6],
            band_grads[0],
            band_grads[1],
            band_grads[2],
            band_grads[3],
            band_grads[4],
            band_grads[5],
            band_grads[6],
        ),
        ("band", "batch"),
    )
    return (
        layer_output,
        input_grad,
        all_grads[0],
        all_grads[1],
        all_grads[2],
        all_grads[3],
        all_grads[4],
        all_grads[5],
        all_grads[6],
        all_grads[7],
        all_grads[8],
        all_grads[9],
        all_grads[10],
        all_grads[11],
        all_grads[12],
        all_grads[13],
    )


BLOCK = 256
LOG2E = 1.4426950408889634
F32 = jnp.float32
BF16 = jnp.bfloat16
NN = (((1,), (0,)), ((), ()))
NT = (((1,), (1,)), ((), ()))
TN = (((0,), (0,)), ((), ()))
VMEM_BYTES = 60 * 2**20


def dg(left, right, dims):
    return lax.dot_general(left, right, dims, preferred_element_type=F32)


def norm_forward(rows, gain):
    scale = lax.rsqrt(jnp.mean(rows * rows, axis=0, keepdims=True) + EPSILON)
    return (rows * scale * gain).astype(BF16)


def norm_backward(rows, gain, grad):
    scale = lax.rsqrt(jnp.mean(rows * rows, axis=0, keepdims=True) + EPSILON)
    unit = rows * scale
    scaled = grad * gain
    inner = jnp.mean(scaled * unit, axis=0, keepdims=True)
    return scale * (scaled - unit * inner), grad * unit


def gelu_pair(values):
    size = jnp.abs(values)
    denominator = 1.0 + (0.3275911 * math.sqrt(0.5)) * size
    t = pl.reciprocal(denominator, approx=True)
    t = t * (2.0 - denominator * t)
    bell = jnp.exp2(values * values * (-0.5 * LOG2E))
    poly = 0.5 * 1.061405429
    for coefficient in (-1.453152027, 1.421413741, -0.284496736, 0.254829592):
        poly = poly * t + 0.5 * coefficient
    tail = poly * t * bell
    upper = jnp.where(values < 0.0, tail, 1.0 - tail)
    slope = upper + values * bell * (1.0 / math.sqrt(2.0 * math.pi))
    return values * upper, slope


def turn(vectors, cos, sin):
    half = cos.shape[0]
    split = vectors.reshape(-1, 2 * half, vectors.shape[-1])
    first = split[:, :half]
    second = split[:, half:]
    turned = jnp.concatenate([first * cos - second * sin, first * sin + second * cos], axis=1)
    return turned.reshape(vectors.shape)


def three_parts(values):
    top = values.astype(BF16).astype(F32)
    rest = values - top
    middle = rest.astype(BF16).astype(F32)
    return top, middle, rest - middle


def extra_rows(rows, width):
    tile = jnp.concatenate(rows + [jnp.zeros((8 - len(rows), width), F32)], axis=0)
    return jnp.concatenate([tile, jnp.zeros((8, width), F32)], axis=0).astype(BF16)


def project_block(normed, wpt_ref, cos, sin, inner, scale):
    queries = turn(dg(wpt_ref[0:inner, :], normed, NN), cos, sin) * scale
    keys = turn(dg(wpt_ref[inner : 2 * inner, :], normed, NN), cos, sin)
    values = dg(wpt_ref[2 * inner : 3 * inner, :], normed, NN)
    return queries.astype(BF16), keys.astype(BF16), values.astype(BF16)


def time_forward_kernel(
    heads,
    x_ref,
    bias_ref,
    cos_ref,
    sin_ref,
    g1_ref,
    g2_ref,
    wpt_ref,
    wgt_ref,
    wot_ref,
    w1t_ref,
    w2t_ref,
    result_ref,
    n_ref,
    q_ref,
    k_ref,
    v_ref,
    p_ref,
    linv_ref,
    gate_ref,
    att_ref,
    mixed_ref,
    mid_ref,
    nf_ref,
    act_ref,
    slope_ref,
    xt_ref,
):
    head = pl.program_id(1)
    frames, model = x_ref.shape[1:]
    inner = q_ref.shape[1]
    size = inner // heads

    @pl.when(head == 0)
    def before():
        def block(i, carry):
            at = pl.ds(pl.multiple_of(i * BLOCK, BLOCK), BLOCK)
            rows = x_ref[0, at, :].astype(F32).T
            xt_ref[:, at] = rows
            normed = norm_forward(rows, g1_ref[...])
            n_ref[0, :, at] = normed
            queries, keys, values = project_block(
                normed, wpt_ref, cos_ref[:, at], sin_ref[:, at], inner, LOG2E * size**-0.5
            )
            q_ref[0, :, at] = queries
            k_ref[0, :, at] = keys
            v_ref[0, :, at] = values
            gate_ref[0, :, at] = dg(wgt_ref[...], normed, NN)
            return carry

        lax.fori_loop(0, frames // BLOCK, block, 0)

    at_head = pl.ds(pl.multiple_of(head * size, size), size)
    ones = jnp.ones((1, frames), F32)
    queries = jnp.concatenate([q_ref[0, at_head, :], extra_rows([ones], frames)], axis=0)
    keys = jnp.concatenate([k_ref[0, at_head, :], extra_rows([bias_ref[...]], frames)], axis=0)
    values = jnp.concatenate([v_ref[0, at_head, :], extra_rows([ones], frames)], axis=0)
    scores = dg(keys, queries, TN)
    weights = jnp.exp2(scores - jnp.max(scores, axis=0, keepdims=True)).astype(BF16)
    p_ref[0, 0] = weights
    sums = dg(values, weights, NN)
    inverse = 1.0 / sums[size : size + 1]
    attended = sums[:size] * inverse
    linv_ref[0, pl.ds(head, 1), :] = inverse
    att_ref[0, at_head, :] = attended
    gate = jax.nn.sigmoid(gate_ref[0, pl.ds(head, 1), :])
    mixed_ref[0, at_head, :] = (attended * gate).astype(BF16)

    @pl.when(head == heads - 1)
    def after():
        def block(i, carry):
            at = pl.ds(pl.multiple_of(i * BLOCK, BLOCK), BLOCK)
            middle = xt_ref[:, at] + dg(wot_ref[...], mixed_ref[0, :, at], NN)
            mid_ref[0, :, at] = middle
            normed = norm_forward(middle, g2_ref[...])
            nf_ref[0, :, at] = normed
            active, slope = gelu_pair(dg(w1t_ref[...], normed, NN))
            active = active.astype(BF16)
            act_ref[0, :, at] = active
            slope_ref[0, :, at] = slope.astype(BF16)
            result = middle + dg(w2t_ref[...], active, NN)
            result_ref[0, at, :] = result.T.astype(BF16)
            return carry

        lax.fori_loop(0, frames // BLOCK, block, 0)


def sum_shapes(*shapes):
    return [jax.ShapeDtypeStruct(shape, BF16) for shape in shapes]


def sum_specs(*shapes):
    return [pl.BlockSpec(shape, lambda *ids: (0, 0)) for shape in shapes]


def cost(flops, exps=0, moved=0):
    return pl.CostEstimate(flops=int(flops), bytes_accessed=int(moved), transcendentals=int(exps))


def whole_spec(array):
    nd = array.ndim
    return pl.BlockSpec(array.shape, lambda *ids: (0,) * nd, pipeline_mode=pl.Buffered(1))


def time_forward(rows, bias, cos, sin, g1, g2, wpt, wgt, wot, w1t, w2t):
    slots, frames, model = rows.shape
    heads = wgt.shape[0]
    inner = wot.shape[1]
    hidden = w1t.shape[0]

    def per_slot(*shape):
        return pl.BlockSpec((1,) + shape, lambda s, h: (s,) + (0,) * len(shape))

    outs = [
        ((frames, model), BF16),
        ((model, frames), BF16),
        ((inner, frames), BF16),
        ((inner, frames), BF16),
        ((inner, frames), BF16),
        None,
        ((heads, frames), F32),
        ((heads, frames), F32),
        ((inner, frames), F32),
        ((inner, frames), BF16),
        ((model, frames), F32),
        ((model, frames), BF16),
        ((hidden, frames), BF16),
        ((hidden, frames), BF16),
    ]
    shapes, specs = [], []
    for entry in outs:
        if entry is None:
            shapes.append(jax.ShapeDtypeStruct((slots, heads, frames, frames), BF16))
            specs.append(pl.BlockSpec((1, 1, frames, frames), lambda s, h: (s, h, 0, 0)))
        else:
            shapes.append(jax.ShapeDtypeStruct((slots,) + entry[0], entry[1]))
            specs.append(per_slot(*entry[0]))
    consts = (bias, cos, sin, g1, g2, wpt, wgt, wot, w1t, w2t)
    return pl.pallas_call(
        lambda *refs: time_forward_kernel(heads, *refs),
        grid=(slots, heads),
        out_shape=shapes,
        in_specs=[per_slot(frames, model)] + [whole_spec(c) for c in consts],
        out_specs=specs,
        scratch_shapes=[pltpu.VMEM((model, frames), F32)],
        compiler_params=pltpu.CompilerParams(vmem_limit_bytes=VMEM_BYTES),
        cost_estimate=cost(2.0e6 * 4 * slots * frames, 2 * slots * heads * frames * frames, 60e6),
        name="time_forward",
    )(rows, *consts)


def ffn_backward(grad, act, slope, normed, middle, gain, w1_ref, w2_ref, dw1_ref, dw2t_ref, dg2_ref):
    branch = grad.astype(BF16)
    d_hidden = (dg(w2_ref[...], branch, NN) * slope.astype(F32)).astype(BF16)
    dw2t_ref[...] += dg(branch, act, NT)
    dw1_ref[...] += dg(normed, d_hidden, NT)
    d_normed = dg(w1_ref[...], d_hidden, NN)
    d_rows, terms = norm_backward(middle, gain, d_normed)
    dg2_ref[...] += jnp.sum(terms, axis=1, keepdims=True)
    return grad + d_rows


def head_backward(d_mixed, attended, gate_logit, inverse):
    gate = jax.nn.sigmoid(gate_logit)
    d_logit = jnp.sum(d_mixed * attended, axis=0, keepdims=True) * gate * (1.0 - gate)
    d_att = (d_mixed * (gate * inverse)).astype(BF16)
    minus = -jnp.sum(d_att.astype(F32) * attended, axis=0, keepdims=True)
    return d_att, minus, d_logit


def scores_backward(queries, keys, values, weights, d_att, minus, cos, sin, scale):
    width = queries.shape[1]
    ones = jnp.ones((1, width), F32)
    d_weights = dg(
        jnp.concatenate([values, extra_rows([ones, ones, ones], width)], axis=0),
        jnp.concatenate([d_att, extra_rows(list(three_parts(minus)), width)], axis=0),
        TN,
    )
    d_scores = (weights.astype(F32) * d_weights).astype(BF16)
    d_values = dg(d_att, weights, NT)
    d_queries = dg(keys, d_scores, NN) * scale
    d_keys = dg(queries, d_scores, NT) * (1.0 / LOG2E)
    return turn(d_queries, cos, -sin), turn(d_keys, cos, -sin), d_values


def time_ffn_backward_kernel(
    heads,
    grad_ref,
    act_ref,
    slope_ref,
    nf_ref,
    mid_ref,
    mixed_ref,
    att_ref,
    gate_ref,
    linv_ref,
    g2_ref,
    w1_ref,
    w2_ref,
    wo_ref,
    dmid_ref,
    datt_ref,
    minus_ref,
    dlogit_ref,
    *refs,
):
    sums_refs, (dw1_ref, dw2t_ref, dwot_ref, dg2_ref) = refs[:4], refs[4:]
    step = pl.program_id(0) * pl.num_programs(1) + pl.program_id(1)
    last = pl.num_programs(0) * pl.num_programs(1) - 1
    size = wo_ref.shape[0] // heads

    @pl.when(step == 0)
    def clear():
        for ref in (dw1_ref, dw2t_ref, dwot_ref, dg2_ref):
            ref[...] = jnp.zeros_like(ref)

    grad = grad_ref[0].astype(F32).T
    d_middle = ffn_backward(
        grad, act_ref[0], slope_ref[0], nf_ref[0], mid_ref[0], g2_ref[...], w1_ref, w2_ref, dw1_ref, dw2t_ref, dg2_ref
    )
    dmid_ref[0] = d_middle
    branch = d_middle.astype(BF16)
    dwot_ref[...] += dg(branch, mixed_ref[0], NT)
    d_mixed = dg(wo_ref[...], branch, NN)
    logits, minuses = [], []
    for head in range(heads):
        at = slice(head * size, (head + 1) * size)
        d_att, minus, d_logit = head_backward(
            d_mixed[at], att_ref[0, at], gate_ref[0, head : head + 1], linv_ref[0, head : head + 1]
        )
        datt_ref[0, at] = d_att
        minuses.append(minus)
        logits.append(d_logit)
    minus_ref[0] = jnp.concatenate(minuses, axis=0)
    dlogit_ref[0] = jnp.concatenate(logits, axis=0)

    @pl.when(step == last)
    def finish():
        finish_sums(sums_refs, ((dw1_ref, False), (dw2t_ref, True), (dwot_ref, True), dg2_ref))


def finish_sums(outs, parts):
    narrow = []
    for out_ref, (ref, flipped) in zip(outs[:-1], parts):
        out_ref[...] = (ref[...].T if flipped else ref[...]).astype(BF16)
    for ref in parts[len(outs) - 1 :]:
        narrow.append(ref[...])
    used = sum(part.shape[1] for part in narrow)
    narrow.append(jnp.zeros((outs[-1].shape[0], 128 - used), F32))
    outs[-1][...] = jnp.concatenate(narrow, axis=1).astype(BF16)


def time_ffn_backward(grad, act, slope, nf, mid, mixed, att, gate, linv, g2, w1, w2, wo):
    slots, frames, model = grad.shape
    heads = gate.shape[1]
    inner, hidden = wo.shape[0], w1.shape[1]
    tokens = min(frames, 512)

    def cut(rows):
        return pl.BlockSpec((1, rows, tokens), lambda s, c: (s, 0, c))

    consts = (g2, w1, w2, wo)
    sums = ((model, hidden), (hidden, model), (inner, model), (model, 128))
    return pl.pallas_call(
        lambda *refs: time_ffn_backward_kernel(heads, *refs),
        grid=(slots, frames // tokens),
        out_shape=[
            jax.ShapeDtypeStruct((slots, model, frames), F32),
            jax.ShapeDtypeStruct((slots, inner, frames), BF16),
            jax.ShapeDtypeStruct((slots, heads, frames), F32),
            jax.ShapeDtypeStruct((slots, heads, frames), F32),
        ]
        + sum_shapes(*sums),
        in_specs=[pl.BlockSpec((1, tokens, model), lambda s, c: (s, c, 0))]
        + [cut(a.shape[1]) for a in (act, slope, nf, mid, mixed, att, gate, linv)]
        + [whole_spec(c) for c in consts],
        out_specs=[cut(model), cut(inner), cut(heads), cut(heads)] + sum_specs(*sums),
        scratch_shapes=[
            pltpu.VMEM((model, hidden), F32),
            pltpu.VMEM((model, hidden), F32),
            pltpu.VMEM((model, inner), F32),
            pltpu.VMEM((model, 1), F32),
        ],
        compiler_params=pltpu.CompilerParams(vmem_limit_bytes=VMEM_BYTES),
        cost_estimate=cost(8.0e6 * slots * frames, 0, 30e6),
        name="time_ffn_backward",
    )(grad, act, slope, nf, mid, mixed, att, gate, linv, *consts)


def time_attention_backward_kernel(
    heads,
    p_ref,
    q_ref,
    k_ref,
    v_ref,
    datt_ref,
    minus_ref,
    dlogit_ref,
    n_ref,
    x_ref,
    dmid_ref,
    cos_ref,
    sin_ref,
    g1_ref,
    wp_ref,
    wg_ref,
    out_ref,
    *refs,
):
    sums_refs, (dproj_ref, dwp_ref, dwg_ref, dg1_ref) = refs[:2], refs[2:]
    slot, head = pl.program_id(0), pl.program_id(1)
    inner = q_ref.shape[1]
    size = inner // heads
    frames = q_ref.shape[2]

    @pl.when((slot == 0) & (head == 0))
    def clear():
        for ref in (dwp_ref, dwg_ref, dg1_ref):
            ref[...] = jnp.zeros_like(ref)

    start = pl.multiple_of(head * size, size)
    at = pl.ds(start, size)
    d_queries, d_keys, d_values = scores_backward(
        q_ref[0, at, :],
        k_ref[0, at, :],
        v_ref[0, at, :],
        p_ref[0, 0],
        datt_ref[0, at, :],
        minus_ref[0, pl.ds(head, 1), :],
        cos_ref[...],
        sin_ref[...],
        size**-0.5,
    )
    dproj_ref[at, :] = d_queries.astype(BF16)
    dproj_ref[pl.ds(inner + start, size), :] = d_keys.astype(BF16)
    dproj_ref[pl.ds(2 * inner + start, size), :] = d_values.astype(BF16)

    @pl.when(head == heads - 1)
    def after():
        d_logit = jnp.concatenate([dlogit_ref[0], jnp.zeros_like(dlogit_ref[0])], axis=0).astype(BF16)
        dwp_ref[...] += dg(n_ref[0], dproj_ref[...], NT)
        dwg_ref[...] += dg(n_ref[0], d_logit, NT)[:, :heads]

        def block(i, carry):
            at = pl.ds(pl.multiple_of(i * BLOCK, BLOCK), BLOCK)
            logit = dlogit_ref[0, :, at].astype(BF16)
            d_normed = dg(wp_ref[...], dproj_ref[:, at], NN) + dg(wg_ref[...], logit, NN)
            d_rows, terms = norm_backward(x_ref[0, at, :].astype(F32).T, g1_ref[...], d_normed)
            dg1_ref[...] += jnp.sum(terms, axis=1, keepdims=True)
            out_ref[0, at, :] = (dmid_ref[0, :, at] + d_rows).T.astype(BF16)
            return carry

        lax.fori_loop(0, frames // BLOCK, block, 0)

    @pl.when((slot == pl.num_programs(0) - 1) & (head == heads - 1))
    def finish():
        finish_sums(sums_refs, ((dwp_ref, False), dwg_ref, dg1_ref))


def time_attention_backward(p, q, k, v, datt, minus, dlogit, n, x, dmid, cos, sin, g1, wp, wg):
    slots, inner, frames = q.shape
    heads = minus.shape[1]
    model = n.shape[1]

    def per_slot(array):
        return pl.BlockSpec((1,) + array.shape[1:], lambda s, h: (s, 0, 0))

    consts = (cos, sin, g1, wp, wg)
    sums = ((model, 3 * inner), (model, 128))
    return pl.pallas_call(
        lambda *refs: time_attention_backward_kernel(heads, *refs),
        grid=(slots, heads),
        out_shape=[
            jax.ShapeDtypeStruct((slots, frames, model), BF16),
        ]
        + sum_shapes(*sums),
        in_specs=[pl.BlockSpec((1, 1, frames, frames), lambda s, h: (s, h, 0, 0))]
        + [per_slot(a) for a in (q, k, v, datt, minus, dlogit, n, x, dmid)]
        + [whole_spec(c) for c in consts],
        out_specs=[
            pl.BlockSpec((1, frames, model), lambda s, h: (s, 0, 0)),
        ]
        + sum_specs(*sums),
        scratch_shapes=[
            pltpu.VMEM((3 * inner, frames), BF16),
            pltpu.VMEM((model, 3 * inner), F32),
            pltpu.VMEM((model, heads), F32),
            pltpu.VMEM((model, 1), F32),
        ],
        compiler_params=pltpu.CompilerParams(vmem_limit_bytes=VMEM_BYTES),
        cost_estimate=cost(20.0e6 * slots * frames, 0, 60e6),
        name="time_attention_backward",
    )(p, q, k, v, datt, minus, dlogit, n, x, dmid, *consts)


def band_kernel(
    heads,
    x_ref,
    cot_ref,
    mask_ref,
    bias_ref,
    cos_ref,
    sin_ref,
    g1_ref,
    g2_ref,
    wpt_ref,
    wgt_ref,
    wot_ref,
    w1t_ref,
    w2t_ref,
    wp_ref,
    wg_ref,
    wo_ref,
    w1_ref,
    w2_ref,
    y_ref,
    dx_ref,
    dwp_out,
    dw1_out,
    dw2_out,
    dwo_out,
    narrow_out,
    q_ref,
    k_ref,
    v_ref,
    p_ref,
    gate_ref,
    linv_ref,
    att_ref,
    mixed_ref,
    act_ref,
    slope_ref,
    datt_ref,
    dmixed_ref,
    dlogit_ref,
    dproj_ref,
    dwp_ref,
    dw1_ref,
    dw2t_ref,
    dwot_ref,
    dwg_ref,
    dg1_ref,
    dg2_ref,
):
    step = pl.program_id(0)
    tokens, model = x_ref.shape
    inner = q_ref.shape[0]
    size = inner // heads
    groups = tokens // BLOCK
    sums_refs = (dwp_out, dw1_out, dw2_out, dwo_out, narrow_out)

    @pl.when(step == 0)
    def clear():
        for ref in (dwp_ref, dw1_ref, dw2t_ref, dwot_ref, dwg_ref, dg1_ref, dg2_ref):
            ref[...] = jnp.zeros_like(ref)

    rows = x_ref[...].astype(F32).T
    normed = norm_forward(rows, g1_ref[...])
    q_ref[...], k_ref[...], v_ref[...] = project_block(
        normed, wpt_ref, cos_ref[...], sin_ref[...], inner, LOG2E * size**-0.5
    )
    gate_ref[...] = dg(wgt_ref[...], normed, NN)
    ones = extra_rows([jnp.ones((1, BLOCK), F32)], BLOCK)

    def attend(head, carry):
        at = pl.ds(pl.multiple_of(head * size, size), size)
        row = pl.ds(head, 1)
        for group in range(groups):
            lanes = slice(group * BLOCK, (group + 1) * BLOCK)
            scores = dg(k_ref[at, lanes], q_ref[at, lanes], TN) + bias_ref[...]
            weights = jnp.exp2(scores - jnp.max(scores, axis=0, keepdims=True)).astype(BF16)
            p_ref[head * groups + group] = weights
            sums = dg(jnp.concatenate([v_ref[at, lanes], ones], axis=0), weights, NN)
            inverse = 1.0 / sums[size : size + 1]
            attended = sums[:size] * inverse
            linv_ref[row, lanes] = inverse
            att_ref[at, lanes] = attended
            gate = jax.nn.sigmoid(gate_ref[row, lanes])
            mixed_ref[at, lanes] = (attended * gate).astype(BF16)
        return carry

    lax.fori_loop(0, heads, attend, 0)
    middle = rows + dg(wot_ref[...], mixed_ref[...], NN)
    normed_ffn = norm_forward(middle, g2_ref[...])

    hidden = w1t_ref.shape[0]
    part = hidden // 4

    def expand(i, carry):
        at = pl.ds(pl.multiple_of(i * part, part), part)
        active, slope = gelu_pair(dg(w1t_ref[at, :], normed_ffn, NN))
        act_ref[at, :] = active.astype(BF16)
        slope_ref[at, :] = slope.astype(BF16)
        return carry

    lax.fori_loop(0, 4, expand, 0)
    mask = mask_ref[0]
    result = (middle + dg(w2t_ref[...], act_ref[...], NN)) * mask
    y_ref[...] = result.T.astype(BF16)

    grad = cot_ref[...].astype(F32).T * mask
    d_middle = ffn_backward(
        grad, act_ref[...], slope_ref[...], normed_ffn, middle, g2_ref[...], w1_ref, w2_ref, dw1_ref, dw2t_ref, dg2_ref
    )
    branch = d_middle.astype(BF16)
    dwot_ref[...] += dg(branch, mixed_ref[...], NT)
    dmixed_ref[...] = dg(wo_ref[...], branch, NN)

    def attend_back(head, carry):
        start = pl.multiple_of(head * size, size)
        at = pl.ds(start, size)
        row = pl.ds(head, 1)
        d_att, minus, d_logit = head_backward(dmixed_ref[at, :], att_ref[at, :], gate_ref[row, :], linv_ref[row, :])
        dlogit_ref[row, :] = d_logit
        for group in range(groups):
            lanes = slice(group * BLOCK, (group + 1) * BLOCK)
            d_queries, d_keys, d_values = scores_backward(
                q_ref[at, lanes],
                k_ref[at, lanes],
                v_ref[at, lanes],
                p_ref[head * groups + group],
                d_att[:, lanes],
                minus[:, lanes],
                cos_ref[:, lanes],
                sin_ref[:, lanes],
                size**-0.5,
            )
            dproj_ref[at, lanes] = d_queries.astype(BF16)
            dproj_ref[pl.ds(inner + start, size), lanes] = d_keys.astype(BF16)
            dproj_ref[pl.ds(2 * inner + start, size), lanes] = d_values.astype(BF16)
        return carry

    lax.fori_loop(0, heads, attend_back, 0)
    d_logit = jnp.concatenate([dlogit_ref[...], jnp.zeros_like(dlogit_ref)], axis=0).astype(BF16)
    dwp_ref[...] += dg(normed, dproj_ref[...], NT)
    dwg_ref[...] += dg(normed, d_logit, NT)[:, :heads]
    d_normed = dg(wp_ref[...], dproj_ref[...], NN) + dg(wg_ref[...], dlogit_ref[...].astype(BF16), NN)
    d_rows, terms = norm_backward(rows, g1_ref[...], d_normed)
    dg1_ref[...] += jnp.sum(terms, axis=1, keepdims=True)
    dx_ref[...] = (d_middle + d_rows).T.astype(BF16)

    @pl.when(step == pl.num_programs(0) - 1)
    def finish():
        finish_sums(
            sums_refs,
            ((dwp_ref, False), (dw1_ref, False), (dw2t_ref, True), (dwot_ref, True), dwg_ref, dg1_ref, dg2_ref),
        )


def band_layer(x, cot, mask, bias, cos, sin, params, turned):
    prenorm, project, gating, output_weight, midnorm, expand, shrink = params
    wpt, wgt, wot, w1t, w2t, g1, g2 = turned
    total, model = x.shape
    steps, _, tokens = mask.shape
    heads, inner, hidden = gating.shape[1], output_weight.shape[0], expand.shape[1]
    groups = tokens // BLOCK
    consts = (bias, cos, sin, g1, g2, wpt, wgt, wot, w1t, w2t, project, gating, output_weight, expand, shrink)
    sums = ((model, 3 * inner), (model, hidden), (hidden, model), (inner, model), (model, 128))
    rows = pl.BlockSpec((tokens, model), lambda i: (i, 0))
    return pl.pallas_call(
        lambda *refs: band_kernel(heads, *refs),
        grid=(steps,),
        out_shape=[
            jax.ShapeDtypeStruct((total, model), BF16),
            jax.ShapeDtypeStruct((total, model), BF16),
        ]
        + sum_shapes(*sums),
        in_specs=[rows, rows, pl.BlockSpec((1, 1, tokens), lambda i: (i, 0, 0))] + [whole_spec(c) for c in consts],
        out_specs=[rows, rows] + sum_specs(*sums),
        scratch_shapes=[
            pltpu.VMEM((inner, tokens), BF16),
            pltpu.VMEM((inner, tokens), BF16),
            pltpu.VMEM((inner, tokens), BF16),
            pltpu.VMEM((heads * groups, BLOCK, BLOCK), BF16),
            pltpu.VMEM((heads, tokens), F32),
            pltpu.VMEM((heads, tokens), F32),
            pltpu.VMEM((inner, tokens), F32),
            pltpu.VMEM((inner, tokens), BF16),
            pltpu.VMEM((hidden, tokens), BF16),
            pltpu.VMEM((hidden, tokens), BF16),
            pltpu.VMEM((inner, tokens), BF16),
            pltpu.VMEM((inner, tokens), F32),
            pltpu.VMEM((heads, tokens), F32),
            pltpu.VMEM((3 * inner, tokens), BF16),
            pltpu.VMEM((model, 3 * inner), F32),
            pltpu.VMEM((model, hidden), F32),
            pltpu.VMEM((model, hidden), F32),
            pltpu.VMEM((model, inner), F32),
            pltpu.VMEM((model, heads), F32),
            pltpu.VMEM((model, 1), F32),
            pltpu.VMEM((model, 1), F32),
        ],
        compiler_params=pltpu.CompilerParams(vmem_limit_bytes=VMEM_BYTES),
        cost_estimate=cost(30.0e6 * total, 0, 60e6),
        name="band_layer",
    )(x, cot, mask, *consts)


def turned_params(params):
    prenorm, project, gating, output_weight, midnorm, expand, shrink = params
    return (
        project.T,
        gating.T,
        output_weight.T,
        expand.T,
        shrink.T,
        prenorm.astype(F32)[:, None],
        midnorm.astype(F32)[:, None],
    )


def slot_shards(activations, cotangent, frame_counts, slot_bands, *weights):
    slot_dev, _, frame_dev, model = activations.shape
    slot_count = slot_bands.shape[0]
    batch, band = lax.axis_size("batch"), lax.axis_size("band")
    frames = frame_dev * batch
    piece = frame_dev // band
    slots = slot_dev // batch
    time_params, band_params = weights[:7], weights[7:]
    heads, inner, hidden = time_params[2].shape[1], time_params[3].shape[0], time_params[5].shape[1]
    size = inner // heads

    positions = jnp.arange(frames, dtype=jnp.int32)
    time_cos, time_sin = rotary_tables(positions.astype(F32), size)
    time_bias = jnp.where(positions[None, :] < frame_counts[:, None], 0.0, NEG_FILL).astype(F32)
    band_cos, band_sin = rotary_tables(jnp.maximum(slot_bands, 0).astype(F32), size)
    tokens = min(2 * BLOCK, piece * slot_count)
    copies = tokens // slot_count
    slot_valid = slot_bands >= 0
    index = jnp.arange(BLOCK, dtype=jnp.int32)
    together = (index[:, None] // slot_count == index[None, :] // slot_count) & jnp.tile(
        slot_valid, BLOCK // slot_count
    )[:, None]
    band_bias = jnp.where(together, 0.0, NEG_FILL).astype(F32)
    own_start = lax.axis_index("batch") * frame_dev + lax.axis_index("band") * piece
    own_frames = own_start + jnp.arange(piece, dtype=jnp.int32)
    mask = ((own_frames < frame_counts[0])[:, None] & slot_valid[None, :]).astype(F32)
    mask = mask.reshape(piece * slot_count // tokens, 1, tokens)

    time_turned = turned_params(time_params)
    band_turned = turned_params(band_params)
    rows = lax.all_to_all(
        activations.reshape(slot_dev, frame_dev, model), "batch", split_axis=0, concat_axis=1, tiled=True
    )
    cot_rows = lax.all_to_all(
        cotangent.reshape(slot_dev, frame_dev, model), "band", split_axis=1, concat_axis=0, tiled=True
    )
    cot_rows = cot_rows.transpose(1, 0, 2).reshape(piece * slot_count, model)
    wpt, wgt, wot, w1t, w2t, g1, g2 = time_turned
    result, n, q, k, v, p, linv, gate, att, mixed, mid, nf, act, slope = time_forward(
        rows, time_bias, time_cos.T, time_sin.T, g1, g2, wpt, wgt, wot, w1t, w2t
    )
    result = result.reshape(slots, batch, band, piece, model).transpose(0, 2, 1, 3, 4)
    frame_rows = lax.all_to_all(
        result.reshape(slots, frames, model), ("band", "batch"), split_axis=1, concat_axis=0, tiled=True
    )
    frame_rows = frame_rows.transpose(1, 0, 2).reshape(piece * slot_count, model)
    y, dx, *band_sums = band_layer(
        frame_rows,
        cot_rows,
        mask,
        band_bias,
        jnp.tile(band_cos.T, (1, copies)),
        jnp.tile(band_sin.T, (1, copies)),
        band_params,
        band_turned,
    )
    band_sums = lax.psum(band_sums, ("band", "batch"))
    dx = dx.reshape(piece, slot_count, model).transpose(1, 0, 2)
    slot_grad = lax.all_to_all(dx, ("band", "batch"), split_axis=0, concat_axis=1, tiled=True)
    slot_grad = slot_grad.reshape(slots, band, batch, piece, model).transpose(0, 2, 1, 3, 4)
    slot_grad = slot_grad.reshape(slots, frames, model)
    y = y.reshape(piece, slot_count, model).transpose(1, 0, 2)
    layer_output = lax.all_to_all(y, "band", split_axis=0, concat_axis=1, tiled=True)
    dmid, datt, minus, dlogit, *ffn_sums = time_ffn_backward(
        slot_grad, act, slope, nf, mid, mixed, att, gate, linv, g2, time_params[5], time_params[6], time_params[3]
    )
    ffn_sums, band_sums = lax.optimization_barrier((ffn_sums, band_sums))
    ffn_sums = lax.psum(ffn_sums, ("band", "batch"))
    grads, *attn_sums = time_attention_backward(
        p, q, k, v, datt, minus, dlogit, n, rows, dmid, time_cos.T, time_sin.T, g1, time_params[1], time_params[2]
    )
    input_grad = lax.all_to_all(grads, "batch", split_axis=1, concat_axis=0, tiled=True)
    attn_sums, ffn_sums = lax.optimization_barrier((attn_sums, ffn_sums))
    attn_sums = lax.psum(attn_sums, ("band", "batch"))

    dwp, attn_narrow = (part.astype(F32) for part in attn_sums)
    dw1, dw2, dwo, ffn_narrow = (part.astype(F32) for part in ffn_sums)
    bwp, bw1, bw2, bwo, band_narrow = (part.astype(F32) for part in band_sums)
    return (
        layer_output.reshape(activations.shape),
        input_grad.astype(F32).reshape(activations.shape),
        attn_narrow[:, heads],
        dwp,
        attn_narrow[:, :heads],
        dwo,
        ffn_narrow[:, 0],
        dw1,
        dw2,
        band_narrow[:, heads],
        bwp,
        band_narrow[:, :heads],
        bwo,
        band_narrow[:, heads + 1],
        bw1,
        bw2,
    )


def shards(activations, cotangent, frame_counts, slot_bands, *weights):
    slot_dev, clips, frame_dev, _ = activations.shape
    batch, band = lax.axis_size("batch"), lax.axis_size("band")
    fits = (
        clips == 1
        and slot_dev % batch == 0
        and frame_dev % band == 0
        and (frame_dev * batch) % (2 * BLOCK) == 0
        and BLOCK % slot_bands.shape[0] == 0
        and (frame_dev // band * slot_bands.shape[0]) % (2 * BLOCK) == 0
        and weights[2].shape[1] == 8
    )
    form = slot_shards if fits else generic_shards
    return form(activations, cotangent, frame_counts, slot_bands, *weights)


def solution(mesh):
    return jax.shard_map(
        shards,
        mesh=mesh,
        in_specs=(
            P("band", None, "batch", None),
            P("band", None, "batch", None),
            P(),
            P(),
            P(),
            P(),
            P(),
            P(),
            P(),
            P(),
            P(),
            P(),
            P(),
            P(),
            P(),
            P(),
            P(),
            P(),
        ),
        out_specs=(
            P("band", None, "batch", None),
            P("band", None, "batch", None),
            P(),
            P(),
            P(),
            P(),
            P(),
            P(),
            P(),
            P(),
            P(),
            P(),
            P(),
            P(),
            P(),
            P(),
        ),
        check_vma=False,
    )
```

```python
import math

import jax
import jax.numpy as jnp
from jax import lax
from jax.experimental import pallas as pl
from jax.experimental.pallas import tpu as pltpu
from jax.sharding import PartitionSpec as P

EPSILON = 1e-05
NEG_FILL = -1000000000.0
TIME_LAYOUT = ("bqhe", "bkhe")
BAND_LAYOUT = ("qbhe", "kbhe")


def rms_scale(residual, gain):
    return (
        residual * lax.rsqrt(jnp.mean(residual * residual, axis=-1, keepdims=True) + EPSILON) * gain
    )


def gelu_exact(values):
    return jax.nn.gelu(values, approximate=False)


def rotary_tables(positions, head_size):
    half_size = head_size // 2
    rates = jnp.exp(-math.log(10000.0) * jnp.arange(half_size, dtype=jnp.float32) / half_size)
    angles = positions[:, None] * rates[None, :]
    return (jnp.cos(angles), jnp.sin(angles))


def rotate(vectors, cos_table, sin_table):
    half_size = vectors.shape[-1] // 2
    first = vectors[..., :half_size]
    second = vectors[..., half_size:]
    return jnp.concatenate(
        [first * cos_table - second * sin_table, first * sin_table + second * cos_table], axis=-1
    )


def token_sum(left, right):
    return lax.dot_general(
        left.reshape(-1, left.shape[-1]),
        right.reshape(-1, right.shape[-1]),
        (((0,), (0,)), ((), ())),
        preferred_element_type=jnp.float32,
    )


def back_dot(gradient, weight):
    return lax.dot_general(
        gradient,
        weight,
        (((gradient.ndim - 1,), (1,)), ((), ())),
        preferred_element_type=jnp.float32,
    )


def block_forward(queries, key_rows, value_rows, key_valid, layout):
    query_form, key_form = layout
    scores = (
        jnp.einsum(
            query_form + "," + key_form + "->bhqk",
            queries,
            key_rows,
            preferred_element_type=jnp.float32,
        )
        * 0.125
    )
    scores = jnp.where(key_valid[:, None, None, :], scores, NEG_FILL)
    highest = jnp.max(scores, axis=-1, keepdims=True)
    exponents = jnp.exp(scores - highest)
    totals = jnp.sum(exponents, axis=-1, keepdims=True)
    soft_weights = (exponents / totals).astype(jnp.bfloat16)
    output = jnp.einsum(
        "bhqk," + key_form + "->" + query_form,
        soft_weights,
        value_rows,
        preferred_element_type=jnp.float32,
    )
    return (output, highest + jnp.log(totals))


def block_backward(queries, key_rows, value_rows, key_valid, log_totals, out_grad, layout):
    query_form, key_form = layout
    scores = (
        jnp.einsum(
            query_form + "," + key_form + "->bhqk",
            queries,
            key_rows,
            preferred_element_type=jnp.float32,
        )
        * 0.125
    )
    soft_weights = jnp.where(key_valid[:, None, None, :], jnp.exp(scores - log_totals), 0.0)
    weight_grad = jnp.einsum(
        query_form + "," + key_form + "->bhqk",
        out_grad,
        value_rows,
        preferred_element_type=jnp.float32,
    )
    score_grad = (
        soft_weights * (weight_grad - jnp.sum(soft_weights * weight_grad, axis=-1, keepdims=True))
    ).astype(jnp.bfloat16)
    query_grad = (
        jnp.einsum(
            "bhqk," + key_form + "->" + query_form,
            score_grad,
            key_rows,
            preferred_element_type=jnp.float32,
        )
        * 0.125
    )
    key_grad = (
        jnp.einsum(
            "bhqk," + query_form + "->" + key_form,
            score_grad,
            queries,
            preferred_element_type=jnp.float32,
        )
        * 0.125
    )
    value_grad = jnp.einsum(
        "bhqk," + query_form + "->" + key_form,
        soft_weights.astype(jnp.bfloat16),
        out_grad,
        preferred_element_type=jnp.float32,
    )
    return (query_grad, key_grad, value_grad)


def time_attend(queries, key_rows, value_rows, key_valid):
    keys_full, values_full = (
        lax.all_gather(key_rows, "batch", axis=1, tiled=True),
        lax.all_gather(value_rows, "batch", axis=1, tiled=True),
    )
    output, log_totals = block_forward(queries, keys_full, values_full, key_valid, TIME_LAYOUT)
    return (output, (log_totals, keys_full, values_full))


def time_attend_back(queries, key_rows, value_rows, key_valid, attn_kept, out_grad):
    log_totals, keys_full, values_full = attn_kept
    query_grad, key_full_grad, value_full_grad = block_backward(
        queries, keys_full, values_full, key_valid, log_totals, out_grad, TIME_LAYOUT
    )
    key_grad, value_grad = (
        lax.psum_scatter(
            key_full_grad.astype(jnp.bfloat16), "batch", scatter_dimension=1, tiled=True
        ).astype(jnp.float32),
        lax.psum_scatter(
            value_full_grad.astype(jnp.bfloat16), "batch", scatter_dimension=1, tiled=True
        ).astype(jnp.float32),
    )
    return (query_grad, key_grad, value_grad)


def band_attend(queries, key_rows, value_rows, key_valid):
    return block_forward(queries, key_rows, value_rows, key_valid, BAND_LAYOUT)


def band_attend_back(queries, key_rows, value_rows, key_valid, attn_kept, out_grad):
    return block_backward(
        queries, key_rows, value_rows, key_valid, attn_kept, out_grad, BAND_LAYOUT
    )


def layer_forward(residual, params, tables, key_valid, attend):
    prenorm, project, gating, output_weight, midnorm, expand, shrink = params
    cos_table, sin_table = tables
    normed = rms_scale(residual, prenorm.astype(jnp.float32)).astype(jnp.bfloat16)
    projected = jnp.dot(normed, project, preferred_element_type=jnp.float32)
    gate_logits = jnp.dot(normed, gating, preferred_element_type=jnp.float32)
    inner_width = output_weight.shape[0]
    head_count = gating.shape[1]
    head_shape = residual.shape[:-1] + (head_count, inner_width // head_count)
    queries = rotate(projected[..., :inner_width].reshape(head_shape), cos_table, sin_table).astype(
        jnp.bfloat16
    )
    key_rows = rotate(
        projected[..., inner_width : 2 * inner_width].reshape(head_shape), cos_table, sin_table
    ).astype(jnp.bfloat16)
    value_rows = projected[..., 2 * inner_width :].reshape(head_shape).astype(jnp.bfloat16)
    attended, attn_kept = attend(queries, key_rows, value_rows, key_valid)
    gate_values = jax.nn.sigmoid(gate_logits)
    mixed_heads = (
        (attended * gate_values[..., None])
        .reshape(residual.shape[:-1] + (inner_width,))
        .astype(jnp.bfloat16)
    )
    middle = residual + jnp.dot(mixed_heads, output_weight, preferred_element_type=jnp.float32)
    normed_ffn = rms_scale(middle, midnorm.astype(jnp.float32)).astype(jnp.bfloat16)
    hidden = jnp.dot(normed_ffn, expand, preferred_element_type=jnp.float32)
    active = gelu_exact(hidden).astype(jnp.bfloat16)
    result = middle + jnp.dot(active, shrink, preferred_element_type=jnp.float32)
    kept_values = (
        residual,
        normed,
        gate_logits,
        queries,
        key_rows,
        value_rows,
        attn_kept,
        attended,
        mixed_heads,
        middle,
        normed_ffn,
        hidden,
        active,
    )
    return (result, kept_values)


def layer_backward(result_grad, params, kept_values, tables, key_valid, attend_back):
    prenorm, project, gating, output_weight, midnorm, expand, shrink = params
    (
        residual,
        normed,
        gate_logits,
        queries,
        key_rows,
        value_rows,
        attn_kept,
        attended,
        mixed_heads,
        middle,
        normed_ffn,
        hidden,
        active,
    ) = kept_values
    cos_table, sin_table = tables
    branch_grad = result_grad.astype(jnp.bfloat16)
    shrink_grad = token_sum(active, branch_grad)
    active_grad = back_dot(branch_grad, shrink)
    hidden_grad = jax.vjp(gelu_exact, hidden)[1](active_grad)[0].astype(jnp.bfloat16)
    expand_grad = token_sum(normed_ffn, hidden_grad)
    normed_ffn_grad = back_dot(hidden_grad, expand)
    middle_norm_grad, midnorm_grad = jax.vjp(rms_scale, middle, midnorm.astype(jnp.float32))[1](
        normed_ffn_grad
    )
    middle_grad = result_grad + middle_norm_grad
    attn_branch = middle_grad.astype(jnp.bfloat16)
    output_grad = token_sum(mixed_heads, attn_branch)
    mixed_grad = back_dot(attn_branch, output_weight).reshape(attended.shape)
    gate_values = jax.nn.sigmoid(gate_logits)
    attended_grad = (mixed_grad * gate_values[..., None]).astype(jnp.bfloat16)
    logit_grad = (
        jnp.sum(mixed_grad * attended, axis=-1) * gate_values * (1.0 - gate_values)
    ).astype(jnp.bfloat16)
    query_grad, key_grad, value_grad = attend_back(
        queries, key_rows, value_rows, key_valid, attn_kept, attended_grad
    )
    flat_shape = residual.shape[:-1] + (-1,)
    projected_grad = jnp.concatenate(
        [
            rotate(query_grad, cos_table, -sin_table).reshape(flat_shape),
            rotate(key_grad, cos_table, -sin_table).reshape(flat_shape),
            value_grad.reshape(flat_shape),
        ],
        axis=-1,
    ).astype(jnp.bfloat16)
    project_grad = token_sum(normed, projected_grad)
    gating_grad = token_sum(normed, logit_grad)
    normed_grad = back_dot(projected_grad, project) + back_dot(logit_grad, gating)
    residual_norm_grad, prenorm_grad = jax.vjp(rms_scale, residual, prenorm.astype(jnp.float32))[1](
        normed_grad
    )
    return (
        middle_grad + residual_norm_grad,
        (
            prenorm_grad,
            project_grad,
            gating_grad,
            output_grad,
            midnorm_grad,
            expand_grad,
            shrink_grad,
        ),
    )


def generic_shards(
    activations,
    cotangent,
    frame_counts,
    slot_bands,
    time_prenorm,
    time_project,
    time_gating,
    time_output,
    time_midnorm,
    time_expand,
    time_shrink,
    band_prenorm,
    band_project,
    band_gating,
    band_output,
    band_midnorm,
    band_expand,
    band_shrink,
):
    slot_dev, clip_count, frame_dev, model_width = activations.shape
    slot_count = slot_bands.shape[0]
    frames_all = frame_dev * lax.axis_size("batch")
    head_size = time_output.shape[0] // time_gating.shape[1]
    time_params = (
        time_prenorm,
        time_project,
        time_gating,
        time_output,
        time_midnorm,
        time_expand,
        time_shrink,
    )
    band_params = (
        band_prenorm,
        band_project,
        band_gating,
        band_output,
        band_midnorm,
        band_expand,
        band_shrink,
    )
    own_bands = lax.dynamic_slice_in_dim(slot_bands, lax.axis_index("band") * slot_dev, slot_dev)
    frame_start = lax.axis_index("batch") * frame_dev
    own_frames = frame_start + jnp.arange(frame_dev, dtype=jnp.int32)
    frame_valid = own_frames[None, :] < frame_counts[:, None]
    row_valid = (own_bands >= 0)[:, None, None] & frame_valid[None]
    full_valid = jnp.arange(frames_all, dtype=jnp.int32)[None, :] < frame_counts[:, None]
    time_valid = jnp.broadcast_to(full_valid[None], (slot_dev, clip_count, frames_all)).reshape(
        slot_dev * clip_count, frames_all
    )
    time_cos, time_sin = rotary_tables(own_frames.astype(jnp.float32), head_size)
    time_tables = (time_cos[None, :, None, :], time_sin[None, :, None, :])
    band_cos, band_sin = rotary_tables(jnp.maximum(slot_bands, 0).astype(jnp.float32), head_size)
    band_tables = (band_cos[:, None, None, :], band_sin[:, None, None, :])
    residual = activations.astype(jnp.float32).reshape(
        slot_dev * clip_count, frame_dev, model_width
    )
    time_result, time_kept = layer_forward(
        residual, time_params, time_tables, time_valid, time_attend
    )
    masked_cot = jnp.where(row_valid[..., None], cotangent, jnp.zeros((), jnp.bfloat16)).reshape(
        slot_dev, clip_count * frame_dev, model_width
    )
    frame_rows = lax.all_to_all(
        time_result.astype(jnp.bfloat16), "band", split_axis=1, concat_axis=0, tiled=True
    ).astype(time_result.dtype)
    band_valid = jnp.broadcast_to((slot_bands >= 0)[None, :], (frame_rows.shape[1], slot_count))
    band_result, band_kept = layer_forward(
        frame_rows, band_params, band_tables, band_valid, band_attend
    )
    back_rows = lax.all_to_all(
        band_result.astype(jnp.bfloat16), "band", split_axis=0, concat_axis=1, tiled=True
    ).astype(band_result.dtype)
    layer_output = jnp.where(
        row_valid[..., None], back_rows.reshape(activations.shape), 0.0
    ).astype(jnp.bfloat16)
    frame_cot = lax.all_to_all(masked_cot, "band", split_axis=1, concat_axis=0, tiled=True)
    frame_grad, band_grads = layer_backward(
        frame_cot.astype(jnp.float32),
        band_params,
        band_kept,
        band_tables,
        band_valid,
        band_attend_back,
    )
    slot_grad = lax.all_to_all(
        frame_grad.astype(jnp.bfloat16), "band", split_axis=0, concat_axis=1, tiled=True
    ).astype(frame_grad.dtype)
    input_grad, time_grads = layer_backward(
        slot_grad, time_params, time_kept, time_tables, time_valid, time_attend_back
    )
    input_grad = input_grad.reshape(activations.shape)
    all_grads = lax.psum(
        (
            time_grads[0],
            time_grads[1],
            time_grads[2],
            time_grads[3],
            time_grads[4],
            time_grads[5],
            time_grads[6],
            band_grads[0],
            band_grads[1],
            band_grads[2],
            band_grads[3],
            band_grads[4],
            band_grads[5],
            band_grads[6],
        ),
        ("band", "batch"),
    )
    return (
        layer_output,
        input_grad,
        all_grads[0],
        all_grads[1],
        all_grads[2],
        all_grads[3],
        all_grads[4],
        all_grads[5],
        all_grads[6],
        all_grads[7],
        all_grads[8],
        all_grads[9],
        all_grads[10],
        all_grads[11],
        all_grads[12],
        all_grads[13],
    )


BLOCK = 256
LOG2E = 1.4426950408889634
F32 = jnp.float32
BF16 = jnp.bfloat16
NN = (((1,), (0,)), ((), ()))
NT = (((1,), (1,)), ((), ()))
TN = (((0,), (0,)), ((), ()))
VMEM_BYTES = 60 * 2**20


def dg(left, right, dims):
    return lax.dot_general(left, right, dims, preferred_element_type=F32)


def norm_forward(rows, gain):
    scale = lax.rsqrt(jnp.mean(rows * rows, axis=0, keepdims=True) + EPSILON)
    return (rows * scale * gain).astype(BF16)


def norm_backward(rows, gain, grad):
    scale = lax.rsqrt(jnp.mean(rows * rows, axis=0, keepdims=True) + EPSILON)
    unit = rows * scale
    scaled = grad * gain
    inner = jnp.mean(scaled * unit, axis=0, keepdims=True)
    return scale * (scaled - unit * inner), grad * unit


def gelu_pair(values):
    size = jnp.abs(values)
    denominator = 1.0 + (0.3275911 * math.sqrt(0.5)) * size
    t = pl.reciprocal(denominator, approx=True)
    t = t * (2.0 - denominator * t)
    bell = jnp.exp2(values * values * (-0.5 * LOG2E))
    poly = 0.5 * 1.061405429
    for coefficient in (-1.453152027, 1.421413741, -0.284496736, 0.254829592):
        poly = poly * t + 0.5 * coefficient
    tail = poly * t * bell
    upper = jnp.where(values < 0.0, tail, 1.0 - tail)
    slope = upper + values * bell * (1.0 / math.sqrt(2.0 * math.pi))
    return values * upper, slope


def turn(vectors, cos, sin):
    half = cos.shape[0]
    split = vectors.reshape(-1, 2 * half, vectors.shape[-1])
    first = split[:, :half]
    second = split[:, half:]
    turned = jnp.concatenate([first * cos - second * sin, first * sin + second * cos], axis=1)
    return turned.reshape(vectors.shape)


def three_parts(values):
    top = values.astype(BF16).astype(F32)
    rest = values - top
    middle = rest.astype(BF16).astype(F32)
    return top, middle, rest - middle


def extra_rows(rows, width):
    tile = jnp.concatenate(rows + [jnp.zeros((8 - len(rows), width), F32)], axis=0)
    return jnp.concatenate([tile, jnp.zeros((8, width), F32)], axis=0).astype(BF16)


def project_block(normed, wpt_ref, cos, sin, inner, scale):
    queries = turn(dg(wpt_ref[0:inner, :], normed, NN), cos, sin) * scale
    keys = turn(dg(wpt_ref[inner : 2 * inner, :], normed, NN), cos, sin)
    values = dg(wpt_ref[2 * inner : 3 * inner, :], normed, NN)
    return queries.astype(BF16), keys.astype(BF16), values.astype(BF16)


def column(row_ref):
    row = row_ref[...].astype(F32)
    return jnp.broadcast_to(row, (8, row.shape[1])).T[:, :1]


def flipped(ref):
    return ref[...].astype(F32).T.astype(BF16)


def greet_all(band_count, batch_count):
    count = band_count * batch_count
    me = lax.axis_index("band") * batch_count + lax.axis_index("batch")
    barrier = pltpu.get_barrier_semaphore()

    def signal(i, carry):
        other = lax.rem(me + i, count)
        pl.semaphore_signal(
            barrier,
            inc=1,
            device_id=(other // batch_count, lax.rem(other, batch_count)),
            device_id_type=pl.DeviceIdType.MESH,
        )
        return carry

    lax.fori_loop(1, count, signal, 0)
    pl.semaphore_wait(barrier, count - 1)


def send(source, target, send_sem, recv_sem, band, batch):
    pltpu.make_async_remote_copy(
        src_ref=source,
        dst_ref=target,
        send_sem=send_sem,
        recv_sem=recv_sem,
        device_id=(band, batch),
        device_id_type=pl.DeviceIdType.MESH,
    ).start()


def await_bytes(ref, sem):
    pltpu.make_async_copy(ref, ref, sem).wait()


def time_forward_kernel(
    heads,
    batch_count,
    band_count,
    act_in,
    cot_in,
    bias_ref,
    cos_ref,
    sin_ref,
    g1_ref,
    g2_ref,
    wp_ref,
    wg_ref,
    wo_ref,
    w1_ref,
    w2_ref,
    band_wp_ref,
    band_wg_ref,
    band_wo_ref,
    band_w1_ref,
    band_w2_ref,
    band_rows,
    band_cot,
    rows_ref,
    n_ref,
    q_ref,
    k_ref,
    v_ref,
    p_ref,
    linv_ref,
    gate_ref,
    att_ref,
    mixed_ref,
    mid_ref,
    nf_ref,
    act_ref,
    slope_ref,
    band_wpt_ref,
    band_wgt_ref,
    band_wot_ref,
    band_w1t_ref,
    band_w2t_ref,
    xt_ref,
    x_ref,
    result_ref,
    wpt_ref,
    wgt_ref,
    wot_ref,
    w1t_ref,
    w2t_ref,
    row_send,
    row_recv,
    cot_send,
    cot_recv,
    result_send,
    result_recv,
    local_sem,
):
    slot, head = pl.program_id(0), pl.program_id(1)
    slots = pl.num_programs(0)
    slot_dev = cot_in.shape[0]
    frames, model = rows_ref.shape[1:]
    inner = q_ref.shape[1]
    size = inner // heads
    my_band, my_batch = lax.axis_index("band"), lax.axis_index("batch")
    frame_dev = frames // batch_count
    piece = frame_dev // band_count
    own_rows = pl.ds(pl.multiple_of(my_batch * frame_dev, frame_dev), frame_dev)
    held = x_ref.shape[0]

    def own_row_copy(j):
        return pltpu.make_async_copy(
            act_in.at[batch_count * j + my_batch], x_ref.at[j, own_rows], local_sem.at[j]
        )

    def own_cot_copy():
        return pltpu.make_async_copy(
            cot_in.at[:, pl.ds(pl.multiple_of(my_band * piece, piece), piece)],
            band_cot.at[pl.ds(my_band * slot_dev, slot_dev)],
            local_sem.at[held],
        )

    @pl.when((slot == 0) & (head == 0))
    def start():
        greet_all(band_count, batch_count)
        for j in range(held):
            for i in range(1, batch_count):
                other = lax.rem(my_batch + i, batch_count)
                send(
                    act_in.at[batch_count * j + other],
                    x_ref.at[j, own_rows],
                    row_send,
                    row_recv.at[j],
                    my_band,
                    other,
                )
            own_row_copy(j).start()

        def send_cot(i, carry):
            other = lax.rem(my_band + i, band_count)
            send(
                cot_in.at[:, pl.ds(pl.multiple_of(other * piece, piece), piece)],
                band_cot.at[pl.ds(my_band * slot_dev, slot_dev)],
                cot_send,
                cot_recv,
                other,
                my_batch,
            )
            return carry

        lax.fori_loop(1, band_count, send_cot, 0)
        own_cot_copy().start()
        wpt_ref[...] = flipped(wp_ref)
        wgt_ref[...] = flipped(wg_ref)
        wot_ref[...] = flipped(wo_ref)
        w1t_ref[...] = flipped(w1_ref)
        w2t_ref[...] = flipped(w2_ref)
        band_wpt_ref[...] = flipped(band_wp_ref)
        band_wgt_ref[...] = flipped(band_wg_ref)
        band_wot_ref[...] = flipped(band_wo_ref)
        band_w1t_ref[...] = flipped(band_w1_ref)
        band_w2t_ref[...] = flipped(band_w2_ref)

    @pl.when(head == 0)
    def before():
        for j in range(held):

            @pl.when(slot == j)
            def arrived():
                await_bytes(x_ref.at[j, pl.ds(0, (batch_count - 1) * frame_dev)], row_recv.at[j])
                own_row_copy(j).wait()

        gain = column(g1_ref)

        def block(i, carry):
            at = pl.ds(pl.multiple_of(i * BLOCK, BLOCK), BLOCK)
            held_rows = x_ref[slot, at, :]
            rows_ref[0, at, :] = held_rows
            rows = held_rows.astype(F32).T
            xt_ref[:, at] = rows
            normed = norm_forward(rows, gain)
            n_ref[0, :, at] = normed
            queries, keys, values = project_block(
                normed, wpt_ref, cos_ref[:, at], sin_ref[:, at], inner, LOG2E * size**-0.5
            )
            q_ref[0, :, at] = queries
            k_ref[0, :, at] = keys
            v_ref[0, :, at] = values
            gate_ref[0, :, at] = dg(wgt_ref[...], normed, NN)
            return carry

        lax.fori_loop(0, frames // BLOCK, block, 0)

    at_head = pl.ds(pl.multiple_of(head * size, size), size)
    ones = jnp.ones((1, frames), F32)
    queries = jnp.concatenate([q_ref[0, at_head, :], extra_rows([ones], frames)], axis=0)
    keys = jnp.concatenate([k_ref[0, at_head, :], extra_rows([bias_ref[...]], frames)], axis=0)
    values = jnp.concatenate([v_ref[0, at_head, :], extra_rows([ones], frames)], axis=0)
    scores = dg(keys, queries, TN)
    weights = jnp.exp2(scores - jnp.max(scores, axis=0, keepdims=True)).astype(BF16)
    p_ref[0, 0] = weights
    sums = dg(values, weights, NN)
    inverse = 1.0 / sums[size : size + 1]
    attended = sums[:size] * inverse
    linv_ref[0, pl.ds(head, 1), :] = inverse
    att_ref[0, at_head, :] = attended
    gate = jax.nn.sigmoid(gate_ref[0, pl.ds(head, 1), :])
    mixed_ref[0, at_head, :] = (attended * gate).astype(BF16)

    @pl.when(head == heads - 1)
    def after():
        gain = column(g2_ref)
        to_slot = my_band * slot_dev + batch_count * slot + my_batch

        def block(i, carry):
            at = pl.ds(pl.multiple_of(i * BLOCK, BLOCK), BLOCK)
            middle = xt_ref[:, at] + dg(wot_ref[...], mixed_ref[0, :, at], NN)
            mid_ref[0, :, at] = middle
            normed = norm_forward(middle, gain)
            nf_ref[0, :, at] = normed
            active, slope = gelu_pair(dg(w1t_ref[...], normed, NN))
            active = active.astype(BF16)
            act_ref[0, :, at] = active
            slope_ref[0, :, at] = slope.astype(BF16)
            result = middle + dg(w2t_ref[...], active, NN)
            result_ref[slot, at, :] = result.T.astype(BF16)

            def send_result(j, carry):
                other = lax.rem(my_band + j, band_count)
                source = result_ref.at[slot, pl.ds(pl.multiple_of(i * frame_dev + other * piece, piece), piece)]
                mine = (other == my_band) & (i == my_batch)

                @pl.when(mine)
                def keep():
                    pltpu.make_async_copy(source, band_rows.at[to_slot], local_sem.at[held + 1]).start()

                @pl.when(jnp.logical_not(mine))
                def give():
                    send(source, band_rows.at[to_slot], result_send, result_recv, other, i)

                return carry

            lax.fori_loop(1, band_count + 1, send_result, 0)
            return carry

        lax.fori_loop(0, frames // BLOCK, block, 0)

    @pl.when((slot == slots - 1) & (head == heads - 1))
    def finish():
        others = held * (band_count * batch_count - 1)
        others_cot = (band_count - 1) * slot_dev
        others_rows = (batch_count - 1) * frame_dev
        await_bytes(band_cot.at[pl.ds(0, others_cot)], cot_recv)
        await_bytes(band_cot.at[pl.ds(0, others_cot)], cot_send)
        own_cot_copy().wait()
        await_bytes(x_ref.at[:, pl.ds(0, others_rows)], row_send)
        await_bytes(band_rows.at[pl.ds(0, others)], result_send)
        await_bytes(band_rows.at[pl.ds(0, held)], local_sem.at[held + 1])
        await_bytes(band_rows.at[pl.ds(0, others)], result_recv)


def sum_shapes(*shapes):
    return [jax.ShapeDtypeStruct(shape, BF16) for shape in shapes]


def sum_specs(*shapes):
    return [pl.BlockSpec(shape, lambda *ids: (0, 0)) for shape in shapes]


def cost(flops, exps=0, moved=0):
    return pl.CostEstimate(flops=int(flops), bytes_accessed=int(moved), transcendentals=int(exps))


def whole_spec(array):
    nd = array.ndim
    return pl.BlockSpec(array.shape, lambda *ids: (0,) * nd, pipeline_mode=pl.Buffered(1))


def time_forward(activations, cotangent, bias, cos, sin, params, band_params, band_count, batch_count):
    g1, wp, wg, wo, g2, w1, w2 = params
    _, bwp, bwg, bwo, _, bw1, bw2 = band_params
    slot_dev, frame_dev, model = activations.shape
    slots, frames = slot_dev // batch_count, frame_dev * batch_count
    heads, inner, hidden = wg.shape[1], wo.shape[0], w1.shape[1]
    piece = frame_dev // band_count

    def per_slot(*shape):
        return pl.BlockSpec((1,) + shape, lambda s, h: (s,) + (0,) * len(shape))

    outs = [
        ((frames, model), BF16),
        ((model, frames), BF16),
        ((inner, frames), BF16),
        ((inner, frames), BF16),
        ((inner, frames), BF16),
        None,
        ((heads, frames), F32),
        ((heads, frames), F32),
        ((inner, frames), F32),
        ((inner, frames), BF16),
        ((model, frames), F32),
        ((model, frames), BF16),
        ((hidden, frames), BF16),
        ((hidden, frames), BF16),
    ]
    flips = [(w.shape[1], w.shape[0]) for w in (bwp, bwg, bwo, bw1, bw2)]
    own_flips = [(w.shape[1], w.shape[0]) for w in (wp, wg, wo, w1, w2)]
    exchanged = jax.ShapeDtypeStruct((slot_dev * band_count, piece, model), BF16)
    anywhere = pl.BlockSpec(memory_space=pl.ANY)
    shapes, specs = [exchanged, exchanged], [anywhere, anywhere]
    for entry in outs:
        if entry is None:
            shapes.append(jax.ShapeDtypeStruct((slots, heads, frames, frames), BF16))
            specs.append(pl.BlockSpec((1, 1, frames, frames), lambda s, h: (s, h, 0, 0)))
        else:
            shapes.append(jax.ShapeDtypeStruct((slots,) + entry[0], entry[1]))
            specs.append(per_slot(*entry[0]))
    for shape in flips:
        shapes.append(jax.ShapeDtypeStruct(shape, BF16))
        specs.append(pl.BlockSpec(shape, lambda s, h: (0, 0), pipeline_mode=pl.Buffered(1)))
    consts = (bias, cos, sin, g1, g2, wp, wg, wo, w1, w2, bwp, bwg, bwo, bw1, bw2)
    dma = pltpu.SemaphoreType.DMA
    return pl.pallas_call(
        lambda *refs: time_forward_kernel(heads, batch_count, band_count, *refs),
        grid=(slots, heads),
        out_shape=shapes,
        in_specs=[anywhere, anywhere] + [whole_spec(c) for c in consts],
        out_specs=specs,
        scratch_shapes=[
            pltpu.VMEM((model, frames), F32),
            pltpu.VMEM((slots, frames, model), BF16),
            pltpu.VMEM((slots, frames, model), BF16),
        ]
        + [pltpu.VMEM(shape, BF16) for shape in own_flips]
        + [dma, dma((slots,)), dma, dma, dma, dma, dma((slots + 2,))],
        compiler_params=pltpu.CompilerParams(
            vmem_limit_bytes=VMEM_BYTES, collective_id=0, has_side_effects=True
        ),
        cost_estimate=cost(2.0e6 * 4 * slots * frames, 2 * slots * heads * frames * frames, 60e6),
        name="time_forward",
    )(activations, cotangent, *consts)


def ffn_backward(grad, act, slope, normed, middle, gain, w1_ref, w2_ref, dw1_ref, dw2t_ref, dg2_ref):
    branch = grad.astype(BF16)
    d_hidden = (dg(w2_ref[...], branch, NN) * slope.astype(F32)).astype(BF16)
    dw2t_ref[...] += dg(branch, act, NT)
    dw1_ref[...] += dg(normed, d_hidden, NT)
    d_normed = dg(w1_ref[...], d_hidden, NN)
    d_rows, terms = norm_backward(middle, gain, d_normed)
    dg2_ref[...] += jnp.sum(terms, axis=1, keepdims=True)
    return grad + d_rows


def head_backward(d_mixed, attended, gate_logit, inverse):
    gate = jax.nn.sigmoid(gate_logit)
    d_logit = jnp.sum(d_mixed * attended, axis=0, keepdims=True) * gate * (1.0 - gate)
    d_att = (d_mixed * (gate * inverse)).astype(BF16)
    minus = -jnp.sum(d_att.astype(F32) * attended, axis=0, keepdims=True)
    return d_att, minus, d_logit


def scores_backward(queries, keys, values, weights, d_att, minus, cos, sin, scale):
    width = queries.shape[1]
    ones = jnp.ones((1, width), F32)
    d_weights = dg(
        jnp.concatenate([values, extra_rows([ones, ones, ones], width)], axis=0),
        jnp.concatenate([d_att, extra_rows(list(three_parts(minus)), width)], axis=0),
        TN,
    )
    d_scores = (weights.astype(F32) * d_weights).astype(BF16)
    d_values = dg(d_att, weights, NT)
    d_queries = dg(keys, d_scores, NN) * scale
    d_keys = dg(queries, d_scores, NT) * (1.0 / LOG2E)
    return turn(d_queries, cos, -sin), turn(d_keys, cos, -sin), d_values


def time_ffn_backward_kernel(
    heads,
    grad_ref,
    act_ref,
    slope_ref,
    nf_ref,
    mid_ref,
    mixed_ref,
    att_ref,
    gate_ref,
    linv_ref,
    g2_ref,
    w1_ref,
    w2_ref,
    wo_ref,
    dmid_ref,
    datt_ref,
    minus_ref,
    dlogit_ref,
    *refs,
):
    sums_refs, (dw1_ref, dw2t_ref, dwot_ref, dg2_ref) = refs[:4], refs[4:]
    step = pl.program_id(0) * pl.num_programs(1) + pl.program_id(1)
    last = pl.num_programs(0) * pl.num_programs(1) - 1
    size = wo_ref.shape[0] // heads

    @pl.when(step == 0)
    def clear():
        for ref in (dw1_ref, dw2t_ref, dwot_ref, dg2_ref):
            ref[...] = jnp.zeros_like(ref)

    grad = grad_ref[0].astype(F32).T
    d_middle = ffn_backward(
        grad, act_ref[0], slope_ref[0], nf_ref[0], mid_ref[0], column(g2_ref), w1_ref, w2_ref, dw1_ref, dw2t_ref, dg2_ref
    )
    dmid_ref[0] = d_middle
    branch = d_middle.astype(BF16)
    dwot_ref[...] += dg(branch, mixed_ref[0], NT)
    d_mixed = dg(wo_ref[...], branch, NN)
    logits, minuses = [], []
    for head in range(heads):
        at = slice(head * size, (head + 1) * size)
        d_att, minus, d_logit = head_backward(
            d_mixed[at], att_ref[0, at], gate_ref[0, head : head + 1], linv_ref[0, head : head + 1]
        )
        datt_ref[0, at] = d_att
        minuses.append(minus)
        logits.append(d_logit)
    minus_ref[0] = jnp.concatenate(minuses, axis=0)
    dlogit_ref[0] = jnp.concatenate(logits, axis=0)

    @pl.when(step == last)
    def finish():
        finish_sums(sums_refs, ((dw1_ref, False), (dw2t_ref, True), (dwot_ref, True), dg2_ref))


def finish_sums(outs, parts):
    narrow = []
    for out_ref, (ref, flipped) in zip(outs[:-1], parts):
        out_ref[...] = (ref[...].T if flipped else ref[...]).astype(BF16)
    for ref in parts[len(outs) - 1 :]:
        narrow.append(ref[...])
    used = sum(part.shape[1] for part in narrow)
    narrow.append(jnp.zeros((outs[-1].shape[0], 128 - used), F32))
    outs[-1][...] = jnp.concatenate(narrow, axis=1).astype(BF16)


def time_ffn_backward(grad, act, slope, nf, mid, mixed, att, gate, linv, g2, w1, w2, wo):
    slots, frames, model = grad.shape
    heads = gate.shape[1]
    inner, hidden = wo.shape[0], w1.shape[1]
    tokens = min(frames, 512)

    def cut(rows):
        return pl.BlockSpec((1, rows, tokens), lambda s, c: (s, 0, c))

    consts = (g2, w1, w2, wo)
    sums = ((model, hidden), (hidden, model), (inner, model), (model, 128))
    return pl.pallas_call(
        lambda *refs: time_ffn_backward_kernel(heads, *refs),
        grid=(slots, frames // tokens),
        out_shape=[
            jax.ShapeDtypeStruct((slots, model, frames), F32),
            jax.ShapeDtypeStruct((slots, inner, frames), BF16),
            jax.ShapeDtypeStruct((slots, heads, frames), F32),
            jax.ShapeDtypeStruct((slots, heads, frames), F32),
        ]
        + sum_shapes(*sums),
        in_specs=[pl.BlockSpec((1, tokens, model), lambda s, c: (s, c, 0))]
        + [cut(a.shape[1]) for a in (act, slope, nf, mid, mixed, att, gate, linv)]
        + [whole_spec(c) for c in consts],
        out_specs=[cut(model), cut(inner), cut(heads), cut(heads)] + sum_specs(*sums),
        scratch_shapes=[
            pltpu.VMEM((model, hidden), F32),
            pltpu.VMEM((model, hidden), F32),
            pltpu.VMEM((model, inner), F32),
            pltpu.VMEM((model, 1), F32),
        ],
        compiler_params=pltpu.CompilerParams(vmem_limit_bytes=VMEM_BYTES),
        cost_estimate=cost(8.0e6 * slots * frames, 0, 30e6),
        name="time_ffn_backward",
    )(grad, act, slope, nf, mid, mixed, att, gate, linv, *consts)


def time_attention_backward_kernel(
    heads,
    p_ref,
    q_ref,
    k_ref,
    v_ref,
    datt_ref,
    minus_ref,
    dlogit_ref,
    n_ref,
    x_ref,
    dmid_ref,
    cos_ref,
    sin_ref,
    g1_ref,
    wp_ref,
    wg_ref,
    out_ref,
    *refs,
):
    sums_refs, (dproj_ref, dwp_ref, dwg_ref, dg1_ref) = refs[:2], refs[2:]
    slot, head = pl.program_id(0), pl.program_id(1)
    inner = q_ref.shape[1]
    size = inner // heads
    frames = q_ref.shape[2]

    @pl.when((slot == 0) & (head == 0))
    def clear():
        for ref in (dwp_ref, dwg_ref, dg1_ref):
            ref[...] = jnp.zeros_like(ref)

    start = pl.multiple_of(head * size, size)
    at = pl.ds(start, size)
    d_queries, d_keys, d_values = scores_backward(
        q_ref[0, at, :],
        k_ref[0, at, :],
        v_ref[0, at, :],
        p_ref[0, 0],
        datt_ref[0, at, :],
        minus_ref[0, pl.ds(head, 1), :],
        cos_ref[...],
        sin_ref[...],
        size**-0.5,
    )
    dproj_ref[at, :] = d_queries.astype(BF16)
    dproj_ref[pl.ds(inner + start, size), :] = d_keys.astype(BF16)
    dproj_ref[pl.ds(2 * inner + start, size), :] = d_values.astype(BF16)

    @pl.when(head == heads - 1)
    def after():
        d_logit = jnp.concatenate([dlogit_ref[0], jnp.zeros_like(dlogit_ref[0])], axis=0).astype(BF16)
        dwp_ref[...] += dg(n_ref[0], dproj_ref[...], NT)
        dwg_ref[...] += dg(n_ref[0], d_logit, NT)[:, :heads]
        gain = column(g1_ref)

        def block(i, carry):
            at = pl.ds(pl.multiple_of(i * BLOCK, BLOCK), BLOCK)
            logit = dlogit_ref[0, :, at].astype(BF16)
            d_normed = dg(wp_ref[...], dproj_ref[:, at], NN) + dg(wg_ref[...], logit, NN)
            d_rows, terms = norm_backward(x_ref[0, at, :].astype(F32).T, gain, d_normed)
            dg1_ref[...] += jnp.sum(terms, axis=1, keepdims=True)
            out_ref[0, at, :] = (dmid_ref[0, :, at] + d_rows).T.astype(BF16)
            return carry

        lax.fori_loop(0, frames // BLOCK, block, 0)

    @pl.when((slot == pl.num_programs(0) - 1) & (head == heads - 1))
    def finish():
        finish_sums(sums_refs, ((dwp_ref, False), dwg_ref, dg1_ref))


def time_attention_backward(p, q, k, v, datt, minus, dlogit, n, x, dmid, cos, sin, g1, wp, wg):
    slots, inner, frames = q.shape
    heads = minus.shape[1]
    model = n.shape[1]

    def per_slot(array):
        return pl.BlockSpec((1,) + array.shape[1:], lambda s, h: (s, 0, 0))

    consts = (cos, sin, g1, wp, wg)
    sums = ((model, 3 * inner), (model, 128))
    return pl.pallas_call(
        lambda *refs: time_attention_backward_kernel(heads, *refs),
        grid=(slots, heads),
        out_shape=[
            jax.ShapeDtypeStruct((slots, frames, model), BF16),
        ]
        + sum_shapes(*sums),
        in_specs=[pl.BlockSpec((1, 1, frames, frames), lambda s, h: (s, h, 0, 0))]
        + [per_slot(a) for a in (q, k, v, datt, minus, dlogit, n, x, dmid)]
        + [whole_spec(c) for c in consts],
        out_specs=[
            pl.BlockSpec((1, frames, model), lambda s, h: (s, 0, 0)),
        ]
        + sum_specs(*sums),
        scratch_shapes=[
            pltpu.VMEM((3 * inner, frames), BF16),
            pltpu.VMEM((model, 3 * inner), F32),
            pltpu.VMEM((model, heads), F32),
            pltpu.VMEM((model, 1), F32),
        ],
        compiler_params=pltpu.CompilerParams(vmem_limit_bytes=VMEM_BYTES),
        cost_estimate=cost(20.0e6 * slots * frames, 0, 60e6),
        name="time_attention_backward",
    )(p, q, k, v, datt, minus, dlogit, n, x, dmid, *consts)


def band_kernel(
    heads,
    batch_count,
    band_count,
    x_ref,
    cot_ref,
    mask_ref,
    bias_ref,
    cos_ref,
    sin_ref,
    g1_ref,
    g2_ref,
    wpt_ref,
    wgt_ref,
    wot_ref,
    w1t_ref,
    w2t_ref,
    wp_ref,
    wg_ref,
    wo_ref,
    w1_ref,
    w2_ref,
    y_out,
    dx_out,
    dwp_out,
    dw1_out,
    dw2_out,
    dwo_out,
    narrow_out,
    q_ref,
    k_ref,
    v_ref,
    p_ref,
    gate_ref,
    linv_ref,
    att_ref,
    mixed_ref,
    act_ref,
    slope_ref,
    datt_ref,
    dmixed_ref,
    dlogit_ref,
    dproj_ref,
    dwp_ref,
    dw1_ref,
    dw2t_ref,
    dwot_ref,
    dwg_ref,
    dg1_ref,
    dg2_ref,
    xs_ref,
    cots_ref,
    ys_ref,
    dxs_ref,
    y_buf,
    dx_buf,
    y_send,
    y_recv,
    dx_send,
    dx_recv,
    local_sem,
):
    step = pl.program_id(0)
    slot_count, part_frames, model = x_ref.shape
    inner, tokens = q_ref.shape
    size = inner // heads
    groups = tokens // BLOCK
    taken = tokens // slot_count
    per_part = part_frames // taken
    part = step // per_part
    first = lax.rem(step, per_part) * taken
    my_band, my_batch = lax.axis_index("band"), lax.axis_index("batch")
    slot_dev = slot_count // band_count
    slots = slot_dev // batch_count
    part_at = pl.multiple_of(part * part_frames, part_frames)
    own_at = pl.multiple_of(my_band * (y_out.shape[1] // band_count) + part * part_frames, part_frames)
    own_chunk = my_batch * band_count + my_band
    chunks = band_count * batch_count

    columns = [slice(at, at + 128) for at in range(0, model, 128)]

    def tokens_of(ref):
        return jnp.concatenate(
            [
                jnp.concatenate(
                    [ref[c, pl.ds(first + i, slot_count, stride=part_frames), :] for i in range(taken)], axis=0
                ).T
                for c in range(len(columns))
            ],
            axis=0,
        )

    def put_tokens(ref, values):
        for c, at in enumerate(columns):
            turned = values[at].T
            for i in range(taken):
                ref[c, pl.ds(first + i, slot_count, stride=part_frames), :] = turned[
                    i * slot_count : (i + 1) * slot_count
                ]

    @pl.when(step == 0)
    def enter():
        greet_all(band_count, batch_count)

    @pl.when(lax.rem(step, per_part) == 0)
    def unpack():
        for c, at in enumerate(columns):
            xs_ref[c] = x_ref[:, :, at].astype(F32).reshape(xs_ref.shape[1:])
            cots_ref[c] = cot_ref[:, :, at].astype(F32).reshape(cots_ref.shape[1:])

    gain1, gain2 = column(g1_ref), column(g2_ref)
    sums_refs = (dwp_out, dw1_out, dw2_out, dwo_out, narrow_out)

    @pl.when(step == 0)
    def clear():
        for ref in (dwp_ref, dw1_ref, dw2t_ref, dwot_ref, dwg_ref, dg1_ref, dg2_ref):
            ref[...] = jnp.zeros_like(ref)

    rows = tokens_of(xs_ref)
    normed = norm_forward(rows, gain1)
    q_ref[...], k_ref[...], v_ref[...] = project_block(
        normed, wpt_ref, cos_ref[...], sin_ref[...], inner, LOG2E * size**-0.5
    )
    gate_ref[...] = dg(wgt_ref[...], normed, NN)
    ones = extra_rows([jnp.ones((1, BLOCK), F32)], BLOCK)

    def attend(head, carry):
        at = pl.ds(pl.multiple_of(head * size, size), size)
        row = pl.ds(head, 1)
        for group in range(groups):
            lanes = slice(group * BLOCK, (group + 1) * BLOCK)
            scores = dg(k_ref[at, lanes], q_ref[at, lanes], TN) + bias_ref[...]
            weights = jnp.exp2(scores - jnp.max(scores, axis=0, keepdims=True)).astype(BF16)
            p_ref[head * groups + group] = weights
            sums = dg(jnp.concatenate([v_ref[at, lanes], ones], axis=0), weights, NN)
            inverse = 1.0 / sums[size : size + 1]
            attended = sums[:size] * inverse
            linv_ref[row, lanes] = inverse
            att_ref[at, lanes] = attended
            gate = jax.nn.sigmoid(gate_ref[row, lanes])
            mixed_ref[at, lanes] = (attended * gate).astype(BF16)
        return carry

    lax.fori_loop(0, heads, attend, 0)
    middle = rows + dg(wot_ref[...], mixed_ref[...], NN)
    normed_ffn = norm_forward(middle, gain2)

    hidden = w1t_ref.shape[0]
    quarter = hidden // 4

    def expand(i, carry):
        at = pl.ds(pl.multiple_of(i * quarter, quarter), quarter)
        active, slope = gelu_pair(dg(w1t_ref[at, :], normed_ffn, NN))
        act_ref[at, :] = active.astype(BF16)
        slope_ref[at, :] = slope.astype(BF16)
        return carry

    lax.fori_loop(0, 4, expand, 0)
    mask = mask_ref[0]
    result = (middle + dg(w2t_ref[...], act_ref[...], NN)) * mask
    put_tokens(ys_ref, result)

    @pl.when(lax.rem(step, per_part) == per_part - 1)
    def send_rows():
        for c, at in enumerate(columns):
            y_buf[part, :, :, at] = ys_ref[c].reshape(slot_count, part_frames, 128).astype(BF16)

        def give(i, carry):
            other = lax.rem(my_band + i, band_count)
            send(
                y_buf.at[part, pl.ds(other * slot_dev, slot_dev)],
                y_out.at[:, pl.ds(own_at, part_frames)],
                y_send,
                y_recv,
                other,
                my_batch,
            )
            return carry

        lax.fori_loop(1, band_count, give, 0)
        pltpu.make_async_copy(
            y_buf.at[part, pl.ds(my_band * slot_dev, slot_dev)],
            y_out.at[:, pl.ds(own_at, part_frames)],
            local_sem.at[0],
        ).start()

    grad = tokens_of(cots_ref) * mask
    d_middle = ffn_backward(
        grad, act_ref[...], slope_ref[...], normed_ffn, middle, gain2, w1_ref, w2_ref, dw1_ref, dw2t_ref, dg2_ref
    )
    branch = d_middle.astype(BF16)
    dwot_ref[...] += dg(branch, mixed_ref[...], NT)
    dmixed_ref[...] = dg(wo_ref[...], branch, NN)

    def attend_back(head, carry):
        start = pl.multiple_of(head * size, size)
        at = pl.ds(start, size)
        row = pl.ds(head, 1)
        d_att, minus, d_logit = head_backward(dmixed_ref[at, :], att_ref[at, :], gate_ref[row, :], linv_ref[row, :])
        dlogit_ref[row, :] = d_logit
        for group in range(groups):
            lanes = slice(group * BLOCK, (group + 1) * BLOCK)
            d_queries, d_keys, d_values = scores_backward(
                q_ref[at, lanes],
                k_ref[at, lanes],
                v_ref[at, lanes],
                p_ref[head * groups + group],
                d_att[:, lanes],
                minus[:, lanes],
                cos_ref[:, lanes],
                sin_ref[:, lanes],
                size**-0.5,
            )
            dproj_ref[at, lanes] = d_queries.astype(BF16)
            dproj_ref[pl.ds(inner + start, size), lanes] = d_keys.astype(BF16)
            dproj_ref[pl.ds(2 * inner + start, size), lanes] = d_values.astype(BF16)
        return carry

    lax.fori_loop(0, heads, attend_back, 0)
    d_logit = jnp.concatenate([dlogit_ref[...], jnp.zeros_like(dlogit_ref)], axis=0).astype(BF16)
    dwp_ref[...] += dg(normed, dproj_ref[...], NT)
    dwg_ref[...] += dg(normed, d_logit, NT)[:, :heads]
    d_normed = dg(wp_ref[...], dproj_ref[...], NN) + dg(wg_ref[...], dlogit_ref[...].astype(BF16), NN)
    d_rows, terms = norm_backward(rows, gain1, d_normed)
    dg1_ref[...] += jnp.sum(terms, axis=1, keepdims=True)
    put_tokens(dxs_ref, d_middle + d_rows)

    @pl.when(lax.rem(step, per_part) == per_part - 1)
    def send_grads():
        for c, at in enumerate(columns):
            dx_buf[part, :, :, at] = dxs_ref[c].reshape(slot_count, part_frames, 128).astype(BF16)

        def give(i, carry):
            other = lax.rem(my_band * batch_count + my_batch + i, chunks)
            band, batch = other // batch_count, lax.rem(other, batch_count)
            for j in range(slots):
                send(
                    dx_buf.at[part, band * slot_dev + batch_count * j + batch],
                    dx_out.at[j * chunks + own_chunk, pl.ds(part_at, part_frames)],
                    dx_send,
                    dx_recv,
                    band,
                    batch,
                )
            return carry

        lax.fori_loop(1, chunks, give, 0)
        for j in range(slots):
            pltpu.make_async_copy(
                dx_buf.at[part, my_band * slot_dev + batch_count * j + my_batch],
                dx_out.at[j * chunks + own_chunk, pl.ds(part_at, part_frames)],
                local_sem.at[1],
            ).start()

    @pl.when(step == pl.num_programs(0) - 1)
    def finish():
        finish_sums(
            sums_refs,
            ((dwp_ref, False), (dw1_ref, False), (dw2t_ref, True), (dwot_ref, True), dwg_ref, dg1_ref, dg2_ref),
        )
        piece = y_out.shape[1] // band_count
        await_bytes(y_out.at[:, pl.ds(0, piece)], local_sem.at[0])
        await_bytes(dx_out.at[pl.ds(0, slots)], local_sem.at[1])
        for sem in (y_send, y_recv):
            await_bytes(y_out.at[:, pl.ds(0, piece * (band_count - 1))], sem)
        for sem in (dx_send, dx_recv):
            await_bytes(dx_out.at[pl.ds(0, slots * (chunks - 1))], sem)


def band_layer(rows, cot, mask, bias, cos, sin, params, flips, band_count, batch_count):
    prenorm, project, gating, output_weight, midnorm, expand, shrink = params
    slot_count, piece, model = rows.shape
    steps, _, tokens = mask.shape
    heads, inner, hidden = gating.shape[1], output_weight.shape[0], expand.shape[1]
    groups = tokens // BLOCK
    taken = tokens // slot_count
    part_frames = 16
    per_part = part_frames // taken
    parts = piece // part_frames
    slot_dev = slot_count // band_count
    consts = (bias, cos, sin, prenorm, midnorm) + flips + (project, gating, output_weight, expand, shrink)
    sums = ((model, 3 * inner), (model, hidden), (hidden, model), (inner, model), (model, 128))
    blocks = pl.BlockSpec((slot_count, part_frames, model), lambda i: (0, i // per_part, 0))
    anywhere = pl.BlockSpec(memory_space=pl.ANY)
    dma = pltpu.SemaphoreType.DMA
    return pl.pallas_call(
        lambda *refs: band_kernel(heads, batch_count, band_count, *refs),
        grid=(steps,),
        out_shape=[
            jax.ShapeDtypeStruct((slot_dev, piece * band_count, model), BF16),
            jax.ShapeDtypeStruct((slot_count, piece, model), BF16),
        ]
        + sum_shapes(*sums),
        in_specs=[blocks, blocks, pl.BlockSpec((1, 1, tokens), lambda i: (i, 0, 0))] + [whole_spec(c) for c in consts],
        out_specs=[anywhere, anywhere] + sum_specs(*sums),
        scratch_shapes=[
            pltpu.VMEM((inner, tokens), BF16),
            pltpu.VMEM((inner, tokens), BF16),
            pltpu.VMEM((inner, tokens), BF16),
            pltpu.VMEM((heads * groups, BLOCK, BLOCK), BF16),
            pltpu.VMEM((heads, tokens), F32),
            pltpu.VMEM((heads, tokens), F32),
            pltpu.VMEM((inner, tokens), F32),
            pltpu.VMEM((inner, tokens), BF16),
            pltpu.VMEM((hidden, tokens), BF16),
            pltpu.VMEM((hidden, tokens), BF16),
            pltpu.VMEM((inner, tokens), BF16),
            pltpu.VMEM((inner, tokens), F32),
            pltpu.VMEM((heads, tokens), F32),
            pltpu.VMEM((3 * inner, tokens), BF16),
            pltpu.VMEM((model, 3 * inner), F32),
            pltpu.VMEM((model, hidden), F32),
            pltpu.VMEM((model, hidden), F32),
            pltpu.VMEM((model, inner), F32),
            pltpu.VMEM((model, heads), F32),
            pltpu.VMEM((model, 1), F32),
            pltpu.VMEM((model, 1), F32),
            pltpu.VMEM((model // 128, slot_count * part_frames, 128), F32),
            pltpu.VMEM((model // 128, slot_count * part_frames, 128), F32),
            pltpu.VMEM((model // 128, slot_count * part_frames, 128), F32),
            pltpu.VMEM((model // 128, slot_count * part_frames, 128), F32),
            pltpu.VMEM((parts, slot_count, part_frames, model), BF16),
            pltpu.VMEM((parts, slot_count, part_frames, model), BF16),
            dma,
            dma,
            dma,
            dma,
            dma((2,)),
        ],
        compiler_params=pltpu.CompilerParams(
            vmem_limit_bytes=VMEM_BYTES, collective_id=1, has_side_effects=True
        ),
        cost_estimate=cost(30.0e6 * slot_count * piece, 0, 60e6),
        name="band_layer",
    )(rows, cot, mask, *consts)


def slot_shards(activations, cotangent, frame_counts, slot_bands, *weights):
    slot_dev, _, frame_dev, model = activations.shape
    slot_count = slot_bands.shape[0]
    batch, band = lax.axis_size("batch"), lax.axis_size("band")
    frames = frame_dev * batch
    piece = frame_dev // band
    slots = slot_dev // batch
    weights = tuple(w[None] if w.ndim == 1 else w for w in weights)
    time_params, band_params = weights[:7], weights[7:]
    heads, inner, hidden = time_params[2].shape[1], time_params[3].shape[0], time_params[5].shape[1]
    size = inner // heads

    positions = jnp.arange(frames, dtype=jnp.int32)
    time_cos, time_sin = rotary_tables(positions.astype(F32), size)
    time_bias = jnp.where(positions[None, :] < frame_counts[:, None], 0.0, NEG_FILL).astype(F32)
    band_cos, band_sin = rotary_tables(jnp.maximum(slot_bands, 0).astype(F32), size)
    tokens = min(2 * BLOCK, piece * slot_count)
    copies = tokens // slot_count
    slot_valid = slot_bands >= 0
    index = jnp.arange(BLOCK, dtype=jnp.int32)
    together = (index[:, None] // slot_count == index[None, :] // slot_count) & jnp.tile(
        slot_valid, BLOCK // slot_count
    )[:, None]
    band_bias = jnp.where(together, 0.0, NEG_FILL).astype(F32)
    own_start = lax.axis_index("batch") * frame_dev + lax.axis_index("band") * piece
    own_frames = own_start + jnp.arange(piece, dtype=jnp.int32)
    mask = ((own_frames < frame_counts[0])[:, None] & slot_valid[None, :]).astype(F32)
    mask = mask.reshape(piece * slot_count // tokens, 1, tokens)

    band_rows, band_cot, rows, n, q, k, v, p, linv, gate, att, mixed, mid, nf, act, slope, *flips = time_forward(
        activations.reshape(slot_dev, frame_dev, model),
        cotangent.reshape(slot_dev, frame_dev, model),
        time_bias,
        time_cos.T,
        time_sin.T,
        time_params,
        band_params,
        band,
        batch,
    )
    layer_output, slot_grad, *band_sums = band_layer(
        band_rows,
        band_cot,
        mask,
        band_bias,
        jnp.tile(band_cos.T, (1, copies)),
        jnp.tile(band_sin.T, (1, copies)),
        band_params,
        tuple(flips),
        band,
        batch,
    )
    slot_grad = slot_grad.reshape(slots, frames, model)
    g1, g2 = time_params[0], time_params[4]
    dmid, datt, minus, dlogit, *ffn_sums = time_ffn_backward(
        slot_grad, act, slope, nf, mid, mixed, att, gate, linv, g2, time_params[5], time_params[6], time_params[3]
    )
    grads, *attn_sums = time_attention_backward(
        p, q, k, v, datt, minus, dlogit, n, rows, dmid, time_cos.T, time_sin.T, g1, time_params[1], time_params[2]
    )
    input_grad = lax.all_to_all(grads, "batch", split_axis=1, concat_axis=0, tiled=True)
    input_grad = input_grad.reshape(batch, slots, frame_dev, model).transpose(1, 0, 2, 3)
    attn_sums, ffn_sums, band_sums = lax.psum((attn_sums, ffn_sums, band_sums), ("band", "batch"))

    dwp, attn_narrow = (part.astype(F32) for part in attn_sums)
    dw1, dw2, dwo, ffn_narrow = (part.astype(F32) for part in ffn_sums)
    bwp, bw1, bw2, bwo, band_narrow = (part.astype(F32) for part in band_sums)
    return (
        layer_output.reshape(activations.shape),
        input_grad.astype(F32).reshape(activations.shape),
        attn_narrow[:, heads],
        dwp,
        attn_narrow[:, :heads],
        dwo,
        ffn_narrow[:, 0],
        dw1,
        dw2,
        band_narrow[:, heads],
        bwp,
        band_narrow[:, :heads],
        bwo,
        band_narrow[:, heads + 1],
        bw1,
        bw2,
    )


def shards(activations, cotangent, frame_counts, slot_bands, *weights):
    slot_dev, clips, frame_dev, _ = activations.shape
    batch, band = lax.axis_size("batch"), lax.axis_size("band")
    fits = (
        clips == 1
        and slot_dev % batch == 0
        and frame_dev == BLOCK
        and frame_dev % (16 * band) == 0
        and slot_bands.shape[0] == 64
        and activations.shape[-1] % 128 == 0
        and (frame_dev // band * slot_bands.shape[0]) % (2 * BLOCK) == 0
        and weights[2].shape[1] == 8
    )
    form = slot_shards if fits else generic_shards
    return form(activations, cotangent, frame_counts, slot_bands, *weights)


def solution(mesh):
    return jax.shard_map(
        shards,
        mesh=mesh,
        in_specs=(
            P("band", None, "batch", None),
            P("band", None, "batch", None),
            P(),
            P(),
            P(),
            P(),
            P(),
            P(),
            P(),
            P(),
            P(),
            P(),
            P(),
            P(),
            P(),
            P(),
            P(),
            P(),
        ),
        out_specs=(
            P("band", None, "batch", None),
            P("band", None, "batch", None),
            P(),
            P(),
            P(),
            P(),
            P(),
            P(),
            P(),
            P(),
            P(),
            P(),
            P(),
            P(),
            P(),
            P(),
        ),
        check_vma=False,
    )
```

```python
import math

import jax
import jax.numpy as jnp
from jax import lax
from jax.experimental import pallas as pl
from jax.experimental.pallas import tpu as pltpu
from jax.sharding import PartitionSpec as P

EPSILON = 1e-05
NEG_FILL = -1000000000.0
TIME_LAYOUT = ("bqhe", "bkhe")
BAND_LAYOUT = ("qbhe", "kbhe")


def rms_scale(residual, gain):
    return (
        residual * lax.rsqrt(jnp.mean(residual * residual, axis=-1, keepdims=True) + EPSILON) * gain
    )


def gelu_exact(values):
    return jax.nn.gelu(values, approximate=False)


def rotary_tables(positions, head_size):
    half_size = head_size // 2
    rates = jnp.exp(-math.log(10000.0) * jnp.arange(half_size, dtype=jnp.float32) / half_size)
    angles = positions[:, None] * rates[None, :]
    return (jnp.cos(angles), jnp.sin(angles))


def rotate(vectors, cos_table, sin_table):
    half_size = vectors.shape[-1] // 2
    first = vectors[..., :half_size]
    second = vectors[..., half_size:]
    return jnp.concatenate(
        [first * cos_table - second * sin_table, first * sin_table + second * cos_table], axis=-1
    )


def token_sum(left, right):
    return lax.dot_general(
        left.reshape(-1, left.shape[-1]),
        right.reshape(-1, right.shape[-1]),
        (((0,), (0,)), ((), ())),
        preferred_element_type=jnp.float32,
    )


def back_dot(gradient, weight):
    return lax.dot_general(
        gradient,
        weight,
        (((gradient.ndim - 1,), (1,)), ((), ())),
        preferred_element_type=jnp.float32,
    )


def block_forward(queries, key_rows, value_rows, key_valid, layout):
    query_form, key_form = layout
    scores = (
        jnp.einsum(
            query_form + "," + key_form + "->bhqk",
            queries,
            key_rows,
            preferred_element_type=jnp.float32,
        )
        * 0.125
    )
    scores = jnp.where(key_valid[:, None, None, :], scores, NEG_FILL)
    highest = jnp.max(scores, axis=-1, keepdims=True)
    exponents = jnp.exp(scores - highest)
    totals = jnp.sum(exponents, axis=-1, keepdims=True)
    soft_weights = (exponents / totals).astype(jnp.bfloat16)
    output = jnp.einsum(
        "bhqk," + key_form + "->" + query_form,
        soft_weights,
        value_rows,
        preferred_element_type=jnp.float32,
    )
    return (output, highest + jnp.log(totals))


def block_backward(queries, key_rows, value_rows, key_valid, log_totals, out_grad, layout):
    query_form, key_form = layout
    scores = (
        jnp.einsum(
            query_form + "," + key_form + "->bhqk",
            queries,
            key_rows,
            preferred_element_type=jnp.float32,
        )
        * 0.125
    )
    soft_weights = jnp.where(key_valid[:, None, None, :], jnp.exp(scores - log_totals), 0.0)
    weight_grad = jnp.einsum(
        query_form + "," + key_form + "->bhqk",
        out_grad,
        value_rows,
        preferred_element_type=jnp.float32,
    )
    score_grad = (
        soft_weights * (weight_grad - jnp.sum(soft_weights * weight_grad, axis=-1, keepdims=True))
    ).astype(jnp.bfloat16)
    query_grad = (
        jnp.einsum(
            "bhqk," + key_form + "->" + query_form,
            score_grad,
            key_rows,
            preferred_element_type=jnp.float32,
        )
        * 0.125
    )
    key_grad = (
        jnp.einsum(
            "bhqk," + query_form + "->" + key_form,
            score_grad,
            queries,
            preferred_element_type=jnp.float32,
        )
        * 0.125
    )
    value_grad = jnp.einsum(
        "bhqk," + query_form + "->" + key_form,
        soft_weights.astype(jnp.bfloat16),
        out_grad,
        preferred_element_type=jnp.float32,
    )
    return (query_grad, key_grad, value_grad)


def time_attend(queries, key_rows, value_rows, key_valid):
    keys_full, values_full = (
        lax.all_gather(key_rows, "batch", axis=1, tiled=True),
        lax.all_gather(value_rows, "batch", axis=1, tiled=True),
    )
    output, log_totals = block_forward(queries, keys_full, values_full, key_valid, TIME_LAYOUT)
    return (output, (log_totals, keys_full, values_full))


def time_attend_back(queries, key_rows, value_rows, key_valid, attn_kept, out_grad):
    log_totals, keys_full, values_full = attn_kept
    query_grad, key_full_grad, value_full_grad = block_backward(
        queries, keys_full, values_full, key_valid, log_totals, out_grad, TIME_LAYOUT
    )
    key_grad, value_grad = (
        lax.psum_scatter(
            key_full_grad.astype(jnp.bfloat16), "batch", scatter_dimension=1, tiled=True
        ).astype(jnp.float32),
        lax.psum_scatter(
            value_full_grad.astype(jnp.bfloat16), "batch", scatter_dimension=1, tiled=True
        ).astype(jnp.float32),
    )
    return (query_grad, key_grad, value_grad)


def band_attend(queries, key_rows, value_rows, key_valid):
    return block_forward(queries, key_rows, value_rows, key_valid, BAND_LAYOUT)


def band_attend_back(queries, key_rows, value_rows, key_valid, attn_kept, out_grad):
    return block_backward(
        queries, key_rows, value_rows, key_valid, attn_kept, out_grad, BAND_LAYOUT
    )


def layer_forward(residual, params, tables, key_valid, attend):
    prenorm, project, gating, output_weight, midnorm, expand, shrink = params
    cos_table, sin_table = tables
    normed = rms_scale(residual, prenorm.astype(jnp.float32)).astype(jnp.bfloat16)
    projected = jnp.dot(normed, project, preferred_element_type=jnp.float32)
    gate_logits = jnp.dot(normed, gating, preferred_element_type=jnp.float32)
    inner_width = output_weight.shape[0]
    head_count = gating.shape[1]
    head_shape = residual.shape[:-1] + (head_count, inner_width // head_count)
    queries = rotate(projected[..., :inner_width].reshape(head_shape), cos_table, sin_table).astype(
        jnp.bfloat16
    )
    key_rows = rotate(
        projected[..., inner_width : 2 * inner_width].reshape(head_shape), cos_table, sin_table
    ).astype(jnp.bfloat16)
    value_rows = projected[..., 2 * inner_width :].reshape(head_shape).astype(jnp.bfloat16)
    attended, attn_kept = attend(queries, key_rows, value_rows, key_valid)
    gate_values = jax.nn.sigmoid(gate_logits)
    mixed_heads = (
        (attended * gate_values[..., None])
        .reshape(residual.shape[:-1] + (inner_width,))
        .astype(jnp.bfloat16)
    )
    middle = residual + jnp.dot(mixed_heads, output_weight, preferred_element_type=jnp.float32)
    normed_ffn = rms_scale(middle, midnorm.astype(jnp.float32)).astype(jnp.bfloat16)
    hidden = jnp.dot(normed_ffn, expand, preferred_element_type=jnp.float32)
    active = gelu_exact(hidden).astype(jnp.bfloat16)
    result = middle + jnp.dot(active, shrink, preferred_element_type=jnp.float32)
    kept_values = (
        residual,
        normed,
        gate_logits,
        queries,
        key_rows,
        value_rows,
        attn_kept,
        attended,
        mixed_heads,
        middle,
        normed_ffn,
        hidden,
        active,
    )
    return (result, kept_values)


def layer_backward(result_grad, params, kept_values, tables, key_valid, attend_back):
    prenorm, project, gating, output_weight, midnorm, expand, shrink = params
    (
        residual,
        normed,
        gate_logits,
        queries,
        key_rows,
        value_rows,
        attn_kept,
        attended,
        mixed_heads,
        middle,
        normed_ffn,
        hidden,
        active,
    ) = kept_values
    cos_table, sin_table = tables
    branch_grad = result_grad.astype(jnp.bfloat16)
    shrink_grad = token_sum(active, branch_grad)
    active_grad = back_dot(branch_grad, shrink)
    hidden_grad = jax.vjp(gelu_exact, hidden)[1](active_grad)[0].astype(jnp.bfloat16)
    expand_grad = token_sum(normed_ffn, hidden_grad)
    normed_ffn_grad = back_dot(hidden_grad, expand)
    middle_norm_grad, midnorm_grad = jax.vjp(rms_scale, middle, midnorm.astype(jnp.float32))[1](
        normed_ffn_grad
    )
    middle_grad = result_grad + middle_norm_grad
    attn_branch = middle_grad.astype(jnp.bfloat16)
    output_grad = token_sum(mixed_heads, attn_branch)
    mixed_grad = back_dot(attn_branch, output_weight).reshape(attended.shape)
    gate_values = jax.nn.sigmoid(gate_logits)
    attended_grad = (mixed_grad * gate_values[..., None]).astype(jnp.bfloat16)
    logit_grad = (
        jnp.sum(mixed_grad * attended, axis=-1) * gate_values * (1.0 - gate_values)
    ).astype(jnp.bfloat16)
    query_grad, key_grad, value_grad = attend_back(
        queries, key_rows, value_rows, key_valid, attn_kept, attended_grad
    )
    flat_shape = residual.shape[:-1] + (-1,)
    projected_grad = jnp.concatenate(
        [
            rotate(query_grad, cos_table, -sin_table).reshape(flat_shape),
            rotate(key_grad, cos_table, -sin_table).reshape(flat_shape),
            value_grad.reshape(flat_shape),
        ],
        axis=-1,
    ).astype(jnp.bfloat16)
    project_grad = token_sum(normed, projected_grad)
    gating_grad = token_sum(normed, logit_grad)
    normed_grad = back_dot(projected_grad, project) + back_dot(logit_grad, gating)
    residual_norm_grad, prenorm_grad = jax.vjp(rms_scale, residual, prenorm.astype(jnp.float32))[1](
        normed_grad
    )
    return (
        middle_grad + residual_norm_grad,
        (
            prenorm_grad,
            project_grad,
            gating_grad,
            output_grad,
            midnorm_grad,
            expand_grad,
            shrink_grad,
        ),
    )


def generic_shards(
    activations,
    cotangent,
    frame_counts,
    slot_bands,
    time_prenorm,
    time_project,
    time_gating,
    time_output,
    time_midnorm,
    time_expand,
    time_shrink,
    band_prenorm,
    band_project,
    band_gating,
    band_output,
    band_midnorm,
    band_expand,
    band_shrink,
):
    slot_dev, clip_count, frame_dev, model_width = activations.shape
    slot_count = slot_bands.shape[0]
    frames_all = frame_dev * lax.axis_size("batch")
    head_size = time_output.shape[0] // time_gating.shape[1]
    time_params = (
        time_prenorm,
        time_project,
        time_gating,
        time_output,
        time_midnorm,
        time_expand,
        time_shrink,
    )
    band_params = (
        band_prenorm,
        band_project,
        band_gating,
        band_output,
        band_midnorm,
        band_expand,
        band_shrink,
    )
    own_bands = lax.dynamic_slice_in_dim(slot_bands, lax.axis_index("band") * slot_dev, slot_dev)
    frame_start = lax.axis_index("batch") * frame_dev
    own_frames = frame_start + jnp.arange(frame_dev, dtype=jnp.int32)
    frame_valid = own_frames[None, :] < frame_counts[:, None]
    row_valid = (own_bands >= 0)[:, None, None] & frame_valid[None]
    full_valid = jnp.arange(frames_all, dtype=jnp.int32)[None, :] < frame_counts[:, None]
    time_valid = jnp.broadcast_to(full_valid[None], (slot_dev, clip_count, frames_all)).reshape(
        slot_dev * clip_count, frames_all
    )
    time_cos, time_sin = rotary_tables(own_frames.astype(jnp.float32), head_size)
    time_tables = (time_cos[None, :, None, :], time_sin[None, :, None, :])
    band_cos, band_sin = rotary_tables(jnp.maximum(slot_bands, 0).astype(jnp.float32), head_size)
    band_tables = (band_cos[:, None, None, :], band_sin[:, None, None, :])
    residual = activations.astype(jnp.float32).reshape(
        slot_dev * clip_count, frame_dev, model_width
    )
    time_result, time_kept = layer_forward(
        residual, time_params, time_tables, time_valid, time_attend
    )
    masked_cot = jnp.where(row_valid[..., None], cotangent, jnp.zeros((), jnp.bfloat16)).reshape(
        slot_dev, clip_count * frame_dev, model_width
    )
    frame_rows = lax.all_to_all(
        time_result.astype(jnp.bfloat16), "band", split_axis=1, concat_axis=0, tiled=True
    ).astype(time_result.dtype)
    band_valid = jnp.broadcast_to((slot_bands >= 0)[None, :], (frame_rows.shape[1], slot_count))
    band_result, band_kept = layer_forward(
        frame_rows, band_params, band_tables, band_valid, band_attend
    )
    back_rows = lax.all_to_all(
        band_result.astype(jnp.bfloat16), "band", split_axis=0, concat_axis=1, tiled=True
    ).astype(band_result.dtype)
    layer_output = jnp.where(
        row_valid[..., None], back_rows.reshape(activations.shape), 0.0
    ).astype(jnp.bfloat16)
    frame_cot = lax.all_to_all(masked_cot, "band", split_axis=1, concat_axis=0, tiled=True)
    frame_grad, band_grads = layer_backward(
        frame_cot.astype(jnp.float32),
        band_params,
        band_kept,
        band_tables,
        band_valid,
        band_attend_back,
    )
    slot_grad = lax.all_to_all(
        frame_grad.astype(jnp.bfloat16), "band", split_axis=0, concat_axis=1, tiled=True
    ).astype(frame_grad.dtype)
    input_grad, time_grads = layer_backward(
        slot_grad, time_params, time_kept, time_tables, time_valid, time_attend_back
    )
    input_grad = input_grad.reshape(activations.shape)
    all_grads = lax.psum(
        (
            time_grads[0],
            time_grads[1],
            time_grads[2],
            time_grads[3],
            time_grads[4],
            time_grads[5],
            time_grads[6],
            band_grads[0],
            band_grads[1],
            band_grads[2],
            band_grads[3],
            band_grads[4],
            band_grads[5],
            band_grads[6],
        ),
        ("band", "batch"),
    )
    return (
        layer_output,
        input_grad,
        all_grads[0],
        all_grads[1],
        all_grads[2],
        all_grads[3],
        all_grads[4],
        all_grads[5],
        all_grads[6],
        all_grads[7],
        all_grads[8],
        all_grads[9],
        all_grads[10],
        all_grads[11],
        all_grads[12],
        all_grads[13],
    )


BLOCK = 256
LOG2E = 1.4426950408889634
F32 = jnp.float32
BF16 = jnp.bfloat16
NN = (((1,), (0,)), ((), ()))
NT = (((1,), (1,)), ((), ()))
TN = (((0,), (0,)), ((), ()))
VMEM_BYTES = 60 * 2**20


def dg(left, right, dims):
    return lax.dot_general(left, right, dims, preferred_element_type=F32)


def norm_forward(rows, gain):
    scale = lax.rsqrt(jnp.mean(rows * rows, axis=0, keepdims=True) + EPSILON)
    return (rows * scale * gain).astype(BF16)


def norm_backward(rows, gain, grad):
    scale = lax.rsqrt(jnp.mean(rows * rows, axis=0, keepdims=True) + EPSILON)
    unit = rows * scale
    scaled = grad * gain
    inner = jnp.mean(scaled * unit, axis=0, keepdims=True)
    return scale * (scaled - unit * inner), grad * unit


def gelu_pair(values):
    size = jnp.abs(values)
    denominator = 1.0 + (0.3275911 * math.sqrt(0.5)) * size
    t = pl.reciprocal(denominator, approx=True)
    t = t * (2.0 - denominator * t)
    bell = jnp.exp2(values * values * (-0.5 * LOG2E))
    poly = 0.5 * 1.061405429
    for coefficient in (-1.453152027, 1.421413741, -0.284496736, 0.254829592):
        poly = poly * t + 0.5 * coefficient
    tail = poly * t * bell
    upper = jnp.where(values < 0.0, tail, 1.0 - tail)
    slope = upper + values * bell * (1.0 / math.sqrt(2.0 * math.pi))
    return values * upper, slope


def turn(vectors, cos, sin):
    half = cos.shape[0]
    split = vectors.reshape(-1, 2 * half, vectors.shape[-1])
    first = split[:, :half]
    second = split[:, half:]
    turned = jnp.concatenate([first * cos - second * sin, first * sin + second * cos], axis=1)
    return turned.reshape(vectors.shape)


def three_parts(values):
    top = values.astype(BF16).astype(F32)
    rest = values - top
    middle = rest.astype(BF16).astype(F32)
    return top, middle, rest - middle


def extra_rows(rows, width):
    tile = jnp.concatenate(rows + [jnp.zeros((8 - len(rows), width), F32)], axis=0)
    return jnp.concatenate([tile, jnp.zeros((8, width), F32)], axis=0).astype(BF16)


def project_block(normed, wpt_ref, cos, sin, inner, scale):
    queries = turn(dg(wpt_ref[0:inner, :], normed, NN), cos, sin) * scale
    keys = turn(dg(wpt_ref[inner : 2 * inner, :], normed, NN), cos, sin)
    values = dg(wpt_ref[2 * inner : 3 * inner, :], normed, NN)
    return queries.astype(BF16), keys.astype(BF16), values.astype(BF16)


def column(row_ref):
    row = row_ref[...].astype(F32)
    return jnp.broadcast_to(row, (8, row.shape[1])).T[:, :1]


def flipped(ref):
    return ref[...].astype(F32).T.astype(BF16)


def greet_all(band_count, batch_count):
    count = band_count * batch_count
    me = lax.axis_index("band") * batch_count + lax.axis_index("batch")
    barrier = pltpu.get_barrier_semaphore()

    def signal(i, carry):
        other = lax.rem(me + i, count)
        pl.semaphore_signal(
            barrier,
            inc=1,
            device_id=(other // batch_count, lax.rem(other, batch_count)),
            device_id_type=pl.DeviceIdType.MESH,
        )
        return carry

    lax.fori_loop(1, count, signal, 0)
    pl.semaphore_wait(barrier, count - 1)


def send(source, target, send_sem, recv_sem, band, batch):
    pltpu.make_async_remote_copy(
        src_ref=source,
        dst_ref=target,
        send_sem=send_sem,
        recv_sem=recv_sem,
        device_id=(band, batch),
        device_id_type=pl.DeviceIdType.MESH,
    ).start()


def await_bytes(ref, sem):
    pltpu.make_async_copy(ref, ref, sem).wait()


class Place:
    def __init__(self):
        self.band, self.batch = lax.axis_index("band"), lax.axis_index("batch")
        self.bits = {
            "core": lax.rem(self.batch, 2),
            "x": self.batch // 2,
            "y": lax.rem(self.band, 2),
        }
        self.z = self.band // 2

    def across(self, axis):
        bit = self.bits[axis]
        if axis == "core":
            return self.band, self.batch + 1 - 2 * bit
        if axis == "x":
            return self.band, self.batch + 2 - 4 * bit
        return self.band + 1 - 2 * bit, self.batch

    def along_z(self, step):
        other = lax.rem(self.z + step, Z_COUNT)
        return other, (other * 2 + self.bits["y"], self.batch)


Z_COUNT = 4


def greet(others):
    barrier = pltpu.get_barrier_semaphore()
    for other in others:
        pl.semaphore_signal(barrier, inc=1, device_id=other, device_id_type=pl.DeviceIdType.MESH)
    pl.semaphore_wait(barrier, len(others))


class Total:
    def __init__(self, place, order, sends, recvs):
        self.place = place
        self.order = order
        self.sends, self.recvs = sends, recvs
        self.core = place.bits["core"]
        self.first, self.second = (place.bits[axis] for axis in order)

    def give(self, step, source, target, other):
        send(source, target, self.sends.at[step], self.recvs.at[step], *other)

    def took(self, step, ref):
        await_bytes(ref, self.recvs.at[step])
        await_bytes(ref, self.sends.at[step])

    def add(self, ref, rows, part):
        ref[rows] = (ref[rows].astype(F32) + part.astype(F32)).astype(BF16)

    def start_core(self, source, recv):
        self.give(0, source.at[1 - self.core], recv, self.place.across("core"))

    def end_core(self, held, recv):
        self.took(0, recv)
        held[...] = (held[...].astype(F32) + recv[...].astype(F32)).astype(BF16)

    def half_rows(self, held, level):
        rows = held.shape[0] // 2
        base = 0
        if level == 2:
            base, rows = self.first * rows, rows // 2
        bit = self.first if level == 1 else self.second
        keep = pl.ds(pl.multiple_of(base + bit * rows, rows), rows)
        away = pl.ds(pl.multiple_of(base + (1 - bit) * rows, rows), rows)
        return keep, away

    def start_half(self, level, held, recv):
        away = self.half_rows(held, level)[1]
        self.give(level, held.at[away], recv, self.place.across(self.order[level - 1]))

    def end_half(self, level, held, recv):
        self.took(level, recv)
        self.add(held, self.half_rows(held, level)[0], recv[...])

    def start_z(self, piece, recv):
        width = recv.shape[2]
        for step in range(1, Z_COUNT):
            index, other = self.place.along_z(step)
            lanes = pl.ds(pl.multiple_of(index * width, 128), width)
            self.give(3, piece.at[:, lanes], recv.at[step - 1], other)

    def z_lanes(self, width):
        return pl.ds(pl.multiple_of(self.place.z * width, 128), width)

    def end_z(self, piece, recv):
        self.took(3, recv)
        lanes = self.z_lanes(recv.shape[2])
        sums = piece[:, lanes].astype(F32)
        for step in range(Z_COUNT - 1):
            sums = sums + recv[step].astype(F32)
        piece[:, lanes] = sums.astype(BF16)

    def own_copy(self, piece, target, width, sem):
        lanes = self.z_lanes(width)
        return pltpu.make_async_copy(piece.at[:, lanes], target.at[:, lanes], sem)

    def start_z_back(self, piece, target, width, sem):
        lanes = self.z_lanes(width)
        for step in range(1, Z_COUNT):
            _, other = self.place.along_z(step)
            self.give(4, piece.at[:, lanes], target.at[:, lanes], other)
        self.own_copy(piece, target, width, sem).start()

    def end_z_back(self, piece, target, width, sem):
        self.took(4, target.at[:, pl.ds(0, (Z_COUNT - 1) * width)])
        self.own_copy(piece, target, width, sem).wait()

    def back_rows(self, out, level):
        rows = out.shape[0] // 2
        base = self.core * rows
        if level >= 1:
            rows = rows // 2
            base = base + self.first * rows
        if level >= 2:
            rows = rows // 2
            base = base + self.second * rows
        return pl.ds(pl.multiple_of(base, rows), rows)

    def start_back(self, level, out, source=None):
        rows = self.back_rows(out, level)
        axis = "core" if level == 0 else self.order[level - 1]
        self.give(7 - level, out.at[rows] if source is None else source, out.at[rows], self.place.across(axis))

    def end_back(self, level, out):
        self.took(7 - level, out.at[self.back_rows(out, level)])


TOTAL_STEPS = 8


def time_forward_kernel(
    heads,
    batch_count,
    band_count,
    act_in,
    cot_in,
    bias_ref,
    cos_ref,
    sin_ref,
    g1_ref,
    g2_ref,
    wp_ref,
    wg_ref,
    wo_ref,
    w1_ref,
    w2_ref,
    band_wp_ref,
    band_wg_ref,
    band_wo_ref,
    band_w1_ref,
    band_w2_ref,
    band_rows,
    band_cot,
    rows_ref,
    n_ref,
    q_ref,
    k_ref,
    v_ref,
    p_ref,
    linv_ref,
    gate_ref,
    att_ref,
    mixed_ref,
    mid_ref,
    nf_ref,
    act_ref,
    slope_ref,
    band_wpt_ref,
    band_wgt_ref,
    band_wot_ref,
    band_w1t_ref,
    band_w2t_ref,
    xt_ref,
    x_ref,
    result_ref,
    wpt_ref,
    wgt_ref,
    wot_ref,
    w1t_ref,
    w2t_ref,
    row_send,
    row_recv,
    cot_send,
    cot_recv,
    result_send,
    result_recv,
    local_sem,
):
    slot, head = pl.program_id(0), pl.program_id(1)
    slots = pl.num_programs(0)
    slot_dev = cot_in.shape[0]
    frames, model = rows_ref.shape[1:]
    inner = q_ref.shape[1]
    size = inner // heads
    my_band, my_batch = lax.axis_index("band"), lax.axis_index("batch")
    frame_dev = frames // batch_count
    piece = frame_dev // band_count
    own_rows = pl.ds(pl.multiple_of(my_batch * frame_dev, frame_dev), frame_dev)
    held = x_ref.shape[0]

    def own_row_copy(j):
        return pltpu.make_async_copy(
            act_in.at[batch_count * j + my_batch], x_ref.at[j, own_rows], local_sem.at[j]
        )

    def own_cot_copy():
        return pltpu.make_async_copy(
            cot_in.at[:, pl.ds(pl.multiple_of(my_band * piece, piece), piece)],
            band_cot.at[pl.ds(my_band * slot_dev, slot_dev)],
            local_sem.at[held],
        )

    @pl.when((slot == 0) & (head == 0))
    def start():
        greet_all(band_count, batch_count)
        for j in range(held):
            for i in range(1, batch_count):
                other = lax.rem(my_batch + i, batch_count)
                send(
                    act_in.at[batch_count * j + other],
                    x_ref.at[j, own_rows],
                    row_send,
                    row_recv.at[j],
                    my_band,
                    other,
                )
            own_row_copy(j).start()

        def send_cot(i, carry):
            other = lax.rem(my_band + i, band_count)
            send(
                cot_in.at[:, pl.ds(pl.multiple_of(other * piece, piece), piece)],
                band_cot.at[pl.ds(my_band * slot_dev, slot_dev)],
                cot_send,
                cot_recv,
                other,
                my_batch,
            )
            return carry

        lax.fori_loop(1, band_count, send_cot, 0)
        own_cot_copy().start()
        wpt_ref[...] = flipped(wp_ref)
        wgt_ref[...] = flipped(wg_ref)
        wot_ref[...] = flipped(wo_ref)
        w1t_ref[...] = flipped(w1_ref)
        w2t_ref[...] = flipped(w2_ref)
        band_wpt_ref[...] = flipped(band_wp_ref)
        band_wgt_ref[...] = flipped(band_wg_ref)
        band_wot_ref[...] = flipped(band_wo_ref)
        band_w1t_ref[...] = flipped(band_w1_ref)
        band_w2t_ref[...] = flipped(band_w2_ref)

    @pl.when(head == 0)
    def before():
        for j in range(held):

            @pl.when(slot == j)
            def arrived():
                await_bytes(x_ref.at[j, pl.ds(0, (batch_count - 1) * frame_dev)], row_recv.at[j])
                own_row_copy(j).wait()

        gain = column(g1_ref)

        def block(i, carry):
            at = pl.ds(pl.multiple_of(i * BLOCK, BLOCK), BLOCK)
            held_rows = x_ref[slot, at, :]
            rows_ref[0, at, :] = held_rows
            rows = held_rows.astype(F32).T
            xt_ref[:, at] = rows
            normed = norm_forward(rows, gain)
            n_ref[0, :, at] = normed
            queries, keys, values = project_block(
                normed, wpt_ref, cos_ref[:, at], sin_ref[:, at], inner, LOG2E * size**-0.5
            )
            q_ref[0, :, at] = queries
            k_ref[0, :, at] = keys
            v_ref[0, :, at] = values
            gate_ref[0, :, at] = dg(wgt_ref[...], normed, NN)
            return carry

        lax.fori_loop(0, frames // BLOCK, block, 0)

    at_head = pl.ds(pl.multiple_of(head * size, size), size)
    ones = jnp.ones((1, frames), F32)
    queries = jnp.concatenate([q_ref[0, at_head, :], extra_rows([ones], frames)], axis=0)
    keys = jnp.concatenate([k_ref[0, at_head, :], extra_rows([bias_ref[...]], frames)], axis=0)
    values = jnp.concatenate([v_ref[0, at_head, :], extra_rows([ones], frames)], axis=0)
    scores = dg(keys, queries, TN)
    weights = jnp.exp2(scores - jnp.max(scores, axis=0, keepdims=True)).astype(BF16)
    p_ref[0, 0] = weights
    sums = dg(values, weights, NN)
    inverse = 1.0 / sums[size : size + 1]
    attended = sums[:size] * inverse
    linv_ref[0, pl.ds(head, 1), :] = inverse
    att_ref[0, at_head, :] = attended
    gate = jax.nn.sigmoid(gate_ref[0, pl.ds(head, 1), :])
    mixed_ref[0, at_head, :] = (attended * gate).astype(BF16)

    @pl.when(head == heads - 1)
    def after():
        gain = column(g2_ref)
        to_slot = my_band * slot_dev + batch_count * slot + my_batch

        def block(i, carry):
            at = pl.ds(pl.multiple_of(i * BLOCK, BLOCK), BLOCK)
            middle = xt_ref[:, at] + dg(wot_ref[...], mixed_ref[0, :, at], NN)
            mid_ref[0, :, at] = middle
            normed = norm_forward(middle, gain)
            nf_ref[0, :, at] = normed
            active, slope = gelu_pair(dg(w1t_ref[...], normed, NN))
            active = active.astype(BF16)
            act_ref[0, :, at] = active
            slope_ref[0, :, at] = slope.astype(BF16)
            result = middle + dg(w2t_ref[...], active, NN)
            result_ref[slot, at, :] = result.T.astype(BF16)

            def send_result(j, carry):
                other = lax.rem(my_band + j, band_count)
                source = result_ref.at[slot, pl.ds(pl.multiple_of(i * frame_dev + other * piece, piece), piece)]
                mine = (other == my_band) & (i == my_batch)

                @pl.when(mine)
                def keep():
                    pltpu.make_async_copy(source, band_rows.at[to_slot], local_sem.at[held + 1]).start()

                @pl.when(jnp.logical_not(mine))
                def give():
                    send(source, band_rows.at[to_slot], result_send, result_recv, other, i)

                return carry

            lax.fori_loop(1, band_count + 1, send_result, 0)
            return carry

        lax.fori_loop(0, frames // BLOCK, block, 0)

    @pl.when((slot == slots - 1) & (head == heads - 1))
    def finish():
        others = held * (band_count * batch_count - 1)
        others_cot = (band_count - 1) * slot_dev
        others_rows = (batch_count - 1) * frame_dev
        await_bytes(band_cot.at[pl.ds(0, others_cot)], cot_recv)
        await_bytes(band_cot.at[pl.ds(0, others_cot)], cot_send)
        own_cot_copy().wait()
        await_bytes(x_ref.at[:, pl.ds(0, others_rows)], row_send)
        await_bytes(band_rows.at[pl.ds(0, others)], result_send)
        await_bytes(band_rows.at[pl.ds(0, held)], local_sem.at[held + 1])
        await_bytes(band_rows.at[pl.ds(0, others)], result_recv)


def cost(flops, exps=0, moved=0):
    return pl.CostEstimate(flops=int(flops), bytes_accessed=int(moved), transcendentals=int(exps))


def whole_spec(array):
    nd = array.ndim
    return pl.BlockSpec(array.shape, lambda *ids: (0,) * nd, pipeline_mode=pl.Buffered(1))


def time_forward(activations, cotangent, bias, cos, sin, params, band_params, band_count, batch_count):
    g1, wp, wg, wo, g2, w1, w2 = params
    _, bwp, bwg, bwo, _, bw1, bw2 = band_params
    slot_dev, frame_dev, model = activations.shape
    slots, frames = slot_dev // batch_count, frame_dev * batch_count
    heads, inner, hidden = wg.shape[1], wo.shape[0], w1.shape[1]
    piece = frame_dev // band_count

    def per_slot(*shape):
        return pl.BlockSpec((1,) + shape, lambda s, h: (s,) + (0,) * len(shape))

    outs = [
        ((frames, model), BF16),
        ((model, frames), BF16),
        ((inner, frames), BF16),
        ((inner, frames), BF16),
        ((inner, frames), BF16),
        None,
        ((heads, frames), F32),
        ((heads, frames), F32),
        ((inner, frames), F32),
        ((inner, frames), BF16),
        ((model, frames), F32),
        ((model, frames), BF16),
        ((hidden, frames), BF16),
        ((hidden, frames), BF16),
    ]
    flips = [(w.shape[1], w.shape[0]) for w in (bwp, bwg, bwo, bw1, bw2)]
    own_flips = [(w.shape[1], w.shape[0]) for w in (wp, wg, wo, w1, w2)]
    exchanged = jax.ShapeDtypeStruct((slot_dev * band_count, piece, model), BF16)
    anywhere = pl.BlockSpec(memory_space=pl.ANY)
    shapes, specs = [exchanged, exchanged], [anywhere, anywhere]
    for entry in outs:
        if entry is None:
            shapes.append(jax.ShapeDtypeStruct((slots, heads, frames, frames), BF16))
            specs.append(pl.BlockSpec((1, 1, frames, frames), lambda s, h: (s, h, 0, 0)))
        else:
            shapes.append(jax.ShapeDtypeStruct((slots,) + entry[0], entry[1]))
            specs.append(per_slot(*entry[0]))
    for shape in flips:
        shapes.append(jax.ShapeDtypeStruct(shape, BF16))
        specs.append(pl.BlockSpec(shape, lambda s, h: (0, 0), pipeline_mode=pl.Buffered(1)))
    consts = (bias, cos, sin, g1, g2, wp, wg, wo, w1, w2, bwp, bwg, bwo, bw1, bw2)
    dma = pltpu.SemaphoreType.DMA
    return pl.pallas_call(
        lambda *refs: time_forward_kernel(heads, batch_count, band_count, *refs),
        grid=(slots, heads),
        out_shape=shapes,
        in_specs=[anywhere, anywhere] + [whole_spec(c) for c in consts],
        out_specs=specs,
        scratch_shapes=[
            pltpu.VMEM((model, frames), F32),
            pltpu.VMEM((slots, frames, model), BF16),
            pltpu.VMEM((slots, frames, model), BF16),
        ]
        + [pltpu.VMEM(shape, BF16) for shape in own_flips]
        + [dma, dma((slots,)), dma, dma, dma, dma, dma((slots + 2,))],
        compiler_params=pltpu.CompilerParams(
            vmem_limit_bytes=VMEM_BYTES, collective_id=0, has_side_effects=True
        ),
        cost_estimate=cost(2.0e6 * 4 * slots * frames, 2 * slots * heads * frames * frames, 60e6),
        name="time_forward",
    )(activations, cotangent, *consts)


def ffn_backward(grad, act, slope, normed, middle, gain, w1_ref, w2_ref, dw1_ref, dw2t_ref, dg2_ref):
    branch = grad.astype(BF16)
    d_hidden = (dg(w2_ref[...], branch, NN) * slope.astype(F32)).astype(BF16)
    dw2t_ref[...] += dg(branch, act, NT)
    dw1_ref[...] += dg(normed, d_hidden, NT)
    d_normed = dg(w1_ref[...], d_hidden, NN)
    d_rows, terms = norm_backward(middle, gain, d_normed)
    dg2_ref[...] += jnp.sum(terms, axis=1, keepdims=True)
    return grad + d_rows


def head_backward(d_mixed, attended, gate_logit, inverse):
    gate = jax.nn.sigmoid(gate_logit)
    d_logit = jnp.sum(d_mixed * attended, axis=0, keepdims=True) * gate * (1.0 - gate)
    d_att = (d_mixed * (gate * inverse)).astype(BF16)
    minus = -jnp.sum(d_att.astype(F32) * attended, axis=0, keepdims=True)
    return d_att, minus, d_logit


def scores_backward(queries, keys, values, weights, d_att, minus, cos, sin, scale):
    width = queries.shape[1]
    ones = jnp.ones((1, width), F32)
    d_weights = dg(
        jnp.concatenate([values, extra_rows([ones, ones, ones], width)], axis=0),
        jnp.concatenate([d_att, extra_rows(list(three_parts(minus)), width)], axis=0),
        TN,
    )
    d_scores = (weights.astype(F32) * d_weights).astype(BF16)
    d_values = dg(d_att, weights, NT)
    d_queries = dg(keys, d_scores, NN) * scale
    d_keys = dg(queries, d_scores, NT) * (1.0 / LOG2E)
    return turn(d_queries, cos, -sin), turn(d_keys, cos, -sin), d_values


def time_ffn_backward_kernel(
    heads,
    orders,
    grad_ref,
    act_ref,
    slope_ref,
    nf_ref,
    mid_ref,
    mixed_ref,
    att_ref,
    gate_ref,
    linv_ref,
    g2_ref,
    w1_ref,
    w2_ref,
    wo_ref,
    part_refs,
    dmid_ref,
    datt_ref,
    minus_ref,
    dlogit_ref,
    sums_refs,
    dg2_out,
    region_refs,
    dw1_ref,
    dw2t_ref,
    dwot_ref,
    dg2_ref,
    piece_refs,
    z_recvs,
    sends,
    recvs,
    local_sem,
):
    place = Place()
    totals = [Total(place, order, sends.at[i], recvs.at[i]) for i, order in enumerate(orders)]
    step = pl.program_id(0) * pl.num_programs(1) + pl.program_id(1)
    last = pl.num_programs(0) * pl.num_programs(1) - 1
    size = wo_ref.shape[0] // heads

    @pl.when(step == 0)
    def clear():
        for ref in (dw1_ref, dw2t_ref, dwot_ref, dg2_ref):
            ref[...] = jnp.zeros_like(ref)
        greet([place.along_z(i)[1] for i in range(1, Z_COUNT)])
        for total, part, piece, recv in zip(totals, part_refs, piece_refs, z_recvs):
            piece[...] = part[...]
            total.start_z(piece, recv)

    @pl.when(step == last // 2 + 1)
    def gather():
        for i, (total, piece, recv, region) in enumerate(zip(totals, piece_refs, z_recvs, region_refs)):
            total.end_z(piece, recv)
            total.start_z_back(piece, region, recv.shape[2], local_sem.at[i])

    grad = grad_ref[0].astype(F32).T
    d_middle = ffn_backward(
        grad, act_ref[0], slope_ref[0], nf_ref[0], mid_ref[0], column(g2_ref), w1_ref, w2_ref, dw1_ref, dw2t_ref, dg2_ref
    )
    dmid_ref[0] = d_middle
    branch = d_middle.astype(BF16)
    dwot_ref[...] += dg(branch, mixed_ref[0], NT)
    d_mixed = dg(wo_ref[...], branch, NN)
    logits, minuses = [], []
    for head in range(heads):
        at = slice(head * size, (head + 1) * size)
        d_att, minus, d_logit = head_backward(
            d_mixed[at], att_ref[0, at], gate_ref[0, head : head + 1], linv_ref[0, head : head + 1]
        )
        datt_ref[0, at] = d_att
        minuses.append(minus)
        logits.append(d_logit)
    minus_ref[0] = jnp.concatenate(minuses, axis=0)
    dlogit_ref[0] = jnp.concatenate(logits, axis=0)

    @pl.when(step == last)
    def finish():
        first, second = sums_refs
        lay_halves(first, 0, dw1_ref)
        lay_halves(first, dw1_ref.shape[1], dwot_ref)
        lay_halves(second, 0, dw2t_ref)
        dg2_out[...] = dg2_ref[...]
        for i, (total, piece, recv, region) in enumerate(zip(totals, piece_refs, z_recvs, region_refs)):
            total.end_z_back(piece, region, recv.shape[2], local_sem.at[i])


def narrow_tile(parts, rows):
    used = sum(part.shape[1] for part in parts)
    return jnp.concatenate(list(parts) + [jnp.zeros((rows, 128 - used), F32)], axis=1)


def lay_halves(target, at, ref):
    rows, width = ref.shape
    for half in range(2):
        target[half, :, at : at + width] = ref[half * rows // 2 : (half + 1) * rows // 2].astype(BF16)


ORDERS = (("x", "y"), ("y", "x"))


def time_ffn_backward(grad, act, slope, nf, mid, mixed, att, gate, linv, g2, w1, w2, wo, parts):
    slots, frames, model = grad.shape
    heads = gate.shape[1]
    inner, hidden = wo.shape[0], w1.shape[1]
    tokens = min(frames, 512)

    def cut(rows):
        return pl.BlockSpec((1, rows, tokens), lambda s, c: (s, 0, c))

    def whole(*shape):
        return pl.BlockSpec(shape, lambda s, c: (0,) * len(shape))

    consts = (g2, w1, w2, wo)
    anywhere = pl.BlockSpec(memory_space=pl.ANY)
    halves = [(2, model // 2, hidden + inner), (2, model // 2, hidden)]
    eighth = parts[0].shape[0]
    widths = [part.shape[1] for part in parts]
    dma = pltpu.SemaphoreType.DMA
    return pl.pallas_call(
        lambda *refs: time_ffn_backward_kernel(heads, ORDERS, *refs),
        grid=(slots, frames // tokens),
        out_shape=(
            jax.ShapeDtypeStruct((slots, model, frames), F32),
            jax.ShapeDtypeStruct((slots, inner, frames), BF16),
            jax.ShapeDtypeStruct((slots, heads, frames), F32),
            jax.ShapeDtypeStruct((slots, heads, frames), F32),
            [jax.ShapeDtypeStruct(shape, BF16) for shape in halves],
            jax.ShapeDtypeStruct((model, 1), F32),
            [jax.ShapeDtypeStruct(part.shape, BF16) for part in parts],
        ),
        in_specs=[pl.BlockSpec((1, tokens, model), lambda s, c: (s, c, 0))]
        + [cut(a.shape[1]) for a in (act, slope, nf, mid, mixed, att, gate, linv)]
        + [whole_spec(c) for c in consts]
        + [[whole_spec(part) for part in parts]],
        out_specs=(
            cut(model),
            cut(inner),
            cut(heads),
            cut(heads),
            [whole(*shape) for shape in halves],
            whole(model, 1),
            [anywhere for _ in parts],
        ),
        scratch_shapes=[
            pltpu.VMEM((model, hidden), F32),
            pltpu.VMEM((model, hidden), F32),
            pltpu.VMEM((model, inner), F32),
            pltpu.VMEM((model, 1), F32),
            [pltpu.VMEM((eighth, width), BF16) for width in widths],
            [pltpu.VMEM((Z_COUNT - 1, eighth, width // Z_COUNT), BF16) for width in widths],
            dma((len(parts), TOTAL_STEPS)),
            dma((len(parts), TOTAL_STEPS)),
            dma((len(parts),)),
        ],
        compiler_params=pltpu.CompilerParams(
            vmem_limit_bytes=VMEM_BYTES, collective_id=2, has_side_effects=True
        ),
        cost_estimate=cost(8.0e6 * slots * frames, 0, 30e6),
        name="time_ffn_backward",
    )(grad, act, slope, nf, mid, mixed, att, gate, linv, *consts, list(parts))


def time_attention_backward_kernel(
    heads,
    slots,
    batch_count,
    p_ref,
    q_ref,
    k_ref,
    v_ref,
    datt_ref,
    minus_ref,
    x_ref,
    dmid_ref,
    logit_block_ref,
    n_ref,
    dlogit_ref,
    cos_ref,
    sin_ref,
    g1_ref,
    wp_ref,
    wg_ref,
    narrow_ref,
    dg2_ref,
    region_refs,
    ffn_refs,
    grad_out,
    band_outs,
    ffn_outs,
    pair_outs,
    dproj_ref,
    wp_turned_ref,
    grad_buf,
    held_refs,
    ffn_recvs,
    pair_refs,
    pair_recvs,
    band_sems,
    ffn_sems,
    pair_sems,
    grad_sems,
    local_sem,
):
    place = Place()
    step = pl.program_id(0)
    steps = heads * slots
    head, slot = step // slots, lax.rem(step, slots)
    size, frames = q_ref.shape[1:]
    model = n_ref.shape[1]
    inner = heads * size
    pairs = heads // 2
    pair_rows = 6 * size
    blocks = frames // BLOCK
    last = pl.num_programs(0) - 1
    my_band, my_batch = place.band, place.batch

    bands = [Total(place, order, band_sems[0].at[i], band_sems[1].at[i]) for i, order in enumerate(ORDERS)]
    ffns = [Total(place, order, ffn_sems[0].at[i], ffn_sems[1].at[i]) for i, order in enumerate(ORDERS)]
    own = [
        Total(place, ORDERS[i % 2], pair_sems[0].at[i], pair_sems[1].at[i]) for i in range(pairs)
    ]

    def region_copy(i):
        rows = bands[i].back_rows(band_outs[i], 2)
        return pltpu.make_async_copy(region_refs[i], band_outs[i].at[rows], local_sem.at[i])

    def half_copy(i):
        return pltpu.make_async_copy(ffn_refs[i].at[place.bits["core"]], held_refs[i], local_sem.at[2 + i])

    def eighth(total, held):
        return held.at[total.half_rows(held, 2)[0]]

    def all_steps(total, source, held, recvs, out, sem):
        width = recvs[3].shape[2]

        def back_region():
            return out.at[total.back_rows(out, 2)]

        def s0():
            total.start_core(source, recvs[0])

        def s1():
            total.end_core(held, recvs[0])
            total.start_half(1, held, recvs[1])

        def s2():
            total.end_half(1, held, recvs[1])
            total.start_half(2, held, recvs[2])

        def s3():
            total.end_half(2, held, recvs[2])
            total.start_z(eighth(total, held), recvs[3])

        def s4():
            total.end_z(eighth(total, held), recvs[3])
            total.start_z_back(eighth(total, held), back_region(), width, sem)

        def s5():
            total.end_z_back(eighth(total, held), back_region(), width, sem)
            total.start_back(2, out)

        def s6():
            total.end_back(2, out)
            total.start_back(1, out)

        def s7():
            total.end_back(1, out)
            total.start_back(0, out)

        def s8():
            total.end_back(0, out)

        return [s0, s1, s2, s3, s4, s5, s6, s7, s8]

    plan = {}

    def at_step(index, action):
        plan.setdefault(index, []).append(action)

    def enter():
        others = [(my_band, lax.rem(my_batch + i, batch_count)) for i in range(1, batch_count)]
        others += [place.across("y")] + [place.along_z(i)[1] for i in range(1, Z_COUNT)]
        greet(others)
        for i in range(2):
            region_copy(i).start()
            bands[i].start_back(2, band_outs[i], region_refs[i])
            half_copy(i).start()

    at_step(0, enter)
    for i in range(2):
        for at, action in zip(
            (2, 4, 6),
            (
                lambda i=i: (
                    region_copy(i).wait(),
                    bands[i].end_back(2, band_outs[i]),
                    bands[i].start_back(1, band_outs[i]),
                ),
                lambda i=i: (bands[i].end_back(1, band_outs[i]), bands[i].start_back(0, band_outs[i])),
                lambda i=i: bands[i].end_back(0, band_outs[i]),
            ),
        ):
            at_step(at, action)
        actions = all_steps(ffns[i], ffn_refs[i], held_refs[i], ffn_recvs[i], ffn_outs[i], local_sem.at[4 + i])
        at_step(0, actions[0])
        at_step(2, lambda i=i: half_copy(i).wait())
        for at, action in zip((2, 4, 6, 8, 10, 12, 14, 16), actions[1:]):
            at_step(at, action)
    for i in range(pairs):
        actions = all_steps(
            own[i],
            pair_refs.at[i],
            pair_refs.at[i, place.bits["core"]],
            [ref.at[i] for ref in pair_recvs],
            pair_outs.at[i],
            local_sem.at[6 + i],
        )
        begin = (i + 1) * 2 * slots
        stride = 2 if i + 1 < pairs else 1
        for n, action in enumerate(actions):
            at_step(min(begin + n * stride, steps + slots * blocks - 1 + (n == len(actions) - 1)), action)

    for index in sorted(plan):
        if index <= steps + slots * blocks - 1:

            @pl.when(step == index)
            def work(index=index):
                for action in plan[index]:
                    action()

    @pl.when(step < steps)
    def attention():
        d_queries, d_keys, d_values = scores_backward(
            q_ref[0],
            k_ref[0],
            v_ref[0],
            p_ref[0, 0],
            datt_ref[0],
            minus_ref[0, pl.ds(head, 1), :],
            cos_ref[...],
            sin_ref[...],
            size**-0.5,
        )
        start = pl.multiple_of((head // 2) * pair_rows + lax.rem(head, 2) * size, size)
        dproj_ref[slot, pl.ds(start, size), :] = d_queries.astype(BF16)
        dproj_ref[slot, pl.ds(start + 2 * size, size), :] = d_keys.astype(BF16)
        dproj_ref[slot, pl.ds(start + 4 * size, size), :] = d_values.astype(BF16)

    @pl.when((step < steps) & (lax.rem(step, 2 * slots) == 2 * slots - 1))
    def pair_done():
        pair = head // 2
        rows = pl.ds(pl.multiple_of(pair * pair_rows, pair_rows), pair_rows)
        sums = dg(n_ref[0], dproj_ref[0, rows, :], NT)
        for j in range(1, slots):
            sums = sums + dg(n_ref[j], dproj_ref[j, rows, :], NT)
        for half in range(2):
            at = slice(half * model // 2, (half + 1) * model // 2)
            pair_refs[pair, half, :, 0:pair_rows] = sums[at].astype(BF16)

    @pl.when(step == 2 * slots - 1)
    def narrow_done():
        gates = 0.0
        for j in range(slots):
            logit = jnp.concatenate([dlogit_ref[j], jnp.zeros_like(dlogit_ref[j])], axis=0).astype(BF16)
            gates = gates + dg(n_ref[j], logit, NT)[:, :heads]
        tile = narrow_tile([narrow_ref[:, : heads + 2], gates, dg2_ref[...]], model)
        for half in range(2):
            at = slice(half * model // 2, (half + 1) * model // 2)
            pair_refs[0, half, :, pair_rows:] = tile[at].astype(BF16)
            for i in range(1, pairs):
                pair_refs[i, half, :, pair_rows:] = jnp.zeros_like(tile[at]).astype(BF16)
        for pair in range(pairs):
            for part in range(3):
                to = pair * pair_rows + part * 2 * size
                source = part * inner + pair * 2 * size
                wp_turned_ref[:, to : to + 2 * size] = wp_ref[:, source : source + 2 * size]

    def message(index):
        j, i = index // blocks, lax.rem(index, blocks)
        source = grad_buf.at[index]
        target = grad_out.at[batch_count * j + my_batch]
        return i, source, target

    @pl.when(step >= steps)
    def rows_done():
        index = step - steps
        j, i = index // blocks, lax.rem(index, blocks)
        at = pl.ds(pl.multiple_of(i * BLOCK, BLOCK), BLOCK)
        logit = logit_block_ref[0].astype(BF16)
        d_normed = dg(wp_turned_ref[...], dproj_ref[j, :, at], NN) + dg(wg_ref[...], logit, NN)
        d_rows, _ = norm_backward(x_ref[0].astype(F32).T, column(g1_ref), d_normed)
        grad_buf[index] = (dmid_ref[0] + d_rows).T.astype(BF16)
        i, source, target = message(index)

        @pl.when(i == my_batch)
        def keep():
            pltpu.make_async_copy(source, target, local_sem.at[6 + pairs]).start()

        @pl.when(i != my_batch)
        def give():
            send(source, target, grad_sems.at[0], grad_sems.at[1], my_band, i)

    @pl.when(step == last)
    def finish():
        for action in plan.get(steps + slots * blocks, []):
            action()
        await_bytes(grad_buf.at[pl.ds(0, slots)], local_sem.at[6 + pairs])
        others = grad_buf.at[pl.ds(0, slots * (batch_count - 1))]
        await_bytes(others, grad_sems.at[0])
        await_bytes(others, grad_sems.at[1])


def time_attention_backward(
    p, q, k, v, datt, minus, dlogit, n, x, dmid, cos, sin, g1, wp, wg, narrow, dg2, regions, ffn_sums, batch_count
):
    slots, inner, frames = q.shape
    heads = minus.shape[1]
    size = inner // heads
    model = n.shape[1]
    pairs = heads // 2
    steps = heads * slots
    blocks = frames // BLOCK

    def clamp(t):
        return jnp.minimum(t, steps - 1)

    def tail(t):
        return jnp.maximum(t - steps, 0)

    def per_head(rows, columns):
        return pl.BlockSpec((1, rows, columns), lambda t: (lax.rem(clamp(t), slots), clamp(t) // slots, 0))

    consts = (n, dlogit, cos, sin, g1, wp, wg, narrow, dg2)
    anywhere = pl.BlockSpec(memory_space=pl.ANY)
    dma = pltpu.SemaphoreType.DMA
    widths = [a.shape[2] for a in ffn_sums]
    pair_width = 8 * size

    def recv_buffers(width, *lead):
        rows = model // 2
        shapes = [(rows, width), (rows // 2, width), (rows // 4, width), (Z_COUNT - 1, rows // 4, width // Z_COUNT)]
        return [pltpu.VMEM(lead + shape, BF16) for shape in shapes]

    return pl.pallas_call(
        lambda *refs: time_attention_backward_kernel(heads, slots, batch_count, *refs),
        grid=(steps + slots * blocks,),
        out_shape=(
            jax.ShapeDtypeStruct((batch_count * slots, BLOCK, model), BF16),
            [jax.ShapeDtypeStruct((model, a.shape[1]), BF16) for a in regions],
            [jax.ShapeDtypeStruct((model, width), BF16) for width in widths],
            jax.ShapeDtypeStruct((pairs, model, pair_width), BF16),
        ),
        in_specs=[
            pl.BlockSpec((1, 1, frames, frames), lambda t: (lax.rem(clamp(t), slots), clamp(t) // slots, 0, 0)),
            per_head(size, frames),
            per_head(size, frames),
            per_head(size, frames),
            per_head(size, frames),
            pl.BlockSpec((1, heads, frames), lambda t: (lax.rem(clamp(t), slots), 0, 0)),
            pl.BlockSpec((1, BLOCK, model), lambda t: (tail(t) // blocks, lax.rem(tail(t), blocks), 0)),
            pl.BlockSpec((1, model, BLOCK), lambda t: (tail(t) // blocks, 0, lax.rem(tail(t), blocks))),
            pl.BlockSpec((1, heads, BLOCK), lambda t: (tail(t) // blocks, 0, lax.rem(tail(t), blocks))),
        ]
        + [whole_spec(c) for c in consts]
        + [[anywhere] * len(regions), [anywhere] * len(ffn_sums)],
        out_specs=(anywhere, [anywhere] * len(regions), [anywhere] * len(ffn_sums), anywhere),
        scratch_shapes=[
            pltpu.VMEM((slots, 3 * inner, frames), BF16),
            pltpu.VMEM((model, 3 * inner), BF16),
            pltpu.VMEM((slots * blocks, BLOCK, model), BF16),
            [pltpu.VMEM((model // 2, width), BF16) for width in widths],
            [recv_buffers(width) for width in widths],
            pltpu.VMEM((pairs, 2, model // 2, pair_width), BF16),
            recv_buffers(pair_width, pairs),
            [dma((2, TOTAL_STEPS)), dma((2, TOTAL_STEPS))],
            [dma((2, TOTAL_STEPS)), dma((2, TOTAL_STEPS))],
            [dma((pairs, TOTAL_STEPS)), dma((pairs, TOTAL_STEPS))],
            dma((2,)),
            dma((7 + pairs,)),
        ],
        compiler_params=pltpu.CompilerParams(
            vmem_limit_bytes=VMEM_BYTES, collective_id=3, has_side_effects=True
        ),
        cost_estimate=cost(20.0e6 * slots * frames, 0, 60e6),
        name="time_attention_backward",
    )(p, q, k, v, datt, minus, x, dmid, dlogit, *consts, list(regions), list(ffn_sums))


def finish_kernel(
    heads,
    grad_ref,
    bwp_ref,
    bw1_ref,
    bw2t_ref,
    bwot_ref,
    w1_ref,
    wot_ref,
    w2t_ref,
    pair_ref,
    first_pair_ref,
    wp_ref,
    wg_ref,
    g1_ref,
    grad_out,
    dg1_out,
    dwp_out,
    dwg_out,
    dwo_out,
    dg2_out,
    dw1_out,
    dw2_out,
    bg1_out,
    bwp_out,
    bwg_out,
    bwo_out,
    bg2_out,
    bw1_out,
    bw2_out,
    scaled_ref,
):
    pair = pl.program_id(0)
    inner = wp_ref.shape[1] // 3
    width = inner // pl.num_programs(0)
    grad_out[...] = grad_ref[...].astype(F32)
    bwp_out[...] = bwp_ref[...].astype(F32)
    bw1_out[...] = bw1_ref[...].astype(F32)
    bw2_out[...] = bw2t_ref[...].astype(F32).T
    bwo_out[...] = bwot_ref[...].astype(F32).T
    dw1_out[...] = w1_ref[...].astype(F32)
    dw2_out[...] = w2t_ref[...].astype(F32).T
    dwo_out[...] = wot_ref[...].astype(F32).T

    @pl.when(pair == 0)
    def clear():
        scaled_ref[...] = jnp.zeros_like(scaled_ref)

    for part in range(3):
        at = pl.ds(pl.multiple_of(part * inner + pair * width, 128), width)
        values = pair_ref[0, :, part * width : (part + 1) * width].astype(F32)
        dwp_out[:, at] = values
        scaled_ref[...] += values * wp_ref[:, at].astype(F32)

    @pl.when(pair == pl.num_programs(0) - 1)
    def narrow():
        tile = first_pair_ref[0, :, 3 * width :].astype(F32)
        rows = tile.T
        bwg_out[...] = tile[:, :heads]
        bg1_out[...] = rows[heads : heads + 1]
        bg2_out[...] = rows[heads + 1 : heads + 2]
        gates = tile[:, heads + 2 : 2 * heads + 2]
        dwg_out[...] = gates
        dg2_out[...] = rows[2 * heads + 2 : 2 * heads + 3]
        sums = jnp.sum(scaled_ref[...], axis=1, keepdims=True)
        sums = sums + jnp.sum(gates * wg_ref[...].astype(F32), axis=1, keepdims=True)
        dg1_out[...] = jnp.broadcast_to(sums, (sums.shape[0], 128)).T[:1] / g1_ref[...].astype(F32)


def finish_sums(grads, band_sums, ffn_sums, pair_sums, params, band_params):
    g1, wp, wg, wo, g2, w1, w2 = params
    model, hidden = w1.shape
    inner, heads = wo.shape[0], wg.shape[1]
    pairs = pair_sums.shape[0]
    split = hidden // pairs
    out_split = inner // pairs
    slot_dev, frame_dev, _ = grads.shape

    def lanes(array, start, width):
        first = start // width
        return pl.BlockSpec((model, width), lambda i: (0, first + i))

    def whole(*shape):
        return pl.BlockSpec(shape, lambda i: (0,) * len(shape))

    def cut_rows(rows):
        return pl.BlockSpec((rows, model), lambda i: (i, 0))

    band_first, band_second = band_sums
    ffn_first, ffn_second = ffn_sums
    grad_block = pl.BlockSpec((slot_dev // pairs, frame_dev, model), lambda i: (i, 0, 0))
    narrow = [((1, model), whole(1, model)), ((model, heads), whole(model, heads))]
    per_layer = [
        narrow[0],
        ((model, 3 * inner), None),
        narrow[1],
        ((inner, model), cut_rows(out_split)),
        narrow[0],
        ((model, hidden), lanes(None, 0, split)),
        ((hidden, model), cut_rows(split)),
    ]
    shapes, specs = [jax.ShapeDtypeStruct(grads.shape, F32)], [grad_block]
    for layer in range(2):
        for shape, spec in per_layer:
            shapes.append(jax.ShapeDtypeStruct(shape, F32))
            if spec is None:
                spec = whole(*shape) if layer == 0 else lanes(None, 0, 3 * inner // pairs)
            specs.append(spec)
    return pl.pallas_call(
        lambda *refs: finish_kernel(heads, *refs),
        grid=(pairs,),
        out_shape=shapes,
        in_specs=[
            grad_block,
            lanes(band_first, 0, 3 * inner // pairs),
            lanes(band_second, 0, split),
            lanes(band_second, hidden, split),
            lanes(band_first, 3 * inner, out_split),
            lanes(ffn_first, 0, split),
            lanes(ffn_first, hidden, out_split),
            lanes(ffn_second, 0, split),
            pl.BlockSpec((1, model, pair_sums.shape[2]), lambda i: (i, 0, 0)),
            pl.BlockSpec((1, model, pair_sums.shape[2]), lambda i: (0, 0, 0)),
            whole_spec(wp),
            whole_spec(wg),
            whole_spec(g1),
        ],
        out_specs=specs,
        scratch_shapes=[pltpu.VMEM((model, inner // pairs), F32)],
        compiler_params=pltpu.CompilerParams(vmem_limit_bytes=VMEM_BYTES),
        name="finish_sums",
    )(
        grads,
        band_first,
        band_second,
        band_second,
        band_first,
        ffn_first,
        ffn_first,
        ffn_second,
        pair_sums,
        pair_sums,
        wp,
        wg,
        g1,
    )


def band_kernel(
    heads,
    batch_count,
    band_count,
    x_ref,
    cot_ref,
    mask_ref,
    bias_ref,
    cos_ref,
    sin_ref,
    g1_ref,
    g2_ref,
    wpt_ref,
    wgt_ref,
    wot_ref,
    w1t_ref,
    w2t_ref,
    wp_ref,
    wg_ref,
    wo_ref,
    w1_ref,
    w2_ref,
    y_out,
    dx_out,
    part_outs,
    narrow_out,
    q_ref,
    k_ref,
    v_ref,
    p_ref,
    gate_ref,
    linv_ref,
    att_ref,
    mixed_ref,
    act_ref,
    slope_ref,
    datt_ref,
    dmixed_ref,
    dlogit_ref,
    dproj_ref,
    dwp_ref,
    dw1_ref,
    dw2t_ref,
    dwot_ref,
    dwg_ref,
    dg1_ref,
    dg2_ref,
    xs_ref,
    cots_ref,
    ys_ref,
    dxs_ref,
    y_buf,
    dx_buf,
    y_send,
    y_recv,
    dx_send,
    dx_recv,
    local_sem,
    halves,
    half_recvs,
    sum_sends,
    sum_recvs,
    part_sem,
):
    step = pl.program_id(0)
    slot_count, part_frames, model = x_ref.shape
    inner, tokens = q_ref.shape
    size = inner // heads
    groups = tokens // BLOCK
    taken = tokens // slot_count
    per_part = part_frames // taken
    part = step // per_part
    first = lax.rem(step, per_part) * taken
    my_band, my_batch = lax.axis_index("band"), lax.axis_index("batch")
    slot_dev = slot_count // band_count
    slots = slot_dev // batch_count
    part_at = pl.multiple_of(part * part_frames, part_frames)
    own_at = pl.multiple_of(my_band * (y_out.shape[1] // band_count) + part * part_frames, part_frames)
    own_chunk = my_batch * band_count + my_band
    chunks = band_count * batch_count

    columns = [slice(at, at + 128) for at in range(0, model, 128)]

    def tokens_of(ref):
        return jnp.concatenate(
            [
                jnp.concatenate(
                    [ref[c, pl.ds(first + i, slot_count, stride=part_frames), :] for i in range(taken)], axis=0
                ).T
                for c in range(len(columns))
            ],
            axis=0,
        )

    def put_tokens(ref, values):
        for c, at in enumerate(columns):
            turned = values[at].T
            for i in range(taken):
                ref[c, pl.ds(first + i, slot_count, stride=part_frames), :] = turned[
                    i * slot_count : (i + 1) * slot_count
                ]

    @pl.when(step == 0)
    def enter():
        greet_all(band_count, batch_count)

    @pl.when(lax.rem(step, per_part) == 0)
    def unpack():
        for c, at in enumerate(columns):
            xs_ref[c] = x_ref[:, :, at].astype(F32).reshape(xs_ref.shape[1:])
            cots_ref[c] = cot_ref[:, :, at].astype(F32).reshape(cots_ref.shape[1:])

    gain1, gain2 = column(g1_ref), column(g2_ref)
    place = Place()
    totals = [Total(place, order, sum_sends.at[i], sum_recvs.at[i]) for i, order in enumerate(ORDERS)]

    @pl.when(step == 0)
    def clear():
        for ref in (dwp_ref, dw1_ref, dw2t_ref, dwot_ref, dwg_ref, dg1_ref, dg2_ref):
            ref[...] = jnp.zeros_like(ref)

    rows = tokens_of(xs_ref)
    normed = norm_forward(rows, gain1)
    q_ref[...], k_ref[...], v_ref[...] = project_block(
        normed, wpt_ref, cos_ref[...], sin_ref[...], inner, LOG2E * size**-0.5
    )
    gate_ref[...] = dg(wgt_ref[...], normed, NN)
    ones = extra_rows([jnp.ones((1, BLOCK), F32)], BLOCK)

    def attend(head, carry):
        at = pl.ds(pl.multiple_of(head * size, size), size)
        row = pl.ds(head, 1)
        for group in range(groups):
            lanes = slice(group * BLOCK, (group + 1) * BLOCK)
            scores = dg(k_ref[at, lanes], q_ref[at, lanes], TN) + bias_ref[...]
            weights = jnp.exp2(scores - jnp.max(scores, axis=0, keepdims=True)).astype(BF16)
            p_ref[head * groups + group] = weights
            sums = dg(jnp.concatenate([v_ref[at, lanes], ones], axis=0), weights, NN)
            inverse = 1.0 / sums[size : size + 1]
            attended = sums[:size] * inverse
            linv_ref[row, lanes] = inverse
            att_ref[at, lanes] = attended
            gate = jax.nn.sigmoid(gate_ref[row, lanes])
            mixed_ref[at, lanes] = (attended * gate).astype(BF16)
        return carry

    lax.fori_loop(0, heads, attend, 0)
    middle = rows + dg(wot_ref[...], mixed_ref[...], NN)
    normed_ffn = norm_forward(middle, gain2)

    hidden = w1t_ref.shape[0]
    quarter = hidden // 4

    def expand(i, carry):
        at = pl.ds(pl.multiple_of(i * quarter, quarter), quarter)
        active, slope = gelu_pair(dg(w1t_ref[at, :], normed_ffn, NN))
        act_ref[at, :] = active.astype(BF16)
        slope_ref[at, :] = slope.astype(BF16)
        return carry

    lax.fori_loop(0, 4, expand, 0)
    mask = mask_ref[0]
    result = (middle + dg(w2t_ref[...], act_ref[...], NN)) * mask
    put_tokens(ys_ref, result)

    @pl.when(lax.rem(step, per_part) == per_part - 1)
    def send_rows():
        for c, at in enumerate(columns):
            y_buf[part, :, :, at] = ys_ref[c].reshape(slot_count, part_frames, 128).astype(BF16)

        def give(i, carry):
            other = lax.rem(my_band + i, band_count)
            send(
                y_buf.at[part, pl.ds(other * slot_dev, slot_dev)],
                y_out.at[:, pl.ds(own_at, part_frames)],
                y_send,
                y_recv,
                other,
                my_batch,
            )
            return carry

        lax.fori_loop(1, band_count, give, 0)
        pltpu.make_async_copy(
            y_buf.at[part, pl.ds(my_band * slot_dev, slot_dev)],
            y_out.at[:, pl.ds(own_at, part_frames)],
            local_sem.at[0],
        ).start()

    grad = tokens_of(cots_ref) * mask
    d_middle = ffn_backward(
        grad, act_ref[...], slope_ref[...], normed_ffn, middle, gain2, w1_ref, w2_ref, dw1_ref, dw2t_ref, dg2_ref
    )
    branch = d_middle.astype(BF16)
    dwot_ref[...] += dg(branch, mixed_ref[...], NT)
    dmixed_ref[...] = dg(wo_ref[...], branch, NN)

    def attend_back(head, carry):
        start = pl.multiple_of(head * size, size)
        at = pl.ds(start, size)
        row = pl.ds(head, 1)
        d_att, minus, d_logit = head_backward(dmixed_ref[at, :], att_ref[at, :], gate_ref[row, :], linv_ref[row, :])
        dlogit_ref[row, :] = d_logit
        for group in range(groups):
            lanes = slice(group * BLOCK, (group + 1) * BLOCK)
            d_queries, d_keys, d_values = scores_backward(
                q_ref[at, lanes],
                k_ref[at, lanes],
                v_ref[at, lanes],
                p_ref[head * groups + group],
                d_att[:, lanes],
                minus[:, lanes],
                cos_ref[:, lanes],
                sin_ref[:, lanes],
                size**-0.5,
            )
            dproj_ref[at, lanes] = d_queries.astype(BF16)
            dproj_ref[pl.ds(inner + start, size), lanes] = d_keys.astype(BF16)
            dproj_ref[pl.ds(2 * inner + start, size), lanes] = d_values.astype(BF16)
        return carry

    lax.fori_loop(0, heads, attend_back, 0)
    d_logit = jnp.concatenate([dlogit_ref[...], jnp.zeros_like(dlogit_ref)], axis=0).astype(BF16)
    dwp_ref[...] += dg(normed, dproj_ref[...], NT)
    dwg_ref[...] += dg(normed, d_logit, NT)[:, :heads]
    d_normed = dg(wp_ref[...], dproj_ref[...], NN) + dg(wg_ref[...], dlogit_ref[...].astype(BF16), NN)
    d_rows, terms = norm_backward(rows, gain1, d_normed)
    dg1_ref[...] += jnp.sum(terms, axis=1, keepdims=True)
    put_tokens(dxs_ref, d_middle + d_rows)

    @pl.when(lax.rem(step, per_part) == per_part - 1)
    def send_grads():
        for c, at in enumerate(columns):
            dx_buf[part, :, :, at] = dxs_ref[c].reshape(slot_count, part_frames, 128).astype(BF16)

        def give(i, carry):
            other = lax.rem(my_band * batch_count + my_batch + i, chunks)
            band, batch = other // batch_count, lax.rem(other, batch_count)
            for j in range(slots):
                send(
                    dx_buf.at[part, band * slot_dev + batch_count * j + batch],
                    dx_out.at[j * chunks + own_chunk, pl.ds(part_at, part_frames)],
                    dx_send,
                    dx_recv,
                    band,
                    batch,
                )
            return carry

        lax.fori_loop(1, chunks, give, 0)
        for j in range(slots):
            pltpu.make_async_copy(
                dx_buf.at[part, my_band * slot_dev + batch_count * j + my_batch],
                dx_out.at[j * chunks + own_chunk, pl.ds(part_at, part_frames)],
                local_sem.at[1],
            ).start()

    @pl.when(step == pl.num_programs(0) - 1)
    def finish():
        narrow_out[...] = narrow_tile([dwg_ref[...], dg1_ref[...], dg2_ref[...]], model)
        core = place.bits["core"]
        lay_halves(halves[0], 0, dwp_ref)
        lay_halves(halves[0], dwp_ref.shape[1], dwot_ref)
        totals[0].start_core(halves[0], half_recvs[0][0])
        lay_halves(halves[1], 0, dw1_ref)
        lay_halves(halves[1], dw1_ref.shape[1], dw2t_ref)
        totals[1].start_core(halves[1], half_recvs[1][0])
        held = [half.at[core] for half in halves]
        for i, total in enumerate(totals):
            total.end_core(held[i], half_recvs[i][0])
            total.start_half(1, held[i], half_recvs[i][1])
        for i, total in enumerate(totals):
            total.end_half(1, held[i], half_recvs[i][1])
            total.start_half(2, held[i], half_recvs[i][2])
        for i, total in enumerate(totals):
            total.end_half(2, held[i], half_recvs[i][2])
            rows = total.half_rows(held[i], 2)[0]
            pltpu.make_async_copy(held[i].at[rows], part_outs[i], part_sem.at[i]).start()
        for i, total in enumerate(totals):
            rows = total.half_rows(held[i], 2)[0]
            pltpu.make_async_copy(held[i].at[rows], part_outs[i], part_sem.at[i]).wait()
        piece = y_out.shape[1] // band_count
        await_bytes(y_out.at[:, pl.ds(0, piece)], local_sem.at[0])
        await_bytes(dx_out.at[pl.ds(0, slots)], local_sem.at[1])
        for sem in (y_send, y_recv):
            await_bytes(y_out.at[:, pl.ds(0, piece * (band_count - 1))], sem)
        for sem in (dx_send, dx_recv):
            await_bytes(dx_out.at[pl.ds(0, slots * (chunks - 1))], sem)


def band_layer(rows, cot, mask, bias, cos, sin, params, flips, band_count, batch_count):
    prenorm, project, gating, output_weight, midnorm, expand, shrink = params
    slot_count, piece, model = rows.shape
    steps, _, tokens = mask.shape
    heads, inner, hidden = gating.shape[1], output_weight.shape[0], expand.shape[1]
    groups = tokens // BLOCK
    taken = tokens // slot_count
    part_frames = 16
    per_part = part_frames // taken
    parts = piece // part_frames
    slot_dev = slot_count // band_count
    consts = (bias, cos, sin, prenorm, midnorm) + flips + (project, gating, output_weight, expand, shrink)
    widths = (3 * inner + inner, 2 * hidden)
    eighth = model // 8
    blocks = pl.BlockSpec((slot_count, part_frames, model), lambda i: (0, i // per_part, 0))
    anywhere = pl.BlockSpec(memory_space=pl.ANY)
    dma = pltpu.SemaphoreType.DMA
    return pl.pallas_call(
        lambda *refs: band_kernel(heads, batch_count, band_count, *refs),
        grid=(steps,),
        out_shape=(
            jax.ShapeDtypeStruct((slot_dev, piece * band_count, model), BF16),
            jax.ShapeDtypeStruct((slot_count, piece, model), BF16),
            [jax.ShapeDtypeStruct((eighth, width), BF16) for width in widths],
            jax.ShapeDtypeStruct((model, 128), F32),
        ),
        in_specs=[blocks, blocks, pl.BlockSpec((1, 1, tokens), lambda i: (i, 0, 0))] + [whole_spec(c) for c in consts],
        out_specs=(anywhere, anywhere, [anywhere] * 2, pl.BlockSpec((model, 128), lambda i: (0, 0))),
        scratch_shapes=[
            pltpu.VMEM((inner, tokens), BF16),
            pltpu.VMEM((inner, tokens), BF16),
            pltpu.VMEM((inner, tokens), BF16),
            pltpu.VMEM((heads * groups, BLOCK, BLOCK), BF16),
            pltpu.VMEM((heads, tokens), F32),
            pltpu.VMEM((heads, tokens), F32),
            pltpu.VMEM((inner, tokens), F32),
            pltpu.VMEM((inner, tokens), BF16),
            pltpu.VMEM((hidden, tokens), BF16),
            pltpu.VMEM((hidden, tokens), BF16),
            pltpu.VMEM((inner, tokens), BF16),
            pltpu.VMEM((inner, tokens), F32),
            pltpu.VMEM((heads, tokens), F32),
            pltpu.VMEM((3 * inner, tokens), BF16),
            pltpu.VMEM((model, 3 * inner), F32),
            pltpu.VMEM((model, hidden), F32),
            pltpu.VMEM((model, hidden), F32),
            pltpu.VMEM((model, inner), F32),
            pltpu.VMEM((model, heads), F32),
            pltpu.VMEM((model, 1), F32),
            pltpu.VMEM((model, 1), F32),
            pltpu.VMEM((model // 128, slot_count * part_frames, 128), F32),
            pltpu.VMEM((model // 128, slot_count * part_frames, 128), F32),
            pltpu.VMEM((model // 128, slot_count * part_frames, 128), F32),
            pltpu.VMEM((model // 128, slot_count * part_frames, 128), F32),
            pltpu.VMEM((parts, slot_count, part_frames, model), BF16),
            pltpu.VMEM((parts, slot_count, part_frames, model), BF16),
            dma,
            dma,
            dma,
            dma,
            dma((2,)),
            [pltpu.VMEM((2, model // 2, width), BF16) for width in widths],
            [
                [pltpu.VMEM((rows, width), BF16) for rows in (model // 2, model // 4, model // 8)]
                for width in widths
            ],
            dma((2, TOTAL_STEPS)),
            dma((2, TOTAL_STEPS)),
            dma((2,)),
        ],
        compiler_params=pltpu.CompilerParams(
            vmem_limit_bytes=VMEM_BYTES, collective_id=1, has_side_effects=True
        ),
        cost_estimate=cost(30.0e6 * slot_count * piece, 0, 60e6),
        name="band_layer",
    )(rows, cot, mask, *consts)


def slot_shards(activations, cotangent, frame_counts, slot_bands, *weights):
    slot_dev, _, frame_dev, model = activations.shape
    slot_count = slot_bands.shape[0]
    batch, band = lax.axis_size("batch"), lax.axis_size("band")
    frames = frame_dev * batch
    piece = frame_dev // band
    slots = slot_dev // batch
    weights = tuple(w[None] if w.ndim == 1 else w for w in weights)
    time_params, band_params = weights[:7], weights[7:]
    heads, inner, hidden = time_params[2].shape[1], time_params[3].shape[0], time_params[5].shape[1]
    size = inner // heads

    positions = jnp.arange(frames, dtype=jnp.int32)
    time_cos, time_sin = rotary_tables(positions.astype(F32), size)
    time_bias = jnp.where(positions[None, :] < frame_counts[:, None], 0.0, NEG_FILL).astype(F32)
    band_cos, band_sin = rotary_tables(jnp.maximum(slot_bands, 0).astype(F32), size)
    tokens = min(2 * BLOCK, piece * slot_count)
    copies = tokens // slot_count
    slot_valid = slot_bands >= 0
    index = jnp.arange(BLOCK, dtype=jnp.int32)
    together = (index[:, None] // slot_count == index[None, :] // slot_count) & jnp.tile(
        slot_valid, BLOCK // slot_count
    )[:, None]
    band_bias = jnp.where(together, 0.0, NEG_FILL).astype(F32)
    own_start = lax.axis_index("batch") * frame_dev + lax.axis_index("band") * piece
    own_frames = own_start + jnp.arange(piece, dtype=jnp.int32)
    mask = ((own_frames < frame_counts[0])[:, None] & slot_valid[None, :]).astype(F32)
    mask = mask.reshape(piece * slot_count // tokens, 1, tokens)

    band_rows, band_cot, rows, n, q, k, v, p, linv, gate, att, mixed, mid, nf, act, slope, *flips = time_forward(
        activations.reshape(slot_dev, frame_dev, model),
        cotangent.reshape(slot_dev, frame_dev, model),
        time_bias,
        time_cos.T,
        time_sin.T,
        time_params,
        band_params,
        band,
        batch,
    )
    layer_output, slot_grad, band_parts, band_narrow = band_layer(
        band_rows,
        band_cot,
        mask,
        band_bias,
        jnp.tile(band_cos.T, (1, copies)),
        jnp.tile(band_sin.T, (1, copies)),
        band_params,
        tuple(flips),
        band,
        batch,
    )
    slot_grad = slot_grad.reshape(slots, frames, model)
    g1, g2 = time_params[0], time_params[4]
    dmid, datt, minus, dlogit, ffn_sums, dg2, regions = time_ffn_backward(
        slot_grad,
        act,
        slope,
        nf,
        mid,
        mixed,
        att,
        gate,
        linv,
        g2,
        time_params[5],
        time_params[6],
        time_params[3],
        band_parts,
    )
    input_grad, band_sums, ffn_sums, pair_sums = time_attention_backward(
        p,
        q,
        k,
        v,
        datt,
        minus,
        dlogit,
        n,
        rows,
        dmid,
        time_cos.T,
        time_sin.T,
        g1,
        time_params[1],
        time_params[2],
        band_narrow,
        dg2,
        regions,
        ffn_sums,
        batch,
    )
    input_grad, *grads = finish_sums(input_grad, band_sums, ffn_sums, pair_sums, time_params, band_params)
    grads = [g[0] if g.shape[0] == 1 else g for g in grads]
    return (layer_output.reshape(activations.shape), input_grad.reshape(activations.shape), *grads)


def shards(activations, cotangent, frame_counts, slot_bands, *weights):
    slot_dev, clips, frame_dev, _ = activations.shape
    batch, band = lax.axis_size("batch"), lax.axis_size("band")
    fits = (
        clips == 1
        and batch == 4
        and band == 2 * Z_COUNT
        and slot_dev % batch == 0
        and frame_dev == BLOCK
        and frame_dev % (16 * band) == 0
        and slot_bands.shape[0] == 64
        and activations.shape[-1] % 128 == 0
        and (frame_dev // band * slot_bands.shape[0]) % (2 * BLOCK) == 0
        and weights[2].shape[1] == 8
    )
    form = slot_shards if fits else generic_shards
    return form(activations, cotangent, frame_counts, slot_bands, *weights)


def solution(mesh):
    return jax.shard_map(
        shards,
        mesh=mesh,
        in_specs=(
            P("band", None, "batch", None),
            P("band", None, "batch", None),
            P(),
            P(),
            P(),
            P(),
            P(),
            P(),
            P(),
            P(),
            P(),
            P(),
            P(),
            P(),
            P(),
            P(),
            P(),
            P(),
        ),
        out_specs=(
            P("band", None, "batch", None),
            P("band", None, "batch", None),
            P(),
            P(),
            P(),
            P(),
            P(),
            P(),
            P(),
            P(),
            P(),
            P(),
            P(),
            P(),
            P(),
            P(),
        ),
        check_vma=False,
    )
```

```python
import math

import jax
import jax.numpy as jnp
from jax import lax
from jax.experimental import pallas as pl
from jax.experimental.pallas import tpu as pltpu
from jax.sharding import PartitionSpec as P

EPSILON = 1e-05
NEG_FILL = -1000000000.0
TIME_LAYOUT = ("bqhe", "bkhe")
BAND_LAYOUT = ("qbhe", "kbhe")


def rms_scale(residual, gain):
    return (
        residual * lax.rsqrt(jnp.mean(residual * residual, axis=-1, keepdims=True) + EPSILON) * gain
    )


def gelu_exact(values):
    return jax.nn.gelu(values, approximate=False)


def rotary_tables(positions, head_size):
    half_size = head_size // 2
    rates = jnp.exp(-math.log(10000.0) * jnp.arange(half_size, dtype=jnp.float32) / half_size)
    angles = positions[:, None] * rates[None, :]
    return (jnp.cos(angles), jnp.sin(angles))


def rotate(vectors, cos_table, sin_table):
    half_size = vectors.shape[-1] // 2
    first = vectors[..., :half_size]
    second = vectors[..., half_size:]
    return jnp.concatenate(
        [first * cos_table - second * sin_table, first * sin_table + second * cos_table], axis=-1
    )


def token_sum(left, right):
    return lax.dot_general(
        left.reshape(-1, left.shape[-1]),
        right.reshape(-1, right.shape[-1]),
        (((0,), (0,)), ((), ())),
        preferred_element_type=jnp.float32,
    )


def back_dot(gradient, weight):
    return lax.dot_general(
        gradient,
        weight,
        (((gradient.ndim - 1,), (1,)), ((), ())),
        preferred_element_type=jnp.float32,
    )


def block_forward(queries, key_rows, value_rows, key_valid, layout):
    query_form, key_form = layout
    scores = (
        jnp.einsum(
            query_form + "," + key_form + "->bhqk",
            queries,
            key_rows,
            preferred_element_type=jnp.float32,
        )
        * 0.125
    )
    scores = jnp.where(key_valid[:, None, None, :], scores, NEG_FILL)
    highest = jnp.max(scores, axis=-1, keepdims=True)
    exponents = jnp.exp(scores - highest)
    totals = jnp.sum(exponents, axis=-1, keepdims=True)
    soft_weights = (exponents / totals).astype(jnp.bfloat16)
    output = jnp.einsum(
        "bhqk," + key_form + "->" + query_form,
        soft_weights,
        value_rows,
        preferred_element_type=jnp.float32,
    )
    return (output, highest + jnp.log(totals))


def block_backward(queries, key_rows, value_rows, key_valid, log_totals, out_grad, layout):
    query_form, key_form = layout
    scores = (
        jnp.einsum(
            query_form + "," + key_form + "->bhqk",
            queries,
            key_rows,
            preferred_element_type=jnp.float32,
        )
        * 0.125
    )
    soft_weights = jnp.where(key_valid[:, None, None, :], jnp.exp(scores - log_totals), 0.0)
    weight_grad = jnp.einsum(
        query_form + "," + key_form + "->bhqk",
        out_grad,
        value_rows,
        preferred_element_type=jnp.float32,
    )
    score_grad = (
        soft_weights * (weight_grad - jnp.sum(soft_weights * weight_grad, axis=-1, keepdims=True))
    ).astype(jnp.bfloat16)
    query_grad = (
        jnp.einsum(
            "bhqk," + key_form + "->" + query_form,
            score_grad,
            key_rows,
            preferred_element_type=jnp.float32,
        )
        * 0.125
    )
    key_grad = (
        jnp.einsum(
            "bhqk," + query_form + "->" + key_form,
            score_grad,
            queries,
            preferred_element_type=jnp.float32,
        )
        * 0.125
    )
    value_grad = jnp.einsum(
        "bhqk," + query_form + "->" + key_form,
        soft_weights.astype(jnp.bfloat16),
        out_grad,
        preferred_element_type=jnp.float32,
    )
    return (query_grad, key_grad, value_grad)


def time_attend(queries, key_rows, value_rows, key_valid):
    keys_full, values_full = (
        lax.all_gather(key_rows, "batch", axis=1, tiled=True),
        lax.all_gather(value_rows, "batch", axis=1, tiled=True),
    )
    output, log_totals = block_forward(queries, keys_full, values_full, key_valid, TIME_LAYOUT)
    return (output, (log_totals, keys_full, values_full))


def time_attend_back(queries, key_rows, value_rows, key_valid, attn_kept, out_grad):
    log_totals, keys_full, values_full = attn_kept
    query_grad, key_full_grad, value_full_grad = block_backward(
        queries, keys_full, values_full, key_valid, log_totals, out_grad, TIME_LAYOUT
    )
    key_grad, value_grad = (
        lax.psum_scatter(
            key_full_grad.astype(jnp.bfloat16), "batch", scatter_dimension=1, tiled=True
        ).astype(jnp.float32),
        lax.psum_scatter(
            value_full_grad.astype(jnp.bfloat16), "batch", scatter_dimension=1, tiled=True
        ).astype(jnp.float32),
    )
    return (query_grad, key_grad, value_grad)


def band_attend(queries, key_rows, value_rows, key_valid):
    return block_forward(queries, key_rows, value_rows, key_valid, BAND_LAYOUT)


def band_attend_back(queries, key_rows, value_rows, key_valid, attn_kept, out_grad):
    return block_backward(
        queries, key_rows, value_rows, key_valid, attn_kept, out_grad, BAND_LAYOUT
    )


def layer_forward(residual, params, tables, key_valid, attend):
    prenorm, project, gating, output_weight, midnorm, expand, shrink = params
    cos_table, sin_table = tables
    normed = rms_scale(residual, prenorm.astype(jnp.float32)).astype(jnp.bfloat16)
    projected = jnp.dot(normed, project, preferred_element_type=jnp.float32)
    gate_logits = jnp.dot(normed, gating, preferred_element_type=jnp.float32)
    inner_width = output_weight.shape[0]
    head_count = gating.shape[1]
    head_shape = residual.shape[:-1] + (head_count, inner_width // head_count)
    queries = rotate(projected[..., :inner_width].reshape(head_shape), cos_table, sin_table).astype(
        jnp.bfloat16
    )
    key_rows = rotate(
        projected[..., inner_width : 2 * inner_width].reshape(head_shape), cos_table, sin_table
    ).astype(jnp.bfloat16)
    value_rows = projected[..., 2 * inner_width :].reshape(head_shape).astype(jnp.bfloat16)
    attended, attn_kept = attend(queries, key_rows, value_rows, key_valid)
    gate_values = jax.nn.sigmoid(gate_logits)
    mixed_heads = (
        (attended * gate_values[..., None])
        .reshape(residual.shape[:-1] + (inner_width,))
        .astype(jnp.bfloat16)
    )
    middle = residual + jnp.dot(mixed_heads, output_weight, preferred_element_type=jnp.float32)
    normed_ffn = rms_scale(middle, midnorm.astype(jnp.float32)).astype(jnp.bfloat16)
    hidden = jnp.dot(normed_ffn, expand, preferred_element_type=jnp.float32)
    active = gelu_exact(hidden).astype(jnp.bfloat16)
    result = middle + jnp.dot(active, shrink, preferred_element_type=jnp.float32)
    kept_values = (
        residual,
        normed,
        gate_logits,
        queries,
        key_rows,
        value_rows,
        attn_kept,
        attended,
        mixed_heads,
        middle,
        normed_ffn,
        hidden,
        active,
    )
    return (result, kept_values)


def layer_backward(result_grad, params, kept_values, tables, key_valid, attend_back):
    prenorm, project, gating, output_weight, midnorm, expand, shrink = params
    (
        residual,
        normed,
        gate_logits,
        queries,
        key_rows,
        value_rows,
        attn_kept,
        attended,
        mixed_heads,
        middle,
        normed_ffn,
        hidden,
        active,
    ) = kept_values
    cos_table, sin_table = tables
    branch_grad = result_grad.astype(jnp.bfloat16)
    shrink_grad = token_sum(active, branch_grad)
    active_grad = back_dot(branch_grad, shrink)
    hidden_grad = jax.vjp(gelu_exact, hidden)[1](active_grad)[0].astype(jnp.bfloat16)
    expand_grad = token_sum(normed_ffn, hidden_grad)
    normed_ffn_grad = back_dot(hidden_grad, expand)
    middle_norm_grad, midnorm_grad = jax.vjp(rms_scale, middle, midnorm.astype(jnp.float32))[1](
        normed_ffn_grad
    )
    middle_grad = result_grad + middle_norm_grad
    attn_branch = middle_grad.astype(jnp.bfloat16)
    output_grad = token_sum(mixed_heads, attn_branch)
    mixed_grad = back_dot(attn_branch, output_weight).reshape(attended.shape)
    gate_values = jax.nn.sigmoid(gate_logits)
    attended_grad = (mixed_grad * gate_values[..., None]).astype(jnp.bfloat16)
    logit_grad = (
        jnp.sum(mixed_grad * attended, axis=-1) * gate_values * (1.0 - gate_values)
    ).astype(jnp.bfloat16)
    query_grad, key_grad, value_grad = attend_back(
        queries, key_rows, value_rows, key_valid, attn_kept, attended_grad
    )
    flat_shape = residual.shape[:-1] + (-1,)
    projected_grad = jnp.concatenate(
        [
            rotate(query_grad, cos_table, -sin_table).reshape(flat_shape),
            rotate(key_grad, cos_table, -sin_table).reshape(flat_shape),
            value_grad.reshape(flat_shape),
        ],
        axis=-1,
    ).astype(jnp.bfloat16)
    project_grad = token_sum(normed, projected_grad)
    gating_grad = token_sum(normed, logit_grad)
    normed_grad = back_dot(projected_grad, project) + back_dot(logit_grad, gating)
    residual_norm_grad, prenorm_grad = jax.vjp(rms_scale, residual, prenorm.astype(jnp.float32))[1](
        normed_grad
    )
    return (
        middle_grad + residual_norm_grad,
        (
            prenorm_grad,
            project_grad,
            gating_grad,
            output_grad,
            midnorm_grad,
            expand_grad,
            shrink_grad,
        ),
    )


def generic_shards(
    activations,
    cotangent,
    frame_counts,
    slot_bands,
    time_prenorm,
    time_project,
    time_gating,
    time_output,
    time_midnorm,
    time_expand,
    time_shrink,
    band_prenorm,
    band_project,
    band_gating,
    band_output,
    band_midnorm,
    band_expand,
    band_shrink,
):
    slot_dev, clip_count, frame_dev, model_width = activations.shape
    slot_count = slot_bands.shape[0]
    frames_all = frame_dev * lax.axis_size("batch")
    head_size = time_output.shape[0] // time_gating.shape[1]
    time_params = (
        time_prenorm,
        time_project,
        time_gating,
        time_output,
        time_midnorm,
        time_expand,
        time_shrink,
    )
    band_params = (
        band_prenorm,
        band_project,
        band_gating,
        band_output,
        band_midnorm,
        band_expand,
        band_shrink,
    )
    own_bands = lax.dynamic_slice_in_dim(slot_bands, lax.axis_index("band") * slot_dev, slot_dev)
    frame_start = lax.axis_index("batch") * frame_dev
    own_frames = frame_start + jnp.arange(frame_dev, dtype=jnp.int32)
    frame_valid = own_frames[None, :] < frame_counts[:, None]
    row_valid = (own_bands >= 0)[:, None, None] & frame_valid[None]
    full_valid = jnp.arange(frames_all, dtype=jnp.int32)[None, :] < frame_counts[:, None]
    time_valid = jnp.broadcast_to(full_valid[None], (slot_dev, clip_count, frames_all)).reshape(
        slot_dev * clip_count, frames_all
    )
    time_cos, time_sin = rotary_tables(own_frames.astype(jnp.float32), head_size)
    time_tables = (time_cos[None, :, None, :], time_sin[None, :, None, :])
    band_cos, band_sin = rotary_tables(jnp.maximum(slot_bands, 0).astype(jnp.float32), head_size)
    band_tables = (band_cos[:, None, None, :], band_sin[:, None, None, :])
    residual = activations.astype(jnp.float32).reshape(
        slot_dev * clip_count, frame_dev, model_width
    )
    time_result, time_kept = layer_forward(
        residual, time_params, time_tables, time_valid, time_attend
    )
    masked_cot = jnp.where(row_valid[..., None], cotangent, jnp.zeros((), jnp.bfloat16)).reshape(
        slot_dev, clip_count * frame_dev, model_width
    )
    frame_rows = lax.all_to_all(
        time_result.astype(jnp.bfloat16), "band", split_axis=1, concat_axis=0, tiled=True
    ).astype(time_result.dtype)
    band_valid = jnp.broadcast_to((slot_bands >= 0)[None, :], (frame_rows.shape[1], slot_count))
    band_result, band_kept = layer_forward(
        frame_rows, band_params, band_tables, band_valid, band_attend
    )
    back_rows = lax.all_to_all(
        band_result.astype(jnp.bfloat16), "band", split_axis=0, concat_axis=1, tiled=True
    ).astype(band_result.dtype)
    layer_output = jnp.where(
        row_valid[..., None], back_rows.reshape(activations.shape), 0.0
    ).astype(jnp.bfloat16)
    frame_cot = lax.all_to_all(masked_cot, "band", split_axis=1, concat_axis=0, tiled=True)
    frame_grad, band_grads = layer_backward(
        frame_cot.astype(jnp.float32),
        band_params,
        band_kept,
        band_tables,
        band_valid,
        band_attend_back,
    )
    slot_grad = lax.all_to_all(
        frame_grad.astype(jnp.bfloat16), "band", split_axis=0, concat_axis=1, tiled=True
    ).astype(frame_grad.dtype)
    input_grad, time_grads = layer_backward(
        slot_grad, time_params, time_kept, time_tables, time_valid, time_attend_back
    )
    input_grad = input_grad.reshape(activations.shape)
    all_grads = lax.psum(
        (
            time_grads[0],
            time_grads[1],
            time_grads[2],
            time_grads[3],
            time_grads[4],
            time_grads[5],
            time_grads[6],
            band_grads[0],
            band_grads[1],
            band_grads[2],
            band_grads[3],
            band_grads[4],
            band_grads[5],
            band_grads[6],
        ),
        ("band", "batch"),
    )
    return (
        layer_output,
        input_grad,
        all_grads[0],
        all_grads[1],
        all_grads[2],
        all_grads[3],
        all_grads[4],
        all_grads[5],
        all_grads[6],
        all_grads[7],
        all_grads[8],
        all_grads[9],
        all_grads[10],
        all_grads[11],
        all_grads[12],
        all_grads[13],
    )


BLOCK = 256
LOG2E = 1.4426950408889634
F32 = jnp.float32
BF16 = jnp.bfloat16
NN = (((1,), (0,)), ((), ()))
NT = (((1,), (1,)), ((), ()))
TN = (((0,), (0,)), ((), ()))
VMEM_BYTES = 60 * 2**20


def dg(left, right, dims):
    return lax.dot_general(left, right, dims, preferred_element_type=F32)


def norm_forward(rows, gain):
    scale = lax.rsqrt(jnp.mean(rows * rows, axis=0, keepdims=True) + EPSILON)
    return (rows * scale * gain).astype(BF16)


def norm_backward(rows, gain, grad):
    scale = lax.rsqrt(jnp.mean(rows * rows, axis=0, keepdims=True) + EPSILON)
    unit = rows * scale
    scaled = grad * gain
    inner = jnp.mean(scaled * unit, axis=0, keepdims=True)
    return scale * (scaled - unit * inner), grad * unit


def gelu_pair(values):
    size = jnp.abs(values)
    denominator = 1.0 + (0.3275911 * math.sqrt(0.5)) * size
    t = pl.reciprocal(denominator, approx=True)
    t = t * (2.0 - denominator * t)
    bell = jnp.exp2(values * values * (-0.5 * LOG2E))
    poly = 0.5 * 1.061405429
    for coefficient in (-1.453152027, 1.421413741, -0.284496736, 0.254829592):
        poly = poly * t + 0.5 * coefficient
    tail = poly * t * bell
    upper = jnp.where(values < 0.0, tail, 1.0 - tail)
    slope = upper + values * bell * (1.0 / math.sqrt(2.0 * math.pi))
    return values * upper, slope


def turn(vectors, cos, sin):
    half = cos.shape[0]
    split = vectors.reshape(-1, 2 * half, vectors.shape[-1])
    first = split[:, :half]
    second = split[:, half:]
    turned = jnp.concatenate([first * cos - second * sin, first * sin + second * cos], axis=1)
    return turned.reshape(vectors.shape)


def three_parts(values):
    top = values.astype(BF16).astype(F32)
    rest = values - top
    middle = rest.astype(BF16).astype(F32)
    return top, middle, rest - middle


def extra_rows(rows, width):
    tile = jnp.concatenate(rows + [jnp.zeros((8 - len(rows), width), F32)], axis=0)
    return jnp.concatenate([tile, jnp.zeros((8, width), F32)], axis=0).astype(BF16)


def project_block(normed, wpt_ref, cos, sin, inner, scale):
    queries = turn(dg(wpt_ref[0:inner, :], normed, NN), cos, sin) * scale
    keys = turn(dg(wpt_ref[inner : 2 * inner, :], normed, NN), cos, sin)
    values = dg(wpt_ref[2 * inner : 3 * inner, :], normed, NN)
    return queries.astype(BF16), keys.astype(BF16), values.astype(BF16)


def column(gain_ref):
    row = gain_ref[...].astype(F32).reshape(1, gain_ref.shape[0])
    return jnp.broadcast_to(row, (8, row.shape[1])).T[:, :1]


def rotary_rows(positions, half):
    rank = lax.broadcasted_iota(jnp.int32, (half, positions.shape[1]), 0).astype(F32)
    angles = positions * jnp.exp(-math.log(10000.0) * rank / half)
    return jnp.cos(angles), jnp.sin(angles)


def flipped(ref):
    return ref[...].astype(F32).T.astype(BF16)


def greet_all(band_count, batch_count):
    count = band_count * batch_count
    me = lax.axis_index("band") * batch_count + lax.axis_index("batch")
    barrier = pltpu.get_barrier_semaphore()

    def signal(i, carry):
        other = lax.rem(me + i, count)
        pl.semaphore_signal(
            barrier,
            inc=1,
            device_id=(other // batch_count, lax.rem(other, batch_count)),
            device_id_type=pl.DeviceIdType.MESH,
        )
        return carry

    lax.fori_loop(1, count, signal, 0)
    pl.semaphore_wait(barrier, count - 1)


def send(source, target, send_sem, recv_sem, band, batch):
    pltpu.make_async_remote_copy(
        src_ref=source,
        dst_ref=target,
        send_sem=send_sem,
        recv_sem=recv_sem,
        device_id=(band, batch),
        device_id_type=pl.DeviceIdType.MESH,
    ).start()


def await_bytes(ref, sem):
    pltpu.make_async_copy(ref, ref, sem).wait()


class Place:
    def __init__(self):
        self.band, self.batch = lax.axis_index("band"), lax.axis_index("batch")
        self.bits = {
            "core": lax.rem(self.batch, 2),
            "x": self.batch // 2,
            "y": lax.rem(self.band, 2),
        }
        self.z = self.band // 2

    def across(self, axis):
        bit = self.bits[axis]
        if axis == "core":
            return self.band, self.batch + 1 - 2 * bit
        if axis == "x":
            return self.band, self.batch + 2 - 4 * bit
        return self.band + 1 - 2 * bit, self.batch

    def along_z(self, step):
        other = lax.rem(self.z + step, Z_COUNT)
        return other, (other * 2 + self.bits["y"], self.batch)


Z_COUNT = 4


def greet(others):
    barrier = pltpu.get_barrier_semaphore()
    for other in others:
        pl.semaphore_signal(barrier, inc=1, device_id=other, device_id_type=pl.DeviceIdType.MESH)
    pl.semaphore_wait(barrier, len(others))


class Total:
    def __init__(self, place, order, sends, recvs):
        self.place = place
        self.order = order
        self.sends, self.recvs = sends, recvs
        self.core = place.bits["core"]
        if order is not None:
            self.first, self.second = (place.bits[axis] for axis in order)

    def give(self, step, source, target, other):
        send(source, target, self.sends.at[step], self.recvs.at[step], *other)

    def took(self, step, ref):
        await_bytes(ref, self.recvs.at[step])
        await_bytes(ref, self.sends.at[step])

    def add(self, ref, rows, part):
        ref[rows] = (ref[rows].astype(F32) + part.astype(F32)).astype(BF16)

    def start_core(self, source, recv):
        self.give(0, source.at[1 - self.core], recv, self.place.across("core"))

    def end_core(self, held, recv):
        self.took(0, recv)
        held[...] = (held[...].astype(F32) + recv[...].astype(F32)).astype(BF16)

    def half_rows(self, held, level):
        rows = held.shape[0] // 2
        base = 0
        if level == 2:
            base, rows = self.first * rows, rows // 2
        bit = self.first if level == 1 else self.second
        keep = pl.ds(pl.multiple_of(base + bit * rows, rows), rows)
        away = pl.ds(pl.multiple_of(base + (1 - bit) * rows, rows), rows)
        return keep, away

    def start_half(self, level, held, recv):
        away = self.half_rows(held, level)[1]
        self.give(level, held.at[away], recv, self.place.across(self.order[level - 1]))

    def end_half(self, level, held, recv):
        self.took(level, recv)
        self.add(held, self.half_rows(held, level)[0], recv[...])

    def start_z(self, piece, recv):
        width = recv.shape[2]
        for step in range(1, Z_COUNT):
            index, other = self.place.along_z(step)
            lanes = pl.ds(pl.multiple_of(index * width, 128), width)
            self.give(3, piece.at[:, lanes], recv.at[step - 1], other)

    def z_lanes(self, width):
        return pl.ds(pl.multiple_of(self.place.z * width, 128), width)

    def end_z(self, piece, recv):
        self.took(3, recv)
        lanes = self.z_lanes(recv.shape[2])
        sums = piece[:, lanes].astype(F32)
        for step in range(Z_COUNT - 1):
            sums = sums + recv[step].astype(F32)
        piece[:, lanes] = sums.astype(BF16)

    def own_copy(self, piece, target, width, sem):
        lanes = self.z_lanes(width)
        return pltpu.make_async_copy(piece.at[:, lanes], target.at[:, lanes], sem)

    def start_z_back(self, piece, target, width, sem):
        lanes = self.z_lanes(width)
        for step in range(1, Z_COUNT):
            _, other = self.place.along_z(step)
            self.give(4, piece.at[:, lanes], target.at[:, lanes], other)
        self.own_copy(piece, target, width, sem).start()

    def end_z_back(self, piece, target, width, sem):
        self.took(4, target.at[:, pl.ds(0, (Z_COUNT - 1) * width)])
        self.own_copy(piece, target, width, sem).wait()

    def around(self):
        found = []
        for step in range(1, 4 * Z_COUNT):
            x = lax.rem(self.place.bits["x"] + step // 2 % 2, 2)
            y = lax.rem(self.place.bits["y"] + step % 2, 2)
            z = lax.rem(self.place.z + step // 4, Z_COUNT)
            found.append((2 * x + y, z, (2 * z + y, 2 * x + self.core)))
        return found

    def tile(self, ref, base, quarter, z, shape):
        rows = pl.ds(pl.multiple_of(base + quarter * shape[0], shape[0]), shape[0])
        return ref.at[rows, pl.ds(pl.multiple_of(z * shape[1], 128), shape[1])]

    def start_around(self, held, recv):
        for i, (quarter, z, other) in enumerate(self.around()):
            self.give(1, self.tile(held, 0, quarter, z, recv.shape[1:]), recv.at[i], other)

    def own_tile(self, ref, base, shape):
        return self.tile(ref, base, 2 * self.place.bits["x"] + self.place.bits["y"], self.place.z, shape)

    def end_around(self, held, recv):
        self.took(1, recv)
        own = self.own_tile(held, 0, recv.shape[1:])
        sums = own[...].astype(F32)
        for i in range(recv.shape[0]):
            sums = sums + recv[i].astype(F32)
        own[...] = sums.astype(BF16)

    def start_around_back(self, held, recv, out, sem):
        shape = recv.shape[1:]
        own = self.own_tile(held, 0, shape)
        target = self.own_tile(out, self.core * (out.shape[0] // 2), shape)
        for _, _, other in self.around():
            self.give(2, own, target, other)
        pltpu.make_async_copy(own, target, sem).start()

    def end_around_back(self, held, recv, out, sem):
        shape = recv.shape[1:]
        self.took(2, recv)
        target = self.own_tile(out, self.core * (out.shape[0] // 2), shape)
        pltpu.make_async_copy(self.own_tile(held, 0, shape), target, sem).wait()

    def back_rows(self, out, level):
        rows = out.shape[0] // 2
        base = self.core * rows
        if level >= 1:
            rows = rows // 2
            base = base + self.first * rows
        if level >= 2:
            rows = rows // 2
            base = base + self.second * rows
        return pl.ds(pl.multiple_of(base, rows), rows)

    def start_back(self, level, out, source=None):
        rows = self.back_rows(out, level)
        axis = "core" if level == 0 else self.order[level - 1]
        self.give(7 - level, out.at[rows] if source is None else source, out.at[rows], self.place.across(axis))

    def end_back(self, level, out):
        self.took(7 - level, out.at[self.back_rows(out, level)])


TOTAL_STEPS = 8


def time_forward_kernel(
    heads,
    batch_count,
    band_count,
    act_in,
    cot_in,
    count_ref,
    g1_ref,
    g2_ref,
    wgt_ref,
    wp_ref,
    wo_ref,
    w1_ref,
    w2_ref,
    band_wp_ref,
    band_wo_ref,
    band_w1_ref,
    band_w2_ref,
    band_rows,
    band_cot,
    rows_ref,
    n_ref,
    q_ref,
    k_ref,
    v_ref,
    p_ref,
    linv_ref,
    gate_ref,
    att_ref,
    mixed_ref,
    mid_ref,
    nf_ref,
    act_ref,
    slope_ref,
    band_wpt_ref,
    band_wot_ref,
    band_w1t_ref,
    band_w2t_ref,
    cos_ref,
    sin_ref,
    xt_ref,
    x_ref,
    result_ref,
    wpt_ref,
    wot_ref,
    w1t_ref,
    w2t_ref,
    row_send,
    row_recv,
    cot_send,
    cot_recv,
    result_send,
    result_recv,
    local_sem,
):
    slot, head = pl.program_id(0), pl.program_id(1)
    slots = pl.num_programs(0)
    slot_dev = cot_in.shape[0]
    frames, model = rows_ref.shape[1:]
    inner = q_ref.shape[1]
    size = inner // heads
    my_band, my_batch = lax.axis_index("band"), lax.axis_index("batch")
    frame_dev = frames // batch_count
    piece = frame_dev // band_count
    own_rows = pl.ds(pl.multiple_of(my_batch * frame_dev, frame_dev), frame_dev)
    held = x_ref.shape[0]
    frame_index = lax.broadcasted_iota(jnp.int32, (1, frames), 1)

    def neighbour(i):
        core, x = lax.rem(my_batch, 2), my_batch // 2
        return lax.rem(x + i // 2, 2) * 2 + lax.rem(core + lax.rem(i, 2), 2)

    def own_row_copy(j):
        return pltpu.make_async_copy(
            act_in.at[batch_count * j + my_batch], x_ref.at[j, own_rows], local_sem.at[j]
        )

    def own_cot_copy():
        return pltpu.make_async_copy(
            cot_in.at[:, pl.ds(pl.multiple_of(my_band * piece, piece), piece)],
            band_cot.at[pl.ds(my_band * slot_dev, slot_dev)],
            local_sem.at[held],
        )

    @pl.when((slot == 0) & (head == 0))
    def start():
        greet_all(band_count, batch_count)
        for j in range(held):
            for i in range(1, batch_count):
                other = neighbour(i)
                send(
                    act_in.at[batch_count * j + other],
                    x_ref.at[j, own_rows],
                    row_send,
                    row_recv.at[j, i],
                    my_band,
                    other,
                )
            own_row_copy(j).start()

        def send_cot(i, carry):
            other = lax.rem(my_band + i, band_count)
            send(
                cot_in.at[:, pl.ds(pl.multiple_of(other * piece, piece), piece)],
                band_cot.at[pl.ds(my_band * slot_dev, slot_dev)],
                cot_send,
                cot_recv,
                other,
                my_batch,
            )
            return carry

        lax.fori_loop(1, band_count, send_cot, 0)
        own_cot_copy().start()
        cos_ref[...], sin_ref[...] = rotary_rows(frame_index.astype(F32), size // 2)
        wpt_ref[...] = flipped(wp_ref)
        wot_ref[...] = flipped(wo_ref)
        w1t_ref[...] = flipped(w1_ref)
        w2t_ref[...] = flipped(w2_ref)
        band_wpt_ref[...] = flipped(band_wp_ref)
        band_wot_ref[...] = flipped(band_wo_ref)
        band_w1t_ref[...] = flipped(band_w1_ref)
        band_w2t_ref[...] = flipped(band_w2_ref)

    @pl.when(head == 0)
    def before():
        gain = column(g1_ref)

        def block(i, carry):
            at = pl.ds(pl.multiple_of(neighbour(i) * BLOCK, BLOCK), BLOCK)

            @pl.when(i == 0)
            def own():
                for j in range(held):

                    @pl.when(slot == j)
                    def kept():
                        own_row_copy(j).wait()

            @pl.when(i > 0)
            def arrived():
                await_bytes(x_ref.at[slot, at], row_recv.at[slot, i])

            held_rows = x_ref[slot, at, :]
            rows_ref[0, at, :] = held_rows
            rows = held_rows.astype(F32).T
            xt_ref[:, at] = rows
            normed = norm_forward(rows, gain)
            n_ref[0, :, at] = normed
            queries, keys, values = project_block(
                normed, wpt_ref, cos_ref[:, at], sin_ref[:, at], inner, LOG2E * size**-0.5
            )
            q_ref[0, :, at] = queries
            k_ref[0, :, at] = keys
            v_ref[0, :, at] = values
            gate_ref[0, :, at] = dg(wgt_ref[...], normed, NN)
            return carry

        lax.fori_loop(0, frames // BLOCK, block, 0)

    at_head = pl.ds(pl.multiple_of(head * size, size), size)
    ones = jnp.ones((1, frames), F32)
    queries = jnp.concatenate([q_ref[0, at_head, :], extra_rows([ones], frames)], axis=0)
    keys = jnp.concatenate([k_ref[0, at_head, :], extra_rows([jnp.where(frame_index < count_ref[0], 0.0, NEG_FILL)], frames)], axis=0)
    values = jnp.concatenate([v_ref[0, at_head, :], extra_rows([ones], frames)], axis=0)
    scores = dg(keys, queries, TN)
    weights = jnp.exp2(scores - jnp.max(scores, axis=0, keepdims=True)).astype(BF16)
    p_ref[0, 0] = weights
    sums = dg(values, weights, NN)
    inverse = 1.0 / sums[size : size + 1]
    attended = sums[:size] * inverse
    linv_ref[0, pl.ds(head, 1), :] = inverse
    att_ref[0, at_head, :] = attended
    gate = jax.nn.sigmoid(gate_ref[0, pl.ds(head, 1), :])
    mixed_ref[0, at_head, :] = (attended * gate).astype(BF16)

    @pl.when(head == heads - 1)
    def after():
        gain = column(g2_ref)
        to_slot = my_band * slot_dev + batch_count * slot + my_batch

        def block(i, carry):
            at = pl.ds(pl.multiple_of(i * BLOCK, BLOCK), BLOCK)
            middle = xt_ref[:, at] + dg(wot_ref[...], mixed_ref[0, :, at], NN)
            mid_ref[0, :, at] = middle
            normed = norm_forward(middle, gain)
            nf_ref[0, :, at] = normed
            active, slope = gelu_pair(dg(w1t_ref[...], normed, NN))
            active = active.astype(BF16)
            act_ref[0, :, at] = active
            slope_ref[0, :, at] = slope.astype(BF16)
            result = middle + dg(w2t_ref[...], active, NN)
            result_ref[slot, at, :] = result.T.astype(BF16)

            def send_result(j, carry):
                other = lax.rem(my_band + j, band_count)
                source = result_ref.at[slot, pl.ds(pl.multiple_of(i * frame_dev + other * piece, piece), piece)]
                mine = (other == my_band) & (i == my_batch)

                @pl.when(mine)
                def keep():
                    pltpu.make_async_copy(source, band_rows.at[to_slot], local_sem.at[held + 1]).start()

                @pl.when(jnp.logical_not(mine))
                def give():
                    send(source, band_rows.at[to_slot], result_send, result_recv, other, i)

                return carry

            lax.fori_loop(1, band_count + 1, send_result, 0)
            return carry

        lax.fori_loop(0, frames // BLOCK, block, 0)

    @pl.when((slot == slots - 1) & (head == heads - 1))
    def finish():
        others = held * (band_count * batch_count - 1)
        others_cot = (band_count - 1) * slot_dev
        others_rows = (batch_count - 1) * frame_dev
        await_bytes(band_cot.at[pl.ds(0, others_cot)], cot_recv)
        await_bytes(band_cot.at[pl.ds(0, others_cot)], cot_send)
        own_cot_copy().wait()
        await_bytes(x_ref.at[:, pl.ds(0, others_rows)], row_send)
        await_bytes(band_rows.at[pl.ds(0, others)], result_send)
        await_bytes(band_rows.at[pl.ds(0, held)], local_sem.at[held + 1])
        await_bytes(band_rows.at[pl.ds(0, others)], result_recv)


def cost(flops, exps=0, moved=0):
    return pl.CostEstimate(flops=int(flops), bytes_accessed=int(moved), transcendentals=int(exps))


def whole_spec(array):
    nd = array.ndim
    return pl.BlockSpec(array.shape, lambda *ids: (0,) * nd, pipeline_mode=pl.Buffered(1))


def time_forward(activations, cotangent, counts, g1, g2, params, band_params, band_count, batch_count):
    wp, wgt, wo, w1, w2 = params
    bwp, _, bwo, bw1, bw2 = band_params
    slot_dev, frame_dev, model = activations.shape
    slots, frames = slot_dev // batch_count, frame_dev * batch_count
    heads, inner, hidden = wgt.shape[0], wo.shape[0], w1.shape[1]
    piece = frame_dev // band_count

    def per_slot(*shape):
        return pl.BlockSpec((1,) + shape, lambda s, h: (s,) + (0,) * len(shape))

    outs = [
        ((frames, model), BF16),
        ((model, frames), BF16),
        ((inner, frames), BF16),
        ((inner, frames), BF16),
        ((inner, frames), BF16),
        None,
        ((heads, frames), F32),
        ((heads, frames), F32),
        ((inner, frames), F32),
        ((inner, frames), BF16),
        ((model, frames), F32),
        ((model, frames), BF16),
        ((hidden, frames), BF16),
        ((hidden, frames), BF16),
    ]
    flips = [(w.shape[1], w.shape[0]) for w in (bwp, bwo, bw1, bw2)]
    own_flips = [(w.shape[1], w.shape[0]) for w in (wp, wo, w1, w2)]
    exchanged = jax.ShapeDtypeStruct((slot_dev * band_count, piece, model), BF16)
    anywhere = pl.BlockSpec(memory_space=pl.ANY)
    shapes, specs = [exchanged, exchanged], [anywhere, anywhere]
    for entry in outs:
        if entry is None:
            shapes.append(jax.ShapeDtypeStruct((slots, heads, frames, frames), BF16))
            specs.append(pl.BlockSpec((1, 1, frames, frames), lambda s, h: (s, h, 0, 0)))
        else:
            shapes.append(jax.ShapeDtypeStruct((slots,) + entry[0], entry[1]))
            specs.append(per_slot(*entry[0]))
    for shape in flips:
        shapes.append(jax.ShapeDtypeStruct(shape, BF16))
        specs.append(pl.BlockSpec(shape, lambda s, h: (0, 0), pipeline_mode=pl.Buffered(1)))
    consts = (g1, g2, wgt, wp, wo, w1, w2, bwp, bwo, bw1, bw2)
    half = inner // heads // 2
    for _ in range(2):
        shapes.append(jax.ShapeDtypeStruct((half, frames), F32))
        specs.append(pl.BlockSpec((half, frames), lambda s, h: (0, 0)))
    dma = pltpu.SemaphoreType.DMA
    return pl.pallas_call(
        lambda *refs: time_forward_kernel(heads, batch_count, band_count, *refs),
        grid=(slots, heads),
        out_shape=shapes,
        in_specs=[anywhere, anywhere, pl.BlockSpec(memory_space=pltpu.SMEM)] + [whole_spec(c) for c in consts],
        out_specs=specs,
        scratch_shapes=[
            pltpu.VMEM((model, frames), F32),
            pltpu.VMEM((slots, frames, model), BF16),
            pltpu.VMEM((slots, frames, model), BF16),
        ]
        + [pltpu.VMEM(shape, BF16) for shape in own_flips]
        + [dma, dma((slots, batch_count)), dma, dma, dma, dma, dma((slots + 2,))],
        compiler_params=pltpu.CompilerParams(
            vmem_limit_bytes=VMEM_BYTES, collective_id=0, has_side_effects=True
        ),
        cost_estimate=cost(2.0e6 * 4 * slots * frames, 2 * slots * heads * frames * frames, 60e6),
        name="time_forward",
    )(activations, cotangent, counts, *consts)


def ffn_backward(grad, act, slope, normed, middle, gain, w1_ref, w2_ref, dw1_ref, dw2t_ref, dg2_ref):
    branch = grad.astype(BF16)
    d_hidden = (dg(w2_ref[...], branch, NN) * slope.astype(F32)).astype(BF16)
    dw2t_ref[...] += dg(branch, act, NT)
    dw1_ref[...] += dg(normed, d_hidden, NT)
    d_normed = dg(w1_ref[...], d_hidden, NN)
    d_rows, terms = norm_backward(middle, gain, d_normed)
    dg2_ref[...] += jnp.sum(terms, axis=1, keepdims=True)
    return grad + d_rows


def head_backward(d_mixed, attended, gate_logit, inverse):
    gate = jax.nn.sigmoid(gate_logit)
    d_logit = jnp.sum(d_mixed * attended, axis=0, keepdims=True) * gate * (1.0 - gate)
    d_att = (d_mixed * (gate * inverse)).astype(BF16)
    minus = -jnp.sum(d_att.astype(F32) * attended, axis=0, keepdims=True)
    return d_att, minus, d_logit


def scores_backward(queries, keys, values, weights, d_att, minus, cos, sin, scale):
    width = queries.shape[1]
    ones = jnp.ones((1, width), F32)
    d_weights = dg(
        jnp.concatenate([values, extra_rows([ones, ones, ones], width)], axis=0),
        jnp.concatenate([d_att, extra_rows(list(three_parts(minus)), width)], axis=0),
        TN,
    )
    d_scores = (weights.astype(F32) * d_weights).astype(BF16)
    d_values = dg(d_att, weights, NT)
    d_queries = dg(keys, d_scores, NN) * scale
    d_keys = dg(queries, d_scores, NT) * (1.0 / LOG2E)
    return turn(d_queries, cos, -sin), turn(d_keys, cos, -sin), d_values


def time_ffn_backward_kernel(
    heads,
    grad_ref,
    act_ref,
    slope_ref,
    nf_ref,
    mid_ref,
    mixed_ref,
    att_ref,
    gate_ref,
    linv_ref,
    g2_ref,
    w1_ref,
    w2_ref,
    wo_ref,
    half_refs,
    dmid_ref,
    datt_ref,
    minus_ref,
    dlogit_ref,
    sums_refs,
    dg2_out,
    part_refs,
    dw1_ref,
    dw2t_ref,
    dwot_ref,
    dg2_ref,
    held_refs,
    half_recvs,
    z_recvs,
    sends,
    recvs,
    local_sem,
):
    place = Place()
    totals = [Total(place, order, sends.at[i], recvs.at[i]) for i, order in enumerate(BAND_ORDERS)]
    early = len(z_recvs)
    work = list(zip(totals, half_refs, held_refs, half_recvs))

    def half_copy(i):
        return pltpu.make_async_copy(half_refs[i], held_refs[i], local_sem.at[i])

    def part_copy(i):
        rows = totals[i].half_rows(held_refs[i], 2)[0]
        return pltpu.make_async_copy(held_refs[i].at[rows], part_refs[i], local_sem.at[len(totals) + i])

    step = pl.program_id(0) * pl.num_programs(1) + pl.program_id(1)
    last = pl.num_programs(0) * pl.num_programs(1) - 1
    size = wo_ref.shape[0] // heads

    @pl.when(step == 0)
    def clear():
        for ref in (dw1_ref, dw2t_ref, dwot_ref, dg2_ref):
            ref[...] = jnp.zeros_like(ref)
        greet([place.across("x"), place.across("y")] + [place.along_z(i)[1] for i in range(1, Z_COUNT)])
        for i, (total, halves, held, recv) in enumerate(work):
            half_copy(i).start()
            total.start_half(1, halves, recv[0])

    def eighth(i):
        return held_refs[i].at[totals[i].half_rows(held_refs[i], 2)[0]]

    @pl.when(step == last - 1)
    def first_half():
        for i, (total, halves, held, recv) in list(enumerate(work))[:early]:
            half_copy(i).wait()
            total.end_half(1, held, recv[0])
            total.start_half(2, held, recv[1])

    @pl.when(step == last)
    def second_half():
        for i, (total, halves, held, recv) in list(enumerate(work))[early:]:
            half_copy(i).wait()
            total.end_half(1, held, recv[0])
            total.start_half(2, held, recv[1])
        for i, (total, halves, held, recv) in list(enumerate(work))[:early]:
            total.end_half(2, held, recv[1])
            total.start_z(eighth(i), z_recvs[i])

    slot = pl.program_id(0)
    chunks, parts, rows, model = grad_ref.shape
    slots = pl.num_programs(0)
    taken = rows // slots
    both = grad_ref[...].astype(F32).reshape(chunks * parts, slots, taken, model)
    grad = both[:, 0]
    for j in range(1, slots):
        grad = jnp.where(slot == j, both[:, j], grad)
    grad = grad.reshape(chunks * parts * taken, model).T
    d_middle = ffn_backward(
        grad, act_ref[0], slope_ref[0], nf_ref[0], mid_ref[0], column(g2_ref), w1_ref, w2_ref, dw1_ref, dw2t_ref, dg2_ref
    )
    dmid_ref[0] = d_middle
    branch = d_middle.astype(BF16)
    dwot_ref[...] += dg(branch, mixed_ref[0], NT)
    d_mixed = dg(wo_ref[...], branch, NN)
    logits, minuses = [], []
    for head in range(heads):
        at = slice(head * size, (head + 1) * size)
        d_att, minus, d_logit = head_backward(
            d_mixed[at], att_ref[0, at], gate_ref[0, head : head + 1], linv_ref[0, head : head + 1]
        )
        datt_ref[0, at] = d_att
        minuses.append(minus)
        logits.append(d_logit)
    minus_ref[0] = jnp.concatenate(minuses, axis=0)
    dlogit_ref[0] = jnp.concatenate(logits, axis=0)

    @pl.when(step == last)
    def finish():
        for sums, ref in zip(sums_refs, (dw2t_ref, dw1_ref, dwot_ref)):
            lay_halves(sums, 0, ref)
        dg2_out[...] = dg2_ref[...]
        for i, (total, halves, held, recv) in list(enumerate(work))[early:]:
            total.end_half(2, held, recv[1])
            part_copy(i).start()
        for i, (total, halves, held, recv) in list(enumerate(work))[:early]:
            total.end_z(eighth(i), z_recvs[i])
            part_copy(i).start()
        for i in range(len(work)):
            part_copy(i).wait()


def narrow_tile(parts, rows):
    used = sum(part.shape[1] for part in parts)
    return jnp.concatenate(list(parts) + [jnp.zeros((rows, 128 - used), F32)], axis=1)


def lay_halves(target, at, ref):
    rows, width = ref.shape
    for half in range(2):
        target[half, :, at : at + width] = ref[half * rows // 2 : (half + 1) * rows // 2].astype(BF16)


XY, YX = ("x", "y"), ("y", "x")
BAND_ORDERS = (YX, XY, YX, XY)
BAND_EARLY = 2
FFN_ORDERS = (YX, XY, YX)
PAIR_ORDERS = (YX, YX, YX, None)


def time_ffn_backward(grad, act, slope, nf, mid, mixed, att, gate, linv, g2, w1, w2, wo, halves_in):
    slots, model, frames = mid.shape
    heads = gate.shape[1]
    inner, hidden = wo.shape[0], w1.shape[1]
    chunks, parts, _, _ = grad.shape
    tokens = frames // 2

    def cut(rows):
        return pl.BlockSpec((1, rows, tokens), lambda s, c: (s, 0, c))

    def whole(*shape):
        return pl.BlockSpec(shape, lambda s, c: (0,) * len(shape))

    consts = (g2, w1, w2, wo)
    anywhere = pl.BlockSpec(memory_space=pl.ANY)
    halves = [(2, model // 2, width) for width in (hidden, hidden, inner)]
    widths = [a.shape[1] for a in halves_in]
    dma = pltpu.SemaphoreType.DMA
    return pl.pallas_call(
        lambda *refs: time_ffn_backward_kernel(heads, *refs),
        grid=(slots, frames // tokens),
        out_shape=(
            jax.ShapeDtypeStruct((slots, model, frames), F32),
            jax.ShapeDtypeStruct((slots, inner, frames), BF16),
            jax.ShapeDtypeStruct((slots, heads, frames), F32),
            jax.ShapeDtypeStruct((slots, heads, frames), F32),
            [jax.ShapeDtypeStruct(shape, BF16) for shape in halves],
            jax.ShapeDtypeStruct((model, 1), F32),
            [jax.ShapeDtypeStruct((model // 8, width), BF16) for width in widths],
        ),
        in_specs=[pl.BlockSpec((chunks // 2,) + grad.shape[1:], lambda s, c: (c, 0, 0, 0))]
        + [cut(a.shape[1]) for a in (act, slope, nf, mid, mixed, att, gate, linv)]
        + [whole_spec(c) for c in consts]
        + [[anywhere for _ in widths]],
        out_specs=(
            cut(model),
            cut(inner),
            cut(heads),
            cut(heads),
            [whole(*shape) for shape in halves],
            whole(model, 1),
            [anywhere for _ in widths],
        ),
        scratch_shapes=[
            pltpu.VMEM((model, hidden), F32),
            pltpu.VMEM((model, hidden), F32),
            pltpu.VMEM((model, inner), F32),
            pltpu.VMEM((model, 1), F32),
            [pltpu.VMEM((model // 2, width), BF16) for width in widths],
            [
                [pltpu.VMEM((rows, width), BF16) for rows in (model // 4, model // 8)]
                for width in widths
            ],
            [pltpu.VMEM((Z_COUNT - 1, model // 8, width // Z_COUNT), BF16) for width in widths[:BAND_EARLY]],
            dma((len(widths), TOTAL_STEPS)),
            dma((len(widths), TOTAL_STEPS)),
            dma((2 * len(widths),)),
        ],
        compiler_params=pltpu.CompilerParams(
            vmem_limit_bytes=VMEM_BYTES, collective_id=2, has_side_effects=True
        ),
        cost_estimate=cost(8.0e6 * slots * frames, 0, 30e6),
        name="time_ffn_backward",
    )(grad, act, slope, nf, mid, mixed, att, gate, linv, *consts, list(halves_in))


BAND_PLACES = ((0, 4, 7, 11, 13), (0, 4, 7, 12, 14), (0, 4, 7, 11, 16, 18), (0, 5, 8, 12, 16, 18))
FFN_PLACES = ((0, 1, 5, 8, 12, 15, 18, 24, 25), (0, 2, 6, 10, 13, 16, 20, 24, 25), (0, 2, 6, 9, 12, 15, 18, 22, 24))
PAIR_PLACES = (
    (4, 5, 8, 12, 15, 18, 22, 24, 25),
    (8, 9, 12, 15, 17, 20, 23, 24, 25),
    (12, 13, 15, 18, 21, 24, 25, 26, 27),
    (16, 17, 21, 24, 25),
)


def time_attention_backward_kernel(
    heads,
    slots,
    batch_count,
    p_ref,
    q_ref,
    k_ref,
    v_ref,
    datt_ref,
    minus_ref,
    x_ref,
    dmid_ref,
    logit_block_ref,
    n_ref,
    dlogit_ref,
    cos_ref,
    sin_ref,
    g1_ref,
    wp_ref,
    wgt_ref,
    narrow_ref,
    dg2_ref,
    part_refs,
    ffn_refs,
    grad_out,
    band_outs,
    ffn_outs,
    pair_outs,
    dproj_ref,
    wp_turned_ref,
    grad_buf,
    piece_refs,
    band_recvs,
    held_refs,
    ffn_recvs,
    pair_refs,
    pair_recvs,
    around_recv,
    band_sems,
    ffn_sems,
    pair_sems,
    grad_sems,
    local_sem,
):
    place = Place()
    step = pl.program_id(0)
    steps = heads * slots
    head, slot = step // slots, lax.rem(step, slots)
    size, frames = q_ref.shape[1:]
    model = n_ref.shape[1]
    inner = heads * size
    pairs = heads // 2
    pair_rows = 6 * size
    blocks = frames // BLOCK
    last = pl.num_programs(0) - 1
    my_band, my_batch = place.band, place.batch

    bands = [Total(place, order, band_sems[0].at[i], band_sems[1].at[i]) for i, order in enumerate(BAND_ORDERS)]
    ffns = [Total(place, order, ffn_sems[0].at[i], ffn_sems[1].at[i]) for i, order in enumerate(FFN_ORDERS)]
    own = [
        Total(place, PAIR_ORDERS[i], pair_sems[0].at[i], pair_sems[1].at[i]) for i in range(pairs)
    ]

    def half_copy(i):
        return pltpu.make_async_copy(ffn_refs[i].at[place.bits["core"]], held_refs[i], local_sem.at[len(bands) + i])

    def eighth(total, held):
        return held.at[total.half_rows(held, 2)[0]]

    def all_steps(total, source, held, recvs, out, sem):
        width = recvs[3].shape[2]

        def back_region():
            return out.at[total.back_rows(out, 2)]

        def s0():
            total.start_core(source, recvs[0])

        def s1():
            total.end_core(held, recvs[0])
            total.start_half(1, held, recvs[1])

        def s2():
            total.end_half(1, held, recvs[1])
            total.start_half(2, held, recvs[2])

        def s3():
            total.end_half(2, held, recvs[2])
            total.start_z(eighth(total, held), recvs[3])

        def s4():
            total.end_z(eighth(total, held), recvs[3])
            total.start_z_back(eighth(total, held), back_region(), width, sem)

        def s5():
            total.end_z_back(eighth(total, held), back_region(), width, sem)
            total.start_back(2, out)

        def s6():
            total.end_back(2, out)
            total.start_back(1, out)

        def s7():
            total.end_back(1, out)
            total.start_back(0, out)

        def s8():
            total.end_back(0, out)

        return [s0, s1, s2, s3, s4, s5, s6, s7, s8]

    plan = {}

    def at_step(index, action):
        plan.setdefault(index, []).append(action)

    def enter():
        other_x = place.across("x")[1] // 2
        diagonal = (my_band, 2 * other_x + 1 - place.bits["core"])
        chips = [other for _, _, other in own[-1].around()]
        greet(chips + [place.across("core"), diagonal])
        for i in range(len(ffns)):
            half_copy(i).start()

    tail = steps + slots * blocks
    at_step(0, enter)

    def schedule(actions, places):
        for at, action in zip(places, actions):
            at_step(at, action)

    for i in range(len(bands)):
        out = band_outs[i]
        region = out.at[bands[i].back_rows(out, 2)]
        quarter = band_outs[i].shape[1] // Z_COUNT

        def z_begin(i=i):
            piece_refs[i][...] = part_refs[i][...]
            if i >= BAND_EARLY:
                bands[i].start_z(piece_refs[i], band_recvs[i - BAND_EARLY])

        def z_turn(i=i, region=region, quarter=quarter):
            if i >= BAND_EARLY:
                bands[i].end_z(piece_refs[i], band_recvs[i - BAND_EARLY])
            bands[i].start_z_back(piece_refs[i], region, quarter, local_sem.at[i])

        def z_end(i=i, region=region, quarter=quarter, out=out):
            bands[i].end_z_back(piece_refs[i], region, quarter, local_sem.at[i])
            bands[i].start_back(2, out)

        def back_two(i=i, out=out):
            bands[i].end_back(2, out)
            bands[i].start_back(1, out)

        def back_one(i=i, out=out):
            bands[i].end_back(1, out)
            bands[i].start_back(0, out)

        actions = [z_begin, z_turn, z_end, back_two, back_one, lambda i=i, out=out: bands[i].end_back(0, out)]
        if i < BAND_EARLY:
            at_step(0, z_begin)
            actions = actions[1:]
        schedule(actions, BAND_PLACES[i])
    ffn_at = len(bands) + len(ffns)
    for i in range(len(ffns)):
        sem = local_sem.at[ffn_at + i]
        actions = all_steps(ffns[i], ffn_refs[i], held_refs[i], ffn_recvs[i], ffn_outs[i], sem)
        at_step(FFN_PLACES[i][1], lambda i=i: half_copy(i).wait())
        schedule(actions, FFN_PLACES[i])
    pair_at = ffn_at + len(ffns)

    def around_steps(total, source, held, recv, out, sem):
        def s0():
            total.start_core(source, recv[0])

        def s1():
            total.end_core(held, recv[0])
            total.start_around(held, recv[1])

        def s2():
            total.end_around(held, recv[1])
            total.start_around_back(held, recv[1], out, sem)

        def s3():
            total.end_around_back(held, recv[1], out, sem)
            total.start_back(0, out)

        def s4():
            total.end_back(0, out)

        return [s0, s1, s2, s3, s4]

    for i in range(pairs):
        source, held = pair_refs.at[i], pair_refs.at[i, place.bits["core"]]
        out, sem = pair_outs.at[i], local_sem.at[pair_at + i]
        recv = [ref.at[i] for ref in pair_recvs]
        if PAIR_ORDERS[i] is None:
            actions = around_steps(own[i], source, held, [recv[0], around_recv], out, sem)
        else:
            actions = all_steps(own[i], source, held, recv, out, sem)
        schedule(actions, PAIR_PLACES[i])

    for index in sorted(plan):
        if index < tail:

            @pl.when(step == index)
            def work(index=index):
                for action in plan[index]:
                    action()

    @pl.when(step < steps)
    def attention():
        d_queries, d_keys, d_values = scores_backward(
            q_ref[0],
            k_ref[0],
            v_ref[0],
            p_ref[0, 0],
            datt_ref[0],
            minus_ref[0, pl.ds(head, 1), :],
            cos_ref[...],
            sin_ref[...],
            size**-0.5,
        )
        start = pl.multiple_of((head // 2) * pair_rows + lax.rem(head, 2) * size, size)
        dproj_ref[slot, pl.ds(start, size), :] = d_queries.astype(BF16)
        dproj_ref[slot, pl.ds(start + 2 * size, size), :] = d_keys.astype(BF16)
        dproj_ref[slot, pl.ds(start + 4 * size, size), :] = d_values.astype(BF16)

    @pl.when((step < steps) & (lax.rem(step, 2 * slots) == 2 * slots - 1))
    def pair_done():
        pair = head // 2
        rows = pl.ds(pl.multiple_of(pair * pair_rows, pair_rows), pair_rows)
        sums = dg(n_ref[0], dproj_ref[0, rows, :], NT)
        for j in range(1, slots):
            sums = sums + dg(n_ref[j], dproj_ref[j, rows, :], NT)
        for half in range(2):
            at = slice(half * model // 2, (half + 1) * model // 2)
            pair_refs[pair, half, :, 0:pair_rows] = sums[at].astype(BF16)

    @pl.when(step == 2 * slots - 1)
    def narrow_done():
        gates = 0.0
        for j in range(slots):
            logit = jnp.concatenate([dlogit_ref[j], jnp.zeros_like(dlogit_ref[j])], axis=0).astype(BF16)
            gates = gates + dg(n_ref[j], logit, NT)[:, :heads]
        tile = narrow_tile([narrow_ref[:, : heads + 2], gates, dg2_ref[...]], model)
        for half in range(2):
            at = slice(half * model // 2, (half + 1) * model // 2)
            pair_refs[0, half, :, pair_rows:] = tile[at].astype(BF16)
            for i in range(1, pairs):
                pair_refs[i, half, :, pair_rows:] = jnp.zeros_like(tile[at]).astype(BF16)
        for pair in range(pairs):
            for part in range(3):
                to = pair * pair_rows + part * 2 * size
                source = part * inner + pair * 2 * size
                wp_turned_ref[:, to : to + 2 * size] = wp_ref[:, source : source + 2 * size]

    def message(index):
        j, i = index // blocks, lax.rem(index, blocks)
        source = grad_buf.at[index]
        target = grad_out.at[batch_count * j + my_batch]
        return i, source, target

    @pl.when(step >= steps)
    def rows_done():
        index = step - steps
        j, i = index // blocks, lax.rem(index, blocks)
        at = pl.ds(pl.multiple_of(i * BLOCK, BLOCK), BLOCK)
        logit = logit_block_ref[0].astype(BF16)
        d_normed = dg(wp_turned_ref[...], dproj_ref[j, :, at], NN) + dg(wgt_ref[...], logit, TN)
        d_rows, _ = norm_backward(x_ref[0].astype(F32).T, column(g1_ref), d_normed)
        grad_buf[index] = (dmid_ref[0] + d_rows).T.astype(BF16)
        i, source, target = message(index)

        @pl.when(i == my_batch)
        def keep():
            pltpu.make_async_copy(source, target, local_sem.at[pair_at + pairs]).start()

        @pl.when(i != my_batch)
        def give():
            send(source, target, grad_sems.at[0], grad_sems.at[1], my_band, i)

    @pl.when(step == last)
    def finish():
        for index in sorted(plan):
            if index >= tail:
                for action in plan[index]:
                    action()
        await_bytes(grad_buf.at[pl.ds(0, slots)], local_sem.at[pair_at + pairs])
        others = grad_buf.at[pl.ds(0, slots * (batch_count - 1))]
        await_bytes(others, grad_sems.at[0])
        await_bytes(others, grad_sems.at[1])


def time_attention_backward(
    p, q, k, v, datt, minus, dlogit, n, x, dmid, cos, sin, g1, wp, wgt, narrow, dg2, parts, ffn_sums, batch_count
):
    slots, inner, frames = q.shape
    heads = minus.shape[1]
    size = inner // heads
    model = n.shape[1]
    pairs = heads // 2
    steps = heads * slots
    blocks = frames // BLOCK

    def clamp(t):
        return jnp.minimum(t, steps - 1)

    def tail(t):
        return jnp.maximum(t - steps, 0)

    def per_head(rows, columns):
        return pl.BlockSpec((1, rows, columns), lambda t: (lax.rem(clamp(t), slots), clamp(t) // slots, 0))

    consts = (n, dlogit, cos, sin, g1, wp, wgt, narrow, dg2)
    anywhere = pl.BlockSpec(memory_space=pl.ANY)
    dma = pltpu.SemaphoreType.DMA
    widths = [a.shape[2] for a in ffn_sums]
    pair_width = 8 * size

    def recv_buffers(width, *lead):
        rows = model // 2
        shapes = [(rows, width), (rows // 2, width), (rows // 4, width), (Z_COUNT - 1, rows // 4, width // Z_COUNT)]
        return [pltpu.VMEM(lead + shape, BF16) for shape in shapes]

    return pl.pallas_call(
        lambda *refs: time_attention_backward_kernel(heads, slots, batch_count, *refs),
        grid=(steps + slots * blocks,),
        out_shape=(
            jax.ShapeDtypeStruct((batch_count * slots, BLOCK, model), BF16),
            [jax.ShapeDtypeStruct((model, a.shape[1]), BF16) for a in parts],
            [jax.ShapeDtypeStruct((model, width), BF16) for width in widths],
            jax.ShapeDtypeStruct((pairs, model, pair_width), BF16),
        ),
        in_specs=[
            pl.BlockSpec((1, 1, frames, frames), lambda t: (lax.rem(clamp(t), slots), clamp(t) // slots, 0, 0)),
            per_head(size, frames),
            per_head(size, frames),
            per_head(size, frames),
            per_head(size, frames),
            pl.BlockSpec((1, heads, frames), lambda t: (lax.rem(clamp(t), slots), 0, 0)),
            pl.BlockSpec((1, BLOCK, model), lambda t: (tail(t) // blocks, lax.rem(tail(t), blocks), 0)),
            pl.BlockSpec((1, model, BLOCK), lambda t: (tail(t) // blocks, 0, lax.rem(tail(t), blocks))),
            pl.BlockSpec((1, heads, BLOCK), lambda t: (tail(t) // blocks, 0, lax.rem(tail(t), blocks))),
        ]
        + [whole_spec(c) for c in consts]
        + [[whole_spec(a) for a in parts], [anywhere] * len(ffn_sums)],
        out_specs=(anywhere, [anywhere] * len(parts), [anywhere] * len(ffn_sums), anywhere),
        scratch_shapes=[
            pltpu.VMEM((slots, 3 * inner, frames), BF16),
            pltpu.VMEM((model, 3 * inner), BF16),
            pltpu.VMEM((slots * blocks, BLOCK, model), BF16),
            [pltpu.VMEM(a.shape, BF16) for a in parts],
            [pltpu.VMEM((Z_COUNT - 1, a.shape[0], a.shape[1] // Z_COUNT), BF16) for a in parts[BAND_EARLY:]],
            [pltpu.VMEM((model // 2, width), BF16) for width in widths],
            [recv_buffers(width) for width in widths],
            pltpu.VMEM((pairs, 2, model // 2, pair_width), BF16),
            recv_buffers(pair_width, pairs),
            pltpu.VMEM((4 * Z_COUNT - 1, model // 8, pair_width // Z_COUNT), BF16),
            [dma((len(parts), TOTAL_STEPS))] * 2,
            [dma((len(widths), TOTAL_STEPS))] * 2,
            [dma((pairs, TOTAL_STEPS)), dma((pairs, TOTAL_STEPS))],
            dma((2,)),
            dma((len(parts) + 2 * len(widths) + pairs + 1,)),
        ],
        compiler_params=pltpu.CompilerParams(
            vmem_limit_bytes=VMEM_BYTES, collective_id=3, has_side_effects=True
        ),
        cost_estimate=cost(20.0e6 * slots * frames, 0, 60e6),
        name="time_attention_backward",
    )(p, q, k, v, datt, minus, x, dmid, dlogit, *consts, list(parts), list(ffn_sums))


def finish_kernel(
    heads,
    grad_ref,
    bwp_ref,
    bw1_ref,
    bw2t_ref,
    bwot_ref,
    w1_ref,
    wot_ref,
    w2t_ref,
    pair_ref,
    first_pair_ref,
    wp_ref,
    wgt_ref,
    g1_ref,
    y_ref,
    y_out,
    grad_out,
    dg1_out,
    dwp_out,
    dwg_out,
    dwo_out,
    dg2_out,
    dw1_out,
    dw2_out,
    bg1_out,
    bwp_out,
    bwg_out,
    bwo_out,
    bg2_out,
    bw1_out,
    bw2_out,
    scaled_ref,
):
    pair = pl.program_id(0)
    inner = wp_ref.shape[1] // 3
    width = inner // pl.num_programs(0)
    pairs, bands, parts, rows, model = y_ref.shape
    split = y_ref[...].astype(F32).reshape(pairs, bands, parts, 2, rows // 2, model)
    for j in range(2):
        values = split[:, :, :, j].reshape(pairs, bands * parts * rows // 2, model)
        for i in range(pairs):
            y_out[2 * i + j] = values[i].astype(BF16)
    grad_out[...] = grad_ref[...].astype(F32)
    bwp_out[...] = bwp_ref[...].astype(F32)
    bw1_out[...] = bw1_ref[...].astype(F32)
    bw2_out[...] = bw2t_ref[...].astype(F32).T
    bwo_out[...] = bwot_ref[...].astype(F32).T
    dw1_out[...] = w1_ref[...].astype(F32)
    dw2_out[...] = w2t_ref[...].astype(F32).T
    dwo_out[...] = wot_ref[...].astype(F32).T

    @pl.when(pair == 0)
    def clear():
        scaled_ref[...] = jnp.zeros_like(scaled_ref)

    for part in range(3):
        at = pl.ds(pl.multiple_of(part * inner + pair * width, 128), width)
        values = pair_ref[0, :, part * width : (part + 1) * width].astype(F32)
        dwp_out[:, at] = values
        scaled_ref[...] += values * wp_ref[:, at].astype(F32)

    @pl.when(pair == pl.num_programs(0) - 1)
    def narrow():
        tile = first_pair_ref[0, :, 3 * width :].astype(F32)
        rows = tile.T
        bwg_out[...] = rows[:heads]
        bg1_out[...] = rows[heads]
        bg2_out[...] = rows[heads + 1]
        gates = tile[:, heads + 2 : 2 * heads + 2]
        dwg_out[...] = rows[heads + 2 : 2 * heads + 2]
        dg2_out[...] = rows[2 * heads + 2]
        sums = jnp.sum(scaled_ref[...], axis=1, keepdims=True)
        sums = sums + jnp.sum(gates * wgt_ref[...].astype(F32).T, axis=1, keepdims=True)
        dg1_out[...] = jnp.broadcast_to(sums, (sums.shape[0], 128)).T[0] / g1_ref[...].astype(F32)


def finish_sums(grads, y, band_sums, ffn_sums, pair_sums, g1, params):
    wp, wgt, wo, w1, w2 = params
    model, hidden = w1.shape
    inner, heads = wo.shape[0], wgt.shape[0]
    pairs = pair_sums.shape[0]
    split = hidden // pairs
    out_split = inner // pairs
    slot_dev, frame_dev, _ = grads.shape

    def lanes(width):
        return pl.BlockSpec((model, width), lambda i: (0, i))

    def whole(*shape):
        return pl.BlockSpec(shape, lambda i: (0,) * len(shape))

    def cut_rows(rows):
        return pl.BlockSpec((rows, model), lambda i: (i, 0))

    band_wp, band_w1, band_w2t, band_wot = band_sums
    time_w2t, time_w1, time_wot = ffn_sums
    grad_block = pl.BlockSpec((slot_dev // pairs, frame_dev, model), lambda i: (i, 0, 0))
    narrow = [((model,), whole(model)), ((heads, model), whole(heads, model))]
    per_layer = [
        narrow[0],
        ((model, 3 * inner), None),
        narrow[1],
        ((inner, model), cut_rows(out_split)),
        narrow[0],
        ((model, hidden), lanes(split)),
        ((hidden, model), cut_rows(split)),
    ]
    shapes, specs = [jax.ShapeDtypeStruct(grads.shape, BF16), jax.ShapeDtypeStruct(grads.shape, F32)], [grad_block] * 2
    y_block = pl.BlockSpec((y.shape[0] // pairs,) + y.shape[1:], lambda i: (i, 0, 0, 0, 0))
    for layer in range(2):
        for shape, spec in per_layer:
            shapes.append(jax.ShapeDtypeStruct(shape, F32))
            if spec is None:
                spec = whole(*shape) if layer == 0 else lanes(3 * inner // pairs)
            specs.append(spec)
    return pl.pallas_call(
        lambda *refs: finish_kernel(heads, *refs),
        grid=(pairs,),
        out_shape=shapes,
        in_specs=[
            grad_block,
            lanes(3 * inner // pairs),
            lanes(split),
            lanes(split),
            lanes(out_split),
            lanes(split),
            lanes(out_split),
            lanes(split),
            pl.BlockSpec((1, model, pair_sums.shape[2]), lambda i: (i, 0, 0)),
            pl.BlockSpec((1, model, pair_sums.shape[2]), lambda i: (0, 0, 0)),
            whole_spec(wp),
            whole_spec(wgt),
            whole_spec(g1),
            y_block,
        ],
        out_specs=specs,
        scratch_shapes=[pltpu.VMEM((model, inner // pairs), F32)],
        compiler_params=pltpu.CompilerParams(vmem_limit_bytes=VMEM_BYTES),
        name="finish_sums",
    )(
        grads,
        band_wp,
        band_w1,
        band_w2t,
        band_wot,
        time_w1,
        time_wot,
        time_w2t,
        pair_sums,
        pair_sums,
        wp,
        wgt,
        g1,
        y,
    )


def band_kernel(
    heads,
    batch_count,
    band_count,
    x_ref,
    cot_ref,
    count_ref,
    slots_ref,
    g1_ref,
    g2_ref,
    wgt_ref,
    wpt_ref,
    wot_ref,
    w1t_ref,
    w2t_ref,
    wp_ref,
    wo_ref,
    w1_ref,
    w2_ref,
    y_out,
    dx_out,
    half_outs,
    narrow_out,
    q_ref,
    k_ref,
    v_ref,
    p_ref,
    gate_ref,
    linv_ref,
    att_ref,
    mixed_ref,
    act_ref,
    slope_ref,
    datt_ref,
    dmixed_ref,
    dlogit_ref,
    dproj_ref,
    dwp_ref,
    dw1_ref,
    dw2t_ref,
    dwot_ref,
    dwg_ref,
    dg1_ref,
    dg2_ref,
    xs_ref,
    cots_ref,
    ys_ref,
    dxs_ref,
    y_buf,
    dx_buf,
    y_send,
    y_recv,
    dx_send,
    dx_recv,
    local_sem,
    bias_ref,
    cos_ref,
    sin_ref,
    valid_ref,
    halves,
    core_recvs,
    core_sems,
    half_sem,
):
    step = pl.program_id(0)
    slot_count, part_frames, model = x_ref.shape
    inner, tokens = q_ref.shape
    size = inner // heads
    groups = tokens // BLOCK
    taken = tokens // slot_count
    per_part = part_frames // taken
    part = step // per_part
    first = lax.rem(step, per_part) * taken
    my_band, my_batch = lax.axis_index("band"), lax.axis_index("batch")
    slot_dev = slot_count // band_count
    slots = slot_dev // batch_count
    own_chunk = my_batch * band_count + my_band
    chunks = band_count * batch_count

    columns = [slice(at, at + 128) for at in range(0, model, 128)]

    def tokens_of(ref):
        return jnp.concatenate(
            [
                jnp.concatenate(
                    [ref[c, pl.ds(first + i, slot_count, stride=part_frames), :] for i in range(taken)], axis=0
                ).T
                for c in range(len(columns))
            ],
            axis=0,
        )

    def put_tokens(ref, values, start, stride):
        for c, at in enumerate(columns):
            turned = values[at].T
            for i in range(taken):
                ref[c, pl.ds(start + i, slot_count, stride=stride), :] = turned[
                    i * slot_count : (i + 1) * slot_count
                ]

    @pl.when(step == 0)
    def enter():
        greet_all(band_count, batch_count)
        bands = slots_ref[...].reshape(1, slot_count)
        cos, sin = rotary_rows(jnp.maximum(bands, 0).astype(F32), size // 2)
        cos_ref[...] = jnp.concatenate([cos] * taken, axis=1)
        sin_ref[...] = jnp.concatenate([sin] * taken, axis=1)
        valid = jnp.concatenate([jnp.where(bands >= 0, 1.0, 0.0)] * taken, axis=1)
        valid_ref[...] = valid
        keys = jnp.broadcast_to(valid[:, :BLOCK], (8, BLOCK)).T[:, :1]
        row = lax.broadcasted_iota(jnp.int32, (BLOCK, BLOCK), 0) // slot_count
        column_index = lax.broadcasted_iota(jnp.int32, (BLOCK, BLOCK), 1) // slot_count
        bias_ref[...] = jnp.where((row == column_index) & (keys > 0.5), 0.0, NEG_FILL)

    @pl.when(lax.rem(step, per_part) == 0)
    def unpack():
        for c, at in enumerate(columns):
            xs_ref[c] = x_ref[:, :, at].astype(F32).reshape(xs_ref.shape[1:])
            cots_ref[c] = cot_ref[:, :, at].astype(F32).reshape(cots_ref.shape[1:])

    place = Place()
    totals = [
        Total(place, order, core_sems.at[0, i], core_sems.at[1, i]) for i, order in enumerate(BAND_ORDERS)
    ]
    gain1, gain2 = column(g1_ref), column(g2_ref)
    piece = part_frames * (pl.num_programs(0) // per_part)
    own_start = (my_batch * band_count + my_band) * piece

    @pl.when(step == 0)
    def clear():
        for ref in (dwp_ref, dw1_ref, dw2t_ref, dwot_ref, dwg_ref, dg1_ref, dg2_ref):
            ref[...] = jnp.zeros_like(ref)

    rows = tokens_of(xs_ref)
    normed = norm_forward(rows, gain1)
    q_ref[...], k_ref[...], v_ref[...] = project_block(
        normed, wpt_ref, cos_ref[...], sin_ref[...], inner, LOG2E * size**-0.5
    )
    gate_ref[...] = dg(wgt_ref[...], normed, NN)
    ones = extra_rows([jnp.ones((1, BLOCK), F32)], BLOCK)

    def attend(head, carry):
        at = pl.ds(pl.multiple_of(head * size, size), size)
        row = pl.ds(head, 1)
        for group in range(groups):
            lanes = slice(group * BLOCK, (group + 1) * BLOCK)
            scores = dg(k_ref[at, lanes], q_ref[at, lanes], TN) + bias_ref[...]
            weights = jnp.exp2(scores - jnp.max(scores, axis=0, keepdims=True)).astype(BF16)
            p_ref[head * groups + group] = weights
            sums = dg(jnp.concatenate([v_ref[at, lanes], ones], axis=0), weights, NN)
            inverse = 1.0 / sums[size : size + 1]
            attended = sums[:size] * inverse
            linv_ref[row, lanes] = inverse
            att_ref[at, lanes] = attended
            gate = jax.nn.sigmoid(gate_ref[row, lanes])
            mixed_ref[at, lanes] = (attended * gate).astype(BF16)
        return carry

    lax.fori_loop(0, heads, attend, 0)
    middle = rows + dg(wot_ref[...], mixed_ref[...], NN)
    normed_ffn = norm_forward(middle, gain2)

    hidden = w1t_ref.shape[0]
    quarter = hidden // 4

    def expand(i, carry):
        at = pl.ds(pl.multiple_of(i * quarter, quarter), quarter)
        active, slope = gelu_pair(dg(w1t_ref[at, :], normed_ffn, NN))
        act_ref[at, :] = active.astype(BF16)
        slope_ref[at, :] = slope.astype(BF16)
        return carry

    lax.fori_loop(0, 4, expand, 0)
    frame = own_start + step * taken + lax.broadcasted_iota(jnp.int32, (1, tokens), 1) // slot_count
    mask = jnp.where(frame < count_ref[0], valid_ref[...], 0.0)
    result = (middle + dg(w2t_ref[...], act_ref[...], NN)) * mask
    put_tokens(ys_ref, result, 0, taken)

    couples = slot_dev // 2
    for c, at in enumerate(columns):
        y_buf[step, :, :, at] = ys_ref[c].reshape(slot_count // 2, 2 * taken, 128).astype(BF16)

    def give_row(i, carry):
        other = lax.rem(my_band + i, band_count)
        send(
            y_buf.at[step, pl.ds(other * couples, couples)],
            y_out.at[:, my_band, step],
            y_send,
            y_recv,
            other,
            my_batch,
        )
        return carry

    lax.fori_loop(1, band_count, give_row, 0)
    pltpu.make_async_copy(
        y_buf.at[step, pl.ds(my_band * couples, couples)], y_out.at[:, my_band, step], local_sem.at[0]
    ).start()

    grad = tokens_of(cots_ref) * mask
    d_middle = ffn_backward(
        grad, act_ref[...], slope_ref[...], normed_ffn, middle, gain2, w1_ref, w2_ref, dw1_ref, dw2t_ref, dg2_ref
    )
    branch = d_middle.astype(BF16)
    dwot_ref[...] += dg(branch, mixed_ref[...], NT)
    dmixed_ref[...] = dg(wo_ref[...], branch, NN)

    def attend_back(head, carry):
        start = pl.multiple_of(head * size, size)
        at = pl.ds(start, size)
        row = pl.ds(head, 1)
        d_att, minus, d_logit = head_backward(dmixed_ref[at, :], att_ref[at, :], gate_ref[row, :], linv_ref[row, :])
        dlogit_ref[row, :] = d_logit
        for group in range(groups):
            lanes = slice(group * BLOCK, (group + 1) * BLOCK)
            d_queries, d_keys, d_values = scores_backward(
                q_ref[at, lanes],
                k_ref[at, lanes],
                v_ref[at, lanes],
                p_ref[head * groups + group],
                d_att[:, lanes],
                minus[:, lanes],
                cos_ref[:, lanes],
                sin_ref[:, lanes],
                size**-0.5,
            )
            dproj_ref[at, lanes] = d_queries.astype(BF16)
            dproj_ref[pl.ds(inner + start, size), lanes] = d_keys.astype(BF16)
            dproj_ref[pl.ds(2 * inner + start, size), lanes] = d_values.astype(BF16)
        return carry

    lax.fori_loop(0, heads, attend_back, 0)
    d_logit = jnp.concatenate([dlogit_ref[...], jnp.zeros_like(dlogit_ref)], axis=0).astype(BF16)
    dwp_ref[...] += dg(normed, dproj_ref[...], NT)
    dwg_ref[...] += dg(normed, d_logit, NT)[:, :heads]
    d_normed = dg(wp_ref[...], dproj_ref[...], NN) + dg(wgt_ref[...], dlogit_ref[...].astype(BF16), TN)
    d_rows, terms = norm_backward(rows, gain1, d_normed)
    dg1_ref[...] += jnp.sum(terms, axis=1, keepdims=True)
    put_tokens(dxs_ref, d_middle + d_rows, 0, taken)
    for c, at in enumerate(columns):
        grouped = dxs_ref[c].reshape(band_count, slots, batch_count, taken, 128)
        grouped = jnp.concatenate([grouped[:, j][:, :, None] for j in range(slots)], axis=2)
        dx_buf[step, :, :, at] = grouped.reshape(chunks, slots * taken, 128).astype(BF16)

    def give_grad(i, carry):
        other = lax.rem(my_band * batch_count + my_batch + i, chunks)
        send(
            dx_buf.at[step, other],
            dx_out.at[own_chunk, step],
            dx_send,
            dx_recv,
            other // batch_count,
            lax.rem(other, batch_count),
        )
        return carry

    lax.fori_loop(1, chunks, give_grad, 0)
    pltpu.make_async_copy(
        dx_buf.at[step, my_band * batch_count + my_batch], dx_out.at[own_chunk, step], local_sem.at[1]
    ).start()

    @pl.when(step == pl.num_programs(0) - 1)
    def finish():
        narrow_out[...] = narrow_tile([dwg_ref[...], dg1_ref[...], dg2_ref[...]], model)
        core = place.bits["core"]
        for i, ref in enumerate((dwp_ref, dw1_ref, dw2t_ref, dwot_ref)):
            lay_halves(halves[i], 0, ref)
            totals[i].start_core(halves[i], core_recvs[i])
        for i, total in enumerate(totals):
            total.end_core(halves[i].at[core], core_recvs[i])
            pltpu.make_async_copy(halves[i].at[core], half_outs[i], half_sem.at[i]).start()
        for i in range(len(totals)):
            pltpu.make_async_copy(halves[i].at[core], half_outs[i], half_sem.at[i]).wait()
        await_bytes(y_out.at[:, 0], local_sem.at[0])
        await_bytes(dx_out.at[0], local_sem.at[1])
        for sem in (y_send, y_recv):
            await_bytes(y_out.at[:, pl.ds(0, band_count - 1)], sem)
        for sem in (dx_send, dx_recv):
            await_bytes(dx_out.at[pl.ds(0, chunks - 1)], sem)


def band_layer(rows, cot, counts, slot_bands, g1, g2, params, flips, band_count, batch_count):
    project, gating, output_weight, expand, shrink = params
    slot_count, piece, model = rows.shape
    tokens = 2 * BLOCK
    steps = slot_count * piece // tokens
    heads, inner, hidden = gating.shape[0], output_weight.shape[0], expand.shape[1]
    groups = tokens // BLOCK
    taken = tokens // slot_count
    part_frames = 16
    per_part = part_frames // taken
    slots = slot_count // (band_count * batch_count)
    slot_dev = slot_count // band_count
    consts = (slot_bands, g1, g2, gating) + flips + (project, output_weight, expand, shrink)
    widths = (3 * inner, hidden, hidden, inner)
    chunks = band_count * batch_count
    blocks = pl.BlockSpec((slot_count, part_frames, model), lambda i: (0, i // per_part, 0))
    anywhere = pl.BlockSpec(memory_space=pl.ANY)
    dma = pltpu.SemaphoreType.DMA
    return pl.pallas_call(
        lambda *refs: band_kernel(heads, batch_count, band_count, *refs),
        grid=(steps,),
        out_shape=(
            jax.ShapeDtypeStruct((slot_dev // 2, band_count, steps, 2 * taken, model), BF16),
            jax.ShapeDtypeStruct((chunks, steps, slots * taken, model), BF16),
            [jax.ShapeDtypeStruct((model // 2, width), BF16) for width in widths],
            jax.ShapeDtypeStruct((model, 128), F32),
        ),
        in_specs=[blocks, blocks, pl.BlockSpec(memory_space=pltpu.SMEM)] + [whole_spec(c) for c in consts],
        out_specs=(
            anywhere,
            anywhere,
            [anywhere for _ in widths],
            pl.BlockSpec((model, 128), lambda i: (0, 0)),
        ),
        scratch_shapes=[
            pltpu.VMEM((inner, tokens), BF16),
            pltpu.VMEM((inner, tokens), BF16),
            pltpu.VMEM((inner, tokens), BF16),
            pltpu.VMEM((heads * groups, BLOCK, BLOCK), BF16),
            pltpu.VMEM((heads, tokens), F32),
            pltpu.VMEM((heads, tokens), F32),
            pltpu.VMEM((inner, tokens), F32),
            pltpu.VMEM((inner, tokens), BF16),
            pltpu.VMEM((hidden, tokens), BF16),
            pltpu.VMEM((hidden, tokens), BF16),
            pltpu.VMEM((inner, tokens), BF16),
            pltpu.VMEM((inner, tokens), F32),
            pltpu.VMEM((heads, tokens), F32),
            pltpu.VMEM((3 * inner, tokens), BF16),
            pltpu.VMEM((model, 3 * inner), F32),
            pltpu.VMEM((model, hidden), F32),
            pltpu.VMEM((model, hidden), F32),
            pltpu.VMEM((model, inner), F32),
            pltpu.VMEM((model, heads), F32),
            pltpu.VMEM((model, 1), F32),
            pltpu.VMEM((model, 1), F32),
            pltpu.VMEM((model // 128, slot_count * part_frames, 128), F32),
            pltpu.VMEM((model // 128, slot_count * part_frames, 128), F32),
            pltpu.VMEM((model // 128, tokens, 128), F32),
            pltpu.VMEM((model // 128, tokens, 128), F32),
            pltpu.VMEM((steps, slot_count // 2, 2 * taken, model), BF16),
            pltpu.VMEM((steps, chunks, slots * taken, model), BF16),
            dma,
            dma,
            dma,
            dma,
            dma((2,)),
            pltpu.VMEM((BLOCK, BLOCK), F32),
            pltpu.VMEM((inner // heads // 2, tokens), F32),
            pltpu.VMEM((inner // heads // 2, tokens), F32),
            pltpu.VMEM((1, tokens), F32),
            [pltpu.VMEM((2, model // 2, width), BF16) for width in widths],
            [pltpu.VMEM((model // 2, width), BF16) for width in widths],
            dma((2, len(widths), TOTAL_STEPS)),
            dma((len(widths),)),
        ],
        compiler_params=pltpu.CompilerParams(
            vmem_limit_bytes=VMEM_BYTES, collective_id=1, has_side_effects=True
        ),
        cost_estimate=cost(30.0e6 * slot_count * piece, 0, 60e6),
        name="band_layer",
    )(rows, cot, counts, *consts)


def slot_shards(activations, cotangent, frame_counts, slot_bands, *weights):
    slot_dev, _, frame_dev, model = activations.shape
    batch, band = lax.axis_size("batch"), lax.axis_size("band")
    g1, wp, wg, wo, g2, w1, w2 = weights[:7]
    band_g1, band_wp, band_wg, band_wo, band_g2, band_w1, band_w2 = weights[7:]
    heads = wg.shape[1]
    time_params = (wp, wg.T, wo, w1, w2)
    band_params = (band_wp, band_wg.T, band_wo, band_w1, band_w2)
    band_rows, band_cot, rows, n, q, k, v, p, linv, gate, att, mixed, mid, nf, act, slope, *turned = time_forward(
        activations.reshape(slot_dev, frame_dev, model),
        cotangent.reshape(slot_dev, frame_dev, model),
        frame_counts,
        g1,
        g2,
        time_params,
        band_params,
        band,
        batch,
    )
    cos, sin = turned[-2:]
    y, slot_grad, band_halves, band_narrow = band_layer(
        band_rows,
        band_cot,
        frame_counts,
        slot_bands,
        band_g1,
        band_g2,
        band_params,
        tuple(turned[:-2]),
        band,
        batch,
    )
    dmid, datt, minus, dlogit, ffn_halves, dg2, band_parts = time_ffn_backward(
        slot_grad, act, slope, nf, mid, mixed, att, gate, linv, g2, w1, w2, wo, band_halves
    )
    input_grad, band_sums, ffn_sums, pair_sums = time_attention_backward(
        p,
        q,
        k,
        v,
        datt,
        minus,
        dlogit,
        n,
        rows,
        dmid,
        cos,
        sin,
        g1,
        wp,
        time_params[1],
        band_narrow,
        dg2,
        band_parts,
        ffn_halves,
        batch,
    )
    layer_output, input_grad, *grads = finish_sums(
        input_grad, y, band_sums, ffn_sums, pair_sums, g1, time_params
    )
    grads = [g.T if g.shape[0] == heads else g for g in grads]
    return (layer_output.reshape(activations.shape), input_grad.reshape(activations.shape), *grads)


def shards(activations, cotangent, frame_counts, slot_bands, *weights):
    slot_dev, clips, frame_dev, _ = activations.shape
    batch, band = lax.axis_size("batch"), lax.axis_size("band")
    fits = (
        clips == 1
        and batch == 4
        and band == 2 * Z_COUNT
        and slot_dev % batch == 0
        and frame_dev == BLOCK
        and frame_dev == 32 * band
        and slot_bands.shape[0] == 64 == slot_dev * band
        and slot_dev == 2 * batch
        and activations.shape[-1] % 128 == 0
        and (frame_dev // band * slot_bands.shape[0]) % (2 * BLOCK) == 0
        and weights[2].shape[1] == 8
    )
    form = slot_shards if fits else generic_shards
    return form(activations, cotangent, frame_counts, slot_bands, *weights)


def solution(mesh):
    return jax.shard_map(
        shards,
        mesh=mesh,
        in_specs=(
            P("band", None, "batch", None),
            P("band", None, "batch", None),
            P(),
            P(),
            P(),
            P(),
            P(),
            P(),
            P(),
            P(),
            P(),
            P(),
            P(),
            P(),
            P(),
            P(),
            P(),
            P(),
        ),
        out_specs=(
            P("band", None, "batch", None),
            P("band", None, "batch", None),
            P(),
            P(),
            P(),
            P(),
            P(),
            P(),
            P(),
            P(),
            P(),
            P(),
            P(),
            P(),
            P(),
            P(),
        ),
        check_vma=False,
    )
```

```python
import math

import jax
import jax.numpy as jnp
from jax import lax
from jax.experimental import pallas as pl
from jax.experimental.pallas import tpu as pltpu
from jax.sharding import PartitionSpec as P

EPSILON = 1e-05
NEG_FILL = -1000000000.0
TIME_LAYOUT = ("bqhe", "bkhe")
BAND_LAYOUT = ("qbhe", "kbhe")


def rms_scale(residual, gain):
    return (
        residual * lax.rsqrt(jnp.mean(residual * residual, axis=-1, keepdims=True) + EPSILON) * gain
    )


def gelu_exact(values):
    return jax.nn.gelu(values, approximate=False)


def rotary_tables(positions, head_size):
    half_size = head_size // 2
    rates = jnp.exp(-math.log(10000.0) * jnp.arange(half_size, dtype=jnp.float32) / half_size)
    angles = positions[:, None] * rates[None, :]
    return (jnp.cos(angles), jnp.sin(angles))


def rotate(vectors, cos_table, sin_table):
    half_size = vectors.shape[-1] // 2
    first = vectors[..., :half_size]
    second = vectors[..., half_size:]
    return jnp.concatenate(
        [first * cos_table - second * sin_table, first * sin_table + second * cos_table], axis=-1
    )


def token_sum(left, right):
    return lax.dot_general(
        left.reshape(-1, left.shape[-1]),
        right.reshape(-1, right.shape[-1]),
        (((0,), (0,)), ((), ())),
        preferred_element_type=jnp.float32,
    )


def back_dot(gradient, weight):
    return lax.dot_general(
        gradient,
        weight,
        (((gradient.ndim - 1,), (1,)), ((), ())),
        preferred_element_type=jnp.float32,
    )


def block_forward(queries, key_rows, value_rows, key_valid, layout):
    query_form, key_form = layout
    scores = (
        jnp.einsum(
            query_form + "," + key_form + "->bhqk",
            queries,
            key_rows,
            preferred_element_type=jnp.float32,
        )
        * 0.125
    )
    scores = jnp.where(key_valid[:, None, None, :], scores, NEG_FILL)
    highest = jnp.max(scores, axis=-1, keepdims=True)
    exponents = jnp.exp(scores - highest)
    totals = jnp.sum(exponents, axis=-1, keepdims=True)
    soft_weights = (exponents / totals).astype(jnp.bfloat16)
    output = jnp.einsum(
        "bhqk," + key_form + "->" + query_form,
        soft_weights,
        value_rows,
        preferred_element_type=jnp.float32,
    )
    return (output, highest + jnp.log(totals))


def block_backward(queries, key_rows, value_rows, key_valid, log_totals, out_grad, layout):
    query_form, key_form = layout
    scores = (
        jnp.einsum(
            query_form + "," + key_form + "->bhqk",
            queries,
            key_rows,
            preferred_element_type=jnp.float32,
        )
        * 0.125
    )
    soft_weights = jnp.where(key_valid[:, None, None, :], jnp.exp(scores - log_totals), 0.0)
    weight_grad = jnp.einsum(
        query_form + "," + key_form + "->bhqk",
        out_grad,
        value_rows,
        preferred_element_type=jnp.float32,
    )
    score_grad = (
        soft_weights * (weight_grad - jnp.sum(soft_weights * weight_grad, axis=-1, keepdims=True))
    ).astype(jnp.bfloat16)
    query_grad = (
        jnp.einsum(
            "bhqk," + key_form + "->" + query_form,
            score_grad,
            key_rows,
            preferred_element_type=jnp.float32,
        )
        * 0.125
    )
    key_grad = (
        jnp.einsum(
            "bhqk," + query_form + "->" + key_form,
            score_grad,
            queries,
            preferred_element_type=jnp.float32,
        )
        * 0.125
    )
    value_grad = jnp.einsum(
        "bhqk," + query_form + "->" + key_form,
        soft_weights.astype(jnp.bfloat16),
        out_grad,
        preferred_element_type=jnp.float32,
    )
    return (query_grad, key_grad, value_grad)


def time_attend(queries, key_rows, value_rows, key_valid):
    keys_full, values_full = (
        lax.all_gather(key_rows, "batch", axis=1, tiled=True),
        lax.all_gather(value_rows, "batch", axis=1, tiled=True),
    )
    output, log_totals = block_forward(queries, keys_full, values_full, key_valid, TIME_LAYOUT)
    return (output, (log_totals, keys_full, values_full))


def time_attend_back(queries, key_rows, value_rows, key_valid, attn_kept, out_grad):
    log_totals, keys_full, values_full = attn_kept
    query_grad, key_full_grad, value_full_grad = block_backward(
        queries, keys_full, values_full, key_valid, log_totals, out_grad, TIME_LAYOUT
    )
    key_grad, value_grad = (
        lax.psum_scatter(
            key_full_grad.astype(jnp.bfloat16), "batch", scatter_dimension=1, tiled=True
        ).astype(jnp.float32),
        lax.psum_scatter(
            value_full_grad.astype(jnp.bfloat16), "batch", scatter_dimension=1, tiled=True
        ).astype(jnp.float32),
    )
    return (query_grad, key_grad, value_grad)


def band_attend(queries, key_rows, value_rows, key_valid):
    return block_forward(queries, key_rows, value_rows, key_valid, BAND_LAYOUT)


def band_attend_back(queries, key_rows, value_rows, key_valid, attn_kept, out_grad):
    return block_backward(
        queries, key_rows, value_rows, key_valid, attn_kept, out_grad, BAND_LAYOUT
    )


def layer_forward(residual, params, tables, key_valid, attend):
    prenorm, project, gating, output_weight, midnorm, expand, shrink = params
    cos_table, sin_table = tables
    normed = rms_scale(residual, prenorm.astype(jnp.float32)).astype(jnp.bfloat16)
    projected = jnp.dot(normed, project, preferred_element_type=jnp.float32)
    gate_logits = jnp.dot(normed, gating, preferred_element_type=jnp.float32)
    inner_width = output_weight.shape[0]
    head_count = gating.shape[1]
    head_shape = residual.shape[:-1] + (head_count, inner_width // head_count)
    queries = rotate(projected[..., :inner_width].reshape(head_shape), cos_table, sin_table).astype(
        jnp.bfloat16
    )
    key_rows = rotate(
        projected[..., inner_width : 2 * inner_width].reshape(head_shape), cos_table, sin_table
    ).astype(jnp.bfloat16)
    value_rows = projected[..., 2 * inner_width :].reshape(head_shape).astype(jnp.bfloat16)
    attended, attn_kept = attend(queries, key_rows, value_rows, key_valid)
    gate_values = jax.nn.sigmoid(gate_logits)
    mixed_heads = (
        (attended * gate_values[..., None])
        .reshape(residual.shape[:-1] + (inner_width,))
        .astype(jnp.bfloat16)
    )
    middle = residual + jnp.dot(mixed_heads, output_weight, preferred_element_type=jnp.float32)
    normed_ffn = rms_scale(middle, midnorm.astype(jnp.float32)).astype(jnp.bfloat16)
    hidden = jnp.dot(normed_ffn, expand, preferred_element_type=jnp.float32)
    active = gelu_exact(hidden).astype(jnp.bfloat16)
    result = middle + jnp.dot(active, shrink, preferred_element_type=jnp.float32)
    kept_values = (
        residual,
        normed,
        gate_logits,
        queries,
        key_rows,
        value_rows,
        attn_kept,
        attended,
        mixed_heads,
        middle,
        normed_ffn,
        hidden,
        active,
    )
    return (result, kept_values)


def layer_backward(result_grad, params, kept_values, tables, key_valid, attend_back):
    prenorm, project, gating, output_weight, midnorm, expand, shrink = params
    (
        residual,
        normed,
        gate_logits,
        queries,
        key_rows,
        value_rows,
        attn_kept,
        attended,
        mixed_heads,
        middle,
        normed_ffn,
        hidden,
        active,
    ) = kept_values
    cos_table, sin_table = tables
    branch_grad = result_grad.astype(jnp.bfloat16)
    shrink_grad = token_sum(active, branch_grad)
    active_grad = back_dot(branch_grad, shrink)
    hidden_grad = jax.vjp(gelu_exact, hidden)[1](active_grad)[0].astype(jnp.bfloat16)
    expand_grad = token_sum(normed_ffn, hidden_grad)
    normed_ffn_grad = back_dot(hidden_grad, expand)
    middle_norm_grad, midnorm_grad = jax.vjp(rms_scale, middle, midnorm.astype(jnp.float32))[1](
        normed_ffn_grad
    )
    middle_grad = result_grad + middle_norm_grad
    attn_branch = middle_grad.astype(jnp.bfloat16)
    output_grad = token_sum(mixed_heads, attn_branch)
    mixed_grad = back_dot(attn_branch, output_weight).reshape(attended.shape)
    gate_values = jax.nn.sigmoid(gate_logits)
    attended_grad = (mixed_grad * gate_values[..., None]).astype(jnp.bfloat16)
    logit_grad = (
        jnp.sum(mixed_grad * attended, axis=-1) * gate_values * (1.0 - gate_values)
    ).astype(jnp.bfloat16)
    query_grad, key_grad, value_grad = attend_back(
        queries, key_rows, value_rows, key_valid, attn_kept, attended_grad
    )
    flat_shape = residual.shape[:-1] + (-1,)
    projected_grad = jnp.concatenate(
        [
            rotate(query_grad, cos_table, -sin_table).reshape(flat_shape),
            rotate(key_grad, cos_table, -sin_table).reshape(flat_shape),
            value_grad.reshape(flat_shape),
        ],
        axis=-1,
    ).astype(jnp.bfloat16)
    project_grad = token_sum(normed, projected_grad)
    gating_grad = token_sum(normed, logit_grad)
    normed_grad = back_dot(projected_grad, project) + back_dot(logit_grad, gating)
    residual_norm_grad, prenorm_grad = jax.vjp(rms_scale, residual, prenorm.astype(jnp.float32))[1](
        normed_grad
    )
    return (
        middle_grad + residual_norm_grad,
        (
            prenorm_grad,
            project_grad,
            gating_grad,
            output_grad,
            midnorm_grad,
            expand_grad,
            shrink_grad,
        ),
    )


def generic_shards(
    activations,
    cotangent,
    frame_counts,
    slot_bands,
    time_prenorm,
    time_project,
    time_gating,
    time_output,
    time_midnorm,
    time_expand,
    time_shrink,
    band_prenorm,
    band_project,
    band_gating,
    band_output,
    band_midnorm,
    band_expand,
    band_shrink,
):
    slot_dev, clip_count, frame_dev, model_width = activations.shape
    slot_count = slot_bands.shape[0]
    frames_all = frame_dev * lax.axis_size("batch")
    head_size = time_output.shape[0] // time_gating.shape[1]
    time_params = (
        time_prenorm,
        time_project,
        time_gating,
        time_output,
        time_midnorm,
        time_expand,
        time_shrink,
    )
    band_params = (
        band_prenorm,
        band_project,
        band_gating,
        band_output,
        band_midnorm,
        band_expand,
        band_shrink,
    )
    own_bands = lax.dynamic_slice_in_dim(slot_bands, lax.axis_index("band") * slot_dev, slot_dev)
    frame_start = lax.axis_index("batch") * frame_dev
    own_frames = frame_start + jnp.arange(frame_dev, dtype=jnp.int32)
    frame_valid = own_frames[None, :] < frame_counts[:, None]
    row_valid = (own_bands >= 0)[:, None, None] & frame_valid[None]
    full_valid = jnp.arange(frames_all, dtype=jnp.int32)[None, :] < frame_counts[:, None]
    time_valid = jnp.broadcast_to(full_valid[None], (slot_dev, clip_count, frames_all)).reshape(
        slot_dev * clip_count, frames_all
    )
    time_cos, time_sin = rotary_tables(own_frames.astype(jnp.float32), head_size)
    time_tables = (time_cos[None, :, None, :], time_sin[None, :, None, :])
    band_cos, band_sin = rotary_tables(jnp.maximum(slot_bands, 0).astype(jnp.float32), head_size)
    band_tables = (band_cos[:, None, None, :], band_sin[:, None, None, :])
    residual = activations.astype(jnp.float32).reshape(
        slot_dev * clip_count, frame_dev, model_width
    )
    time_result, time_kept = layer_forward(
        residual, time_params, time_tables, time_valid, time_attend
    )
    masked_cot = jnp.where(row_valid[..., None], cotangent, jnp.zeros((), jnp.bfloat16)).reshape(
        slot_dev, clip_count * frame_dev, model_width
    )
    frame_rows = lax.all_to_all(
        time_result.astype(jnp.bfloat16), "band", split_axis=1, concat_axis=0, tiled=True
    ).astype(time_result.dtype)
    band_valid = jnp.broadcast_to((slot_bands >= 0)[None, :], (frame_rows.shape[1], slot_count))
    band_result, band_kept = layer_forward(
        frame_rows, band_params, band_tables, band_valid, band_attend
    )
    back_rows = lax.all_to_all(
        band_result.astype(jnp.bfloat16), "band", split_axis=0, concat_axis=1, tiled=True
    ).astype(band_result.dtype)
    layer_output = jnp.where(
        row_valid[..., None], back_rows.reshape(activations.shape), 0.0
    ).astype(jnp.bfloat16)
    frame_cot = lax.all_to_all(masked_cot, "band", split_axis=1, concat_axis=0, tiled=True)
    frame_grad, band_grads = layer_backward(
        frame_cot.astype(jnp.float32),
        band_params,
        band_kept,
        band_tables,
        band_valid,
        band_attend_back,
    )
    slot_grad = lax.all_to_all(
        frame_grad.astype(jnp.bfloat16), "band", split_axis=0, concat_axis=1, tiled=True
    ).astype(frame_grad.dtype)
    input_grad, time_grads = layer_backward(
        slot_grad, time_params, time_kept, time_tables, time_valid, time_attend_back
    )
    input_grad = input_grad.reshape(activations.shape)
    all_grads = lax.psum(
        (
            time_grads[0],
            time_grads[1],
            time_grads[2],
            time_grads[3],
            time_grads[4],
            time_grads[5],
            time_grads[6],
            band_grads[0],
            band_grads[1],
            band_grads[2],
            band_grads[3],
            band_grads[4],
            band_grads[5],
            band_grads[6],
        ),
        ("band", "batch"),
    )
    return (
        layer_output,
        input_grad,
        all_grads[0],
        all_grads[1],
        all_grads[2],
        all_grads[3],
        all_grads[4],
        all_grads[5],
        all_grads[6],
        all_grads[7],
        all_grads[8],
        all_grads[9],
        all_grads[10],
        all_grads[11],
        all_grads[12],
        all_grads[13],
    )


BLOCK = 256
LOG2E = 1.4426950408889634
F32 = jnp.float32
BF16 = jnp.bfloat16
NN = (((1,), (0,)), ((), ()))
NT = (((1,), (1,)), ((), ()))
TN = (((0,), (0,)), ((), ()))
VMEM_BYTES = 60 * 2**20


def dg(left, right, dims):
    return lax.dot_general(left, right, dims, preferred_element_type=F32)


def norm_forward(rows, gain):
    scale = lax.rsqrt(jnp.mean(rows * rows, axis=0, keepdims=True) + EPSILON)
    return (rows * scale * gain).astype(BF16)


def norm_backward(rows, gain, grad):
    scale = lax.rsqrt(jnp.mean(rows * rows, axis=0, keepdims=True) + EPSILON)
    unit = rows * scale
    scaled = grad * gain
    inner = jnp.mean(scaled * unit, axis=0, keepdims=True)
    return scale * (scaled - unit * inner), grad * unit


def gelu_pair(values):
    size = jnp.abs(values)
    denominator = 1.0 + (0.3275911 * math.sqrt(0.5)) * size
    t = pl.reciprocal(denominator, approx=True)
    t = t * (2.0 - denominator * t)
    bell = jnp.exp2(values * values * (-0.5 * LOG2E))
    poly = 0.5 * 1.061405429
    for coefficient in (-1.453152027, 1.421413741, -0.284496736, 0.254829592):
        poly = poly * t + 0.5 * coefficient
    tail = poly * t * bell
    upper = jnp.where(values < 0.0, tail, 1.0 - tail)
    slope = upper + values * bell * (1.0 / math.sqrt(2.0 * math.pi))
    return values * upper, slope


def feed_forward(middle, normed, w1t_ref, w2t_ref, act_ref, slope_ref):
    part = w1t_ref.shape[0] // 3
    result = middle
    hidden = dg(w1t_ref[0:part, :], normed, NN)
    for i in range(3):
        rows = slice(i * part, (i + 1) * part)
        later = None
        if i < 2:
            later = dg(w1t_ref[(i + 1) * part : (i + 2) * part, :], normed, NN)
        active, slope = gelu_pair(hidden)
        active = active.astype(BF16)
        act_ref[rows, :] = active
        slope_ref[rows, :] = slope.astype(BF16)
        result = result + dg(w2t_ref[:, rows], active, NN)
        hidden = later
    return result


def turn(vectors, cos, sin):
    half = cos.shape[0]
    split = vectors.reshape(-1, 2 * half, vectors.shape[-1])
    first = split[:, :half]
    second = split[:, half:]
    turned = jnp.concatenate([first * cos - second * sin, first * sin + second * cos], axis=1)
    return turned.reshape(vectors.shape)


def three_parts(values):
    top = values.astype(BF16).astype(F32)
    rest = values - top
    middle = rest.astype(BF16).astype(F32)
    return top, middle, rest - middle


def extra_rows(rows, width):
    tile = jnp.concatenate(rows + [jnp.zeros((8 - len(rows), width), F32)], axis=0)
    return jnp.concatenate([tile, jnp.zeros((8, width), F32)], axis=0).astype(BF16)


def project_block(normed, wpt_ref, cos, sin, inner, scale):
    queries = turn(dg(wpt_ref[0:inner, :], normed, NN), cos, sin) * scale
    keys = turn(dg(wpt_ref[inner : 2 * inner, :], normed, NN), cos, sin)
    values = dg(wpt_ref[2 * inner : 3 * inner, :], normed, NN)
    return queries.astype(BF16), keys.astype(BF16), values.astype(BF16)


def column(gain_ref):
    row = gain_ref[...].astype(F32).reshape(1, gain_ref.shape[0])
    return jnp.broadcast_to(row, (8, row.shape[1])).T[:, :1]


def rotary_rows(positions, half):
    rank = lax.broadcasted_iota(jnp.int32, (half, positions.shape[1]), 0).astype(F32)
    angles = positions * jnp.exp(-math.log(10000.0) * rank / half)
    return jnp.cos(angles), jnp.sin(angles)


def flipped(ref):
    return ref[...].astype(F32).T.astype(BF16)


def greet_all(band_count, batch_count):
    count = band_count * batch_count
    me = lax.axis_index("band") * batch_count + lax.axis_index("batch")
    barrier = pltpu.get_barrier_semaphore()

    def signal(i, carry):
        other = lax.rem(me + i, count)
        pl.semaphore_signal(
            barrier,
            inc=1,
            device_id=(other // batch_count, lax.rem(other, batch_count)),
            device_id_type=pl.DeviceIdType.MESH,
        )
        return carry

    lax.fori_loop(1, count, signal, 0)
    pl.semaphore_wait(barrier, count - 1)


def send(source, target, send_sem, recv_sem, band, batch):
    pltpu.make_async_remote_copy(
        src_ref=source,
        dst_ref=target,
        send_sem=send_sem,
        recv_sem=recv_sem,
        device_id=(band, batch),
        device_id_type=pl.DeviceIdType.MESH,
    ).start()


def await_bytes(ref, sem):
    pltpu.make_async_copy(ref, ref, sem).wait()


class Place:
    def __init__(self):
        self.band, self.batch = lax.axis_index("band"), lax.axis_index("batch")
        self.bits = {
            "core": lax.rem(self.batch, 2),
            "x": self.batch // 2,
            "y": lax.rem(self.band, 2),
        }
        self.z = self.band // 2

    def across(self, axis):
        bit = self.bits[axis]
        if axis == "core":
            return self.band, self.batch + 1 - 2 * bit
        if axis == "x":
            return self.band, self.batch + 2 - 4 * bit
        return self.band + 1 - 2 * bit, self.batch

    def along_z(self, step):
        other = lax.rem(self.z + step, Z_COUNT)
        return other, (other * 2 + self.bits["y"], self.batch)


Z_COUNT = 4


def greet(others):
    barrier = pltpu.get_barrier_semaphore()
    for other in others:
        pl.semaphore_signal(barrier, inc=1, device_id=other, device_id_type=pl.DeviceIdType.MESH)
    pl.semaphore_wait(barrier, len(others))


class Total:
    def __init__(self, place, order, sends, recvs):
        self.place = place
        self.order = order
        self.sends, self.recvs = sends, recvs
        self.core = place.bits["core"]
        if order is not None:
            self.first, self.second = (place.bits[axis] for axis in order)

    def give(self, step, source, target, other):
        send(source, target, self.sends.at[step], self.recvs.at[step], *other)

    def took(self, step, ref):
        await_bytes(ref, self.recvs.at[step])
        await_bytes(ref, self.sends.at[step])

    def add(self, ref, rows, part):
        ref[rows] = (ref[rows].astype(F32) + part.astype(F32)).astype(BF16)

    def start_core(self, source, recv):
        self.give(0, source.at[1 - self.core], recv, self.place.across("core"))

    def end_core(self, held, recv):
        self.took(0, recv)
        held[...] = (held[...].astype(F32) + recv[...].astype(F32)).astype(BF16)

    def half_rows(self, held, level):
        rows = held.shape[0] // 2
        base = 0
        if level == 2:
            base, rows = self.first * rows, rows // 2
        bit = self.first if level == 1 else self.second
        keep = pl.ds(pl.multiple_of(base + bit * rows, rows), rows)
        away = pl.ds(pl.multiple_of(base + (1 - bit) * rows, rows), rows)
        return keep, away

    def start_half(self, level, held, recv):
        away = self.half_rows(held, level)[1]
        self.give(level, held.at[away], recv, self.place.across(self.order[level - 1]))

    def end_half(self, level, held, recv):
        self.took(level, recv)
        self.add(held, self.half_rows(held, level)[0], recv[...])

    def start_z(self, piece, recv):
        width = recv.shape[2]
        for step in range(1, Z_COUNT):
            index, other = self.place.along_z(step)
            lanes = pl.ds(pl.multiple_of(index * width, 128), width)
            self.give(3, piece.at[:, lanes], recv.at[step - 1], other)

    def z_lanes(self, width):
        return pl.ds(pl.multiple_of(self.place.z * width, 128), width)

    def end_z(self, piece, recv):
        self.took(3, recv)
        lanes = self.z_lanes(recv.shape[2])
        sums = piece[:, lanes].astype(F32)
        for step in range(Z_COUNT - 1):
            sums = sums + recv[step].astype(F32)
        piece[:, lanes] = sums.astype(BF16)

    def own_copy(self, piece, target, width, sem):
        lanes = self.z_lanes(width)
        return pltpu.make_async_copy(piece.at[:, lanes], target.at[:, lanes], sem)

    def start_z_back(self, piece, target, width, sem):
        lanes = self.z_lanes(width)
        for step in range(1, Z_COUNT):
            _, other = self.place.along_z(step)
            self.give(4, piece.at[:, lanes], target.at[:, lanes], other)
        self.own_copy(piece, target, width, sem).start()

    def end_z_back(self, piece, target, width, sem):
        self.took(4, target.at[:, pl.ds(0, (Z_COUNT - 1) * width)])
        self.own_copy(piece, target, width, sem).wait()

    def around(self):
        found = []
        for step in range(1, 4 * Z_COUNT):
            x = lax.rem(self.place.bits["x"] + step // 2 % 2, 2)
            y = lax.rem(self.place.bits["y"] + step % 2, 2)
            z = lax.rem(self.place.z + step // 4, Z_COUNT)
            found.append((2 * x + y, z, (2 * z + y, 2 * x + self.core)))
        return found

    def tile(self, ref, base, quarter, z, shape):
        rows = pl.ds(pl.multiple_of(base + quarter * shape[0], shape[0]), shape[0])
        return ref.at[rows, pl.ds(pl.multiple_of(z * shape[1], 128), shape[1])]

    def start_around(self, held, recv):
        for i, (quarter, z, other) in enumerate(self.around()):
            self.give(1, self.tile(held, 0, quarter, z, recv.shape[1:]), recv.at[i], other)

    def own_tile(self, ref, base, shape):
        return self.tile(ref, base, 2 * self.place.bits["x"] + self.place.bits["y"], self.place.z, shape)

    def end_around(self, held, recv):
        self.took(1, recv)
        own = self.own_tile(held, 0, recv.shape[1:])
        sums = own[...].astype(F32)
        for i in range(recv.shape[0]):
            sums = sums + recv[i].astype(F32)
        own[...] = sums.astype(BF16)

    def start_around_back(self, held, recv, out, sem):
        shape = recv.shape[1:]
        own = self.own_tile(held, 0, shape)
        target = self.own_tile(out, self.core * (out.shape[0] // 2), shape)
        for _, _, other in self.around():
            self.give(2, own, target, other)
        pltpu.make_async_copy(own, target, sem).start()

    def end_around_back(self, held, recv, out, sem):
        shape = recv.shape[1:]
        self.took(2, recv)
        target = self.own_tile(out, self.core * (out.shape[0] // 2), shape)
        pltpu.make_async_copy(self.own_tile(held, 0, shape), target, sem).wait()

    def back_rows(self, out, level):
        rows = out.shape[0] // 2
        base = self.core * rows
        if level >= 1:
            rows = rows // 2
            base = base + self.first * rows
        if level >= 2:
            rows = rows // 2
            base = base + self.second * rows
        return pl.ds(pl.multiple_of(base, rows), rows)

    def start_back(self, level, out, source=None):
        rows = self.back_rows(out, level)
        axis = "core" if level == 0 else self.order[level - 1]
        self.give(7 - level, out.at[rows] if source is None else source, out.at[rows], self.place.across(axis))

    def end_back(self, level, out):
        self.took(7 - level, out.at[self.back_rows(out, level)])


TOTAL_STEPS = 8


def time_forward_kernel(
    heads,
    batch_count,
    band_count,
    act_in,
    cot_in,
    count_ref,
    g1_ref,
    g2_ref,
    wgt_ref,
    wp_ref,
    wo_ref,
    w1_ref,
    w2_ref,
    band_wp_ref,
    band_wo_ref,
    band_w1_ref,
    band_w2_ref,
    band_rows,
    band_cot,
    rows_ref,
    n_ref,
    q_ref,
    k_ref,
    v_ref,
    p_ref,
    linv_ref,
    gate_ref,
    att_ref,
    mixed_ref,
    mid_ref,
    nf_ref,
    act_ref,
    slope_ref,
    band_wpt_ref,
    band_wot_ref,
    band_w1t_ref,
    band_w2t_ref,
    cos_ref,
    sin_ref,
    xt_ref,
    x_ref,
    result_ref,
    wpt_ref,
    wot_ref,
    w1t_ref,
    w2t_ref,
    row_send,
    row_recv,
    cot_send,
    cot_recv,
    result_send,
    result_recv,
    local_sem,
):
    slot, head = pl.program_id(0), pl.program_id(1)
    slots = pl.num_programs(0)
    slot_dev = cot_in.shape[0]
    frames, model = rows_ref.shape[1:]
    inner = q_ref.shape[1]
    size = inner // heads
    my_band, my_batch = lax.axis_index("band"), lax.axis_index("batch")
    frame_dev = frames // batch_count
    piece = frame_dev // band_count
    own_rows = pl.ds(pl.multiple_of(my_batch * frame_dev, frame_dev), frame_dev)
    held = x_ref.shape[0]
    frame_index = lax.broadcasted_iota(jnp.int32, (1, frames), 1)

    def neighbour(i):
        core, x = lax.rem(my_batch, 2), my_batch // 2
        return lax.rem(x + i // 2, 2) * 2 + lax.rem(core + lax.rem(i, 2), 2)

    def own_row_copy(j):
        return pltpu.make_async_copy(
            act_in.at[batch_count * j + my_batch], x_ref.at[j, own_rows], local_sem.at[j]
        )

    def own_cot_copy():
        return pltpu.make_async_copy(
            cot_in.at[:, pl.ds(pl.multiple_of(my_band * piece, piece), piece)],
            band_cot.at[pl.ds(my_band * slot_dev, slot_dev)],
            local_sem.at[held],
        )

    @pl.when((slot == 0) & (head == 0))
    def start():
        greet_all(band_count, batch_count)
        for j in range(held):
            for i in range(1, batch_count):
                other = neighbour(i)
                send(
                    act_in.at[batch_count * j + other],
                    x_ref.at[j, own_rows],
                    row_send,
                    row_recv.at[j, i],
                    my_band,
                    other,
                )
            own_row_copy(j).start()

        def send_cot(i, carry):
            other = lax.rem(my_band + i, band_count)
            send(
                cot_in.at[:, pl.ds(pl.multiple_of(other * piece, piece), piece)],
                band_cot.at[pl.ds(my_band * slot_dev, slot_dev)],
                cot_send,
                cot_recv,
                other,
                my_batch,
            )
            return carry

        lax.fori_loop(1, band_count, send_cot, 0)
        own_cot_copy().start()
        cos_ref[...], sin_ref[...] = rotary_rows(frame_index.astype(F32), size // 2)
        wpt_ref[...] = flipped(wp_ref)
        wot_ref[...] = flipped(wo_ref)
        w1t_ref[...] = flipped(w1_ref)
        w2t_ref[...] = flipped(w2_ref)
        band_wpt_ref[...] = flipped(band_wp_ref)
        band_wot_ref[...] = flipped(band_wo_ref)
        band_w1t_ref[...] = flipped(band_w1_ref)
        band_w2t_ref[...] = flipped(band_w2_ref)

    @pl.when(head == 0)
    def before():
        gain = column(g1_ref)

        def block(i, carry):
            at = pl.ds(pl.multiple_of(neighbour(i) * BLOCK, BLOCK), BLOCK)

            @pl.when(i == 0)
            def own():
                for j in range(held):

                    @pl.when(slot == j)
                    def kept():
                        own_row_copy(j).wait()

            @pl.when(i > 0)
            def arrived():
                await_bytes(x_ref.at[slot, at], row_recv.at[slot, i])

            held_rows = x_ref[slot, at, :]
            rows_ref[0, at, :] = held_rows
            rows = held_rows.astype(F32).T
            xt_ref[:, at] = rows
            normed = norm_forward(rows, gain)
            n_ref[0, :, at] = normed
            queries, keys, values = project_block(
                normed, wpt_ref, cos_ref[:, at], sin_ref[:, at], inner, LOG2E * size**-0.5
            )
            q_ref[0, :, at] = queries
            k_ref[0, :, at] = keys
            v_ref[0, :, at] = values
            gate_ref[0, :, at] = dg(wgt_ref[...], normed, NN)
            return carry

        lax.fori_loop(0, frames // BLOCK, block, 0, unroll=True)

    at_head = pl.ds(pl.multiple_of(head * size, size), size)
    ones = jnp.ones((1, frames), F32)
    queries = jnp.concatenate([q_ref[0, at_head, :], extra_rows([ones], frames)], axis=0)
    keys = jnp.concatenate([k_ref[0, at_head, :], extra_rows([jnp.where(frame_index < count_ref[0], 0.0, NEG_FILL)], frames)], axis=0)
    values = jnp.concatenate([v_ref[0, at_head, :], extra_rows([ones], frames)], axis=0)
    scores = dg(keys, queries, TN)
    weights = jnp.exp2(scores - jnp.max(scores, axis=0, keepdims=True)).astype(BF16)
    p_ref[0, 0] = weights
    sums = dg(values, weights, NN)
    inverse = 1.0 / sums[size : size + 1]
    attended = sums[:size] * inverse
    linv_ref[0, pl.ds(head, 1), :] = inverse
    att_ref[0, at_head, :] = attended
    gate = jax.nn.sigmoid(gate_ref[0, pl.ds(head, 1), :])
    mixed_ref[0, at_head, :] = (attended * gate).astype(BF16)

    @pl.when(head == heads - 1)
    def after():
        gain = column(g2_ref)
        to_slot = my_band * slot_dev + batch_count * slot + my_batch

        def block(i, carry):
            at = pl.ds(pl.multiple_of(i * BLOCK, BLOCK), BLOCK)
            middle = xt_ref[:, at] + dg(wot_ref[...], mixed_ref[0, :, at], NN)
            mid_ref[0, :, at] = middle
            normed = norm_forward(middle, gain)
            nf_ref[0, :, at] = normed
            result = feed_forward(
                middle, normed, w1t_ref, w2t_ref, act_ref.at[0, :, at], slope_ref.at[0, :, at]
            )
            result_ref[slot, at, :] = result.T.astype(BF16)

            def send_result(j, carry):
                other = lax.rem(my_band + j, band_count)
                source = result_ref.at[slot, pl.ds(pl.multiple_of(i * frame_dev + other * piece, piece), piece)]
                mine = (other == my_band) & (i == my_batch)

                @pl.when(mine)
                def keep():
                    pltpu.make_async_copy(source, band_rows.at[to_slot], local_sem.at[held + 1]).start()

                @pl.when(jnp.logical_not(mine))
                def give():
                    send(source, band_rows.at[to_slot], result_send, result_recv, other, i)

                return carry

            lax.fori_loop(1, band_count + 1, send_result, 0)
            return carry

        lax.fori_loop(0, frames // BLOCK, block, 0, unroll=True)

    @pl.when((slot == slots - 1) & (head == heads - 1))
    def finish():
        others = held * (band_count * batch_count - 1)
        others_cot = (band_count - 1) * slot_dev
        others_rows = (batch_count - 1) * frame_dev
        await_bytes(band_cot.at[pl.ds(0, others_cot)], cot_recv)
        await_bytes(band_cot.at[pl.ds(0, others_cot)], cot_send)
        own_cot_copy().wait()
        await_bytes(x_ref.at[:, pl.ds(0, others_rows)], row_send)
        await_bytes(band_rows.at[pl.ds(0, others)], result_send)
        await_bytes(band_rows.at[pl.ds(0, held)], local_sem.at[held + 1])
        await_bytes(band_rows.at[pl.ds(0, others)], result_recv)


def cost(flops, exps=0, moved=0):
    return pl.CostEstimate(flops=int(flops), bytes_accessed=int(moved), transcendentals=int(exps))


def whole_spec(array):
    nd = array.ndim
    return pl.BlockSpec(array.shape, lambda *ids: (0,) * nd, pipeline_mode=pl.Buffered(1))


def time_forward(activations, cotangent, counts, g1, g2, params, band_params, band_count, batch_count):
    wp, wgt, wo, w1, w2 = params
    bwp, _, bwo, bw1, bw2 = band_params
    slot_dev, frame_dev, model = activations.shape
    slots, frames = slot_dev // batch_count, frame_dev * batch_count
    heads, inner, hidden = wgt.shape[0], wo.shape[0], w1.shape[1]
    piece = frame_dev // band_count

    def per_slot(*shape):
        return pl.BlockSpec((1,) + shape, lambda s, h: (s,) + (0,) * len(shape))

    outs = [
        ((frames, model), BF16),
        ((model, frames), BF16),
        ((inner, frames), BF16),
        ((inner, frames), BF16),
        ((inner, frames), BF16),
        None,
        ((heads, frames), F32),
        ((heads, frames), F32),
        ((inner, frames), F32),
        ((inner, frames), BF16),
        ((model, frames), F32),
        ((model, frames), BF16),
        ((hidden, frames), BF16),
        ((hidden, frames), BF16),
    ]
    flips = [(w.shape[1], w.shape[0]) for w in (bwp, bwo, bw1, bw2)]
    own_flips = [(w.shape[1], w.shape[0]) for w in (wp, wo, w1, w2)]
    exchanged = jax.ShapeDtypeStruct((slot_dev * band_count, piece, model), BF16)
    anywhere = pl.BlockSpec(memory_space=pl.ANY)
    shapes, specs = [exchanged, exchanged], [anywhere, anywhere]
    for entry in outs:
        if entry is None:
            shapes.append(jax.ShapeDtypeStruct((slots, heads, frames, frames), BF16))
            specs.append(pl.BlockSpec((1, 1, frames, frames), lambda s, h: (s, h, 0, 0)))
        else:
            shapes.append(jax.ShapeDtypeStruct((slots,) + entry[0], entry[1]))
            specs.append(per_slot(*entry[0]))
    for shape in flips:
        shapes.append(jax.ShapeDtypeStruct(shape, BF16))
        specs.append(pl.BlockSpec(shape, lambda s, h: (0, 0), pipeline_mode=pl.Buffered(1)))
    consts = (g1, g2, wgt, wp, wo, w1, w2, bwp, bwo, bw1, bw2)
    half = inner // heads // 2
    for _ in range(2):
        shapes.append(jax.ShapeDtypeStruct((half, frames), F32))
        specs.append(pl.BlockSpec((half, frames), lambda s, h: (0, 0)))
    dma = pltpu.SemaphoreType.DMA
    return pl.pallas_call(
        lambda *refs: time_forward_kernel(heads, batch_count, band_count, *refs),
        grid=(slots, heads),
        out_shape=shapes,
        in_specs=[anywhere, anywhere, pl.BlockSpec(memory_space=pltpu.SMEM)] + [whole_spec(c) for c in consts],
        out_specs=specs,
        scratch_shapes=[
            pltpu.VMEM((model, frames), F32),
            pltpu.VMEM((slots, frames, model), BF16),
            pltpu.VMEM((slots, frames, model), BF16),
        ]
        + [pltpu.VMEM(shape, BF16) for shape in own_flips]
        + [dma, dma((slots, batch_count)), dma, dma, dma, dma, dma((slots + 2,))],
        compiler_params=pltpu.CompilerParams(
            vmem_limit_bytes=VMEM_BYTES, collective_id=0, has_side_effects=True
        ),
        cost_estimate=cost(2.0e6 * 4 * slots * frames, 2 * slots * heads * frames * frames, 60e6),
        name="time_forward",
    )(activations, cotangent, counts, *consts)


def ffn_backward(grad, slope, middle, gain, w1_ref, w2_ref, dg2_ref):
    branch = grad.astype(BF16)
    d_hidden = (dg(w2_ref[...], branch, NN) * slope.astype(F32)).astype(BF16)
    d_normed = dg(w1_ref[...], d_hidden, NN)
    d_rows, terms = norm_backward(middle, gain, d_normed)
    dg2_ref[...] += jnp.sum(terms, axis=1, keepdims=True)
    return grad + d_rows, branch, d_hidden


def add_ffn_sums(dw1_ref, dw2t_ref, branch, act, normed, d_hidden):
    dw2t_ref[...] += dg(branch, act, NT)
    dw1_ref[...] += dg(normed, d_hidden, NT)


def head_backward(d_mixed, attended, gate_logit, inverse):
    gate = jax.nn.sigmoid(gate_logit)
    d_logit = jnp.sum(d_mixed * attended, axis=0, keepdims=True) * gate * (1.0 - gate)
    d_att = (d_mixed * (gate * inverse)).astype(BF16)
    minus = -jnp.sum(d_att.astype(F32) * attended, axis=0, keepdims=True)
    return d_att, minus, d_logit


def scores_backward(queries, keys, values, weights, d_att, minus, cos, sin, scale):
    width = queries.shape[1]
    ones = jnp.ones((1, width), F32)
    d_weights = dg(
        jnp.concatenate([values, extra_rows([ones, ones, ones], width)], axis=0),
        jnp.concatenate([d_att, extra_rows(list(three_parts(minus)), width)], axis=0),
        TN,
    )
    d_scores = (weights.astype(F32) * d_weights).astype(BF16)
    d_values = dg(d_att, weights, NT)
    d_queries = dg(keys, d_scores, NN) * scale
    d_keys = dg(queries, d_scores, NT) * (1.0 / LOG2E)
    return turn(d_queries, cos, -sin), turn(d_keys, cos, -sin), d_values


def time_ffn_backward_kernel(
    heads,
    grad_ref,
    act_ref,
    slope_ref,
    nf_ref,
    mid_ref,
    mixed_ref,
    att_ref,
    gate_ref,
    linv_ref,
    g2_ref,
    w1_ref,
    w2_ref,
    wo_ref,
    half_refs,
    dmid_ref,
    datt_ref,
    minus_ref,
    dlogit_ref,
    sums_refs,
    dg2_out,
    part_refs,
    dw1_ref,
    dw2t_ref,
    dwot_ref,
    dg2_ref,
    held_refs,
    half_recvs,
    z_recvs,
    sends,
    recvs,
    local_sem,
):
    place = Place()
    totals = [Total(place, order, sends.at[i], recvs.at[i]) for i, order in enumerate(BAND_ORDERS)]
    early = len(z_recvs)
    work = list(zip(totals, half_refs, held_refs, half_recvs))

    def half_copy(i):
        return pltpu.make_async_copy(half_refs[i], held_refs[i], local_sem.at[i])

    def part_copy(i):
        rows = totals[i].half_rows(held_refs[i], 2)[0]
        return pltpu.make_async_copy(held_refs[i].at[rows], part_refs[i], local_sem.at[len(totals) + i])

    step = pl.program_id(0) * pl.num_programs(1) + pl.program_id(1)
    last = pl.num_programs(0) * pl.num_programs(1) - 1
    size = wo_ref.shape[0] // heads

    @pl.when(step == 0)
    def clear():
        for ref in (dw1_ref, dw2t_ref, dwot_ref, dg2_ref):
            ref[...] = jnp.zeros_like(ref)
        greet([place.across("x"), place.across("y")] + [place.along_z(i)[1] for i in range(1, Z_COUNT)])
        for i, (total, halves, held, recv) in enumerate(work):
            half_copy(i).start()
            total.start_half(1, halves, recv[0])

    def eighth(i):
        return held_refs[i].at[totals[i].half_rows(held_refs[i], 2)[0]]

    @pl.when(step == last - 1)
    def first_half():
        for i, (total, halves, held, recv) in list(enumerate(work))[:early]:
            half_copy(i).wait()
            total.end_half(1, held, recv[0])
            total.start_half(2, held, recv[1])

    @pl.when(step == last)
    def second_half():
        for i, (total, halves, held, recv) in list(enumerate(work))[early:]:
            half_copy(i).wait()
            total.end_half(1, held, recv[0])
            total.start_half(2, held, recv[1])
        for i, (total, halves, held, recv) in list(enumerate(work))[:early]:
            total.end_half(2, held, recv[1])
            total.start_z(eighth(i), z_recvs[i])

    slot = pl.program_id(0)
    chunks, parts, rows, model = grad_ref.shape
    slots = pl.num_programs(0)
    taken = rows // slots
    both = grad_ref[...].astype(F32).reshape(chunks * parts, slots, taken, model)
    grad = both[:, 0]
    for j in range(1, slots):
        grad = jnp.where(slot == j, both[:, j], grad)
    grad = grad.reshape(chunks * parts * taken, model).T
    d_middle, branch, d_hidden = ffn_backward(
        grad, slope_ref[0], mid_ref[0], column(g2_ref), w1_ref, w2_ref, dg2_ref
    )
    add_ffn_sums(dw1_ref, dw2t_ref, branch, act_ref[0], nf_ref[0], d_hidden)
    dmid_ref[0] = d_middle
    branch = d_middle.astype(BF16)
    dwot_ref[...] += dg(branch, mixed_ref[0], NT)
    d_mixed = dg(wo_ref[...], branch, NN)
    logits, minuses = [], []
    for head in range(heads):
        at = slice(head * size, (head + 1) * size)
        d_att, minus, d_logit = head_backward(
            d_mixed[at], att_ref[0, at], gate_ref[0, head : head + 1], linv_ref[0, head : head + 1]
        )
        datt_ref[0, at] = d_att
        minuses.append(minus)
        logits.append(d_logit)
    minus_ref[0] = jnp.concatenate(minuses, axis=0)
    dlogit_ref[0] = jnp.concatenate(logits, axis=0)

    @pl.when(step == last)
    def finish():
        for sums, ref in zip(sums_refs, (dw2t_ref, dw1_ref, dwot_ref)):
            lay_halves(sums, 0, ref)
        dg2_out[...] = dg2_ref[...]
        for i, (total, halves, held, recv) in list(enumerate(work))[early:]:
            total.end_half(2, held, recv[1])
            part_copy(i).start()
        for i, (total, halves, held, recv) in list(enumerate(work))[:early]:
            total.end_z(eighth(i), z_recvs[i])
            part_copy(i).start()
        for i in range(len(work)):
            part_copy(i).wait()


def narrow_tile(parts, rows):
    used = sum(part.shape[1] for part in parts)
    return jnp.concatenate(list(parts) + [jnp.zeros((rows, 128 - used), F32)], axis=1)


def lay_halves(target, at, ref):
    rows, width = ref.shape
    for half in range(2):
        target[half, :, at : at + width] = ref[half * rows // 2 : (half + 1) * rows // 2].astype(BF16)


XY, YX = ("x", "y"), ("y", "x")
BAND_ORDERS = (YX, XY, YX, XY)
BAND_EARLY = 2
FFN_ORDERS = (YX, XY, YX)
PAIR_ORDERS = (YX, YX, YX, None)


def time_ffn_backward(grad, act, slope, nf, mid, mixed, att, gate, linv, g2, w1, w2, wo, halves_in):
    slots, model, frames = mid.shape
    heads = gate.shape[1]
    inner, hidden = wo.shape[0], w1.shape[1]
    chunks, parts, _, _ = grad.shape
    tokens = frames // 2

    def cut(rows):
        return pl.BlockSpec((1, rows, tokens), lambda s, c: (s, 0, c))

    def whole(*shape):
        return pl.BlockSpec(shape, lambda s, c: (0,) * len(shape))

    consts = (g2, w1, w2, wo)
    anywhere = pl.BlockSpec(memory_space=pl.ANY)
    halves = [(2, model // 2, width) for width in (hidden, hidden, inner)]
    widths = [a.shape[1] for a in halves_in]
    dma = pltpu.SemaphoreType.DMA
    return pl.pallas_call(
        lambda *refs: time_ffn_backward_kernel(heads, *refs),
        grid=(slots, frames // tokens),
        out_shape=(
            jax.ShapeDtypeStruct((slots, model, frames), F32),
            jax.ShapeDtypeStruct((slots, inner, frames), BF16),
            jax.ShapeDtypeStruct((slots, heads, frames), F32),
            jax.ShapeDtypeStruct((slots, heads, frames), F32),
            [jax.ShapeDtypeStruct(shape, BF16) for shape in halves],
            jax.ShapeDtypeStruct((model, 1), F32),
            [jax.ShapeDtypeStruct((model // 8, width), BF16) for width in widths],
        ),
        in_specs=[pl.BlockSpec((chunks // 2,) + grad.shape[1:], lambda s, c: (c, 0, 0, 0))]
        + [cut(a.shape[1]) for a in (act, slope, nf, mid, mixed, att, gate, linv)]
        + [whole_spec(c) for c in consts]
        + [[anywhere for _ in widths]],
        out_specs=(
            cut(model),
            cut(inner),
            cut(heads),
            cut(heads),
            [whole(*shape) for shape in halves],
            whole(model, 1),
            [anywhere for _ in widths],
        ),
        scratch_shapes=[
            pltpu.VMEM((model, hidden), F32),
            pltpu.VMEM((model, hidden), F32),
            pltpu.VMEM((model, inner), F32),
            pltpu.VMEM((model, 1), F32),
            [pltpu.VMEM((model // 2, width), BF16) for width in widths],
            [
                [pltpu.VMEM((rows, width), BF16) for rows in (model // 4, model // 8)]
                for width in widths
            ],
            [pltpu.VMEM((Z_COUNT - 1, model // 8, width // Z_COUNT), BF16) for width in widths[:BAND_EARLY]],
            dma((len(widths), TOTAL_STEPS)),
            dma((len(widths), TOTAL_STEPS)),
            dma((2 * len(widths),)),
        ],
        compiler_params=pltpu.CompilerParams(
            vmem_limit_bytes=VMEM_BYTES, collective_id=2, has_side_effects=True
        ),
        cost_estimate=cost(8.0e6 * slots * frames, 0, 30e6),
        name="time_ffn_backward",
    )(grad, act, slope, nf, mid, mixed, att, gate, linv, *consts, list(halves_in))


BAND_PLACES = ((0, 4, 7, 11, 13), (0, 4, 7, 12, 14), (0, 4, 7, 11, 16, 18), (0, 5, 8, 12, 16, 18))
FFN_PLACES = ((0, 1, 5, 8, 12, 15, 18, 24, 25), (0, 2, 6, 10, 13, 16, 20, 24, 25), (0, 2, 6, 9, 12, 15, 18, 22, 24))
PAIR_PLACES = (
    (4, 5, 8, 12, 15, 18, 22, 24, 25),
    (8, 9, 12, 15, 17, 20, 23, 24, 25),
    (12, 13, 15, 18, 21, 24, 25, 26, 27),
    (16, 17, 21, 24, 25),
)


def time_attention_backward_kernel(
    heads,
    slots,
    batch_count,
    p_ref,
    q_ref,
    k_ref,
    v_ref,
    datt_ref,
    minus_ref,
    x_ref,
    dmid_ref,
    logit_block_ref,
    n_ref,
    dlogit_ref,
    cos_ref,
    sin_ref,
    g1_ref,
    wp_ref,
    wgt_ref,
    narrow_ref,
    dg2_ref,
    part_refs,
    ffn_refs,
    grad_out,
    band_outs,
    ffn_outs,
    pair_outs,
    dproj_ref,
    wp_turned_ref,
    grad_buf,
    piece_refs,
    band_recvs,
    held_refs,
    ffn_recvs,
    pair_refs,
    pair_recvs,
    around_recv,
    band_sems,
    ffn_sems,
    pair_sems,
    grad_sems,
    local_sem,
):
    place = Place()
    step = pl.program_id(0)
    steps = heads * slots
    head, slot = step // slots, lax.rem(step, slots)
    size, frames = q_ref.shape[1:]
    model = n_ref.shape[1]
    inner = heads * size
    pairs = heads // 2
    pair_rows = 6 * size
    blocks = frames // BLOCK
    last = pl.num_programs(0) - 1
    my_band, my_batch = place.band, place.batch

    bands = [Total(place, order, band_sems[0].at[i], band_sems[1].at[i]) for i, order in enumerate(BAND_ORDERS)]
    ffns = [Total(place, order, ffn_sems[0].at[i], ffn_sems[1].at[i]) for i, order in enumerate(FFN_ORDERS)]
    own = [
        Total(place, PAIR_ORDERS[i], pair_sems[0].at[i], pair_sems[1].at[i]) for i in range(pairs)
    ]

    def half_copy(i):
        return pltpu.make_async_copy(ffn_refs[i].at[place.bits["core"]], held_refs[i], local_sem.at[len(bands) + i])

    def eighth(total, held):
        return held.at[total.half_rows(held, 2)[0]]

    def all_steps(total, source, held, recvs, out, sem):
        width = recvs[3].shape[2]

        def back_region():
            return out.at[total.back_rows(out, 2)]

        def s0():
            total.start_core(source, recvs[0])

        def s1():
            total.end_core(held, recvs[0])
            total.start_half(1, held, recvs[1])

        def s2():
            total.end_half(1, held, recvs[1])
            total.start_half(2, held, recvs[2])

        def s3():
            total.end_half(2, held, recvs[2])
            total.start_z(eighth(total, held), recvs[3])

        def s4():
            total.end_z(eighth(total, held), recvs[3])
            total.start_z_back(eighth(total, held), back_region(), width, sem)

        def s5():
            total.end_z_back(eighth(total, held), back_region(), width, sem)
            total.start_back(2, out)

        def s6():
            total.end_back(2, out)
            total.start_back(1, out)

        def s7():
            total.end_back(1, out)
            total.start_back(0, out)

        def s8():
            total.end_back(0, out)

        return [s0, s1, s2, s3, s4, s5, s6, s7, s8]

    plan = {}

    def at_step(index, action):
        plan.setdefault(index, []).append(action)

    def enter():
        other_x = place.across("x")[1] // 2
        diagonal = (my_band, 2 * other_x + 1 - place.bits["core"])
        chips = [other for _, _, other in own[-1].around()]
        greet(chips + [place.across("core"), diagonal])
        for i in range(len(ffns)):
            half_copy(i).start()

    tail = steps + slots * blocks
    at_step(0, enter)

    def schedule(actions, places):
        for at, action in zip(places, actions):
            at_step(at, action)

    for i in range(len(bands)):
        out = band_outs[i]
        region = out.at[bands[i].back_rows(out, 2)]
        quarter = band_outs[i].shape[1] // Z_COUNT

        def z_begin(i=i):
            piece_refs[i][...] = part_refs[i][...]
            if i >= BAND_EARLY:
                bands[i].start_z(piece_refs[i], band_recvs[i - BAND_EARLY])

        def z_turn(i=i, region=region, quarter=quarter):
            if i >= BAND_EARLY:
                bands[i].end_z(piece_refs[i], band_recvs[i - BAND_EARLY])
            bands[i].start_z_back(piece_refs[i], region, quarter, local_sem.at[i])

        def z_end(i=i, region=region, quarter=quarter, out=out):
            bands[i].end_z_back(piece_refs[i], region, quarter, local_sem.at[i])
            bands[i].start_back(2, out)

        def back_two(i=i, out=out):
            bands[i].end_back(2, out)
            bands[i].start_back(1, out)

        def back_one(i=i, out=out):
            bands[i].end_back(1, out)
            bands[i].start_back(0, out)

        actions = [z_begin, z_turn, z_end, back_two, back_one, lambda i=i, out=out: bands[i].end_back(0, out)]
        if i < BAND_EARLY:
            at_step(0, z_begin)
            actions = actions[1:]
        schedule(actions, BAND_PLACES[i])
    ffn_at = len(bands) + len(ffns)
    for i in range(len(ffns)):
        sem = local_sem.at[ffn_at + i]
        actions = all_steps(ffns[i], ffn_refs[i], held_refs[i], ffn_recvs[i], ffn_outs[i], sem)
        at_step(FFN_PLACES[i][1], lambda i=i: half_copy(i).wait())
        schedule(actions, FFN_PLACES[i])
    pair_at = ffn_at + len(ffns)

    def around_steps(total, source, held, recv, out, sem):
        def s0():
            total.start_core(source, recv[0])

        def s1():
            total.end_core(held, recv[0])
            total.start_around(held, recv[1])

        def s2():
            total.end_around(held, recv[1])
            total.start_around_back(held, recv[1], out, sem)

        def s3():
            total.end_around_back(held, recv[1], out, sem)
            total.start_back(0, out)

        def s4():
            total.end_back(0, out)

        return [s0, s1, s2, s3, s4]

    for i in range(pairs):
        source, held = pair_refs.at[i], pair_refs.at[i, place.bits["core"]]
        out, sem = pair_outs.at[i], local_sem.at[pair_at + i]
        recv = [ref.at[i] for ref in pair_recvs]
        if PAIR_ORDERS[i] is None:
            actions = around_steps(own[i], source, held, [recv[0], around_recv], out, sem)
        else:
            actions = all_steps(own[i], source, held, recv, out, sem)
        schedule(actions, PAIR_PLACES[i])

    for index in sorted(plan):
        if index < tail:

            @pl.when(step == index)
            def work(index=index):
                for action in plan[index]:
                    action()

    @pl.when(step < steps)
    def attention():
        d_queries, d_keys, d_values = scores_backward(
            q_ref[0],
            k_ref[0],
            v_ref[0],
            p_ref[0, 0],
            datt_ref[0],
            minus_ref[0, pl.ds(head, 1), :],
            cos_ref[...],
            sin_ref[...],
            size**-0.5,
        )
        start = pl.multiple_of((head // 2) * pair_rows + lax.rem(head, 2) * size, size)
        dproj_ref[slot, pl.ds(start, size), :] = d_queries.astype(BF16)
        dproj_ref[slot, pl.ds(start + 2 * size, size), :] = d_keys.astype(BF16)
        dproj_ref[slot, pl.ds(start + 4 * size, size), :] = d_values.astype(BF16)

    @pl.when((step < steps) & (lax.rem(step, 2 * slots) == 2 * slots - 1))
    def pair_done():
        pair = head // 2
        rows = pl.ds(pl.multiple_of(pair * pair_rows, pair_rows), pair_rows)
        sums = dg(n_ref[0], dproj_ref[0, rows, :], NT)
        for j in range(1, slots):
            sums = sums + dg(n_ref[j], dproj_ref[j, rows, :], NT)
        for half in range(2):
            at = slice(half * model // 2, (half + 1) * model // 2)
            pair_refs[pair, half, :, 0:pair_rows] = sums[at].astype(BF16)

    @pl.when(step == 2 * slots - 1)
    def narrow_done():
        gates = 0.0
        for j in range(slots):
            logit = jnp.concatenate([dlogit_ref[j], jnp.zeros_like(dlogit_ref[j])], axis=0).astype(BF16)
            gates = gates + dg(n_ref[j], logit, NT)[:, :heads]
        tile = narrow_tile([narrow_ref[:, : heads + 2], gates, dg2_ref[...]], model)
        for half in range(2):
            at = slice(half * model // 2, (half + 1) * model // 2)
            pair_refs[0, half, :, pair_rows:] = tile[at].astype(BF16)
            for i in range(1, pairs):
                pair_refs[i, half, :, pair_rows:] = jnp.zeros_like(tile[at]).astype(BF16)
        for pair in range(pairs):
            for part in range(3):
                to = pair * pair_rows + part * 2 * size
                source = part * inner + pair * 2 * size
                wp_turned_ref[:, to : to + 2 * size] = wp_ref[:, source : source + 2 * size]

    def message(index):
        j, i = index // blocks, lax.rem(index, blocks)
        source = grad_buf.at[index]
        target = grad_out.at[batch_count * j + my_batch]
        return i, source, target

    @pl.when(step >= steps)
    def rows_done():
        index = step - steps
        j, i = index // blocks, lax.rem(index, blocks)
        at = pl.ds(pl.multiple_of(i * BLOCK, BLOCK), BLOCK)
        logit = logit_block_ref[0].astype(BF16)
        d_normed = dg(wp_turned_ref[...], dproj_ref[j, :, at], NN) + dg(wgt_ref[...], logit, TN)
        d_rows, _ = norm_backward(x_ref[0].astype(F32).T, column(g1_ref), d_normed)
        grad_buf[index] = (dmid_ref[0] + d_rows).T.astype(BF16)
        i, source, target = message(index)

        @pl.when(i == my_batch)
        def keep():
            pltpu.make_async_copy(source, target, local_sem.at[pair_at + pairs]).start()

        @pl.when(i != my_batch)
        def give():
            send(source, target, grad_sems.at[0], grad_sems.at[1], my_band, i)

    @pl.when(step == last)
    def finish():
        for index in sorted(plan):
            if index >= tail:
                for action in plan[index]:
                    action()
        await_bytes(grad_buf.at[pl.ds(0, slots)], local_sem.at[pair_at + pairs])
        others = grad_buf.at[pl.ds(0, slots * (batch_count - 1))]
        await_bytes(others, grad_sems.at[0])
        await_bytes(others, grad_sems.at[1])


def time_attention_backward(
    p, q, k, v, datt, minus, dlogit, n, x, dmid, cos, sin, g1, wp, wgt, narrow, dg2, parts, ffn_sums, batch_count
):
    slots, inner, frames = q.shape
    heads = minus.shape[1]
    size = inner // heads
    model = n.shape[1]
    pairs = heads // 2
    steps = heads * slots
    blocks = frames // BLOCK

    def clamp(t):
        return jnp.minimum(t, steps - 1)

    def tail(t):
        return jnp.maximum(t - steps, 0)

    def per_head(rows, columns):
        return pl.BlockSpec((1, rows, columns), lambda t: (lax.rem(clamp(t), slots), clamp(t) // slots, 0))

    consts = (n, dlogit, cos, sin, g1, wp, wgt, narrow, dg2)
    anywhere = pl.BlockSpec(memory_space=pl.ANY)
    dma = pltpu.SemaphoreType.DMA
    widths = [a.shape[2] for a in ffn_sums]
    pair_width = 8 * size

    def recv_buffers(width, *lead):
        rows = model // 2
        shapes = [(rows, width), (rows // 2, width), (rows // 4, width), (Z_COUNT - 1, rows // 4, width // Z_COUNT)]
        return [pltpu.VMEM(lead + shape, BF16) for shape in shapes]

    return pl.pallas_call(
        lambda *refs: time_attention_backward_kernel(heads, slots, batch_count, *refs),
        grid=(steps + slots * blocks,),
        out_shape=(
            jax.ShapeDtypeStruct((batch_count * slots, BLOCK, model), BF16),
            [jax.ShapeDtypeStruct((model, a.shape[1]), BF16) for a in parts],
            [jax.ShapeDtypeStruct((model, width), BF16) for width in widths],
            jax.ShapeDtypeStruct((pairs, model, pair_width), BF16),
        ),
        in_specs=[
            pl.BlockSpec((1, 1, frames, frames), lambda t: (lax.rem(clamp(t), slots), clamp(t) // slots, 0, 0)),
            per_head(size, frames),
            per_head(size, frames),
            per_head(size, frames),
            per_head(size, frames),
            pl.BlockSpec((1, heads, frames), lambda t: (lax.rem(clamp(t), slots), 0, 0)),
            pl.BlockSpec((1, BLOCK, model), lambda t: (tail(t) // blocks, lax.rem(tail(t), blocks), 0)),
            pl.BlockSpec((1, model, BLOCK), lambda t: (tail(t) // blocks, 0, lax.rem(tail(t), blocks))),
            pl.BlockSpec((1, heads, BLOCK), lambda t: (tail(t) // blocks, 0, lax.rem(tail(t), blocks))),
        ]
        + [whole_spec(c) for c in consts]
        + [[whole_spec(a) for a in parts], [anywhere] * len(ffn_sums)],
        out_specs=(anywhere, [anywhere] * len(parts), [anywhere] * len(ffn_sums), anywhere),
        scratch_shapes=[
            pltpu.VMEM((slots, 3 * inner, frames), BF16),
            pltpu.VMEM((model, 3 * inner), BF16),
            pltpu.VMEM((slots * blocks, BLOCK, model), BF16),
            [pltpu.VMEM(a.shape, BF16) for a in parts],
            [pltpu.VMEM((Z_COUNT - 1, a.shape[0], a.shape[1] // Z_COUNT), BF16) for a in parts[BAND_EARLY:]],
            [pltpu.VMEM((model // 2, width), BF16) for width in widths],
            [recv_buffers(width) for width in widths],
            pltpu.VMEM((pairs, 2, model // 2, pair_width), BF16),
            recv_buffers(pair_width, pairs),
            pltpu.VMEM((4 * Z_COUNT - 1, model // 8, pair_width // Z_COUNT), BF16),
            [dma((len(parts), TOTAL_STEPS))] * 2,
            [dma((len(widths), TOTAL_STEPS))] * 2,
            [dma((pairs, TOTAL_STEPS)), dma((pairs, TOTAL_STEPS))],
            dma((2,)),
            dma((len(parts) + 2 * len(widths) + pairs + 1,)),
        ],
        compiler_params=pltpu.CompilerParams(
            vmem_limit_bytes=VMEM_BYTES, collective_id=3, has_side_effects=True
        ),
        cost_estimate=cost(20.0e6 * slots * frames, 0, 60e6),
        name="time_attention_backward",
    )(p, q, k, v, datt, minus, x, dmid, dlogit, *consts, list(parts), list(ffn_sums))


def finish_kernel(
    heads,
    grad_ref,
    bwp_ref,
    bw1_ref,
    bw2t_ref,
    bwot_ref,
    w1_ref,
    wot_ref,
    w2t_ref,
    pair_ref,
    first_pair_ref,
    wp_ref,
    wgt_ref,
    g1_ref,
    y_ref,
    y_out,
    grad_out,
    dg1_out,
    dwp_out,
    dwg_out,
    dwo_out,
    dg2_out,
    dw1_out,
    dw2_out,
    bg1_out,
    bwp_out,
    bwg_out,
    bwo_out,
    bg2_out,
    bw1_out,
    bw2_out,
    scaled_ref,
):
    pair = pl.program_id(0)
    inner = wp_ref.shape[1] // 3
    width = inner // pl.num_programs(0)
    pairs, bands, parts, rows, model = y_ref.shape
    split = y_ref[...].astype(F32).reshape(pairs, bands, parts, 2, rows // 2, model)
    for j in range(2):
        values = split[:, :, :, j].reshape(pairs, bands * parts * rows // 2, model)
        for i in range(pairs):
            y_out[2 * i + j] = values[i].astype(BF16)
    grad_out[...] = grad_ref[...].astype(F32)
    bwp_out[...] = bwp_ref[...].astype(F32)
    bw1_out[...] = bw1_ref[...].astype(F32)
    bw2_out[...] = bw2t_ref[...].astype(F32).T
    bwo_out[...] = bwot_ref[...].astype(F32).T
    dw1_out[...] = w1_ref[...].astype(F32)
    dw2_out[...] = w2t_ref[...].astype(F32).T
    dwo_out[...] = wot_ref[...].astype(F32).T

    @pl.when(pair == 0)
    def clear():
        scaled_ref[...] = jnp.zeros_like(scaled_ref)

    for part in range(3):
        at = pl.ds(pl.multiple_of(part * inner + pair * width, 128), width)
        values = pair_ref[0, :, part * width : (part + 1) * width].astype(F32)
        dwp_out[:, at] = values
        scaled_ref[...] += values * wp_ref[:, at].astype(F32)

    @pl.when(pair == pl.num_programs(0) - 1)
    def narrow():
        tile = first_pair_ref[0, :, 3 * width :].astype(F32)
        rows = tile.T
        bwg_out[...] = rows[:heads]
        bg1_out[...] = rows[heads]
        bg2_out[...] = rows[heads + 1]
        gates = tile[:, heads + 2 : 2 * heads + 2]
        dwg_out[...] = rows[heads + 2 : 2 * heads + 2]
        dg2_out[...] = rows[2 * heads + 2]
        sums = jnp.sum(scaled_ref[...], axis=1, keepdims=True)
        sums = sums + jnp.sum(gates * wgt_ref[...].astype(F32).T, axis=1, keepdims=True)
        dg1_out[...] = jnp.broadcast_to(sums, (sums.shape[0], 128)).T[0] / g1_ref[...].astype(F32)


def finish_sums(grads, y, band_sums, ffn_sums, pair_sums, g1, params):
    wp, wgt, wo, w1, w2 = params
    model, hidden = w1.shape
    inner, heads = wo.shape[0], wgt.shape[0]
    pairs = pair_sums.shape[0]
    split = hidden // pairs
    out_split = inner // pairs
    slot_dev, frame_dev, _ = grads.shape

    def lanes(width):
        return pl.BlockSpec((model, width), lambda i: (0, i))

    def whole(*shape):
        return pl.BlockSpec(shape, lambda i: (0,) * len(shape))

    def cut_rows(rows):
        return pl.BlockSpec((rows, model), lambda i: (i, 0))

    band_wp, band_w1, band_w2t, band_wot = band_sums
    time_w2t, time_w1, time_wot = ffn_sums
    grad_block = pl.BlockSpec((slot_dev // pairs, frame_dev, model), lambda i: (i, 0, 0))
    narrow = [((model,), whole(model)), ((heads, model), whole(heads, model))]
    per_layer = [
        narrow[0],
        ((model, 3 * inner), None),
        narrow[1],
        ((inner, model), cut_rows(out_split)),
        narrow[0],
        ((model, hidden), lanes(split)),
        ((hidden, model), cut_rows(split)),
    ]
    shapes, specs = [jax.ShapeDtypeStruct(grads.shape, BF16), jax.ShapeDtypeStruct(grads.shape, F32)], [grad_block] * 2
    y_block = pl.BlockSpec((y.shape[0] // pairs,) + y.shape[1:], lambda i: (i, 0, 0, 0, 0))
    for layer in range(2):
        for shape, spec in per_layer:
            shapes.append(jax.ShapeDtypeStruct(shape, F32))
            if spec is None:
                spec = whole(*shape) if layer == 0 else lanes(3 * inner // pairs)
            specs.append(spec)
    return pl.pallas_call(
        lambda *refs: finish_kernel(heads, *refs),
        grid=(pairs,),
        out_shape=shapes,
        in_specs=[
            grad_block,
            lanes(3 * inner // pairs),
            lanes(split),
            lanes(split),
            lanes(out_split),
            lanes(split),
            lanes(out_split),
            lanes(split),
            pl.BlockSpec((1, model, pair_sums.shape[2]), lambda i: (i, 0, 0)),
            pl.BlockSpec((1, model, pair_sums.shape[2]), lambda i: (0, 0, 0)),
            whole_spec(wp),
            whole_spec(wgt),
            whole_spec(g1),
            y_block,
        ],
        out_specs=specs,
        scratch_shapes=[pltpu.VMEM((model, inner // pairs), F32)],
        compiler_params=pltpu.CompilerParams(vmem_limit_bytes=VMEM_BYTES),
        name="finish_sums",
    )(
        grads,
        band_wp,
        band_w1,
        band_w2t,
        band_wot,
        time_w1,
        time_wot,
        time_w2t,
        pair_sums,
        pair_sums,
        wp,
        wgt,
        g1,
        y,
    )


def band_kernel(
    heads,
    batch_count,
    band_count,
    x_ref,
    cot_ref,
    count_ref,
    slots_ref,
    g1_ref,
    g2_ref,
    wgt_ref,
    wpt_ref,
    wot_ref,
    w1t_ref,
    w2t_ref,
    wp_ref,
    wo_ref,
    w1_ref,
    w2_ref,
    y_out,
    dx_out,
    half_outs,
    narrow_out,
    q_ref,
    k_ref,
    v_ref,
    p_ref,
    turned_ref,
    gate_ref,
    linv_ref,
    att_ref,
    mixed_ref,
    act_ref,
    slope_ref,
    hidden_ref,
    dmixed_ref,
    dlogit_ref,
    dproj_ref,
    dwp_ref,
    dw1_ref,
    dw2t_ref,
    dwot_ref,
    dwg_ref,
    dg1_ref,
    dg2_ref,
    xs_ref,
    cots_ref,
    ys_ref,
    dxs_ref,
    y_buf,
    dx_buf,
    y_send,
    y_recv,
    dx_send,
    dx_recv,
    local_sem,
    bias_ref,
    cos_ref,
    sin_ref,
    valid_ref,
    halves,
    core_recvs,
    core_sems,
    half_sem,
):
    step = pl.program_id(0)
    slot_count, part_frames, model = x_ref.shape
    inner, tokens = q_ref.shape
    size = inner // heads
    groups = tokens // BLOCK
    taken = tokens // slot_count
    per_part = part_frames // taken
    part = step // per_part
    first = lax.rem(step, per_part) * taken
    my_band, my_batch = lax.axis_index("band"), lax.axis_index("batch")
    slot_dev = slot_count // band_count
    slots = slot_dev // batch_count
    own_chunk = my_batch * band_count + my_band
    chunks = band_count * batch_count

    columns = [slice(at, at + 128) for at in range(0, model, 128)]

    def tokens_of(ref):
        return jnp.concatenate(
            [
                jnp.concatenate(
                    [ref[c, pl.ds(first + i, slot_count, stride=part_frames), :] for i in range(taken)], axis=0
                ).T
                for c in range(len(columns))
            ],
            axis=0,
        )

    def put_tokens(ref, values, start, stride):
        for c, at in enumerate(columns):
            turned = values[at].T
            for i in range(taken):
                ref[c, pl.ds(start + i, slot_count, stride=stride), :] = turned[
                    i * slot_count : (i + 1) * slot_count
                ]

    @pl.when(step == 0)
    def enter():
        greet_all(band_count, batch_count)
        bands = slots_ref[...].reshape(1, slot_count)
        cos, sin = rotary_rows(jnp.maximum(bands, 0).astype(F32), size // 2)
        cos_ref[...] = jnp.concatenate([cos] * taken, axis=1)
        sin_ref[...] = jnp.concatenate([sin] * taken, axis=1)
        valid = jnp.concatenate([jnp.where(bands >= 0, 1.0, 0.0)] * taken, axis=1)
        valid_ref[...] = valid
        keys = jnp.broadcast_to(valid[:, :BLOCK], (8, BLOCK)).T[:, :1]
        row = lax.broadcasted_iota(jnp.int32, (BLOCK, BLOCK), 0) // slot_count
        column_index = lax.broadcasted_iota(jnp.int32, (BLOCK, BLOCK), 1) // slot_count
        bias_ref[...] = jnp.where((row == column_index) & (keys > 0.5), 0.0, NEG_FILL)

    @pl.when(lax.rem(step, per_part) == 0)
    def unpack():
        for c, at in enumerate(columns):
            xs_ref[c] = x_ref[:, :, at].astype(F32).reshape(xs_ref.shape[1:])
            cots_ref[c] = cot_ref[:, :, at].astype(F32).reshape(cots_ref.shape[1:])

    place = Place()
    totals = [
        Total(place, order, core_sems.at[0, i], core_sems.at[1, i]) for i, order in enumerate(BAND_ORDERS)
    ]
    gain1, gain2 = column(g1_ref), column(g2_ref)
    piece = part_frames * (pl.num_programs(0) // per_part)
    own_start = (my_batch * band_count + my_band) * piece

    @pl.when(step == 0)
    def clear():
        for ref in (dwp_ref, dw1_ref, dw2t_ref, dwot_ref, dwg_ref, dg1_ref, dg2_ref):
            ref[...] = jnp.zeros_like(ref)

    rows = tokens_of(xs_ref)
    normed = norm_forward(rows, gain1)
    q_ref[...], k_ref[...], v_ref[...] = project_block(
        normed, wpt_ref, cos_ref[...], sin_ref[...], inner, LOG2E * size**-0.5
    )
    gate_ref[...] = dg(wgt_ref[...], normed, NN)
    ones = extra_rows([jnp.ones((1, BLOCK), F32)], BLOCK)
    nothing = jnp.zeros((size, BLOCK), BF16)

    def apart(first, second):
        return jnp.concatenate(
            [jnp.concatenate([first, nothing], axis=1), jnp.concatenate([nothing, second], axis=1)], axis=0
        )

    turned_ref[...] = k_ref[...].T
    bias = jnp.concatenate([bias_ref[...]] * 2, axis=1)

    for pair in range(heads // 2):
        both = slice(2 * pair * size, 2 * (pair + 1) * size)
        for group in range(groups):
            lanes = slice(group * BLOCK, (group + 1) * BLOCK)
            at = [slice((2 * pair + i) * size, (2 * pair + i + 1) * size) for i in range(2)]
            scores = dg(turned_ref[lanes, both], apart(*(q_ref[one, lanes] for one in at)), NN) + bias
            weights = jnp.exp2(scores - jnp.max(scores, axis=0, keepdims=True)).astype(BF16)
            p_ref[pair * groups + group] = weights
            for i, one in enumerate(at):
                row = slice(2 * pair + i, 2 * pair + i + 1)
                own = weights[:, i * BLOCK : (i + 1) * BLOCK]
                sums = dg(jnp.concatenate([v_ref[one, lanes], ones], axis=0), own, NN)
                inverse = 1.0 / sums[size : size + 1]
                attended = sums[:size] * inverse
                linv_ref[row, lanes] = inverse
                att_ref[one, lanes] = attended
                gate = jax.nn.sigmoid(gate_ref[row, lanes])
                mixed_ref[one, lanes] = (attended * gate).astype(BF16)
    middle = rows + dg(wot_ref[...], mixed_ref[...], NN)
    normed_ffn = norm_forward(middle, gain2)

    result = feed_forward(middle, normed_ffn, w1t_ref, w2t_ref, act_ref, slope_ref)
    frame = own_start + step * taken + lax.broadcasted_iota(jnp.int32, (1, tokens), 1) // slot_count
    mask = jnp.where(frame < count_ref[0], valid_ref[...], 0.0)
    result = result * mask
    put_tokens(ys_ref, result, 0, taken)

    couples = slot_dev // 2
    for c, at in enumerate(columns):
        y_buf[step, :, :, at] = ys_ref[c].reshape(slot_count // 2, 2 * taken, 128).astype(BF16)

    def give_row(i, carry):
        other = lax.rem(my_band + i, band_count)
        send(
            y_buf.at[step, pl.ds(other * couples, couples)],
            y_out.at[:, my_band, step],
            y_send,
            y_recv,
            other,
            my_batch,
        )
        return carry

    lax.fori_loop(1, band_count, give_row, 0)
    pltpu.make_async_copy(
        y_buf.at[step, pl.ds(my_band * couples, couples)], y_out.at[:, my_band, step], local_sem.at[0]
    ).start()

    grad = tokens_of(cots_ref) * mask
    d_middle, ffn_branch, d_hidden = ffn_backward(grad, slope_ref[...], middle, gain2, w1_ref, w2_ref, dg2_ref)
    hidden_ref[...] = d_hidden
    branch = d_middle.astype(BF16)
    dmixed_ref[...] = dg(wo_ref[...], branch, NN)

    turned_ref[...] = v_ref[...].T
    for pair in range(heads // 2):
        both = slice(2 * pair * size, 2 * (pair + 1) * size)
        at = [slice((2 * pair + i) * size, (2 * pair + i + 1) * size) for i in range(2)]
        d_atts, minuses = [], []
        for i, one in enumerate(at):
            row = slice(2 * pair + i, 2 * pair + i + 1)
            d_att, minus, d_logit = head_backward(
                dmixed_ref[one, :], att_ref[one, :], gate_ref[row, :], linv_ref[row, :]
            )
            dlogit_ref[row, :] = d_logit
            d_atts.append(d_att)
            minuses.append(minus)
        for group in range(groups):
            lanes = slice(group * BLOCK, (group + 1) * BLOCK)
            weights = p_ref[pair * groups + group]
            d_weights = dg(turned_ref[lanes, both], apart(*(d_att[:, lanes] for d_att in d_atts)), NN)
            minus = jnp.concatenate([minus[:, lanes] for minus in minuses], axis=1)
            d_scores = (weights.astype(F32) * (d_weights + minus)).astype(BF16)
            for i, one in enumerate(at):
                own = slice(i * BLOCK, (i + 1) * BLOCK)
                d_queries = dg(k_ref[one, lanes], d_scores[:, own], NN) * size**-0.5
                d_keys = dg(q_ref[one, lanes], d_scores[:, own], NT) * (1.0 / LOG2E)
                d_values = dg(d_atts[i][:, lanes], weights[:, own], NT)
                start = one.start
                cos, sin = cos_ref[:, lanes], -sin_ref[:, lanes]
                dproj_ref[start : start + size, lanes] = turn(d_queries, cos, sin).astype(BF16)
                dproj_ref[inner + start : inner + start + size, lanes] = turn(d_keys, cos, sin).astype(BF16)
                dproj_ref[2 * inner + start : 2 * inner + start + size, lanes] = d_values.astype(BF16)
    d_logit = jnp.concatenate([dlogit_ref[...], jnp.zeros_like(dlogit_ref)], axis=0).astype(BF16)
    d_normed = dg(wp_ref[...], dproj_ref[...], NN) + dg(wgt_ref[...], dlogit_ref[...].astype(BF16), TN)
    d_rows, terms = norm_backward(rows, gain1, d_normed)
    dg1_ref[...] += jnp.sum(terms, axis=1, keepdims=True)
    put_tokens(dxs_ref, d_middle + d_rows, 0, taken)
    for c, at in enumerate(columns):
        grouped = dxs_ref[c].reshape(band_count, slots, batch_count, taken, 128)
        grouped = jnp.concatenate([grouped[:, j][:, :, None] for j in range(slots)], axis=2)
        dx_buf[step, :, :, at] = grouped.reshape(chunks, slots * taken, 128).astype(BF16)

    def give_grad(i, carry):
        other = lax.rem(my_band * batch_count + my_batch + i, chunks)
        send(
            dx_buf.at[step, other],
            dx_out.at[own_chunk, step],
            dx_send,
            dx_recv,
            other // batch_count,
            lax.rem(other, batch_count),
        )
        return carry

    lax.fori_loop(1, chunks, give_grad, 0)
    pltpu.make_async_copy(
        dx_buf.at[step, my_band * batch_count + my_batch], dx_out.at[own_chunk, step], local_sem.at[1]
    ).start()

    dwp_ref[...] += dg(normed, dproj_ref[...], NT)
    dwg_ref[...] += dg(normed, d_logit, NT)[:, :heads]
    dwot_ref[...] += dg(branch, mixed_ref[...], NT)
    add_ffn_sums(dw1_ref, dw2t_ref, ffn_branch, act_ref[...], normed_ffn, hidden_ref[...])

    @pl.when(step == pl.num_programs(0) - 1)
    def finish():
        narrow_out[...] = narrow_tile([dwg_ref[...], dg1_ref[...], dg2_ref[...]], model)
        core = place.bits["core"]
        for i, ref in enumerate((dwp_ref, dw1_ref, dw2t_ref, dwot_ref)):
            lay_halves(halves[i], 0, ref)
            totals[i].start_core(halves[i], core_recvs[i])
        for i, total in enumerate(totals):
            total.end_core(halves[i].at[core], core_recvs[i])
            pltpu.make_async_copy(halves[i].at[core], half_outs[i], half_sem.at[i]).start()
        for i in range(len(totals)):
            pltpu.make_async_copy(halves[i].at[core], half_outs[i], half_sem.at[i]).wait()
        await_bytes(y_out.at[:, 0], local_sem.at[0])
        await_bytes(dx_out.at[0], local_sem.at[1])
        for sem in (y_send, y_recv):
            await_bytes(y_out.at[:, pl.ds(0, band_count - 1)], sem)
        for sem in (dx_send, dx_recv):
            await_bytes(dx_out.at[pl.ds(0, chunks - 1)], sem)


def band_layer(rows, cot, counts, slot_bands, g1, g2, params, flips, band_count, batch_count):
    project, gating, output_weight, expand, shrink = params
    slot_count, piece, model = rows.shape
    tokens = 2 * BLOCK
    steps = slot_count * piece // tokens
    heads, inner, hidden = gating.shape[0], output_weight.shape[0], expand.shape[1]
    groups = tokens // BLOCK
    taken = tokens // slot_count
    part_frames = 16
    per_part = part_frames // taken
    slots = slot_count // (band_count * batch_count)
    slot_dev = slot_count // band_count
    consts = (slot_bands, g1, g2, gating) + flips + (project, output_weight, expand, shrink)
    widths = (3 * inner, hidden, hidden, inner)
    chunks = band_count * batch_count
    blocks = pl.BlockSpec((slot_count, part_frames, model), lambda i: (0, i // per_part, 0))
    anywhere = pl.BlockSpec(memory_space=pl.ANY)
    dma = pltpu.SemaphoreType.DMA
    return pl.pallas_call(
        lambda *refs: band_kernel(heads, batch_count, band_count, *refs),
        grid=(steps,),
        out_shape=(
            jax.ShapeDtypeStruct((slot_dev // 2, band_count, steps, 2 * taken, model), BF16),
            jax.ShapeDtypeStruct((chunks, steps, slots * taken, model), BF16),
            [jax.ShapeDtypeStruct((model // 2, width), BF16) for width in widths],
            jax.ShapeDtypeStruct((model, 128), F32),
        ),
        in_specs=[blocks, blocks, pl.BlockSpec(memory_space=pltpu.SMEM)] + [whole_spec(c) for c in consts],
        out_specs=(
            anywhere,
            anywhere,
            [anywhere for _ in widths],
            pl.BlockSpec((model, 128), lambda i: (0, 0)),
        ),
        scratch_shapes=[
            pltpu.VMEM((inner, tokens), BF16),
            pltpu.VMEM((inner, tokens), BF16),
            pltpu.VMEM((inner, tokens), BF16),
            pltpu.VMEM((heads // 2 * groups, BLOCK, 2 * BLOCK), BF16),
            pltpu.VMEM((tokens, inner), BF16),
            pltpu.VMEM((heads, tokens), F32),
            pltpu.VMEM((heads, tokens), F32),
            pltpu.VMEM((inner, tokens), F32),
            pltpu.VMEM((inner, tokens), BF16),
            pltpu.VMEM((hidden, tokens), BF16),
            pltpu.VMEM((hidden, tokens), BF16),
            pltpu.VMEM((hidden, tokens), BF16),
            pltpu.VMEM((inner, tokens), F32),
            pltpu.VMEM((heads, tokens), F32),
            pltpu.VMEM((3 * inner, tokens), BF16),
            pltpu.VMEM((model, 3 * inner), F32),
            pltpu.VMEM((model, hidden), F32),
            pltpu.VMEM((model, hidden), F32),
            pltpu.VMEM((model, inner), F32),
            pltpu.VMEM((model, heads), F32),
            pltpu.VMEM((model, 1), F32),
            pltpu.VMEM((model, 1), F32),
            pltpu.VMEM((model // 128, slot_count * part_frames, 128), F32),
            pltpu.VMEM((model // 128, slot_count * part_frames, 128), F32),
            pltpu.VMEM((model // 128, tokens, 128), F32),
            pltpu.VMEM((model // 128, tokens, 128), F32),
            pltpu.VMEM((steps, slot_count // 2, 2 * taken, model), BF16),
            pltpu.VMEM((steps, chunks, slots * taken, model), BF16),
            dma,
            dma,
            dma,
            dma,
            dma((2,)),
            pltpu.VMEM((BLOCK, BLOCK), F32),
            pltpu.VMEM((inner // heads // 2, tokens), F32),
            pltpu.VMEM((inner // heads // 2, tokens), F32),
            pltpu.VMEM((1, tokens), F32),
            [pltpu.VMEM((2, model // 2, width), BF16) for width in widths],
            [pltpu.VMEM((model // 2, width), BF16) for width in widths],
            dma((2, len(widths), TOTAL_STEPS)),
            dma((len(widths),)),
        ],
        compiler_params=pltpu.CompilerParams(
            vmem_limit_bytes=VMEM_BYTES, collective_id=1, has_side_effects=True
        ),
        cost_estimate=cost(30.0e6 * slot_count * piece, 0, 60e6),
        name="band_layer",
    )(rows, cot, counts, *consts)


def slot_shards(activations, cotangent, frame_counts, slot_bands, *weights):
    slot_dev, _, frame_dev, model = activations.shape
    batch, band = lax.axis_size("batch"), lax.axis_size("band")
    g1, wp, wg, wo, g2, w1, w2 = weights[:7]
    band_g1, band_wp, band_wg, band_wo, band_g2, band_w1, band_w2 = weights[7:]
    heads = wg.shape[1]
    time_params = (wp, wg.T, wo, w1, w2)
    band_params = (band_wp, band_wg.T, band_wo, band_w1, band_w2)
    band_rows, band_cot, rows, n, q, k, v, p, linv, gate, att, mixed, mid, nf, act, slope, *turned = time_forward(
        activations.reshape(slot_dev, frame_dev, model),
        cotangent.reshape(slot_dev, frame_dev, model),
        frame_counts,
        g1,
        g2,
        time_params,
        band_params,
        band,
        batch,
    )
    cos, sin = turned[-2:]
    y, slot_grad, band_halves, band_narrow = band_layer(
        band_rows,
        band_cot,
        frame_counts,
        slot_bands,
        band_g1,
        band_g2,
        band_params,
        tuple(turned[:-2]),
        band,
        batch,
    )
    dmid, datt, minus, dlogit, ffn_halves, dg2, band_parts = time_ffn_backward(
        slot_grad, act, slope, nf, mid, mixed, att, gate, linv, g2, w1, w2, wo, band_halves
    )
    input_grad, band_sums, ffn_sums, pair_sums = time_attention_backward(
        p,
        q,
        k,
        v,
        datt,
        minus,
        dlogit,
        n,
        rows,
        dmid,
        cos,
        sin,
        g1,
        wp,
        time_params[1],
        band_narrow,
        dg2,
        band_parts,
        ffn_halves,
        batch,
    )
    layer_output, input_grad, *grads = finish_sums(
        input_grad, y, band_sums, ffn_sums, pair_sums, g1, time_params
    )
    grads = [g.T if g.shape[0] == heads else g for g in grads]
    return (layer_output.reshape(activations.shape), input_grad.reshape(activations.shape), *grads)


def shards(activations, cotangent, frame_counts, slot_bands, *weights):
    slot_dev, clips, frame_dev, _ = activations.shape
    batch, band = lax.axis_size("batch"), lax.axis_size("band")
    fits = (
        clips == 1
        and batch == 4
        and band == 2 * Z_COUNT
        and slot_dev % batch == 0
        and frame_dev == BLOCK
        and frame_dev == 32 * band
        and slot_bands.shape[0] == 64 == slot_dev * band
        and slot_dev == 2 * batch
        and activations.shape[-1] % 128 == 0
        and (frame_dev // band * slot_bands.shape[0]) % (2 * BLOCK) == 0
        and weights[2].shape[1] == 8
    )
    form = slot_shards if fits else generic_shards
    return form(activations, cotangent, frame_counts, slot_bands, *weights)


def solution(mesh):
    return jax.shard_map(
        shards,
        mesh=mesh,
        in_specs=(
            P("band", None, "batch", None),
            P("band", None, "batch", None),
            P(),
            P(),
            P(),
            P(),
            P(),
            P(),
            P(),
            P(),
            P(),
            P(),
            P(),
            P(),
            P(),
            P(),
            P(),
            P(),
        ),
        out_specs=(
            P("band", None, "batch", None),
            P("band", None, "batch", None),
            P(),
            P(),
            P(),
            P(),
            P(),
            P(),
            P(),
            P(),
            P(),
            P(),
            P(),
            P(),
            P(),
            P(),
        ),
        check_vma=False,
    )
```

```python
import math

import jax
import jax.numpy as jnp
from jax import lax
from jax.experimental import pallas as pl
from jax.experimental.pallas import tpu as pltpu
from jax.sharding import PartitionSpec as P

EPSILON = 1e-05
NEG_FILL = -1000000000.0
TIME_LAYOUT = ("bqhe", "bkhe")
BAND_LAYOUT = ("qbhe", "kbhe")


def rms_scale(residual, gain):
    return (
        residual * lax.rsqrt(jnp.mean(residual * residual, axis=-1, keepdims=True) + EPSILON) * gain
    )


def gelu_exact(values):
    return jax.nn.gelu(values, approximate=False)


def rotary_tables(positions, head_size):
    half_size = head_size // 2
    rates = jnp.exp(-math.log(10000.0) * jnp.arange(half_size, dtype=jnp.float32) / half_size)
    angles = positions[:, None] * rates[None, :]
    return (jnp.cos(angles), jnp.sin(angles))


def rotate(vectors, cos_table, sin_table):
    half_size = vectors.shape[-1] // 2
    first = vectors[..., :half_size]
    second = vectors[..., half_size:]
    return jnp.concatenate(
        [first * cos_table - second * sin_table, first * sin_table + second * cos_table], axis=-1
    )


def token_sum(left, right):
    return lax.dot_general(
        left.reshape(-1, left.shape[-1]),
        right.reshape(-1, right.shape[-1]),
        (((0,), (0,)), ((), ())),
        preferred_element_type=jnp.float32,
    )


def back_dot(gradient, weight):
    return lax.dot_general(
        gradient,
        weight,
        (((gradient.ndim - 1,), (1,)), ((), ())),
        preferred_element_type=jnp.float32,
    )


def block_forward(queries, key_rows, value_rows, key_valid, layout):
    query_form, key_form = layout
    scores = (
        jnp.einsum(
            query_form + "," + key_form + "->bhqk",
            queries,
            key_rows,
            preferred_element_type=jnp.float32,
        )
        * 0.125
    )
    scores = jnp.where(key_valid[:, None, None, :], scores, NEG_FILL)
    highest = jnp.max(scores, axis=-1, keepdims=True)
    exponents = jnp.exp(scores - highest)
    totals = jnp.sum(exponents, axis=-1, keepdims=True)
    soft_weights = (exponents / totals).astype(jnp.bfloat16)
    output = jnp.einsum(
        "bhqk," + key_form + "->" + query_form,
        soft_weights,
        value_rows,
        preferred_element_type=jnp.float32,
    )
    return (output, highest + jnp.log(totals))


def block_backward(queries, key_rows, value_rows, key_valid, log_totals, out_grad, layout):
    query_form, key_form = layout
    scores = (
        jnp.einsum(
            query_form + "," + key_form + "->bhqk",
            queries,
            key_rows,
            preferred_element_type=jnp.float32,
        )
        * 0.125
    )
    soft_weights = jnp.where(key_valid[:, None, None, :], jnp.exp(scores - log_totals), 0.0)
    weight_grad = jnp.einsum(
        query_form + "," + key_form + "->bhqk",
        out_grad,
        value_rows,
        preferred_element_type=jnp.float32,
    )
    score_grad = (
        soft_weights * (weight_grad - jnp.sum(soft_weights * weight_grad, axis=-1, keepdims=True))
    ).astype(jnp.bfloat16)
    query_grad = (
        jnp.einsum(
            "bhqk," + key_form + "->" + query_form,
            score_grad,
            key_rows,
            preferred_element_type=jnp.float32,
        )
        * 0.125
    )
    key_grad = (
        jnp.einsum(
            "bhqk," + query_form + "->" + key_form,
            score_grad,
            queries,
            preferred_element_type=jnp.float32,
        )
        * 0.125
    )
    value_grad = jnp.einsum(
        "bhqk," + query_form + "->" + key_form,
        soft_weights.astype(jnp.bfloat16),
        out_grad,
        preferred_element_type=jnp.float32,
    )
    return (query_grad, key_grad, value_grad)


def time_attend(queries, key_rows, value_rows, key_valid):
    keys_full, values_full = (
        lax.all_gather(key_rows, "batch", axis=1, tiled=True),
        lax.all_gather(value_rows, "batch", axis=1, tiled=True),
    )
    output, log_totals = block_forward(queries, keys_full, values_full, key_valid, TIME_LAYOUT)
    return (output, (log_totals, keys_full, values_full))


def time_attend_back(queries, key_rows, value_rows, key_valid, attn_kept, out_grad):
    log_totals, keys_full, values_full = attn_kept
    query_grad, key_full_grad, value_full_grad = block_backward(
        queries, keys_full, values_full, key_valid, log_totals, out_grad, TIME_LAYOUT
    )
    key_grad, value_grad = (
        lax.psum_scatter(
            key_full_grad.astype(jnp.bfloat16), "batch", scatter_dimension=1, tiled=True
        ).astype(jnp.float32),
        lax.psum_scatter(
            value_full_grad.astype(jnp.bfloat16), "batch", scatter_dimension=1, tiled=True
        ).astype(jnp.float32),
    )
    return (query_grad, key_grad, value_grad)


def band_attend(queries, key_rows, value_rows, key_valid):
    return block_forward(queries, key_rows, value_rows, key_valid, BAND_LAYOUT)


def band_attend_back(queries, key_rows, value_rows, key_valid, attn_kept, out_grad):
    return block_backward(
        queries, key_rows, value_rows, key_valid, attn_kept, out_grad, BAND_LAYOUT
    )


def layer_forward(residual, params, tables, key_valid, attend):
    prenorm, project, gating, output_weight, midnorm, expand, shrink = params
    cos_table, sin_table = tables
    normed = rms_scale(residual, prenorm.astype(jnp.float32)).astype(jnp.bfloat16)
    projected = jnp.dot(normed, project, preferred_element_type=jnp.float32)
    gate_logits = jnp.dot(normed, gating, preferred_element_type=jnp.float32)
    inner_width = output_weight.shape[0]
    head_count = gating.shape[1]
    head_shape = residual.shape[:-1] + (head_count, inner_width // head_count)
    queries = rotate(projected[..., :inner_width].reshape(head_shape), cos_table, sin_table).astype(
        jnp.bfloat16
    )
    key_rows = rotate(
        projected[..., inner_width : 2 * inner_width].reshape(head_shape), cos_table, sin_table
    ).astype(jnp.bfloat16)
    value_rows = projected[..., 2 * inner_width :].reshape(head_shape).astype(jnp.bfloat16)
    attended, attn_kept = attend(queries, key_rows, value_rows, key_valid)
    gate_values = jax.nn.sigmoid(gate_logits)
    mixed_heads = (
        (attended * gate_values[..., None])
        .reshape(residual.shape[:-1] + (inner_width,))
        .astype(jnp.bfloat16)
    )
    middle = residual + jnp.dot(mixed_heads, output_weight, preferred_element_type=jnp.float32)
    normed_ffn = rms_scale(middle, midnorm.astype(jnp.float32)).astype(jnp.bfloat16)
    hidden = jnp.dot(normed_ffn, expand, preferred_element_type=jnp.float32)
    active = gelu_exact(hidden).astype(jnp.bfloat16)
    result = middle + jnp.dot(active, shrink, preferred_element_type=jnp.float32)
    kept_values = (
        residual,
        normed,
        gate_logits,
        queries,
        key_rows,
        value_rows,
        attn_kept,
        attended,
        mixed_heads,
        middle,
        normed_ffn,
        hidden,
        active,
    )
    return (result, kept_values)


def layer_backward(result_grad, params, kept_values, tables, key_valid, attend_back):
    prenorm, project, gating, output_weight, midnorm, expand, shrink = params
    (
        residual,
        normed,
        gate_logits,
        queries,
        key_rows,
        value_rows,
        attn_kept,
        attended,
        mixed_heads,
        middle,
        normed_ffn,
        hidden,
        active,
    ) = kept_values
    cos_table, sin_table = tables
    branch_grad = result_grad.astype(jnp.bfloat16)
    shrink_grad = token_sum(active, branch_grad)
    active_grad = back_dot(branch_grad, shrink)
    hidden_grad = jax.vjp(gelu_exact, hidden)[1](active_grad)[0].astype(jnp.bfloat16)
    expand_grad = token_sum(normed_ffn, hidden_grad)
    normed_ffn_grad = back_dot(hidden_grad, expand)
    middle_norm_grad, midnorm_grad = jax.vjp(rms_scale, middle, midnorm.astype(jnp.float32))[1](
        normed_ffn_grad
    )
    middle_grad = result_grad + middle_norm_grad
    attn_branch = middle_grad.astype(jnp.bfloat16)
    output_grad = token_sum(mixed_heads, attn_branch)
    mixed_grad = back_dot(attn_branch, output_weight).reshape(attended.shape)
    gate_values = jax.nn.sigmoid(gate_logits)
    attended_grad = (mixed_grad * gate_values[..., None]).astype(jnp.bfloat16)
    logit_grad = (
        jnp.sum(mixed_grad * attended, axis=-1) * gate_values * (1.0 - gate_values)
    ).astype(jnp.bfloat16)
    query_grad, key_grad, value_grad = attend_back(
        queries, key_rows, value_rows, key_valid, attn_kept, attended_grad
    )
    flat_shape = residual.shape[:-1] + (-1,)
    projected_grad = jnp.concatenate(
        [
            rotate(query_grad, cos_table, -sin_table).reshape(flat_shape),
            rotate(key_grad, cos_table, -sin_table).reshape(flat_shape),
            value_grad.reshape(flat_shape),
        ],
        axis=-1,
    ).astype(jnp.bfloat16)
    project_grad = token_sum(normed, projected_grad)
    gating_grad = token_sum(normed, logit_grad)
    normed_grad = back_dot(projected_grad, project) + back_dot(logit_grad, gating)
    residual_norm_grad, prenorm_grad = jax.vjp(rms_scale, residual, prenorm.astype(jnp.float32))[1](
        normed_grad
    )
    return (
        middle_grad + residual_norm_grad,
        (
            prenorm_grad,
            project_grad,
            gating_grad,
            output_grad,
            midnorm_grad,
            expand_grad,
            shrink_grad,
        ),
    )


def generic_shards(
    activations,
    cotangent,
    frame_counts,
    slot_bands,
    time_prenorm,
    time_project,
    time_gating,
    time_output,
    time_midnorm,
    time_expand,
    time_shrink,
    band_prenorm,
    band_project,
    band_gating,
    band_output,
    band_midnorm,
    band_expand,
    band_shrink,
):
    slot_dev, clip_count, frame_dev, model_width = activations.shape
    slot_count = slot_bands.shape[0]
    frames_all = frame_dev * lax.axis_size("batch")
    head_size = time_output.shape[0] // time_gating.shape[1]
    time_params = (
        time_prenorm,
        time_project,
        time_gating,
        time_output,
        time_midnorm,
        time_expand,
        time_shrink,
    )
    band_params = (
        band_prenorm,
        band_project,
        band_gating,
        band_output,
        band_midnorm,
        band_expand,
        band_shrink,
    )
    own_bands = lax.dynamic_slice_in_dim(slot_bands, lax.axis_index("band") * slot_dev, slot_dev)
    frame_start = lax.axis_index("batch") * frame_dev
    own_frames = frame_start + jnp.arange(frame_dev, dtype=jnp.int32)
    frame_valid = own_frames[None, :] < frame_counts[:, None]
    row_valid = (own_bands >= 0)[:, None, None] & frame_valid[None]
    full_valid = jnp.arange(frames_all, dtype=jnp.int32)[None, :] < frame_counts[:, None]
    time_valid = jnp.broadcast_to(full_valid[None], (slot_dev, clip_count, frames_all)).reshape(
        slot_dev * clip_count, frames_all
    )
    time_cos, time_sin = rotary_tables(own_frames.astype(jnp.float32), head_size)
    time_tables = (time_cos[None, :, None, :], time_sin[None, :, None, :])
    band_cos, band_sin = rotary_tables(jnp.maximum(slot_bands, 0).astype(jnp.float32), head_size)
    band_tables = (band_cos[:, None, None, :], band_sin[:, None, None, :])
    residual = activations.astype(jnp.float32).reshape(
        slot_dev * clip_count, frame_dev, model_width
    )
    time_result, time_kept = layer_forward(
        residual, time_params, time_tables, time_valid, time_attend
    )
    masked_cot = jnp.where(row_valid[..., None], cotangent, jnp.zeros((), jnp.bfloat16)).reshape(
        slot_dev, clip_count * frame_dev, model_width
    )
    frame_rows = lax.all_to_all(
        time_result.astype(jnp.bfloat16), "band", split_axis=1, concat_axis=0, tiled=True
    ).astype(time_result.dtype)
    band_valid = jnp.broadcast_to((slot_bands >= 0)[None, :], (frame_rows.shape[1], slot_count))
    band_result, band_kept = layer_forward(
        frame_rows, band_params, band_tables, band_valid, band_attend
    )
    back_rows = lax.all_to_all(
        band_result.astype(jnp.bfloat16), "band", split_axis=0, concat_axis=1, tiled=True
    ).astype(band_result.dtype)
    layer_output = jnp.where(
        row_valid[..., None], back_rows.reshape(activations.shape), 0.0
    ).astype(jnp.bfloat16)
    frame_cot = lax.all_to_all(masked_cot, "band", split_axis=1, concat_axis=0, tiled=True)
    frame_grad, band_grads = layer_backward(
        frame_cot.astype(jnp.float32),
        band_params,
        band_kept,
        band_tables,
        band_valid,
        band_attend_back,
    )
    slot_grad = lax.all_to_all(
        frame_grad.astype(jnp.bfloat16), "band", split_axis=0, concat_axis=1, tiled=True
    ).astype(frame_grad.dtype)
    input_grad, time_grads = layer_backward(
        slot_grad, time_params, time_kept, time_tables, time_valid, time_attend_back
    )
    input_grad = input_grad.reshape(activations.shape)
    all_grads = lax.psum(
        (
            time_grads[0],
            time_grads[1],
            time_grads[2],
            time_grads[3],
            time_grads[4],
            time_grads[5],
            time_grads[6],
            band_grads[0],
            band_grads[1],
            band_grads[2],
            band_grads[3],
            band_grads[4],
            band_grads[5],
            band_grads[6],
        ),
        ("band", "batch"),
    )
    return (
        layer_output,
        input_grad,
        all_grads[0],
        all_grads[1],
        all_grads[2],
        all_grads[3],
        all_grads[4],
        all_grads[5],
        all_grads[6],
        all_grads[7],
        all_grads[8],
        all_grads[9],
        all_grads[10],
        all_grads[11],
        all_grads[12],
        all_grads[13],
    )


BLOCK = 256
LOG2E = 1.4426950408889634
F32 = jnp.float32
BF16 = jnp.bfloat16
NN = (((1,), (0,)), ((), ()))
NT = (((1,), (1,)), ((), ()))
TN = (((0,), (0,)), ((), ()))
VMEM_BYTES = 60 * 2**20


def dg(left, right, dims):
    return lax.dot_general(left, right, dims, preferred_element_type=F32)


def norm_forward(rows, gain):
    scale = lax.rsqrt(jnp.mean(rows * rows, axis=0, keepdims=True) + EPSILON)
    return (rows * scale * gain).astype(BF16)


def norm_backward(rows, gain, grad):
    scale = lax.rsqrt(jnp.mean(rows * rows, axis=0, keepdims=True) + EPSILON)
    unit = rows * scale
    scaled = grad * gain
    inner = jnp.mean(scaled * unit, axis=0, keepdims=True)
    return scale * (scaled - unit * inner), grad * unit


def gelu_pair(values):
    size = jnp.abs(values)
    denominator = 1.0 + (0.3275911 * math.sqrt(0.5)) * size
    t = pl.reciprocal(denominator, approx=True)
    t = t * (2.0 - denominator * t)
    bell = jnp.exp2(values * values * (-0.5 * LOG2E))
    poly = 0.5 * 1.061405429
    for coefficient in (-1.453152027, 1.421413741, -0.284496736, 0.254829592):
        poly = poly * t + 0.5 * coefficient
    tail = poly * t * bell
    upper = jnp.where(values < 0.0, tail, 1.0 - tail)
    slope = upper + values * bell * (1.0 / math.sqrt(2.0 * math.pi))
    return values * upper, slope


def feed_forward(middle, normed, w1t_ref, w2t_ref, act_ref, slope_ref):
    part = w1t_ref.shape[0] // 3
    result = middle
    hidden = dg(w1t_ref[0:part, :], normed, NN)
    for i in range(3):
        rows = slice(i * part, (i + 1) * part)
        later = None
        if i < 2:
            later = dg(w1t_ref[(i + 1) * part : (i + 2) * part, :], normed, NN)
        active, slope = gelu_pair(hidden)
        active = active.astype(BF16)
        act_ref[rows, :] = active
        slope_ref[rows, :] = slope.astype(BF16)
        result = result + dg(w2t_ref[:, rows], active, NN)
        hidden = later
    return result


def turn(vectors, cos, sin):
    half = cos.shape[0]
    split = vectors.reshape(-1, 2 * half, vectors.shape[-1])
    first = split[:, :half]
    second = split[:, half:]
    turned = jnp.concatenate([first * cos - second * sin, first * sin + second * cos], axis=1)
    return turned.reshape(vectors.shape)


def three_parts(values):
    top = values.astype(BF16).astype(F32)
    rest = values - top
    middle = rest.astype(BF16).astype(F32)
    return top, middle, rest - middle


def extra_rows(rows, width):
    tile = jnp.concatenate(rows + [jnp.zeros((8 - len(rows), width), F32)], axis=0)
    return jnp.concatenate([tile, jnp.zeros((8, width), F32)], axis=0).astype(BF16)


def project_block(normed, wpt_ref, cos, sin, inner, scale):
    queries = turn(dg(wpt_ref[0:inner, :], normed, NN), cos, sin) * scale
    keys = turn(dg(wpt_ref[inner : 2 * inner, :], normed, NN), cos, sin)
    values = dg(wpt_ref[2 * inner : 3 * inner, :], normed, NN)
    return queries.astype(BF16), keys.astype(BF16), values.astype(BF16)


def column(gain_ref):
    row = gain_ref[...].astype(F32).reshape(1, gain_ref.shape[0])
    return jnp.broadcast_to(row, (8, row.shape[1])).T[:, :1]


def rotary_rows(positions, half):
    rank = lax.broadcasted_iota(jnp.int32, (half, positions.shape[1]), 0).astype(F32)
    angles = positions * jnp.exp(-math.log(10000.0) * rank / half)
    return jnp.cos(angles), jnp.sin(angles)


def flipped(ref):
    return ref[...].astype(F32).T.astype(BF16)


def greet_all(band_count, batch_count):
    count = band_count * batch_count
    me = lax.axis_index("band") * batch_count + lax.axis_index("batch")
    barrier = pltpu.get_barrier_semaphore()

    def signal(i, carry):
        other = lax.rem(me + i, count)
        pl.semaphore_signal(
            barrier,
            inc=1,
            device_id=(other // batch_count, lax.rem(other, batch_count)),
            device_id_type=pl.DeviceIdType.MESH,
        )
        return carry

    lax.fori_loop(1, count, signal, 0)
    pl.semaphore_wait(barrier, count - 1)


def send(source, target, send_sem, recv_sem, band, batch):
    pltpu.make_async_remote_copy(
        src_ref=source,
        dst_ref=target,
        send_sem=send_sem,
        recv_sem=recv_sem,
        device_id=(band, batch),
        device_id_type=pl.DeviceIdType.MESH,
    ).start()


def await_bytes(ref, sem):
    pltpu.make_async_copy(ref, ref, sem).wait()


class Place:
    def __init__(self):
        self.band, self.batch = lax.axis_index("band"), lax.axis_index("batch")
        self.bits = {
            "core": lax.rem(self.batch, 2),
            "x": self.batch // 2,
            "y": lax.rem(self.band, 2),
        }
        self.z = self.band // 2

    def across(self, axis):
        bit = self.bits[axis]
        if axis == "core":
            return self.band, self.batch + 1 - 2 * bit
        if axis == "x":
            return self.band, self.batch + 2 - 4 * bit
        return self.band + 1 - 2 * bit, self.batch

    def along_z(self, step):
        other = lax.rem(self.z + step, Z_COUNT)
        return other, (other * 2 + self.bits["y"], self.batch)


Z_COUNT = 4


def greet(others):
    barrier = pltpu.get_barrier_semaphore()
    for other in others:
        pl.semaphore_signal(barrier, inc=1, device_id=other, device_id_type=pl.DeviceIdType.MESH)
    pl.semaphore_wait(barrier, len(others))


class Total:
    def __init__(self, place, order, sends, recvs):
        self.place = place
        self.order = order
        self.sends, self.recvs = sends, recvs
        self.core = place.bits["core"]
        if order is not None:
            self.first, self.second = (place.bits[axis] for axis in order)

    def give(self, step, source, target, other):
        send(source, target, self.sends.at[step], self.recvs.at[step], *other)

    def took(self, step, ref):
        await_bytes(ref, self.recvs.at[step])
        await_bytes(ref, self.sends.at[step])

    def add(self, ref, rows, part):
        ref[rows] = (ref[rows].astype(F32) + part.astype(F32)).astype(BF16)

    def start_core(self, source, recv):
        self.give(0, source.at[1 - self.core], recv, self.place.across("core"))

    def end_core(self, held, recv):
        self.took(0, recv)
        held[...] = (held[...].astype(F32) + recv[...].astype(F32)).astype(BF16)

    def half_rows(self, held, level):
        rows = held.shape[0] // 2
        base = 0
        if level == 2:
            base, rows = self.first * rows, rows // 2
        bit = self.first if level == 1 else self.second
        keep = pl.ds(pl.multiple_of(base + bit * rows, rows), rows)
        away = pl.ds(pl.multiple_of(base + (1 - bit) * rows, rows), rows)
        return keep, away

    def start_half(self, level, held, recv):
        away = self.half_rows(held, level)[1]
        self.give(level, held.at[away], recv, self.place.across(self.order[level - 1]))

    def end_half(self, level, held, recv):
        self.took(level, recv)
        self.add(held, self.half_rows(held, level)[0], recv[...])

    def start_z(self, piece, recv):
        width = recv.shape[2]
        for step in range(1, Z_COUNT):
            index, other = self.place.along_z(step)
            lanes = pl.ds(pl.multiple_of(index * width, 128), width)
            self.give(3, piece.at[:, lanes], recv.at[step - 1], other)

    def z_lanes(self, width):
        return pl.ds(pl.multiple_of(self.place.z * width, 128), width)

    def end_z(self, piece, recv):
        self.took(3, recv)
        lanes = self.z_lanes(recv.shape[2])
        sums = piece[:, lanes].astype(F32)
        for step in range(Z_COUNT - 1):
            sums = sums + recv[step].astype(F32)
        piece[:, lanes] = sums.astype(BF16)

    def own_copy(self, piece, target, width, sem):
        lanes = self.z_lanes(width)
        return pltpu.make_async_copy(piece.at[:, lanes], target.at[:, lanes], sem)

    def start_z_back(self, piece, target, width, sem):
        lanes = self.z_lanes(width)
        for step in range(1, Z_COUNT):
            _, other = self.place.along_z(step)
            self.give(4, piece.at[:, lanes], target.at[:, lanes], other)
        self.own_copy(piece, target, width, sem).start()

    def end_z_back(self, piece, target, width, sem):
        self.took(4, target.at[:, pl.ds(0, (Z_COUNT - 1) * width)])
        self.own_copy(piece, target, width, sem).wait()

    def around(self):
        found = []
        for step in range(1, 4 * Z_COUNT):
            x = lax.rem(self.place.bits["x"] + step // 2 % 2, 2)
            y = lax.rem(self.place.bits["y"] + step % 2, 2)
            z = lax.rem(self.place.z + step // 4, Z_COUNT)
            found.append((2 * x + y, z, (2 * z + y, 2 * x + self.core)))
        return found

    def tile(self, ref, base, quarter, z, shape):
        rows = pl.ds(pl.multiple_of(base + quarter * shape[0], shape[0]), shape[0])
        return ref.at[rows, pl.ds(pl.multiple_of(z * shape[1], 128), shape[1])]

    def start_around(self, held, recv):
        for i, (quarter, z, other) in enumerate(self.around()):
            self.give(1, self.tile(held, 0, quarter, z, recv.shape[1:]), recv.at[i], other)

    def own_tile(self, ref, base, shape):
        return self.tile(ref, base, 2 * self.place.bits["x"] + self.place.bits["y"], self.place.z, shape)

    def end_around(self, held, recv):
        self.took(1, recv)
        own = self.own_tile(held, 0, recv.shape[1:])
        sums = own[...].astype(F32)
        for i in range(recv.shape[0]):
            sums = sums + recv[i].astype(F32)
        own[...] = sums.astype(BF16)

    def start_around_back(self, held, recv, out, sem):
        shape = recv.shape[1:]
        own = self.own_tile(held, 0, shape)
        target = self.own_tile(out, self.core * (out.shape[0] // 2), shape)
        for _, _, other in self.around():
            self.give(2, own, target, other)
        pltpu.make_async_copy(own, target, sem).start()

    def end_around_back(self, held, recv, out, sem):
        shape = recv.shape[1:]
        self.took(2, recv)
        target = self.own_tile(out, self.core * (out.shape[0] // 2), shape)
        pltpu.make_async_copy(self.own_tile(held, 0, shape), target, sem).wait()

    def back_rows(self, out, level):
        rows = out.shape[0] // 2
        base = self.core * rows
        if level >= 1:
            rows = rows // 2
            base = base + self.first * rows
        if level >= 2:
            rows = rows // 2
            base = base + self.second * rows
        return pl.ds(pl.multiple_of(base, rows), rows)

    def start_back(self, level, out, source=None):
        rows = self.back_rows(out, level)
        axis = "core" if level == 0 else self.order[level - 1]
        self.give(7 - level, out.at[rows] if source is None else source, out.at[rows], self.place.across(axis))

    def end_back(self, level, out):
        self.took(7 - level, out.at[self.back_rows(out, level)])


TOTAL_STEPS = 8


def time_forward_kernel(
    heads,
    batch_count,
    band_count,
    act_in,
    cot_in,
    count_ref,
    g1_ref,
    g2_ref,
    wgt_ref,
    wp_ref,
    wo_ref,
    w1_ref,
    w2_ref,
    band_wp_ref,
    band_wo_ref,
    band_w1_ref,
    band_w2_ref,
    band_rows,
    band_cot,
    rows_ref,
    n_ref,
    q_ref,
    k_ref,
    v_ref,
    p_ref,
    linv_ref,
    gate_ref,
    att_ref,
    mixed_ref,
    mid_ref,
    nf_ref,
    act_ref,
    slope_ref,
    band_wpt_ref,
    band_wot_ref,
    band_w1t_ref,
    band_w2t_ref,
    cos_ref,
    sin_ref,
    xt_ref,
    x_ref,
    result_ref,
    wpt_ref,
    wot_ref,
    w1t_ref,
    w2t_ref,
    row_send,
    row_recv,
    cot_send,
    cot_recv,
    result_send,
    result_recv,
    local_sem,
):
    slot, head = pl.program_id(0), pl.program_id(1)
    slots = pl.num_programs(0)
    slot_dev = cot_in.shape[0]
    frames, model = rows_ref.shape[1:]
    inner = q_ref.shape[1]
    size = inner // heads
    my_band, my_batch = lax.axis_index("band"), lax.axis_index("batch")
    frame_dev = frames // batch_count
    piece = frame_dev // band_count
    own_rows = pl.ds(pl.multiple_of(my_batch * frame_dev, frame_dev), frame_dev)
    held = x_ref.shape[0]
    frame_index = lax.broadcasted_iota(jnp.int32, (1, frames), 1)

    def neighbour(i):
        core, x = lax.rem(my_batch, 2), my_batch // 2
        return lax.rem(x + i // 2, 2) * 2 + lax.rem(core + lax.rem(i, 2), 2)

    def own_row_copy(j):
        return pltpu.make_async_copy(
            act_in.at[batch_count * j + my_batch], x_ref.at[j, own_rows], local_sem.at[j]
        )

    def own_cot_copy():
        return pltpu.make_async_copy(
            cot_in.at[:, pl.ds(pl.multiple_of(my_band * piece, piece), piece)],
            band_cot.at[pl.ds(my_band * slot_dev, slot_dev)],
            local_sem.at[held],
        )

    @pl.when((slot == 0) & (head == 0))
    def start():
        greet_all(band_count, batch_count)
        for j in range(held):
            for i in range(1, batch_count):
                other = neighbour(i)
                send(
                    act_in.at[batch_count * j + other],
                    x_ref.at[j, own_rows],
                    row_send,
                    row_recv.at[j, i],
                    my_band,
                    other,
                )
            own_row_copy(j).start()

        def send_cot(i, carry):
            other = lax.rem(my_band + i, band_count)
            send(
                cot_in.at[:, pl.ds(pl.multiple_of(other * piece, piece), piece)],
                band_cot.at[pl.ds(my_band * slot_dev, slot_dev)],
                cot_send,
                cot_recv,
                other,
                my_batch,
            )
            return carry

        lax.fori_loop(1, band_count, send_cot, 0)
        own_cot_copy().start()
        cos_ref[...], sin_ref[...] = rotary_rows(frame_index.astype(F32), size // 2)
        wpt_ref[...] = flipped(wp_ref)
        wot_ref[...] = flipped(wo_ref)
        w1t_ref[...] = flipped(w1_ref)
        w2t_ref[...] = flipped(w2_ref)
        band_wpt_ref[...] = flipped(band_wp_ref)
        band_wot_ref[...] = flipped(band_wo_ref)
        band_w1t_ref[...] = flipped(band_w1_ref)
        band_w2t_ref[...] = flipped(band_w2_ref)

    @pl.when(head == 0)
    def before():
        gain = column(g1_ref)

        def block(i, carry):
            at = pl.ds(pl.multiple_of(neighbour(i) * BLOCK, BLOCK), BLOCK)

            @pl.when(i == 0)
            def own():
                for j in range(held):

                    @pl.when(slot == j)
                    def kept():
                        own_row_copy(j).wait()

            @pl.when(i > 0)
            def arrived():
                await_bytes(x_ref.at[slot, at], row_recv.at[slot, i])

            held_rows = x_ref[slot, at, :]
            rows_ref[0, at, :] = held_rows
            rows = held_rows.astype(F32).T
            xt_ref[:, at] = rows
            normed = norm_forward(rows, gain)
            n_ref[0, :, at] = normed
            queries, keys, values = project_block(
                normed, wpt_ref, cos_ref[:, at], sin_ref[:, at], inner, LOG2E * size**-0.5
            )
            q_ref[0, :, at] = queries
            k_ref[0, :, at] = keys
            v_ref[0, :, at] = values
            gate_ref[0, :, at] = dg(wgt_ref[...], normed, NN)
            return carry

        lax.fori_loop(0, frames // BLOCK, block, 0, unroll=1)

    at_head = pl.ds(pl.multiple_of(head * size, size), size)
    ones = jnp.ones((1, frames), F32)
    queries = jnp.concatenate([q_ref[0, at_head, :], extra_rows([ones], frames)], axis=0)
    keys = jnp.concatenate([k_ref[0, at_head, :], extra_rows([jnp.where(frame_index < count_ref[0], 0.0, NEG_FILL)], frames)], axis=0)
    values = jnp.concatenate([v_ref[0, at_head, :], extra_rows([ones], frames)], axis=0)
    scores = dg(keys, queries, TN)
    weights = jnp.exp2(scores - jnp.max(scores, axis=0, keepdims=True)).astype(BF16)
    p_ref[0, 0] = weights
    sums = dg(values, weights, NN)
    inverse = 1.0 / sums[size : size + 1]
    attended = sums[:size] * inverse
    linv_ref[0, pl.ds(head, 1), :] = inverse
    att_ref[0, at_head, :] = attended
    gate = jax.nn.sigmoid(gate_ref[0, pl.ds(head, 1), :])
    mixed_ref[0, at_head, :] = (attended * gate).astype(BF16)

    @pl.when(head == heads - 1)
    def after():
        gain = column(g2_ref)
        to_slot = my_band * slot_dev + batch_count * slot + my_batch

        def block(i, carry):
            at = pl.ds(pl.multiple_of(i * BLOCK, BLOCK), BLOCK)
            middle = xt_ref[:, at] + dg(wot_ref[...], mixed_ref[0, :, at], NN)
            mid_ref[0, :, at] = middle
            normed = norm_forward(middle, gain)
            nf_ref[0, :, at] = normed
            result = feed_forward(
                middle, normed, w1t_ref, w2t_ref, act_ref.at[0, :, at], slope_ref.at[0, :, at]
            )
            result_ref[slot, at, :] = result.T.astype(BF16)

            def send_result(j, carry):
                other = lax.rem(my_band + j, band_count)
                source = result_ref.at[slot, pl.ds(pl.multiple_of(i * frame_dev + other * piece, piece), piece)]
                mine = (other == my_band) & (i == my_batch)

                @pl.when(mine)
                def keep():
                    pltpu.make_async_copy(source, band_rows.at[to_slot], local_sem.at[held + 1]).start()

                @pl.when(jnp.logical_not(mine))
                def give():
                    send(source, band_rows.at[to_slot], result_send, result_recv, other, i)

                return carry

            lax.fori_loop(1, band_count + 1, send_result, 0)
            return carry

        lax.fori_loop(0, frames // BLOCK, block, 0, unroll=1)

    @pl.when((slot == slots - 1) & (head == heads - 1))
    def finish():
        others = held * (band_count * batch_count - 1)
        others_cot = (band_count - 1) * slot_dev
        others_rows = (batch_count - 1) * frame_dev
        await_bytes(band_cot.at[pl.ds(0, others_cot)], cot_recv)
        await_bytes(band_cot.at[pl.ds(0, others_cot)], cot_send)
        own_cot_copy().wait()
        await_bytes(x_ref.at[:, pl.ds(0, others_rows)], row_send)
        await_bytes(band_rows.at[pl.ds(0, others)], result_send)
        await_bytes(band_rows.at[pl.ds(0, held)], local_sem.at[held + 1])
        await_bytes(band_rows.at[pl.ds(0, others)], result_recv)


def cost(flops, exps=0, moved=0):
    return pl.CostEstimate(flops=int(flops), bytes_accessed=int(moved), transcendentals=int(exps))


def whole_spec(array):
    nd = array.ndim
    return pl.BlockSpec(array.shape, lambda *ids: (0,) * nd, pipeline_mode=pl.Buffered(1))


def time_forward(activations, cotangent, counts, g1, g2, params, band_params, band_count, batch_count):
    wp, wgt, wo, w1, w2 = params
    bwp, _, bwo, bw1, bw2 = band_params
    slot_dev, frame_dev, model = activations.shape
    slots, frames = slot_dev // batch_count, frame_dev * batch_count
    heads, inner, hidden = wgt.shape[0], wo.shape[0], w1.shape[1]
    piece = frame_dev // band_count

    def per_slot(*shape):
        return pl.BlockSpec((1,) + shape, lambda s, h: (s,) + (0,) * len(shape))

    outs = [
        ((frames, model), BF16),
        ((model, frames), BF16),
        ((inner, frames), BF16),
        ((inner, frames), BF16),
        ((inner, frames), BF16),
        None,
        ((heads, frames), F32),
        ((heads, frames), F32),
        ((inner, frames), F32),
        ((inner, frames), BF16),
        ((model, frames), F32),
        ((model, frames), BF16),
        ((hidden, frames), BF16),
        ((hidden, frames), BF16),
    ]
    flips = [(w.shape[1], w.shape[0]) for w in (bwp, bwo, bw1, bw2)]
    own_flips = [(w.shape[1], w.shape[0]) for w in (wp, wo, w1, w2)]
    exchanged = jax.ShapeDtypeStruct((slot_dev * band_count, piece, model), BF16)
    anywhere = pl.BlockSpec(memory_space=pl.ANY)
    shapes, specs = [exchanged, exchanged], [anywhere, anywhere]
    for entry in outs:
        if entry is None:
            shapes.append(jax.ShapeDtypeStruct((slots, heads, frames, frames), BF16))
            specs.append(pl.BlockSpec((1, 1, frames, frames), lambda s, h: (s, h, 0, 0)))
        else:
            shapes.append(jax.ShapeDtypeStruct((slots,) + entry[0], entry[1]))
            specs.append(per_slot(*entry[0]))
    for shape in flips:
        shapes.append(jax.ShapeDtypeStruct(shape, BF16))
        specs.append(pl.BlockSpec(shape, lambda s, h: (0, 0), pipeline_mode=pl.Buffered(1)))
    consts = (g1, g2, wgt, wp, wo, w1, w2, bwp, bwo, bw1, bw2)
    half = inner // heads // 2
    for _ in range(2):
        shapes.append(jax.ShapeDtypeStruct((half, frames), F32))
        specs.append(pl.BlockSpec((half, frames), lambda s, h: (0, 0)))
    dma = pltpu.SemaphoreType.DMA
    return pl.pallas_call(
        lambda *refs: time_forward_kernel(heads, batch_count, band_count, *refs),
        grid=(slots, heads),
        out_shape=shapes,
        in_specs=[anywhere, anywhere, pl.BlockSpec(memory_space=pltpu.SMEM)] + [whole_spec(c) for c in consts],
        out_specs=specs,
        scratch_shapes=[
            pltpu.VMEM((model, frames), F32),
            pltpu.VMEM((slots, frames, model), BF16),
            pltpu.VMEM((slots, frames, model), BF16),
        ]
        + [pltpu.VMEM(shape, BF16) for shape in own_flips]
        + [dma, dma((slots, batch_count)), dma, dma, dma, dma, dma((slots + 2,))],
        compiler_params=pltpu.CompilerParams(
            vmem_limit_bytes=VMEM_BYTES, collective_id=0, has_side_effects=True
        ),
        cost_estimate=cost(2.0e6 * 4 * slots * frames, 2 * slots * heads * frames * frames, 60e6),
        name="time_forward",
    )(activations, cotangent, counts, *consts)


def ffn_backward(grad, slope, middle, gain, w1_ref, w2_ref, dg2_ref):
    branch = grad.astype(BF16)
    d_hidden = (dg(w2_ref[...], branch, NN) * slope.astype(F32)).astype(BF16)
    d_normed = dg(w1_ref[...], d_hidden, NN)
    d_rows, terms = norm_backward(middle, gain, d_normed)
    dg2_ref[...] += jnp.sum(terms, axis=1, keepdims=True)
    return grad + d_rows, branch, d_hidden


def add_ffn_sums(dw1_ref, dw2t_ref, branch, act, normed, d_hidden):
    dw2t_ref[...] += dg(branch, act, NT)
    dw1_ref[...] += dg(normed, d_hidden, NT)


def head_backward(d_mixed, attended, gate_logit, inverse):
    gate = jax.nn.sigmoid(gate_logit)
    d_logit = jnp.sum(d_mixed * attended, axis=0, keepdims=True) * gate * (1.0 - gate)
    d_att = (d_mixed * (gate * inverse)).astype(BF16)
    minus = -jnp.sum(d_att.astype(F32) * attended, axis=0, keepdims=True)
    return d_att, minus, d_logit


def scores_backward(queries, keys, values, weights, d_att, minus, cos, sin, scale):
    width = queries.shape[1]
    ones = jnp.ones((1, width), F32)
    d_weights = dg(
        jnp.concatenate([values, extra_rows([ones, ones, ones], width)], axis=0),
        jnp.concatenate([d_att, extra_rows(list(three_parts(minus)), width)], axis=0),
        TN,
    )
    d_scores = (weights.astype(F32) * d_weights).astype(BF16)
    d_values = dg(d_att, weights, NT)
    d_queries = dg(keys, d_scores, NN) * scale
    d_keys = dg(queries, d_scores, NT) * (1.0 / LOG2E)
    return turn(d_queries, cos, -sin), turn(d_keys, cos, -sin), d_values


def time_ffn_backward_kernel(
    heads,
    grad_ref,
    act_ref,
    slope_ref,
    nf_ref,
    mid_ref,
    mixed_ref,
    att_ref,
    gate_ref,
    linv_ref,
    g2_ref,
    w1_ref,
    w2_ref,
    wo_ref,
    half_refs,
    dmid_ref,
    datt_ref,
    minus_ref,
    dlogit_ref,
    sums_refs,
    dg2_out,
    part_refs,
    dw1_ref,
    dw2t_ref,
    dwot_ref,
    dg2_ref,
    held_refs,
    half_recvs,
    z_recvs,
    sends,
    recvs,
    local_sem,
):
    place = Place()
    totals = [Total(place, order, sends.at[i], recvs.at[i]) for i, order in enumerate(BAND_ORDERS)]
    early = len(z_recvs)
    work = list(zip(totals, half_refs, held_refs, half_recvs))

    def half_copy(i):
        return pltpu.make_async_copy(half_refs[i], held_refs[i], local_sem.at[i])

    def part_copy(i):
        rows = totals[i].half_rows(held_refs[i], 2)[0]
        return pltpu.make_async_copy(held_refs[i].at[rows], part_refs[i], local_sem.at[len(totals) + i])

    step = pl.program_id(0) * pl.num_programs(1) + pl.program_id(1)
    last = pl.num_programs(0) * pl.num_programs(1) - 1
    size = wo_ref.shape[0] // heads

    @pl.when(step == 0)
    def clear():
        for ref in (dw1_ref, dw2t_ref, dwot_ref, dg2_ref):
            ref[...] = jnp.zeros_like(ref)
        greet([place.across("x"), place.across("y")] + [place.along_z(i)[1] for i in range(1, Z_COUNT)])
        for i, (total, halves, held, recv) in enumerate(work):
            half_copy(i).start()
            total.start_half(1, halves, recv[0])

    def eighth(i):
        return held_refs[i].at[totals[i].half_rows(held_refs[i], 2)[0]]

    @pl.when(step == last - 1)
    def first_half():
        for i, (total, halves, held, recv) in list(enumerate(work))[:early]:
            half_copy(i).wait()
            total.end_half(1, held, recv[0])
            total.start_half(2, held, recv[1])

    @pl.when(step == last)
    def second_half():
        for i, (total, halves, held, recv) in list(enumerate(work))[early:]:
            half_copy(i).wait()
            total.end_half(1, held, recv[0])
            total.start_half(2, held, recv[1])
        for i, (total, halves, held, recv) in list(enumerate(work))[:early]:
            total.end_half(2, held, recv[1])
            total.start_z(eighth(i), z_recvs[i])

    slot = pl.program_id(0)
    chunks, parts, rows, model = grad_ref.shape
    slots = pl.num_programs(0)
    taken = rows // slots
    both = grad_ref[...].astype(F32).reshape(chunks * parts, slots, taken, model)
    grad = both[:, 0]
    for j in range(1, slots):
        grad = jnp.where(slot == j, both[:, j], grad)
    grad = grad.reshape(chunks * parts * taken, model).T
    d_middle, branch, d_hidden = ffn_backward(
        grad, slope_ref[0], mid_ref[0], column(g2_ref), w1_ref, w2_ref, dg2_ref
    )
    add_ffn_sums(dw1_ref, dw2t_ref, branch, act_ref[0], nf_ref[0], d_hidden)
    dmid_ref[0] = d_middle
    branch = d_middle.astype(BF16)
    dwot_ref[...] += dg(branch, mixed_ref[0], NT)
    d_mixed = dg(wo_ref[...], branch, NN)
    logits, minuses = [], []
    for head in range(heads):
        at = slice(head * size, (head + 1) * size)
        d_att, minus, d_logit = head_backward(
            d_mixed[at], att_ref[0, at], gate_ref[0, head : head + 1], linv_ref[0, head : head + 1]
        )
        datt_ref[0, at] = d_att
        minuses.append(minus)
        logits.append(d_logit)
    minus_ref[0] = jnp.concatenate(minuses, axis=0)
    dlogit_ref[0] = jnp.concatenate(logits, axis=0)

    @pl.when(step == last)
    def finish():
        for sums, ref in zip(sums_refs, (dw2t_ref, dw1_ref, dwot_ref)):
            lay_halves(sums, 0, ref)
        dg2_out[...] = dg2_ref[...]
        for i, (total, halves, held, recv) in list(enumerate(work))[early:]:
            total.end_half(2, held, recv[1])
            part_copy(i).start()
        for i, (total, halves, held, recv) in list(enumerate(work))[:early]:
            total.end_z(eighth(i), z_recvs[i])
            part_copy(i).start()
        for i in range(len(work)):
            part_copy(i).wait()


def narrow_tile(parts, rows):
    used = sum(part.shape[1] for part in parts)
    return jnp.concatenate(list(parts) + [jnp.zeros((rows, 128 - used), F32)], axis=1)


def lay_halves(target, at, ref):
    rows, width = ref.shape
    for half in range(2):
        target[half, :, at : at + width] = ref[half * rows // 2 : (half + 1) * rows // 2].astype(BF16)


XY, YX = ("x", "y"), ("y", "x")
BAND_ORDERS = (YX, XY, YX, XY)
BAND_EARLY = 2
FFN_ORDERS = (YX, XY, YX)
PAIR_ORDERS = (YX, YX, YX, None)


def time_ffn_backward(grad, act, slope, nf, mid, mixed, att, gate, linv, g2, w1, w2, wo, halves_in):
    slots, model, frames = mid.shape
    heads = gate.shape[1]
    inner, hidden = wo.shape[0], w1.shape[1]
    chunks, parts, _, _ = grad.shape
    tokens = frames // 2

    def cut(rows):
        return pl.BlockSpec((1, rows, tokens), lambda s, c: (s, 0, c))

    def whole(*shape):
        return pl.BlockSpec(shape, lambda s, c: (0,) * len(shape))

    consts = (g2, w1, w2, wo)
    anywhere = pl.BlockSpec(memory_space=pl.ANY)
    halves = [(2, model // 2, width) for width in (hidden, hidden, inner)]
    widths = [a.shape[1] for a in halves_in]
    dma = pltpu.SemaphoreType.DMA
    return pl.pallas_call(
        lambda *refs: time_ffn_backward_kernel(heads, *refs),
        grid=(slots, frames // tokens),
        out_shape=(
            jax.ShapeDtypeStruct((slots, model, frames), F32),
            jax.ShapeDtypeStruct((slots, inner, frames), BF16),
            jax.ShapeDtypeStruct((slots, heads, frames), F32),
            jax.ShapeDtypeStruct((slots, heads, frames), F32),
            [jax.ShapeDtypeStruct(shape, BF16) for shape in halves],
            jax.ShapeDtypeStruct((model, 1), F32),
            [jax.ShapeDtypeStruct((model // 8, width), BF16) for width in widths],
        ),
        in_specs=[pl.BlockSpec((chunks // 2,) + grad.shape[1:], lambda s, c: (c, 0, 0, 0))]
        + [cut(a.shape[1]) for a in (act, slope, nf, mid, mixed, att, gate, linv)]
        + [whole_spec(c) for c in consts]
        + [[anywhere for _ in widths]],
        out_specs=(
            cut(model),
            cut(inner),
            cut(heads),
            cut(heads),
            [whole(*shape) for shape in halves],
            whole(model, 1),
            [anywhere for _ in widths],
        ),
        scratch_shapes=[
            pltpu.VMEM((model, hidden), F32),
            pltpu.VMEM((model, hidden), F32),
            pltpu.VMEM((model, inner), F32),
            pltpu.VMEM((model, 1), F32),
            [pltpu.VMEM((model // 2, width), BF16) for width in widths],
            [
                [pltpu.VMEM((rows, width), BF16) for rows in (model // 4, model // 8)]
                for width in widths
            ],
            [pltpu.VMEM((Z_COUNT - 1, model // 8, width // Z_COUNT), BF16) for width in widths[:BAND_EARLY]],
            dma((len(widths), TOTAL_STEPS)),
            dma((len(widths), TOTAL_STEPS)),
            dma((2 * len(widths),)),
        ],
        compiler_params=pltpu.CompilerParams(
            vmem_limit_bytes=VMEM_BYTES, collective_id=2, has_side_effects=True
        ),
        cost_estimate=cost(8.0e6 * slots * frames, 0, 30e6),
        name="time_ffn_backward",
    )(grad, act, slope, nf, mid, mixed, att, gate, linv, *consts, list(halves_in))


BAND_PLACES = ((0, 4, 7, 11, 13), (0, 4, 7, 12, 14), (0, 4, 7, 11, 16, 18), (0, 5, 8, 12, 16, 18))
FFN_PLACES = ((0, 1, 5, 8, 12, 15, 18, 24, 25), (0, 2, 6, 10, 13, 16, 20, 24, 25), (0, 2, 6, 9, 12, 15, 18, 22, 24))
PAIR_PLACES = (
    (4, 5, 8, 12, 15, 18, 22, 24, 25),
    (8, 9, 12, 15, 17, 20, 23, 24, 25),
    (12, 13, 15, 18, 21, 24, 25, 26, 27),
    (16, 17, 21, 24, 25),
)


def time_attention_backward_kernel(
    heads,
    slots,
    batch_count,
    p_ref,
    q_ref,
    k_ref,
    v_ref,
    datt_ref,
    minus_ref,
    x_ref,
    dmid_ref,
    logit_block_ref,
    n_ref,
    dlogit_ref,
    cos_ref,
    sin_ref,
    g1_ref,
    wp_ref,
    wgt_ref,
    narrow_ref,
    dg2_ref,
    part_refs,
    ffn_refs,
    grad_out,
    band_outs,
    ffn_outs,
    pair_outs,
    dproj_ref,
    wp_turned_ref,
    grad_buf,
    piece_refs,
    band_recvs,
    held_refs,
    ffn_recvs,
    pair_refs,
    pair_recvs,
    around_recv,
    band_sems,
    ffn_sems,
    pair_sems,
    grad_sems,
    local_sem,
):
    place = Place()
    step = pl.program_id(0)
    steps = heads * slots
    head, slot = step // slots, lax.rem(step, slots)
    size, frames = q_ref.shape[1:]
    model = n_ref.shape[1]
    inner = heads * size
    pairs = heads // 2
    pair_rows = 6 * size
    blocks = frames // BLOCK
    last = pl.num_programs(0) - 1
    my_band, my_batch = place.band, place.batch

    bands = [Total(place, order, band_sems[0].at[i], band_sems[1].at[i]) for i, order in enumerate(BAND_ORDERS)]
    ffns = [Total(place, order, ffn_sems[0].at[i], ffn_sems[1].at[i]) for i, order in enumerate(FFN_ORDERS)]
    own = [
        Total(place, PAIR_ORDERS[i], pair_sems[0].at[i], pair_sems[1].at[i]) for i in range(pairs)
    ]

    def half_copy(i):
        return pltpu.make_async_copy(ffn_refs[i].at[place.bits["core"]], held_refs[i], local_sem.at[len(bands) + i])

    def eighth(total, held):
        return held.at[total.half_rows(held, 2)[0]]

    def all_steps(total, source, held, recvs, out, sem):
        width = recvs[3].shape[2]

        def back_region():
            return out.at[total.back_rows(out, 2)]

        def s0():
            total.start_core(source, recvs[0])

        def s1():
            total.end_core(held, recvs[0])
            total.start_half(1, held, recvs[1])

        def s2():
            total.end_half(1, held, recvs[1])
            total.start_half(2, held, recvs[2])

        def s3():
            total.end_half(2, held, recvs[2])
            total.start_z(eighth(total, held), recvs[3])

        def s4():
            total.end_z(eighth(total, held), recvs[3])
            total.start_z_back(eighth(total, held), back_region(), width, sem)

        def s5():
            total.end_z_back(eighth(total, held), back_region(), width, sem)
            total.start_back(2, out)

        def s6():
            total.end_back(2, out)
            total.start_back(1, out)

        def s7():
            total.end_back(1, out)
            total.start_back(0, out)

        def s8():
            total.end_back(0, out)

        return [s0, s1, s2, s3, s4, s5, s6, s7, s8]

    plan = {}

    def at_step(index, action):
        plan.setdefault(index, []).append(action)

    def enter():
        other_x = place.across("x")[1] // 2
        diagonal = (my_band, 2 * other_x + 1 - place.bits["core"])
        chips = [other for _, _, other in own[-1].around()]
        greet(chips + [place.across("core"), diagonal])
        for i in range(len(ffns)):
            half_copy(i).start()

    tail = steps + slots * blocks
    at_step(0, enter)

    def schedule(actions, places):
        for at, action in zip(places, actions):
            at_step(at, action)

    for i in range(len(bands)):
        out = band_outs[i]
        region = out.at[bands[i].back_rows(out, 2)]
        quarter = band_outs[i].shape[1] // Z_COUNT

        def z_begin(i=i):
            piece_refs[i][...] = part_refs[i][...]
            if i >= BAND_EARLY:
                bands[i].start_z(piece_refs[i], band_recvs[i - BAND_EARLY])

        def z_turn(i=i, region=region, quarter=quarter):
            if i >= BAND_EARLY:
                bands[i].end_z(piece_refs[i], band_recvs[i - BAND_EARLY])
            bands[i].start_z_back(piece_refs[i], region, quarter, local_sem.at[i])

        def z_end(i=i, region=region, quarter=quarter, out=out):
            bands[i].end_z_back(piece_refs[i], region, quarter, local_sem.at[i])
            bands[i].start_back(2, out)

        def back_two(i=i, out=out):
            bands[i].end_back(2, out)
            bands[i].start_back(1, out)

        def back_one(i=i, out=out):
            bands[i].end_back(1, out)
            bands[i].start_back(0, out)

        actions = [z_begin, z_turn, z_end, back_two, back_one, lambda i=i, out=out: bands[i].end_back(0, out)]
        if i < BAND_EARLY:
            at_step(0, z_begin)
            actions = actions[1:]
        schedule(actions, BAND_PLACES[i])
    ffn_at = len(bands) + len(ffns)
    for i in range(len(ffns)):
        sem = local_sem.at[ffn_at + i]
        actions = all_steps(ffns[i], ffn_refs[i], held_refs[i], ffn_recvs[i], ffn_outs[i], sem)
        at_step(FFN_PLACES[i][1], lambda i=i: half_copy(i).wait())
        schedule(actions, FFN_PLACES[i])
    pair_at = ffn_at + len(ffns)

    def around_steps(total, source, held, recv, out, sem):
        def s0():
            total.start_core(source, recv[0])

        def s1():
            total.end_core(held, recv[0])
            total.start_around(held, recv[1])

        def s2():
            total.end_around(held, recv[1])
            total.start_around_back(held, recv[1], out, sem)

        def s3():
            total.end_around_back(held, recv[1], out, sem)
            total.start_back(0, out)

        def s4():
            total.end_back(0, out)

        return [s0, s1, s2, s3, s4]

    for i in range(pairs):
        source, held = pair_refs.at[i], pair_refs.at[i, place.bits["core"]]
        out, sem = pair_outs.at[i], local_sem.at[pair_at + i]
        recv = [ref.at[i] for ref in pair_recvs]
        if PAIR_ORDERS[i] is None:
            actions = around_steps(own[i], source, held, [recv[0], around_recv], out, sem)
        else:
            actions = all_steps(own[i], source, held, recv, out, sem)
        schedule(actions, PAIR_PLACES[i])

    for index in sorted(plan):
        if index < tail:

            @pl.when(step == index)
            def work(index=index):
                for action in plan[index]:
                    action()

    @pl.when(step < steps)
    def attention():
        d_queries, d_keys, d_values = scores_backward(
            q_ref[0],
            k_ref[0],
            v_ref[0],
            p_ref[0, 0],
            datt_ref[0],
            minus_ref[0, pl.ds(head, 1), :],
            cos_ref[...],
            sin_ref[...],
            size**-0.5,
        )
        start = pl.multiple_of((head // 2) * pair_rows + lax.rem(head, 2) * size, size)
        dproj_ref[slot, pl.ds(start, size), :] = d_queries.astype(BF16)
        dproj_ref[slot, pl.ds(start + 2 * size, size), :] = d_keys.astype(BF16)
        dproj_ref[slot, pl.ds(start + 4 * size, size), :] = d_values.astype(BF16)

    @pl.when((step < steps) & (lax.rem(step, 2 * slots) == 2 * slots - 1))
    def pair_done():
        pair = head // 2
        rows = pl.ds(pl.multiple_of(pair * pair_rows, pair_rows), pair_rows)
        sums = dg(n_ref[0], dproj_ref[0, rows, :], NT)
        for j in range(1, slots):
            sums = sums + dg(n_ref[j], dproj_ref[j, rows, :], NT)
        for half in range(2):
            at = slice(half * model // 2, (half + 1) * model // 2)
            pair_refs[pair, half, :, 0:pair_rows] = sums[at].astype(BF16)

    @pl.when(step == 2 * slots - 1)
    def narrow_done():
        gates = 0.0
        for j in range(slots):
            logit = jnp.concatenate([dlogit_ref[j], jnp.zeros_like(dlogit_ref[j])], axis=0).astype(BF16)
            gates = gates + dg(n_ref[j], logit, NT)[:, :heads]
        tile = narrow_tile([narrow_ref[:, : heads + 2], gates, dg2_ref[...]], model)
        for half in range(2):
            at = slice(half * model // 2, (half + 1) * model // 2)
            pair_refs[0, half, :, pair_rows:] = tile[at].astype(BF16)
            for i in range(1, pairs):
                pair_refs[i, half, :, pair_rows:] = jnp.zeros_like(tile[at]).astype(BF16)
        for pair in range(pairs):
            for part in range(3):
                to = pair * pair_rows + part * 2 * size
                source = part * inner + pair * 2 * size
                wp_turned_ref[:, to : to + 2 * size] = wp_ref[:, source : source + 2 * size]

    def message(index):
        j, i = index // blocks, lax.rem(index, blocks)
        source = grad_buf.at[index]
        target = grad_out.at[batch_count * j + my_batch]
        return i, source, target

    @pl.when(step >= steps)
    def rows_done():
        index = step - steps
        j, i = index // blocks, lax.rem(index, blocks)
        at = pl.ds(pl.multiple_of(i * BLOCK, BLOCK), BLOCK)
        logit = logit_block_ref[0].astype(BF16)
        d_normed = dg(wp_turned_ref[...], dproj_ref[j, :, at], NN) + dg(wgt_ref[...], logit, TN)
        d_rows, _ = norm_backward(x_ref[0].astype(F32).T, column(g1_ref), d_normed)
        grad_buf[index] = (dmid_ref[0] + d_rows).T.astype(BF16)
        i, source, target = message(index)

        @pl.when(i == my_batch)
        def keep():
            pltpu.make_async_copy(source, target, local_sem.at[pair_at + pairs]).start()

        @pl.when(i != my_batch)
        def give():
            send(source, target, grad_sems.at[0], grad_sems.at[1], my_band, i)

    @pl.when(step == last)
    def finish():
        for index in sorted(plan):
            if index >= tail:
                for action in plan[index]:
                    action()
        await_bytes(grad_buf.at[pl.ds(0, slots)], local_sem.at[pair_at + pairs])
        others = grad_buf.at[pl.ds(0, slots * (batch_count - 1))]
        await_bytes(others, grad_sems.at[0])
        await_bytes(others, grad_sems.at[1])


def time_attention_backward(
    p, q, k, v, datt, minus, dlogit, n, x, dmid, cos, sin, g1, wp, wgt, narrow, dg2, parts, ffn_sums, batch_count
):
    slots, inner, frames = q.shape
    heads = minus.shape[1]
    size = inner // heads
    model = n.shape[1]
    pairs = heads // 2
    steps = heads * slots
    blocks = frames // BLOCK

    def clamp(t):
        return jnp.minimum(t, steps - 1)

    def tail(t):
        return jnp.maximum(t - steps, 0)

    def per_head(rows, columns):
        return pl.BlockSpec((1, rows, columns), lambda t: (lax.rem(clamp(t), slots), clamp(t) // slots, 0))

    consts = (n, dlogit, cos, sin, g1, wp, wgt, narrow, dg2)
    anywhere = pl.BlockSpec(memory_space=pl.ANY)
    dma = pltpu.SemaphoreType.DMA
    widths = [a.shape[2] for a in ffn_sums]
    pair_width = 8 * size

    def recv_buffers(width, *lead):
        rows = model // 2
        shapes = [(rows, width), (rows // 2, width), (rows // 4, width), (Z_COUNT - 1, rows // 4, width // Z_COUNT)]
        return [pltpu.VMEM(lead + shape, BF16) for shape in shapes]

    return pl.pallas_call(
        lambda *refs: time_attention_backward_kernel(heads, slots, batch_count, *refs),
        grid=(steps + slots * blocks,),
        out_shape=(
            jax.ShapeDtypeStruct((batch_count * slots, BLOCK, model), BF16),
            [jax.ShapeDtypeStruct((model, a.shape[1]), BF16) for a in parts],
            [jax.ShapeDtypeStruct((model, width), BF16) for width in widths],
            jax.ShapeDtypeStruct((pairs, model, pair_width), BF16),
        ),
        in_specs=[
            pl.BlockSpec((1, 1, frames, frames), lambda t: (lax.rem(clamp(t), slots), clamp(t) // slots, 0, 0)),
            per_head(size, frames),
            per_head(size, frames),
            per_head(size, frames),
            per_head(size, frames),
            pl.BlockSpec((1, heads, frames), lambda t: (lax.rem(clamp(t), slots), 0, 0)),
            pl.BlockSpec((1, BLOCK, model), lambda t: (tail(t) // blocks, lax.rem(tail(t), blocks), 0)),
            pl.BlockSpec((1, model, BLOCK), lambda t: (tail(t) // blocks, 0, lax.rem(tail(t), blocks))),
            pl.BlockSpec((1, heads, BLOCK), lambda t: (tail(t) // blocks, 0, lax.rem(tail(t), blocks))),
        ]
        + [whole_spec(c) for c in consts]
        + [[whole_spec(a) for a in parts], [anywhere] * len(ffn_sums)],
        out_specs=(anywhere, [anywhere] * len(parts), [anywhere] * len(ffn_sums), anywhere),
        scratch_shapes=[
            pltpu.VMEM((slots, 3 * inner, frames), BF16),
            pltpu.VMEM((model, 3 * inner), BF16),
            pltpu.VMEM((slots * blocks, BLOCK, model), BF16),
            [pltpu.VMEM(a.shape, BF16) for a in parts],
            [pltpu.VMEM((Z_COUNT - 1, a.shape[0], a.shape[1] // Z_COUNT), BF16) for a in parts[BAND_EARLY:]],
            [pltpu.VMEM((model // 2, width), BF16) for width in widths],
            [recv_buffers(width) for width in widths],
            pltpu.VMEM((pairs, 2, model // 2, pair_width), BF16),
            recv_buffers(pair_width, pairs),
            pltpu.VMEM((4 * Z_COUNT - 1, model // 8, pair_width // Z_COUNT), BF16),
            [dma((len(parts), TOTAL_STEPS))] * 2,
            [dma((len(widths), TOTAL_STEPS))] * 2,
            [dma((pairs, TOTAL_STEPS)), dma((pairs, TOTAL_STEPS))],
            dma((2,)),
            dma((len(parts) + 2 * len(widths) + pairs + 1,)),
        ],
        compiler_params=pltpu.CompilerParams(
            vmem_limit_bytes=VMEM_BYTES, collective_id=3, has_side_effects=True
        ),
        cost_estimate=cost(20.0e6 * slots * frames, 0, 60e6),
        name="time_attention_backward",
    )(p, q, k, v, datt, minus, x, dmid, dlogit, *consts, list(parts), list(ffn_sums))


def finish_kernel(
    heads,
    grad_ref,
    bwp_ref,
    bw1_ref,
    bw2t_ref,
    bwot_ref,
    w1_ref,
    wot_ref,
    w2t_ref,
    pair_ref,
    first_pair_ref,
    wp_ref,
    wgt_ref,
    g1_ref,
    y_ref,
    y_out,
    grad_out,
    dg1_out,
    dwp_out,
    dwg_out,
    dwo_out,
    dg2_out,
    dw1_out,
    dw2_out,
    bg1_out,
    bwp_out,
    bwg_out,
    bwo_out,
    bg2_out,
    bw1_out,
    bw2_out,
    scaled_ref,
):
    pair = pl.program_id(0)
    inner = wp_ref.shape[1] // 3
    width = inner // pl.num_programs(0)
    pairs, bands, parts, rows, model = y_ref.shape
    split = y_ref[...].astype(F32).reshape(pairs, bands, parts, 2, rows // 2, model)
    for j in range(2):
        values = split[:, :, :, j].reshape(pairs, bands * parts * rows // 2, model)
        for i in range(pairs):
            y_out[2 * i + j] = values[i].astype(BF16)
    grad_out[...] = grad_ref[...].astype(F32)
    bwp_out[...] = bwp_ref[...].astype(F32)
    bw1_out[...] = bw1_ref[...].astype(F32)
    bw2_out[...] = bw2t_ref[...].astype(F32).T
    bwo_out[...] = bwot_ref[...].astype(F32).T
    dw1_out[...] = w1_ref[...].astype(F32)
    dw2_out[...] = w2t_ref[...].astype(F32).T
    dwo_out[...] = wot_ref[...].astype(F32).T

    @pl.when(pair == 0)
    def clear():
        scaled_ref[...] = jnp.zeros_like(scaled_ref)

    for part in range(3):
        at = pl.ds(pl.multiple_of(part * inner + pair * width, 128), width)
        values = pair_ref[0, :, part * width : (part + 1) * width].astype(F32)
        dwp_out[:, at] = values
        scaled_ref[...] += values * wp_ref[:, at].astype(F32)

    @pl.when(pair == pl.num_programs(0) - 1)
    def narrow():
        tile = first_pair_ref[0, :, 3 * width :].astype(F32)
        rows = tile.T
        bwg_out[...] = rows[:heads]
        bg1_out[...] = rows[heads]
        bg2_out[...] = rows[heads + 1]
        gates = tile[:, heads + 2 : 2 * heads + 2]
        dwg_out[...] = rows[heads + 2 : 2 * heads + 2]
        dg2_out[...] = rows[2 * heads + 2]
        sums = jnp.sum(scaled_ref[...], axis=1, keepdims=True)
        sums = sums + jnp.sum(gates * wgt_ref[...].astype(F32).T, axis=1, keepdims=True)
        dg1_out[...] = jnp.broadcast_to(sums, (sums.shape[0], 128)).T[0] / g1_ref[...].astype(F32)


def finish_sums(grads, y, band_sums, ffn_sums, pair_sums, g1, params):
    wp, wgt, wo, w1, w2 = params
    model, hidden = w1.shape
    inner, heads = wo.shape[0], wgt.shape[0]
    pairs = pair_sums.shape[0]
    split = hidden // pairs
    out_split = inner // pairs
    slot_dev, frame_dev, _ = grads.shape

    def lanes(width):
        return pl.BlockSpec((model, width), lambda i: (0, i))

    def whole(*shape):
        return pl.BlockSpec(shape, lambda i: (0,) * len(shape))

    def cut_rows(rows):
        return pl.BlockSpec((rows, model), lambda i: (i, 0))

    band_wp, band_w1, band_w2t, band_wot = band_sums
    time_w2t, time_w1, time_wot = ffn_sums
    grad_block = pl.BlockSpec((slot_dev // pairs, frame_dev, model), lambda i: (i, 0, 0))
    narrow = [((model,), whole(model)), ((heads, model), whole(heads, model))]
    per_layer = [
        narrow[0],
        ((model, 3 * inner), None),
        narrow[1],
        ((inner, model), cut_rows(out_split)),
        narrow[0],
        ((model, hidden), lanes(split)),
        ((hidden, model), cut_rows(split)),
    ]
    shapes, specs = [jax.ShapeDtypeStruct(grads.shape, BF16), jax.ShapeDtypeStruct(grads.shape, F32)], [grad_block] * 2
    y_block = pl.BlockSpec((y.shape[0] // pairs,) + y.shape[1:], lambda i: (i, 0, 0, 0, 0))
    for layer in range(2):
        for shape, spec in per_layer:
            shapes.append(jax.ShapeDtypeStruct(shape, F32))
            if spec is None:
                spec = whole(*shape) if layer == 0 else lanes(3 * inner // pairs)
            specs.append(spec)
    return pl.pallas_call(
        lambda *refs: finish_kernel(heads, *refs),
        grid=(pairs,),
        out_shape=shapes,
        in_specs=[
            grad_block,
            lanes(3 * inner // pairs),
            lanes(split),
            lanes(split),
            lanes(out_split),
            lanes(split),
            lanes(out_split),
            lanes(split),
            pl.BlockSpec((1, model, pair_sums.shape[2]), lambda i: (i, 0, 0)),
            pl.BlockSpec((1, model, pair_sums.shape[2]), lambda i: (0, 0, 0)),
            whole_spec(wp),
            whole_spec(wgt),
            whole_spec(g1),
            y_block,
        ],
        out_specs=specs,
        scratch_shapes=[pltpu.VMEM((model, inner // pairs), F32)],
        compiler_params=pltpu.CompilerParams(vmem_limit_bytes=VMEM_BYTES),
        name="finish_sums",
    )(
        grads,
        band_wp,
        band_w1,
        band_w2t,
        band_wot,
        time_w1,
        time_wot,
        time_w2t,
        pair_sums,
        pair_sums,
        wp,
        wgt,
        g1,
        y,
    )


def band_kernel(
    heads,
    batch_count,
    band_count,
    x_ref,
    cot_ref,
    count_ref,
    slots_ref,
    g1_ref,
    g2_ref,
    wgt_ref,
    wpt_ref,
    wot_ref,
    w1t_ref,
    w2t_ref,
    wp_ref,
    wo_ref,
    w1_ref,
    w2_ref,
    y_out,
    dx_out,
    half_outs,
    narrow_out,
    q_ref,
    k_ref,
    v_ref,
    p_ref,
    turned_ref,
    gate_ref,
    linv_ref,
    att_ref,
    mixed_ref,
    act_ref,
    slope_ref,
    hidden_ref,
    dmixed_ref,
    dlogit_ref,
    dproj_ref,
    dwp_ref,
    dw1_ref,
    dw2t_ref,
    dwot_ref,
    dwg_ref,
    dg1_ref,
    dg2_ref,
    xs_ref,
    cots_ref,
    ys_ref,
    dxs_ref,
    y_buf,
    dx_buf,
    y_send,
    y_recv,
    dx_send,
    dx_recv,
    local_sem,
    bias_ref,
    cos_ref,
    sin_ref,
    valid_ref,
    halves,
    core_recvs,
    core_sems,
    half_sem,
):
    step = pl.program_id(0)
    slot_count, part_frames, model = x_ref.shape
    inner, tokens = q_ref.shape
    size = inner // heads
    groups = tokens // BLOCK
    taken = tokens // slot_count
    per_part = part_frames // taken
    part = step // per_part
    first = lax.rem(step, per_part) * taken
    my_band, my_batch = lax.axis_index("band"), lax.axis_index("batch")
    slot_dev = slot_count // band_count
    slots = slot_dev // batch_count
    own_chunk = my_batch * band_count + my_band
    chunks = band_count * batch_count

    columns = [slice(at, at + 128) for at in range(0, model, 128)]

    def tokens_of(ref):
        return jnp.concatenate(
            [
                jnp.concatenate(
                    [ref[c, pl.ds(first + i, slot_count, stride=part_frames), :] for i in range(taken)], axis=0
                ).T
                for c in range(len(columns))
            ],
            axis=0,
        )

    def put_tokens(ref, values, start, stride):
        for c, at in enumerate(columns):
            turned = values[at].T
            for i in range(taken):
                ref[c, pl.ds(start + i, slot_count, stride=stride), :] = turned[
                    i * slot_count : (i + 1) * slot_count
                ]

    @pl.when(step == 0)
    def enter():
        greet_all(band_count, batch_count)
        bands = slots_ref[...].reshape(1, slot_count)
        cos, sin = rotary_rows(jnp.maximum(bands, 0).astype(F32), size // 2)
        cos_ref[...] = jnp.concatenate([cos] * taken, axis=1)
        sin_ref[...] = jnp.concatenate([sin] * taken, axis=1)
        valid = jnp.concatenate([jnp.where(bands >= 0, 1.0, 0.0)] * taken, axis=1)
        valid_ref[...] = valid
        keys = jnp.broadcast_to(valid[:, :BLOCK], (8, BLOCK)).T[:, :1]
        row = lax.broadcasted_iota(jnp.int32, (BLOCK, BLOCK), 0) // slot_count
        column_index = lax.broadcasted_iota(jnp.int32, (BLOCK, BLOCK), 1) // slot_count
        bias_ref[...] = jnp.where((row == column_index) & (keys > 0.5), 0.0, NEG_FILL)

    @pl.when(lax.rem(step, per_part) == 0)
    def unpack():
        for c, at in enumerate(columns):
            xs_ref[c] = x_ref[:, :, at].astype(F32).reshape(xs_ref.shape[1:])
            cots_ref[c] = cot_ref[:, :, at].astype(F32).reshape(cots_ref.shape[1:])

    place = Place()
    totals = [
        Total(place, order, core_sems.at[0, i], core_sems.at[1, i]) for i, order in enumerate(BAND_ORDERS)
    ]
    gain1, gain2 = column(g1_ref), column(g2_ref)
    piece = part_frames * (pl.num_programs(0) // per_part)
    own_start = (my_batch * band_count + my_band) * piece

    @pl.when(step == 0)
    def clear():
        for ref in (dwp_ref, dw1_ref, dw2t_ref, dwot_ref, dwg_ref, dg1_ref, dg2_ref):
            ref[...] = jnp.zeros_like(ref)

    rows = tokens_of(xs_ref)
    normed = norm_forward(rows, gain1)
    q_ref[...], k_ref[...], v_ref[...] = project_block(
        normed, wpt_ref, cos_ref[...], sin_ref[...], inner, LOG2E * size**-0.5
    )
    gate_ref[...] = dg(wgt_ref[...], normed, NN)
    ones = extra_rows([jnp.ones((1, BLOCK), F32)], BLOCK)
    nothing = jnp.zeros((size, BLOCK), BF16)

    def apart(first, second):
        return jnp.concatenate(
            [jnp.concatenate([first, nothing], axis=1), jnp.concatenate([nothing, second], axis=1)], axis=0
        )

    turned_ref[...] = k_ref[...].T
    bias = jnp.concatenate([bias_ref[...]] * 2, axis=1)

    def attend(pair, carry):
        both = pl.ds(pl.multiple_of(2 * pair * size, 2 * size), 2 * size)
        at = [pl.ds(pl.multiple_of((2 * pair + i) * size, size), size) for i in range(2)]
        for group in range(groups):
            lanes = slice(group * BLOCK, (group + 1) * BLOCK)
            scores = dg(turned_ref[lanes, both], apart(*(q_ref[one, lanes] for one in at)), NN) + bias
            weights = jnp.exp2(scores - jnp.max(scores, axis=0, keepdims=True)).astype(BF16)
            p_ref[pair * groups + group] = weights
            for i, one in enumerate(at):
                row = pl.ds(2 * pair + i, 1)
                own = weights[:, i * BLOCK : (i + 1) * BLOCK]
                sums = dg(jnp.concatenate([v_ref[one, lanes], ones], axis=0), own, NN)
                inverse = 1.0 / sums[size : size + 1]
                attended = sums[:size] * inverse
                linv_ref[row, lanes] = inverse
                att_ref[one, lanes] = attended
                gate = jax.nn.sigmoid(gate_ref[row, lanes])
                mixed_ref[one, lanes] = (attended * gate).astype(BF16)
        return carry

    lax.fori_loop(0, heads // 2, attend, 0, unroll=4)
    middle = rows + dg(wot_ref[...], mixed_ref[...], NN)
    normed_ffn = norm_forward(middle, gain2)

    result = feed_forward(middle, normed_ffn, w1t_ref, w2t_ref, act_ref, slope_ref)
    frame = own_start + step * taken + lax.broadcasted_iota(jnp.int32, (1, tokens), 1) // slot_count
    mask = jnp.where(frame < count_ref[0], valid_ref[...], 0.0)
    result = result * mask
    put_tokens(ys_ref, result, 0, taken)

    couples = slot_dev // 2
    for c, at in enumerate(columns):
        y_buf[step, :, :, at] = ys_ref[c].reshape(slot_count // 2, 2 * taken, 128).astype(BF16)

    def give_row(i, carry):
        other = lax.rem(my_band + i, band_count)
        send(
            y_buf.at[step, pl.ds(other * couples, couples)],
            y_out.at[:, my_band, step],
            y_send,
            y_recv,
            other,
            my_batch,
        )
        return carry

    lax.fori_loop(1, band_count, give_row, 0)
    pltpu.make_async_copy(
        y_buf.at[step, pl.ds(my_band * couples, couples)], y_out.at[:, my_band, step], local_sem.at[0]
    ).start()

    grad = tokens_of(cots_ref) * mask
    d_middle, ffn_branch, d_hidden = ffn_backward(grad, slope_ref[...], middle, gain2, w1_ref, w2_ref, dg2_ref)
    hidden_ref[...] = d_hidden
    branch = d_middle.astype(BF16)
    dmixed_ref[...] = dg(wo_ref[...], branch, NN)

    turned_ref[...] = v_ref[...].T
    def attend_back(pair, carry):
        both = pl.ds(pl.multiple_of(2 * pair * size, 2 * size), 2 * size)
        starts = [pl.multiple_of((2 * pair + i) * size, size) for i in range(2)]
        at = [pl.ds(start, size) for start in starts]
        d_atts, minuses = [], []
        for i, one in enumerate(at):
            row = pl.ds(2 * pair + i, 1)
            d_att, minus, d_logit = head_backward(
                dmixed_ref[one, :], att_ref[one, :], gate_ref[row, :], linv_ref[row, :]
            )
            dlogit_ref[row, :] = d_logit
            d_atts.append(d_att)
            minuses.append(minus)
        for group in range(groups):
            lanes = slice(group * BLOCK, (group + 1) * BLOCK)
            weights = p_ref[pair * groups + group]
            d_weights = dg(turned_ref[lanes, both], apart(*(d_att[:, lanes] for d_att in d_atts)), NN)
            minus = jnp.concatenate([minus[:, lanes] for minus in minuses], axis=1)
            d_scores = (weights.astype(F32) * (d_weights + minus)).astype(BF16)
            cos, sin = cos_ref[:, lanes], -sin_ref[:, lanes]
            for i, one in enumerate(at):
                own = slice(i * BLOCK, (i + 1) * BLOCK)
                d_queries = dg(k_ref[one, lanes], d_scores[:, own], NN) * size**-0.5
                d_keys = dg(q_ref[one, lanes], d_scores[:, own], NT) * (1.0 / LOG2E)
                d_values = dg(d_atts[i][:, lanes], weights[:, own], NT)
                dproj_ref[one, lanes] = turn(d_queries, cos, sin).astype(BF16)
                dproj_ref[pl.ds(inner + starts[i], size), lanes] = turn(d_keys, cos, sin).astype(BF16)
                dproj_ref[pl.ds(2 * inner + starts[i], size), lanes] = d_values.astype(BF16)
        return carry

    lax.fori_loop(0, heads // 2, attend_back, 0, unroll=4)
    d_logit = jnp.concatenate([dlogit_ref[...], jnp.zeros_like(dlogit_ref)], axis=0).astype(BF16)
    d_normed = dg(wp_ref[...], dproj_ref[...], NN) + dg(wgt_ref[...], dlogit_ref[...].astype(BF16), TN)
    d_rows, terms = norm_backward(rows, gain1, d_normed)
    dg1_ref[...] += jnp.sum(terms, axis=1, keepdims=True)
    put_tokens(dxs_ref, d_middle + d_rows, 0, taken)
    for c, at in enumerate(columns):
        grouped = dxs_ref[c].reshape(band_count, slots, batch_count, taken, 128)
        grouped = jnp.concatenate([grouped[:, j][:, :, None] for j in range(slots)], axis=2)
        dx_buf[step, :, :, at] = grouped.reshape(chunks, slots * taken, 128).astype(BF16)

    def give_grad(i, carry):
        other = lax.rem(my_band * batch_count + my_batch + i, chunks)
        send(
            dx_buf.at[step, other],
            dx_out.at[own_chunk, step],
            dx_send,
            dx_recv,
            other // batch_count,
            lax.rem(other, batch_count),
        )
        return carry

    lax.fori_loop(1, chunks, give_grad, 0)
    pltpu.make_async_copy(
        dx_buf.at[step, my_band * batch_count + my_batch], dx_out.at[own_chunk, step], local_sem.at[1]
    ).start()

    dwp_ref[...] += dg(normed, dproj_ref[...], NT)
    dwg_ref[...] += dg(normed, d_logit, NT)[:, :heads]
    dwot_ref[...] += dg(branch, mixed_ref[...], NT)
    add_ffn_sums(dw1_ref, dw2t_ref, ffn_branch, act_ref[...], normed_ffn, hidden_ref[...])

    @pl.when(step == pl.num_programs(0) - 1)
    def finish():
        narrow_out[...] = narrow_tile([dwg_ref[...], dg1_ref[...], dg2_ref[...]], model)
        core = place.bits["core"]
        for i, ref in enumerate((dwp_ref, dw1_ref, dw2t_ref, dwot_ref)):
            lay_halves(halves[i], 0, ref)
            totals[i].start_core(halves[i], core_recvs[i])
        for i, total in enumerate(totals):
            total.end_core(halves[i].at[core], core_recvs[i])
            pltpu.make_async_copy(halves[i].at[core], half_outs[i], half_sem.at[i]).start()
        for i in range(len(totals)):
            pltpu.make_async_copy(halves[i].at[core], half_outs[i], half_sem.at[i]).wait()
        await_bytes(y_out.at[:, 0], local_sem.at[0])
        await_bytes(dx_out.at[0], local_sem.at[1])
        for sem in (y_send, y_recv):
            await_bytes(y_out.at[:, pl.ds(0, band_count - 1)], sem)
        for sem in (dx_send, dx_recv):
            await_bytes(dx_out.at[pl.ds(0, chunks - 1)], sem)


def band_layer(rows, cot, counts, slot_bands, g1, g2, params, flips, band_count, batch_count):
    project, gating, output_weight, expand, shrink = params
    slot_count, piece, model = rows.shape
    tokens = 2 * BLOCK
    steps = slot_count * piece // tokens
    heads, inner, hidden = gating.shape[0], output_weight.shape[0], expand.shape[1]
    groups = tokens // BLOCK
    taken = tokens // slot_count
    part_frames = 16
    per_part = part_frames // taken
    slots = slot_count // (band_count * batch_count)
    slot_dev = slot_count // band_count
    consts = (slot_bands, g1, g2, gating) + flips + (project, output_weight, expand, shrink)
    widths = (3 * inner, hidden, hidden, inner)
    chunks = band_count * batch_count
    blocks = pl.BlockSpec((slot_count, part_frames, model), lambda i: (0, i // per_part, 0))
    anywhere = pl.BlockSpec(memory_space=pl.ANY)
    dma = pltpu.SemaphoreType.DMA
    return pl.pallas_call(
        lambda *refs: band_kernel(heads, batch_count, band_count, *refs),
        grid=(steps,),
        out_shape=(
            jax.ShapeDtypeStruct((slot_dev // 2, band_count, steps, 2 * taken, model), BF16),
            jax.ShapeDtypeStruct((chunks, steps, slots * taken, model), BF16),
            [jax.ShapeDtypeStruct((model // 2, width), BF16) for width in widths],
            jax.ShapeDtypeStruct((model, 128), F32),
        ),
        in_specs=[blocks, blocks, pl.BlockSpec(memory_space=pltpu.SMEM)] + [whole_spec(c) for c in consts],
        out_specs=(
            anywhere,
            anywhere,
            [anywhere for _ in widths],
            pl.BlockSpec((model, 128), lambda i: (0, 0)),
        ),
        scratch_shapes=[
            pltpu.VMEM((inner, tokens), BF16),
            pltpu.VMEM((inner, tokens), BF16),
            pltpu.VMEM((inner, tokens), BF16),
            pltpu.VMEM((heads // 2 * groups, BLOCK, 2 * BLOCK), BF16),
            pltpu.VMEM((tokens, inner), BF16),
            pltpu.VMEM((heads, tokens), F32),
            pltpu.VMEM((heads, tokens), F32),
            pltpu.VMEM((inner, tokens), F32),
            pltpu.VMEM((inner, tokens), BF16),
            pltpu.VMEM((hidden, tokens), BF16),
            pltpu.VMEM((hidden, tokens), BF16),
            pltpu.VMEM((hidden, tokens), BF16),
            pltpu.VMEM((inner, tokens), F32),
            pltpu.VMEM((heads, tokens), F32),
            pltpu.VMEM((3 * inner, tokens), BF16),
            pltpu.VMEM((model, 3 * inner), F32),
            pltpu.VMEM((model, hidden), F32),
            pltpu.VMEM((model, hidden), F32),
            pltpu.VMEM((model, inner), F32),
            pltpu.VMEM((model, heads), F32),
            pltpu.VMEM((model, 1), F32),
            pltpu.VMEM((model, 1), F32),
            pltpu.VMEM((model // 128, slot_count * part_frames, 128), F32),
            pltpu.VMEM((model // 128, slot_count * part_frames, 128), F32),
            pltpu.VMEM((model // 128, tokens, 128), F32),
            pltpu.VMEM((model // 128, tokens, 128), F32),
            pltpu.VMEM((steps, slot_count // 2, 2 * taken, model), BF16),
            pltpu.VMEM((steps, chunks, slots * taken, model), BF16),
            dma,
            dma,
            dma,
            dma,
            dma((2,)),
            pltpu.VMEM((BLOCK, BLOCK), F32),
            pltpu.VMEM((inner // heads // 2, tokens), F32),
            pltpu.VMEM((inner // heads // 2, tokens), F32),
            pltpu.VMEM((1, tokens), F32),
            [pltpu.VMEM((2, model // 2, width), BF16) for width in widths],
            [pltpu.VMEM((model // 2, width), BF16) for width in widths],
            dma((2, len(widths), TOTAL_STEPS)),
            dma((len(widths),)),
        ],
        compiler_params=pltpu.CompilerParams(
            vmem_limit_bytes=VMEM_BYTES, collective_id=1, has_side_effects=True
        ),
        cost_estimate=cost(30.0e6 * slot_count * piece, 0, 60e6),
        name="band_layer",
    )(rows, cot, counts, *consts)


def slot_shards(activations, cotangent, frame_counts, slot_bands, *weights):
    slot_dev, _, frame_dev, model = activations.shape
    batch, band = lax.axis_size("batch"), lax.axis_size("band")
    g1, wp, wg, wo, g2, w1, w2 = weights[:7]
    band_g1, band_wp, band_wg, band_wo, band_g2, band_w1, band_w2 = weights[7:]
    heads = wg.shape[1]
    time_params = (wp, wg.T, wo, w1, w2)
    band_params = (band_wp, band_wg.T, band_wo, band_w1, band_w2)
    band_rows, band_cot, rows, n, q, k, v, p, linv, gate, att, mixed, mid, nf, act, slope, *turned = time_forward(
        activations.reshape(slot_dev, frame_dev, model),
        cotangent.reshape(slot_dev, frame_dev, model),
        frame_counts,
        g1,
        g2,
        time_params,
        band_params,
        band,
        batch,
    )
    cos, sin = turned[-2:]
    y, slot_grad, band_halves, band_narrow = band_layer(
        band_rows,
        band_cot,
        frame_counts,
        slot_bands,
        band_g1,
        band_g2,
        band_params,
        tuple(turned[:-2]),
        band,
        batch,
    )
    dmid, datt, minus, dlogit, ffn_halves, dg2, band_parts = time_ffn_backward(
        slot_grad, act, slope, nf, mid, mixed, att, gate, linv, g2, w1, w2, wo, band_halves
    )
    input_grad, band_sums, ffn_sums, pair_sums = time_attention_backward(
        p,
        q,
        k,
        v,
        datt,
        minus,
        dlogit,
        n,
        rows,
        dmid,
        cos,
        sin,
        g1,
        wp,
        time_params[1],
        band_narrow,
        dg2,
        band_parts,
        ffn_halves,
        batch,
    )
    layer_output, input_grad, *grads = finish_sums(
        input_grad, y, band_sums, ffn_sums, pair_sums, g1, time_params
    )
    grads = [g.T if g.shape[0] == heads else g for g in grads]
    return (layer_output.reshape(activations.shape), input_grad.reshape(activations.shape), *grads)


def shards(activations, cotangent, frame_counts, slot_bands, *weights):
    slot_dev, clips, frame_dev, _ = activations.shape
    batch, band = lax.axis_size("batch"), lax.axis_size("band")
    fits = (
        clips == 1
        and batch == 4
        and band == 2 * Z_COUNT
        and slot_dev % batch == 0
        and frame_dev == BLOCK
        and frame_dev == 32 * band
        and slot_bands.shape[0] == 64 == slot_dev * band
        and slot_dev == 2 * batch
        and activations.shape[-1] % 128 == 0
        and (frame_dev // band * slot_bands.shape[0]) % (2 * BLOCK) == 0
        and weights[2].shape[1] == 8
    )
    form = slot_shards if fits else generic_shards
    return form(activations, cotangent, frame_counts, slot_bands, *weights)


def solution(mesh):
    return jax.shard_map(
        shards,
        mesh=mesh,
        in_specs=(
            P("band", None, "batch", None),
            P("band", None, "batch", None),
            P(),
            P(),
            P(),
            P(),
            P(),
            P(),
            P(),
            P(),
            P(),
            P(),
            P(),
            P(),
            P(),
            P(),
            P(),
            P(),
        ),
        out_specs=(
            P("band", None, "batch", None),
            P("band", None, "batch", None),
            P(),
            P(),
            P(),
            P(),
            P(),
            P(),
            P(),
            P(),
            P(),
            P(),
            P(),
            P(),
            P(),
            P(),
        ),
        check_vma=False,
    )
```

```python
import math

import jax
import jax.numpy as jnp
from jax import lax
from jax.experimental import pallas as pl
from jax.experimental.pallas import tpu as pltpu
from jax.sharding import PartitionSpec as P

EPSILON = 1e-05
NEG_FILL = -1000000000.0
TIME_LAYOUT = ("bqhe", "bkhe")
BAND_LAYOUT = ("qbhe", "kbhe")


def rms_scale(residual, gain):
    return (
        residual * lax.rsqrt(jnp.mean(residual * residual, axis=-1, keepdims=True) + EPSILON) * gain
    )


def gelu_exact(values):
    return jax.nn.gelu(values, approximate=False)


def rotary_tables(positions, head_size):
    half_size = head_size // 2
    rates = jnp.exp(-math.log(10000.0) * jnp.arange(half_size, dtype=jnp.float32) / half_size)
    angles = positions[:, None] * rates[None, :]
    return (jnp.cos(angles), jnp.sin(angles))


def rotate(vectors, cos_table, sin_table):
    half_size = vectors.shape[-1] // 2
    first = vectors[..., :half_size]
    second = vectors[..., half_size:]
    return jnp.concatenate(
        [first * cos_table - second * sin_table, first * sin_table + second * cos_table], axis=-1
    )


def token_sum(left, right):
    return lax.dot_general(
        left.reshape(-1, left.shape[-1]),
        right.reshape(-1, right.shape[-1]),
        (((0,), (0,)), ((), ())),
        preferred_element_type=jnp.float32,
    )


def back_dot(gradient, weight):
    return lax.dot_general(
        gradient,
        weight,
        (((gradient.ndim - 1,), (1,)), ((), ())),
        preferred_element_type=jnp.float32,
    )


def block_forward(queries, key_rows, value_rows, key_valid, layout):
    query_form, key_form = layout
    scores = (
        jnp.einsum(
            query_form + "," + key_form + "->bhqk",
            queries,
            key_rows,
            preferred_element_type=jnp.float32,
        )
        * 0.125
    )
    scores = jnp.where(key_valid[:, None, None, :], scores, NEG_FILL)
    highest = jnp.max(scores, axis=-1, keepdims=True)
    exponents = jnp.exp(scores - highest)
    totals = jnp.sum(exponents, axis=-1, keepdims=True)
    soft_weights = (exponents / totals).astype(jnp.bfloat16)
    output = jnp.einsum(
        "bhqk," + key_form + "->" + query_form,
        soft_weights,
        value_rows,
        preferred_element_type=jnp.float32,
    )
    return (output, highest + jnp.log(totals))


def block_backward(queries, key_rows, value_rows, key_valid, log_totals, out_grad, layout):
    query_form, key_form = layout
    scores = (
        jnp.einsum(
            query_form + "," + key_form + "->bhqk",
            queries,
            key_rows,
            preferred_element_type=jnp.float32,
        )
        * 0.125
    )
    soft_weights = jnp.where(key_valid[:, None, None, :], jnp.exp(scores - log_totals), 0.0)
    weight_grad = jnp.einsum(
        query_form + "," + key_form + "->bhqk",
        out_grad,
        value_rows,
        preferred_element_type=jnp.float32,
    )
    score_grad = (
        soft_weights * (weight_grad - jnp.sum(soft_weights * weight_grad, axis=-1, keepdims=True))
    ).astype(jnp.bfloat16)
    query_grad = (
        jnp.einsum(
            "bhqk," + key_form + "->" + query_form,
            score_grad,
            key_rows,
            preferred_element_type=jnp.float32,
        )
        * 0.125
    )
    key_grad = (
        jnp.einsum(
            "bhqk," + query_form + "->" + key_form,
            score_grad,
            queries,
            preferred_element_type=jnp.float32,
        )
        * 0.125
    )
    value_grad = jnp.einsum(
        "bhqk," + query_form + "->" + key_form,
        soft_weights.astype(jnp.bfloat16),
        out_grad,
        preferred_element_type=jnp.float32,
    )
    return (query_grad, key_grad, value_grad)


def time_attend(queries, key_rows, value_rows, key_valid):
    keys_full, values_full = (
        lax.all_gather(key_rows, "batch", axis=1, tiled=True),
        lax.all_gather(value_rows, "batch", axis=1, tiled=True),
    )
    output, log_totals = block_forward(queries, keys_full, values_full, key_valid, TIME_LAYOUT)
    return (output, (log_totals, keys_full, values_full))


def time_attend_back(queries, key_rows, value_rows, key_valid, attn_kept, out_grad):
    log_totals, keys_full, values_full = attn_kept
    query_grad, key_full_grad, value_full_grad = block_backward(
        queries, keys_full, values_full, key_valid, log_totals, out_grad, TIME_LAYOUT
    )
    key_grad, value_grad = (
        lax.psum_scatter(
            key_full_grad.astype(jnp.bfloat16), "batch", scatter_dimension=1, tiled=True
        ).astype(jnp.float32),
        lax.psum_scatter(
            value_full_grad.astype(jnp.bfloat16), "batch", scatter_dimension=1, tiled=True
        ).astype(jnp.float32),
    )
    return (query_grad, key_grad, value_grad)


def band_attend(queries, key_rows, value_rows, key_valid):
    return block_forward(queries, key_rows, value_rows, key_valid, BAND_LAYOUT)


def band_attend_back(queries, key_rows, value_rows, key_valid, attn_kept, out_grad):
    return block_backward(
        queries, key_rows, value_rows, key_valid, attn_kept, out_grad, BAND_LAYOUT
    )


def layer_forward(residual, params, tables, key_valid, attend):
    prenorm, project, gating, output_weight, midnorm, expand, shrink = params
    cos_table, sin_table = tables
    normed = rms_scale(residual, prenorm.astype(jnp.float32)).astype(jnp.bfloat16)
    projected = jnp.dot(normed, project, preferred_element_type=jnp.float32)
    gate_logits = jnp.dot(normed, gating, preferred_element_type=jnp.float32)
    inner_width = output_weight.shape[0]
    head_count = gating.shape[1]
    head_shape = residual.shape[:-1] + (head_count, inner_width // head_count)
    queries = rotate(projected[..., :inner_width].reshape(head_shape), cos_table, sin_table).astype(
        jnp.bfloat16
    )
    key_rows = rotate(
        projected[..., inner_width : 2 * inner_width].reshape(head_shape), cos_table, sin_table
    ).astype(jnp.bfloat16)
    value_rows = projected[..., 2 * inner_width :].reshape(head_shape).astype(jnp.bfloat16)
    attended, attn_kept = attend(queries, key_rows, value_rows, key_valid)
    gate_values = jax.nn.sigmoid(gate_logits)
    mixed_heads = (
        (attended * gate_values[..., None])
        .reshape(residual.shape[:-1] + (inner_width,))
        .astype(jnp.bfloat16)
    )
    middle = residual + jnp.dot(mixed_heads, output_weight, preferred_element_type=jnp.float32)
    normed_ffn = rms_scale(middle, midnorm.astype(jnp.float32)).astype(jnp.bfloat16)
    hidden = jnp.dot(normed_ffn, expand, preferred_element_type=jnp.float32)
    active = gelu_exact(hidden).astype(jnp.bfloat16)
    result = middle + jnp.dot(active, shrink, preferred_element_type=jnp.float32)
    kept_values = (
        residual,
        normed,
        gate_logits,
        queries,
        key_rows,
        value_rows,
        attn_kept,
        attended,
        mixed_heads,
        middle,
        normed_ffn,
        hidden,
        active,
    )
    return (result, kept_values)


def layer_backward(result_grad, params, kept_values, tables, key_valid, attend_back):
    prenorm, project, gating, output_weight, midnorm, expand, shrink = params
    (
        residual,
        normed,
        gate_logits,
        queries,
        key_rows,
        value_rows,
        attn_kept,
        attended,
        mixed_heads,
        middle,
        normed_ffn,
        hidden,
        active,
    ) = kept_values
    cos_table, sin_table = tables
    branch_grad = result_grad.astype(jnp.bfloat16)
    shrink_grad = token_sum(active, branch_grad)
    active_grad = back_dot(branch_grad, shrink)
    hidden_grad = jax.vjp(gelu_exact, hidden)[1](active_grad)[0].astype(jnp.bfloat16)
    expand_grad = token_sum(normed_ffn, hidden_grad)
    normed_ffn_grad = back_dot(hidden_grad, expand)
    middle_norm_grad, midnorm_grad = jax.vjp(rms_scale, middle, midnorm.astype(jnp.float32))[1](
        normed_ffn_grad
    )
    middle_grad = result_grad + middle_norm_grad
    attn_branch = middle_grad.astype(jnp.bfloat16)
    output_grad = token_sum(mixed_heads, attn_branch)
    mixed_grad = back_dot(attn_branch, output_weight).reshape(attended.shape)
    gate_values = jax.nn.sigmoid(gate_logits)
    attended_grad = (mixed_grad * gate_values[..., None]).astype(jnp.bfloat16)
    logit_grad = (
        jnp.sum(mixed_grad * attended, axis=-1) * gate_values * (1.0 - gate_values)
    ).astype(jnp.bfloat16)
    query_grad, key_grad, value_grad = attend_back(
        queries, key_rows, value_rows, key_valid, attn_kept, attended_grad
    )
    flat_shape = residual.shape[:-1] + (-1,)
    projected_grad = jnp.concatenate(
        [
            rotate(query_grad, cos_table, -sin_table).reshape(flat_shape),
            rotate(key_grad, cos_table, -sin_table).reshape(flat_shape),
            value_grad.reshape(flat_shape),
        ],
        axis=-1,
    ).astype(jnp.bfloat16)
    project_grad = token_sum(normed, projected_grad)
    gating_grad = token_sum(normed, logit_grad)
    normed_grad = back_dot(projected_grad, project) + back_dot(logit_grad, gating)
    residual_norm_grad, prenorm_grad = jax.vjp(rms_scale, residual, prenorm.astype(jnp.float32))[1](
        normed_grad
    )
    return (
        middle_grad + residual_norm_grad,
        (
            prenorm_grad,
            project_grad,
            gating_grad,
            output_grad,
            midnorm_grad,
            expand_grad,
            shrink_grad,
        ),
    )


def generic_shards(
    activations,
    cotangent,
    frame_counts,
    slot_bands,
    time_prenorm,
    time_project,
    time_gating,
    time_output,
    time_midnorm,
    time_expand,
    time_shrink,
    band_prenorm,
    band_project,
    band_gating,
    band_output,
    band_midnorm,
    band_expand,
    band_shrink,
):
    slot_dev, clip_count, frame_dev, model_width = activations.shape
    slot_count = slot_bands.shape[0]
    frames_all = frame_dev * lax.axis_size("batch")
    head_size = time_output.shape[0] // time_gating.shape[1]
    time_params = (
        time_prenorm,
        time_project,
        time_gating,
        time_output,
        time_midnorm,
        time_expand,
        time_shrink,
    )
    band_params = (
        band_prenorm,
        band_project,
        band_gating,
        band_output,
        band_midnorm,
        band_expand,
        band_shrink,
    )
    own_bands = lax.dynamic_slice_in_dim(slot_bands, lax.axis_index("band") * slot_dev, slot_dev)
    frame_start = lax.axis_index("batch") * frame_dev
    own_frames = frame_start + jnp.arange(frame_dev, dtype=jnp.int32)
    frame_valid = own_frames[None, :] < frame_counts[:, None]
    row_valid = (own_bands >= 0)[:, None, None] & frame_valid[None]
    full_valid = jnp.arange(frames_all, dtype=jnp.int32)[None, :] < frame_counts[:, None]
    time_valid = jnp.broadcast_to(full_valid[None], (slot_dev, clip_count, frames_all)).reshape(
        slot_dev * clip_count, frames_all
    )
    time_cos, time_sin = rotary_tables(own_frames.astype(jnp.float32), head_size)
    time_tables = (time_cos[None, :, None, :], time_sin[None, :, None, :])
    band_cos, band_sin = rotary_tables(jnp.maximum(slot_bands, 0).astype(jnp.float32), head_size)
    band_tables = (band_cos[:, None, None, :], band_sin[:, None, None, :])
    residual = activations.astype(jnp.float32).reshape(
        slot_dev * clip_count, frame_dev, model_width
    )
    time_result, time_kept = layer_forward(
        residual, time_params, time_tables, time_valid, time_attend
    )
    masked_cot = jnp.where(row_valid[..., None], cotangent, jnp.zeros((), jnp.bfloat16)).reshape(
        slot_dev, clip_count * frame_dev, model_width
    )
    frame_rows = lax.all_to_all(
        time_result.astype(jnp.bfloat16), "band", split_axis=1, concat_axis=0, tiled=True
    ).astype(time_result.dtype)
    band_valid = jnp.broadcast_to((slot_bands >= 0)[None, :], (frame_rows.shape[1], slot_count))
    band_result, band_kept = layer_forward(
        frame_rows, band_params, band_tables, band_valid, band_attend
    )
    back_rows = lax.all_to_all(
        band_result.astype(jnp.bfloat16), "band", split_axis=0, concat_axis=1, tiled=True
    ).astype(band_result.dtype)
    layer_output = jnp.where(
        row_valid[..., None], back_rows.reshape(activations.shape), 0.0
    ).astype(jnp.bfloat16)
    frame_cot = lax.all_to_all(masked_cot, "band", split_axis=1, concat_axis=0, tiled=True)
    frame_grad, band_grads = layer_backward(
        frame_cot.astype(jnp.float32),
        band_params,
        band_kept,
        band_tables,
        band_valid,
        band_attend_back,
    )
    slot_grad = lax.all_to_all(
        frame_grad.astype(jnp.bfloat16), "band", split_axis=0, concat_axis=1, tiled=True
    ).astype(frame_grad.dtype)
    input_grad, time_grads = layer_backward(
        slot_grad, time_params, time_kept, time_tables, time_valid, time_attend_back
    )
    input_grad = input_grad.reshape(activations.shape)
    all_grads = lax.psum(
        (
            time_grads[0],
            time_grads[1],
            time_grads[2],
            time_grads[3],
            time_grads[4],
            time_grads[5],
            time_grads[6],
            band_grads[0],
            band_grads[1],
            band_grads[2],
            band_grads[3],
            band_grads[4],
            band_grads[5],
            band_grads[6],
        ),
        ("band", "batch"),
    )
    return (
        layer_output,
        input_grad,
        all_grads[0],
        all_grads[1],
        all_grads[2],
        all_grads[3],
        all_grads[4],
        all_grads[5],
        all_grads[6],
        all_grads[7],
        all_grads[8],
        all_grads[9],
        all_grads[10],
        all_grads[11],
        all_grads[12],
        all_grads[13],
    )


BLOCK = 256
LOG2E = 1.4426950408889634
F32 = jnp.float32
BF16 = jnp.bfloat16
NN = (((1,), (0,)), ((), ()))
NT = (((1,), (1,)), ((), ()))
TN = (((0,), (0,)), ((), ()))
VMEM_BYTES = 60 * 2**20


def dg(left, right, dims):
    return lax.dot_general(left, right, dims, preferred_element_type=F32)


def norm_forward(rows, gain):
    scale = lax.rsqrt(jnp.mean(rows * rows, axis=0, keepdims=True) + EPSILON)
    return (rows * scale * gain).astype(BF16)


def norm_backward(rows, gain, grad):
    scale = lax.rsqrt(jnp.mean(rows * rows, axis=0, keepdims=True) + EPSILON)
    unit = rows * scale
    scaled = grad * gain
    inner = jnp.mean(scaled * unit, axis=0, keepdims=True)
    return scale * (scaled - unit * inner), grad * unit


def gelu_pair(values):
    size = jnp.abs(values)
    denominator = 1.0 + (0.3275911 * math.sqrt(0.5)) * size
    t = pl.reciprocal(denominator, approx=True)
    t = t * (2.0 - denominator * t)
    bell = jnp.exp2(values * values * (-0.5 * LOG2E))
    poly = 0.5 * 1.061405429
    for coefficient in (-1.453152027, 1.421413741, -0.284496736, 0.254829592):
        poly = poly * t + 0.5 * coefficient
    tail = poly * t * bell
    upper = jnp.where(values < 0.0, tail, 1.0 - tail)
    slope = upper + values * bell * (1.0 / math.sqrt(2.0 * math.pi))
    return values * upper, slope


def feed_forward(middle, normed, w1t_ref, w2t_ref, act_ref, slope_ref):
    part = w1t_ref.shape[0] // 3
    result = middle
    hidden = dg(w1t_ref[0:part, :], normed, NN)
    for i in range(3):
        rows = slice(i * part, (i + 1) * part)
        later = None
        if i < 2:
            later = dg(w1t_ref[(i + 1) * part : (i + 2) * part, :], normed, NN)
        active, slope = gelu_pair(hidden)
        active = active.astype(BF16)
        act_ref[rows, :] = active
        slope_ref[rows, :] = slope.astype(BF16)
        result = result + dg(w2t_ref[:, rows], active, NN)
        hidden = later
    return result


def turn(vectors, cos, sin):
    half = cos.shape[0]
    split = vectors.reshape(-1, 2 * half, vectors.shape[-1])
    first = split[:, :half]
    second = split[:, half:]
    turned = jnp.concatenate([first * cos - second * sin, first * sin + second * cos], axis=1)
    return turned.reshape(vectors.shape)


def three_parts(values):
    top = values.astype(BF16).astype(F32)
    rest = values - top
    middle = rest.astype(BF16).astype(F32)
    return top, middle, rest - middle


def extra_rows(rows, width):
    tile = jnp.concatenate(rows + [jnp.zeros((8 - len(rows), width), F32)], axis=0)
    return jnp.concatenate([tile, jnp.zeros((8, width), F32)], axis=0).astype(BF16)


def project_block(normed, wpt_ref, cos, sin, inner, scale):
    queries = turn(dg(wpt_ref[0:inner, :], normed, NN), cos, sin) * scale
    keys = turn(dg(wpt_ref[inner : 2 * inner, :], normed, NN), cos, sin)
    values = dg(wpt_ref[2 * inner : 3 * inner, :], normed, NN)
    return queries.astype(BF16), keys.astype(BF16), values.astype(BF16)


def column(gain_ref):
    row = gain_ref[...].astype(F32).reshape(1, gain_ref.shape[0])
    return jnp.broadcast_to(row, (8, row.shape[1])).T[:, :1]


def rotary_rows(positions, half):
    rank = lax.broadcasted_iota(jnp.int32, (half, positions.shape[1]), 0).astype(F32)
    angles = positions * jnp.exp(-math.log(10000.0) * rank / half)
    return jnp.cos(angles), jnp.sin(angles)


def flipped(ref):
    return ref[...].astype(F32).T.astype(BF16)


def greet_all(band_count, batch_count):
    count = band_count * batch_count
    me = lax.axis_index("band") * batch_count + lax.axis_index("batch")
    barrier = pltpu.get_barrier_semaphore()

    def signal(i, carry):
        other = lax.rem(me + i, count)
        pl.semaphore_signal(
            barrier,
            inc=1,
            device_id=(other // batch_count, lax.rem(other, batch_count)),
            device_id_type=pl.DeviceIdType.MESH,
        )
        return carry

    lax.fori_loop(1, count, signal, 0)
    pl.semaphore_wait(barrier, count - 1)


def send(source, target, send_sem, recv_sem, band, batch):
    pltpu.make_async_remote_copy(
        src_ref=source,
        dst_ref=target,
        send_sem=send_sem,
        recv_sem=recv_sem,
        device_id=(band, batch),
        device_id_type=pl.DeviceIdType.MESH,
    ).start()


def await_bytes(ref, sem):
    pltpu.make_async_copy(ref, ref, sem).wait()


def by_rows(rows, action):
    def block(i, carry):
        action(pl.multiple_of(i * 16, 16))
        return carry

    lax.fori_loop(0, rows // 16, block, 0)


class Place:
    def __init__(self):
        self.band, self.batch = lax.axis_index("band"), lax.axis_index("batch")
        self.bits = {
            "core": lax.rem(self.batch, 2),
            "x": self.batch // 2,
            "y": lax.rem(self.band, 2),
        }
        self.z = self.band // 2

    def across(self, axis):
        bit = self.bits[axis]
        if axis == "core":
            return self.band, self.batch + 1 - 2 * bit
        if axis == "x":
            return self.band, self.batch + 2 - 4 * bit
        return self.band + 1 - 2 * bit, self.batch

    def along_z(self, step):
        other = lax.rem(self.z + step, Z_COUNT)
        return other, (other * 2 + self.bits["y"], self.batch)


Z_COUNT = 4


def greet(others):
    barrier = pltpu.get_barrier_semaphore()
    for other in others:
        pl.semaphore_signal(barrier, inc=1, device_id=other, device_id_type=pl.DeviceIdType.MESH)
    pl.semaphore_wait(barrier, len(others))


class Total:
    def __init__(self, place, order, sends, recvs):
        self.place = place
        self.order = order
        self.sends, self.recvs = sends, recvs
        self.core = place.bits["core"]
        if order is not None:
            self.first, self.second = (place.bits[axis] for axis in order)

    def give(self, step, source, target, other):
        send(source, target, self.sends.at[step], self.recvs.at[step], *other)

    def took(self, step, ref):
        await_bytes(ref, self.recvs.at[step])
        await_bytes(ref, self.sends.at[step])

    def add(self, ref, start, part):
        def some(i):
            at, own = pl.ds(pl.multiple_of(start + i, 16), 16), pl.ds(i, 16)
            ref[at] = (ref[at].astype(F32) + part[own].astype(F32)).astype(BF16)

        by_rows(part.shape[0], some)

    def start_core(self, source, recv):
        self.give(0, source.at[1 - self.core], recv, self.place.across("core"))

    def end_core(self, held, recv):
        self.took(0, recv)
        self.add(held, 0, recv)

    def half_rows(self, held, level):
        rows = held.shape[0] // 2
        base = 0
        if level == 2:
            base, rows = self.first * rows, rows // 2
        bit = self.first if level == 1 else self.second
        keep = pl.ds(pl.multiple_of(base + bit * rows, rows), rows)
        away = pl.ds(pl.multiple_of(base + (1 - bit) * rows, rows), rows)
        return keep, away

    def start_half(self, level, held, recv):
        away = self.half_rows(held, level)[1]
        self.give(level, held.at[away], recv, self.place.across(self.order[level - 1]))

    def end_half(self, level, held, recv):
        self.took(level, recv)
        self.add(held, self.half_rows(held, level)[0].start, recv)

    def start_z(self, piece, recv):
        width = recv.shape[2]
        for step in range(1, Z_COUNT):
            index, other = self.place.along_z(step)
            lanes = pl.ds(pl.multiple_of(index * width, 128), width)
            self.give(3, piece.at[:, lanes], recv.at[step - 1], other)

    def z_lanes(self, width):
        return pl.ds(pl.multiple_of(self.place.z * width, 128), width)

    def end_z(self, piece, recv):
        self.took(3, recv)
        lanes = self.z_lanes(recv.shape[2])
        sums = piece[:, lanes].astype(F32)
        for step in range(Z_COUNT - 1):
            sums = sums + recv[step].astype(F32)
        piece[:, lanes] = sums.astype(BF16)

    def own_copy(self, piece, target, width, sem):
        lanes = self.z_lanes(width)
        return pltpu.make_async_copy(piece.at[:, lanes], target.at[:, lanes], sem)

    def start_z_back(self, piece, target, width, sem):
        lanes = self.z_lanes(width)
        for step in range(1, Z_COUNT):
            _, other = self.place.along_z(step)
            self.give(4, piece.at[:, lanes], target.at[:, lanes], other)
        self.own_copy(piece, target, width, sem).start()

    def end_z_back(self, piece, target, width, sem):
        self.took(4, target.at[:, pl.ds(0, (Z_COUNT - 1) * width)])
        self.own_copy(piece, target, width, sem).wait()

    def chip(self, step):
        x = lax.rem(self.place.bits["x"] + lax.rem(step // 2, 2), 2)
        y = lax.rem(self.place.bits["y"] + lax.rem(step, 2), 2)
        z = lax.rem(self.place.z + step // 4, Z_COUNT)
        return 2 * x + y, z, (2 * z + y, 2 * x + self.core)

    def around(self, action):
        def one(step, carry):
            action(step, *self.chip(step))
            return carry

        lax.fori_loop(1, 4 * Z_COUNT, one, 0)

    def tile(self, ref, base, quarter, z, shape):
        rows = pl.ds(pl.multiple_of(base + quarter * shape[0], shape[0]), shape[0])
        return ref.at[rows, pl.ds(pl.multiple_of(z * shape[1], 128), shape[1])]

    def start_around(self, held, recv):
        def one(step, quarter, z, other):
            self.give(1, self.tile(held, 0, quarter, z, recv.shape[1:]), recv.at[step - 1], other)

        self.around(one)

    def own_tile(self, ref, base, shape):
        return self.tile(ref, base, 2 * self.place.bits["x"] + self.place.bits["y"], self.place.z, shape)

    def end_around(self, held, recv):
        self.took(1, recv)
        own = self.own_tile(held, 0, recv.shape[1:])
        sums = own[...].astype(F32)
        for i in range(recv.shape[0]):
            sums = sums + recv[i].astype(F32)
        own[...] = sums.astype(BF16)

    def start_around_back(self, held, recv, out, sem):
        shape = recv.shape[1:]
        own = self.own_tile(held, 0, shape)
        target = self.own_tile(out, self.core * (out.shape[0] // 2), shape)
        self.around(lambda step, quarter, z, other: self.give(2, own, target, other))
        pltpu.make_async_copy(own, target, sem).start()

    def end_around_back(self, held, recv, out, sem):
        shape = recv.shape[1:]
        self.took(2, recv)
        target = self.own_tile(out, self.core * (out.shape[0] // 2), shape)
        pltpu.make_async_copy(self.own_tile(held, 0, shape), target, sem).wait()

    def back_rows(self, out, level):
        rows = out.shape[0] // 2
        base = self.core * rows
        if level >= 1:
            rows = rows // 2
            base = base + self.first * rows
        if level >= 2:
            rows = rows // 2
            base = base + self.second * rows
        return pl.ds(pl.multiple_of(base, rows), rows)

    def start_back(self, level, out, source=None):
        rows = self.back_rows(out, level)
        axis = "core" if level == 0 else self.order[level - 1]
        self.give(7 - level, out.at[rows] if source is None else source, out.at[rows], self.place.across(axis))

    def end_back(self, level, out):
        self.took(7 - level, out.at[self.back_rows(out, level)])


TOTAL_STEPS = 8


def time_forward_kernel(
    heads,
    batch_count,
    band_count,
    act_in,
    cot_in,
    count_ref,
    g1_ref,
    g2_ref,
    wgt_ref,
    wp_ref,
    wo_ref,
    w1_ref,
    w2_ref,
    band_wp_ref,
    band_wo_ref,
    band_w1_ref,
    band_w2_ref,
    band_rows,
    band_cot,
    rows_ref,
    n_ref,
    q_ref,
    k_ref,
    v_ref,
    p_ref,
    linv_ref,
    gate_ref,
    att_ref,
    mixed_ref,
    mid_ref,
    nf_ref,
    act_ref,
    slope_ref,
    band_wpt_ref,
    band_wot_ref,
    band_w1t_ref,
    band_w2t_ref,
    cos_ref,
    sin_ref,
    xt_ref,
    x_ref,
    result_ref,
    wpt_ref,
    wot_ref,
    w1t_ref,
    w2t_ref,
    row_send,
    row_recv,
    cot_send,
    cot_recv,
    result_send,
    result_recv,
    local_sem,
):
    slot, head = pl.program_id(0), pl.program_id(1)
    slots = pl.num_programs(0)
    slot_dev = cot_in.shape[0]
    frames, model = rows_ref.shape[1:]
    inner = q_ref.shape[1]
    size = inner // heads
    my_band, my_batch = lax.axis_index("band"), lax.axis_index("batch")
    frame_dev = frames // batch_count
    piece = frame_dev // band_count
    own_rows = pl.ds(pl.multiple_of(my_batch * frame_dev, frame_dev), frame_dev)
    held = x_ref.shape[0]
    frame_index = lax.broadcasted_iota(jnp.int32, (1, frames), 1)

    def neighbour(i):
        core, x = lax.rem(my_batch, 2), my_batch // 2
        return lax.rem(x + i // 2, 2) * 2 + lax.rem(core + lax.rem(i, 2), 2)

    def own_row_copy(j):
        return pltpu.make_async_copy(
            act_in.at[batch_count * j + my_batch], x_ref.at[j, own_rows], local_sem.at[j]
        )

    def own_cot_copy():
        return pltpu.make_async_copy(
            cot_in.at[:, pl.ds(pl.multiple_of(my_band * piece, piece), piece)],
            band_cot.at[pl.ds(my_band * slot_dev, slot_dev)],
            local_sem.at[held],
        )

    @pl.when((slot == 0) & (head == 0))
    def start():
        greet_all(band_count, batch_count)
        for j in range(held):
            for i in range(1, batch_count):
                other = neighbour(i)
                send(
                    act_in.at[batch_count * j + other],
                    x_ref.at[j, own_rows],
                    row_send,
                    row_recv.at[j, i],
                    my_band,
                    other,
                )
            own_row_copy(j).start()

        def send_cot(i, carry):
            other = lax.rem(my_band + i, band_count)
            send(
                cot_in.at[:, pl.ds(pl.multiple_of(other * piece, piece), piece)],
                band_cot.at[pl.ds(my_band * slot_dev, slot_dev)],
                cot_send,
                cot_recv,
                other,
                my_batch,
            )
            return carry

        lax.fori_loop(1, band_count, send_cot, 0)
        own_cot_copy().start()
        cos_ref[...], sin_ref[...] = rotary_rows(frame_index.astype(F32), size // 2)
        wpt_ref[...] = flipped(wp_ref)
        wot_ref[...] = flipped(wo_ref)
        w1t_ref[...] = flipped(w1_ref)
        w2t_ref[...] = flipped(w2_ref)
        band_wpt_ref[...] = flipped(band_wp_ref)
        band_wot_ref[...] = flipped(band_wo_ref)
        band_w1t_ref[...] = flipped(band_w1_ref)
        band_w2t_ref[...] = flipped(band_w2_ref)

    @pl.when(head == 0)
    def before():
        gain = column(g1_ref)

        def block(i, carry):
            at = pl.ds(pl.multiple_of(neighbour(i) * BLOCK, BLOCK), BLOCK)

            @pl.when(i == 0)
            def own():
                for j in range(held):

                    @pl.when(slot == j)
                    def kept():
                        own_row_copy(j).wait()

            @pl.when(i > 0)
            def arrived():
                await_bytes(x_ref.at[slot, at], row_recv.at[slot, i])

            held_rows = x_ref[slot, at, :]
            rows_ref[0, at, :] = held_rows
            rows = held_rows.astype(F32).T
            xt_ref[:, at] = rows
            normed = norm_forward(rows, gain)
            n_ref[0, :, at] = normed
            queries, keys, values = project_block(
                normed, wpt_ref, cos_ref[:, at], sin_ref[:, at], inner, LOG2E * size**-0.5
            )
            q_ref[0, :, at] = queries
            k_ref[0, :, at] = keys
            v_ref[0, :, at] = values
            gate_ref[0, :, at] = dg(wgt_ref[...], normed, NN)
            return carry

        lax.fori_loop(0, frames // BLOCK, block, 0, unroll=1)

    at_head = pl.ds(pl.multiple_of(head * size, size), size)
    ones = jnp.ones((1, frames), F32)
    queries = jnp.concatenate([q_ref[0, at_head, :], extra_rows([ones], frames)], axis=0)
    keys = jnp.concatenate([k_ref[0, at_head, :], extra_rows([jnp.where(frame_index < count_ref[0], 0.0, NEG_FILL)], frames)], axis=0)
    values = jnp.concatenate([v_ref[0, at_head, :], extra_rows([ones], frames)], axis=0)
    scores = dg(keys, queries, TN)
    weights = jnp.exp2(scores - jnp.max(scores, axis=0, keepdims=True)).astype(BF16)
    p_ref[0, 0] = weights
    sums = dg(values, weights, NN)
    inverse = 1.0 / sums[size : size + 1]
    attended = sums[:size] * inverse
    linv_ref[0, pl.ds(head, 1), :] = inverse
    att_ref[0, at_head, :] = attended
    gate = jax.nn.sigmoid(gate_ref[0, pl.ds(head, 1), :])
    mixed_ref[0, at_head, :] = (attended * gate).astype(BF16)

    @pl.when(head == heads - 1)
    def after():
        gain = column(g2_ref)
        to_slot = my_band * slot_dev + batch_count * slot + my_batch

        def block(i, carry):
            at = pl.ds(pl.multiple_of(i * BLOCK, BLOCK), BLOCK)
            middle = xt_ref[:, at] + dg(wot_ref[...], mixed_ref[0, :, at], NN)
            mid_ref[0, :, at] = middle
            normed = norm_forward(middle, gain)
            nf_ref[0, :, at] = normed
            result = feed_forward(
                middle, normed, w1t_ref, w2t_ref, act_ref.at[0, :, at], slope_ref.at[0, :, at]
            )
            result_ref[slot, at, :] = result.T.astype(BF16)

            def send_result(j, carry):
                other = lax.rem(my_band + j, band_count)
                source = result_ref.at[slot, pl.ds(pl.multiple_of(i * frame_dev + other * piece, piece), piece)]
                mine = (other == my_band) & (i == my_batch)

                @pl.when(mine)
                def keep():
                    pltpu.make_async_copy(source, band_rows.at[to_slot], local_sem.at[held + 1]).start()

                @pl.when(jnp.logical_not(mine))
                def give():
                    send(source, band_rows.at[to_slot], result_send, result_recv, other, i)

                return carry

            lax.fori_loop(1, band_count + 1, send_result, 0)
            return carry

        lax.fori_loop(0, frames // BLOCK, block, 0, unroll=1)

    @pl.when((slot == slots - 1) & (head == heads - 1))
    def finish():
        others = held * (band_count * batch_count - 1)
        others_cot = (band_count - 1) * slot_dev
        others_rows = (batch_count - 1) * frame_dev
        await_bytes(band_cot.at[pl.ds(0, others_cot)], cot_recv)
        await_bytes(band_cot.at[pl.ds(0, others_cot)], cot_send)
        own_cot_copy().wait()
        await_bytes(x_ref.at[:, pl.ds(0, others_rows)], row_send)
        await_bytes(band_rows.at[pl.ds(0, others)], result_send)
        await_bytes(band_rows.at[pl.ds(0, held)], local_sem.at[held + 1])
        await_bytes(band_rows.at[pl.ds(0, others)], result_recv)


def cost(flops, exps=0, moved=0):
    return pl.CostEstimate(flops=int(flops), bytes_accessed=int(moved), transcendentals=int(exps))


def whole_spec(array):
    nd = array.ndim
    return pl.BlockSpec(array.shape, lambda *ids: (0,) * nd, pipeline_mode=pl.Buffered(1))


def time_forward(activations, cotangent, counts, g1, g2, params, band_params, band_count, batch_count):
    wp, wgt, wo, w1, w2 = params
    bwp, _, bwo, bw1, bw2 = band_params
    slot_dev, frame_dev, model = activations.shape
    slots, frames = slot_dev // batch_count, frame_dev * batch_count
    heads, inner, hidden = wgt.shape[0], wo.shape[0], w1.shape[1]
    piece = frame_dev // band_count

    def per_slot(*shape):
        return pl.BlockSpec((1,) + shape, lambda s, h: (s,) + (0,) * len(shape))

    outs = [
        ((frames, model), BF16),
        ((model, frames), BF16),
        ((inner, frames), BF16),
        ((inner, frames), BF16),
        ((inner, frames), BF16),
        None,
        ((heads, frames), F32),
        ((heads, frames), F32),
        ((inner, frames), F32),
        ((inner, frames), BF16),
        ((model, frames), F32),
        ((model, frames), BF16),
        ((hidden, frames), BF16),
        ((hidden, frames), BF16),
    ]
    flips = [(w.shape[1], w.shape[0]) for w in (bwp, bwo, bw1, bw2)]
    own_flips = [(w.shape[1], w.shape[0]) for w in (wp, wo, w1, w2)]
    exchanged = jax.ShapeDtypeStruct((slot_dev * band_count, piece, model), BF16)
    anywhere = pl.BlockSpec(memory_space=pl.ANY)
    shapes, specs = [exchanged, exchanged], [anywhere, anywhere]
    for entry in outs:
        if entry is None:
            shapes.append(jax.ShapeDtypeStruct((slots, heads, frames, frames), BF16))
            specs.append(pl.BlockSpec((1, 1, frames, frames), lambda s, h: (s, h, 0, 0)))
        else:
            shapes.append(jax.ShapeDtypeStruct((slots,) + entry[0], entry[1]))
            specs.append(per_slot(*entry[0]))
    for shape in flips:
        shapes.append(jax.ShapeDtypeStruct(shape, BF16))
        specs.append(pl.BlockSpec(shape, lambda s, h: (0, 0), pipeline_mode=pl.Buffered(1)))
    consts = (g1, g2, wgt, wp, wo, w1, w2, bwp, bwo, bw1, bw2)
    half = inner // heads // 2
    for _ in range(2):
        shapes.append(jax.ShapeDtypeStruct((half, frames), F32))
        specs.append(pl.BlockSpec((half, frames), lambda s, h: (0, 0)))
    dma = pltpu.SemaphoreType.DMA
    return pl.pallas_call(
        lambda *refs: time_forward_kernel(heads, batch_count, band_count, *refs),
        grid=(slots, heads),
        out_shape=shapes,
        in_specs=[anywhere, anywhere, pl.BlockSpec(memory_space=pltpu.SMEM)] + [whole_spec(c) for c in consts],
        out_specs=specs,
        scratch_shapes=[
            pltpu.VMEM((model, frames), F32),
            pltpu.VMEM((slots, frames, model), BF16),
            pltpu.VMEM((slots, frames, model), BF16),
        ]
        + [pltpu.VMEM(shape, BF16) for shape in own_flips]
        + [dma, dma((slots, batch_count)), dma, dma, dma, dma, dma((slots + 2,))],
        compiler_params=pltpu.CompilerParams(
            vmem_limit_bytes=VMEM_BYTES, collective_id=0, has_side_effects=True
        ),
        cost_estimate=cost(2.0e6 * 4 * slots * frames, 2 * slots * heads * frames * frames, 60e6),
        name="time_forward",
    )(activations, cotangent, counts, *consts)


def ffn_backward(grad, slope, middle, gain, w1_ref, w2_ref, dg2_ref):
    branch = grad.astype(BF16)
    d_hidden = (dg(w2_ref[...], branch, NN) * slope.astype(F32)).astype(BF16)
    d_normed = dg(w1_ref[...], d_hidden, NN)
    d_rows, terms = norm_backward(middle, gain, d_normed)
    dg2_ref[...] += jnp.sum(terms, axis=1, keepdims=True)
    return grad + d_rows, branch, d_hidden


def add_ffn_sums(dw1_ref, dw2t_ref, branch, act, normed, d_hidden):
    dw2t_ref[...] += dg(branch, act, NT)
    dw1_ref[...] += dg(normed, d_hidden, NT)


def head_backward(d_mixed, attended, gate_logit, inverse):
    gate = jax.nn.sigmoid(gate_logit)
    d_logit = jnp.sum(d_mixed * attended, axis=0, keepdims=True) * gate * (1.0 - gate)
    d_att = (d_mixed * (gate * inverse)).astype(BF16)
    minus = -jnp.sum(d_att.astype(F32) * attended, axis=0, keepdims=True)
    return d_att, minus, d_logit


def scores_backward(queries, keys, values, weights, d_att, minus, cos, sin, scale):
    width = queries.shape[1]
    ones = jnp.ones((1, width), F32)
    d_weights = dg(
        jnp.concatenate([values, extra_rows([ones, ones, ones], width)], axis=0),
        jnp.concatenate([d_att, extra_rows(list(three_parts(minus)), width)], axis=0),
        TN,
    )
    d_scores = (weights.astype(F32) * d_weights).astype(BF16)
    d_values = dg(d_att, weights, NT)
    d_queries = dg(keys, d_scores, NN) * scale
    d_keys = dg(queries, d_scores, NT) * (1.0 / LOG2E)
    return turn(d_queries, cos, -sin), turn(d_keys, cos, -sin), d_values


def time_ffn_backward_kernel(
    heads,
    grad_ref,
    act_ref,
    slope_ref,
    nf_ref,
    mid_ref,
    mixed_ref,
    att_ref,
    gate_ref,
    linv_ref,
    g2_ref,
    w1_ref,
    w2_ref,
    wo_ref,
    half_refs,
    dmid_ref,
    datt_ref,
    minus_ref,
    dlogit_ref,
    sums_refs,
    dg2_out,
    part_refs,
    dw1_ref,
    dw2t_ref,
    dwot_ref,
    dg2_ref,
    held_refs,
    half_recvs,
    z_recvs,
    sends,
    recvs,
    local_sem,
):
    place = Place()
    totals = [Total(place, order, sends.at[i], recvs.at[i]) for i, order in enumerate(BAND_ORDERS)]
    early = len(z_recvs)
    work = list(zip(totals, half_refs, held_refs, half_recvs))

    def half_copy(i):
        return pltpu.make_async_copy(half_refs[i], held_refs[i], local_sem.at[i])

    def part_copy(i):
        rows = totals[i].half_rows(held_refs[i], 2)[0]
        return pltpu.make_async_copy(held_refs[i].at[rows], part_refs[i], local_sem.at[len(totals) + i])

    step = pl.program_id(0) * pl.num_programs(1) + pl.program_id(1)
    last = pl.num_programs(0) * pl.num_programs(1) - 1
    size = wo_ref.shape[0] // heads

    @pl.when(step == 0)
    def clear():
        for ref in (dw1_ref, dw2t_ref, dwot_ref, dg2_ref):
            ref[...] = jnp.zeros_like(ref)
        greet([place.across("x"), place.across("y")] + [place.along_z(i)[1] for i in range(1, Z_COUNT)])
        for i, (total, halves, held, recv) in enumerate(work):
            half_copy(i).start()
            total.start_half(1, halves, recv[0])

    def eighth(i):
        return held_refs[i].at[totals[i].half_rows(held_refs[i], 2)[0]]

    @pl.when(step == last - 1)
    def first_half():
        for i, (total, halves, held, recv) in list(enumerate(work))[:early]:
            half_copy(i).wait()
            total.end_half(1, held, recv[0])
            total.start_half(2, held, recv[1])

    @pl.when(step == last)
    def second_half():
        for i, (total, halves, held, recv) in list(enumerate(work))[early:]:
            half_copy(i).wait()
            total.end_half(1, held, recv[0])
            total.start_half(2, held, recv[1])
        for i, (total, halves, held, recv) in list(enumerate(work))[:early]:
            total.end_half(2, held, recv[1])
            total.start_z(eighth(i), z_recvs[i])

    slot = pl.program_id(0)
    chunks, parts, rows, model = grad_ref.shape
    slots = pl.num_programs(0)
    taken = rows // slots
    both = grad_ref[...].astype(F32).reshape(chunks * parts, slots, taken, model)
    grad = both[:, 0]
    for j in range(1, slots):
        grad = jnp.where(slot == j, both[:, j], grad)
    grad = grad.reshape(chunks * parts * taken, model).T
    d_middle, branch, d_hidden = ffn_backward(
        grad, slope_ref[0], mid_ref[0], column(g2_ref), w1_ref, w2_ref, dg2_ref
    )
    add_ffn_sums(dw1_ref, dw2t_ref, branch, act_ref[0], nf_ref[0], d_hidden)
    dmid_ref[0] = d_middle
    branch = d_middle.astype(BF16)
    dwot_ref[...] += dg(branch, mixed_ref[0], NT)
    d_mixed = dg(wo_ref[...], branch, NN)
    logits, minuses = [], []
    for head in range(heads):
        at = slice(head * size, (head + 1) * size)
        d_att, minus, d_logit = head_backward(
            d_mixed[at], att_ref[0, at], gate_ref[0, head : head + 1], linv_ref[0, head : head + 1]
        )
        datt_ref[0, at] = d_att
        minuses.append(minus)
        logits.append(d_logit)
    minus_ref[0] = jnp.concatenate(minuses, axis=0)
    dlogit_ref[0] = jnp.concatenate(logits, axis=0)

    @pl.when(step == last)
    def finish():
        for sums, ref in zip(sums_refs, (dw2t_ref, dw1_ref, dwot_ref)):
            lay_halves(sums, ref)
        dg2_out[...] = dg2_ref[...]
        for i, (total, halves, held, recv) in list(enumerate(work))[early:]:
            total.end_half(2, held, recv[1])
            part_copy(i).start()
        for i, (total, halves, held, recv) in list(enumerate(work))[:early]:
            total.end_z(eighth(i), z_recvs[i])
            part_copy(i).start()
        for i in range(len(work)):
            part_copy(i).wait()


def narrow_tile(parts, rows):
    used = sum(part.shape[1] for part in parts)
    return jnp.concatenate(list(parts) + [jnp.zeros((rows, 128 - used), F32)], axis=1)


def lay_halves(target, ref):
    half_rows = ref.shape[0] // 2
    for half in range(2):

        def some(i, half=half):
            target[half, pl.ds(i, 16), :] = ref[pl.ds(half * half_rows + i, 16), :].astype(BF16)

        by_rows(half_rows, some)


XY, YX = ("x", "y"), ("y", "x")
BAND_ORDERS = (YX, XY, YX, XY)
BAND_EARLY = 2
FFN_ORDERS = (YX, XY, YX)
PAIR_ORDERS = (YX, YX, None, None)


def time_ffn_backward(grad, act, slope, nf, mid, mixed, att, gate, linv, g2, w1, w2, wo, halves_in):
    slots, model, frames = mid.shape
    heads = gate.shape[1]
    inner, hidden = wo.shape[0], w1.shape[1]
    chunks, parts, _, _ = grad.shape
    tokens = frames // 2

    def cut(rows):
        return pl.BlockSpec((1, rows, tokens), lambda s, c: (s, 0, c))

    def whole(*shape):
        return pl.BlockSpec(shape, lambda s, c: (0,) * len(shape))

    consts = (g2, w1, w2, wo)
    anywhere = pl.BlockSpec(memory_space=pl.ANY)
    halves = [(2, model // 2, width) for width in (hidden, hidden, inner)]
    widths = [a.shape[1] for a in halves_in]
    dma = pltpu.SemaphoreType.DMA
    return pl.pallas_call(
        lambda *refs: time_ffn_backward_kernel(heads, *refs),
        grid=(slots, frames // tokens),
        out_shape=(
            jax.ShapeDtypeStruct((slots, model, frames), F32),
            jax.ShapeDtypeStruct((slots, inner, frames), BF16),
            jax.ShapeDtypeStruct((slots, heads, frames), F32),
            jax.ShapeDtypeStruct((slots, heads, frames), F32),
            [jax.ShapeDtypeStruct(shape, BF16) for shape in halves],
            jax.ShapeDtypeStruct((model, 1), F32),
            [jax.ShapeDtypeStruct((model // 8, width), BF16) for width in widths],
        ),
        in_specs=[pl.BlockSpec((chunks // 2,) + grad.shape[1:], lambda s, c: (c, 0, 0, 0))]
        + [cut(a.shape[1]) for a in (act, slope, nf, mid, mixed, att, gate, linv)]
        + [whole_spec(c) for c in consts]
        + [[anywhere for _ in widths]],
        out_specs=(
            cut(model),
            cut(inner),
            cut(heads),
            cut(heads),
            [whole(*shape) for shape in halves],
            whole(model, 1),
            [anywhere for _ in widths],
        ),
        scratch_shapes=[
            pltpu.VMEM((model, hidden), F32),
            pltpu.VMEM((model, hidden), F32),
            pltpu.VMEM((model, inner), F32),
            pltpu.VMEM((model, 1), F32),
            [pltpu.VMEM((model // 2, width), BF16) for width in widths],
            [
                [pltpu.VMEM((rows, width), BF16) for rows in (model // 4, model // 8)]
                for width in widths
            ],
            [pltpu.VMEM((Z_COUNT - 1, model // 8, width // Z_COUNT), BF16) for width in widths[:BAND_EARLY]],
            dma((len(widths), TOTAL_STEPS)),
            dma((len(widths), TOTAL_STEPS)),
            dma((2 * len(widths),)),
        ],
        compiler_params=pltpu.CompilerParams(
            vmem_limit_bytes=VMEM_BYTES, collective_id=2, has_side_effects=True
        ),
        cost_estimate=cost(8.0e6 * slots * frames, 0, 30e6),
        name="time_ffn_backward",
    )(grad, act, slope, nf, mid, mixed, att, gate, linv, *consts, list(halves_in))


BAND_PLACES = ((0, 2, 5, 9, 10), (0, 3, 6, 9, 10), (0, 4, 6, 10, 13, 14), (0, 5, 7, 10, 12, 13))
FFN_PLACES = ((0, 1, 4, 6, 8, 11, 13, 16, 18), (0, 1, 4, 7, 9, 12, 14, 18, 20), (0, 2, 5, 7, 10, 12, 14, 19, 20))
PAIR_PLACES = ((4, 5, 10, 12, 14, 16, 18, 23, 24), (8, 9, 11, 14, 16, 18, 24, 25, 26), (12, 13, 18, 24, 25), (16, 18, 22, 24, 25))


def time_attention_backward_kernel(
    heads,
    slots,
    batch_count,
    p_ref,
    q_ref,
    k_ref,
    v_ref,
    datt_ref,
    minus_ref,
    x_ref,
    dmid_ref,
    logit_block_ref,
    n_ref,
    dlogit_ref,
    cos_ref,
    sin_ref,
    g1_ref,
    wp_ref,
    wgt_ref,
    narrow_ref,
    dg2_ref,
    part_refs,
    ffn_refs,
    grad_out,
    band_outs,
    ffn_outs,
    pair_outs,
    dproj_ref,
    wp_turned_ref,
    grad_buf,
    piece_refs,
    band_recvs,
    held_refs,
    ffn_recvs,
    pair_refs,
    pair_recvs,
    around_recv,
    band_sems,
    ffn_sems,
    pair_sems,
    grad_sems,
    local_sem,
):
    place = Place()
    step = pl.program_id(0)
    steps = heads * slots
    head, slot = step // slots, lax.rem(step, slots)
    size, frames = q_ref.shape[1:]
    model = n_ref.shape[1]
    inner = heads * size
    pairs = heads // 2
    pair_rows = 6 * size
    blocks = frames // BLOCK
    last = pl.num_programs(0) - 1
    my_band, my_batch = place.band, place.batch

    bands = [Total(place, order, band_sems[0].at[i], band_sems[1].at[i]) for i, order in enumerate(BAND_ORDERS)]
    ffns = [Total(place, order, ffn_sems[0].at[i], ffn_sems[1].at[i]) for i, order in enumerate(FFN_ORDERS)]
    own = [
        Total(place, PAIR_ORDERS[i], pair_sems[0].at[i], pair_sems[1].at[i]) for i in range(pairs)
    ]

    def half_copy(i):
        return pltpu.make_async_copy(ffn_refs[i].at[place.bits["core"]], held_refs[i], local_sem.at[len(bands) + i])

    def eighth(total, held):
        return held.at[total.half_rows(held, 2)[0]]

    def all_steps(total, source, held, recvs, out, sem):
        width = recvs[3].shape[2]

        def back_region():
            return out.at[total.back_rows(out, 2)]

        def s0():
            total.start_core(source, recvs[0])

        def s1():
            total.end_core(held, recvs[0])
            total.start_half(1, held, recvs[1])

        def s2():
            total.end_half(1, held, recvs[1])
            total.start_half(2, held, recvs[2])

        def s3():
            total.end_half(2, held, recvs[2])
            total.start_z(eighth(total, held), recvs[3])

        def s4():
            total.end_z(eighth(total, held), recvs[3])
            total.start_z_back(eighth(total, held), back_region(), width, sem)

        def s5():
            total.end_z_back(eighth(total, held), back_region(), width, sem)
            total.start_back(2, out)

        def s6():
            total.end_back(2, out)
            total.start_back(1, out)

        def s7():
            total.end_back(1, out)
            total.start_back(0, out)

        def s8():
            total.end_back(0, out)

        return [s0, s1, s2, s3, s4, s5, s6, s7, s8]

    plan = {}

    def at_step(index, action):
        plan.setdefault(index, []).append(action)

    def enter():
        other_x = place.across("x")[1] // 2
        diagonal = (my_band, 2 * other_x + 1 - place.bits["core"])
        barrier = pltpu.get_barrier_semaphore()

        def call(other):
            pl.semaphore_signal(barrier, inc=1, device_id=other, device_id_type=pl.DeviceIdType.MESH)

        own[-1].around(lambda step, quarter, z, other: call(other))
        call(place.across("core"))
        call(diagonal)
        pl.semaphore_wait(barrier, 4 * Z_COUNT + 1)
        for i in range(len(ffns)):
            half_copy(i).start()

    tail = steps + slots * blocks
    at_step(0, enter)

    def schedule(actions, places):
        for at, action in zip(places, actions):
            at_step(at, action)

    for i in range(len(bands)):
        out = band_outs[i]
        region = out.at[bands[i].back_rows(out, 2)]
        quarter = band_outs[i].shape[1] // Z_COUNT

        def z_begin(i=i):
            piece_refs[i][...] = part_refs[i][...]
            if i >= BAND_EARLY:
                bands[i].start_z(piece_refs[i], band_recvs[i - BAND_EARLY])

        def z_turn(i=i, region=region, quarter=quarter):
            if i >= BAND_EARLY:
                bands[i].end_z(piece_refs[i], band_recvs[i - BAND_EARLY])
            bands[i].start_z_back(piece_refs[i], region, quarter, local_sem.at[i])

        def z_end(i=i, region=region, quarter=quarter, out=out):
            bands[i].end_z_back(piece_refs[i], region, quarter, local_sem.at[i])
            bands[i].start_back(2, out)

        def back_two(i=i, out=out):
            bands[i].end_back(2, out)
            bands[i].start_back(1, out)

        def back_one(i=i, out=out):
            bands[i].end_back(1, out)
            bands[i].start_back(0, out)

        actions = [z_begin, z_turn, z_end, back_two, back_one, lambda i=i, out=out: bands[i].end_back(0, out)]
        if i < BAND_EARLY:
            at_step(0, z_begin)
            actions = actions[1:]
        schedule(actions, BAND_PLACES[i])
    ffn_at = len(bands) + len(ffns)
    for i in range(len(ffns)):
        sem = local_sem.at[ffn_at + i]
        actions = all_steps(ffns[i], ffn_refs[i], held_refs[i], ffn_recvs[i], ffn_outs[i], sem)
        at_step(FFN_PLACES[i][1], lambda i=i: half_copy(i).wait())
        schedule(actions, FFN_PLACES[i])
    pair_at = ffn_at + len(ffns)

    def around_steps(total, source, held, recv, out, sem):
        def s0():
            total.start_core(source, recv[0])

        def s1():
            total.end_core(held, recv[0])
            total.start_around(held, recv[1])

        def s2():
            total.end_around(held, recv[1])
            total.start_around_back(held, recv[1], out, sem)

        def s3():
            total.end_around_back(held, recv[1], out, sem)
            total.start_back(0, out)

        def s4():
            total.end_back(0, out)

        return [s0, s1, s2, s3, s4]

    for i in range(pairs):
        source, held = pair_refs.at[i], pair_refs.at[i, place.bits["core"]]
        out, sem = pair_outs.at[i], local_sem.at[pair_at + i]
        recv = [ref.at[i] for ref in pair_recvs]
        if PAIR_ORDERS[i] is None:
            actions = around_steps(own[i], source, held, [recv[0], around_recv.at[PAIR_ORDERS[:i].count(None)]], out, sem)
        else:
            actions = all_steps(own[i], source, held, recv, out, sem)
        schedule(actions, PAIR_PLACES[i])

    for index in sorted(plan):
        if index < tail:

            @pl.when(step == index)
            def work(index=index):
                for action in plan[index]:
                    action()

    @pl.when(step < steps)
    def attention():
        d_queries, d_keys, d_values = scores_backward(
            q_ref[0],
            k_ref[0],
            v_ref[0],
            p_ref[0, 0],
            datt_ref[0],
            minus_ref[0, pl.ds(head, 1), :],
            cos_ref[...],
            sin_ref[...],
            size**-0.5,
        )
        start = pl.multiple_of((head // 2) * pair_rows + lax.rem(head, 2) * size, size)
        dproj_ref[slot, pl.ds(start, size), :] = d_queries.astype(BF16)
        dproj_ref[slot, pl.ds(start + 2 * size, size), :] = d_keys.astype(BF16)
        dproj_ref[slot, pl.ds(start + 4 * size, size), :] = d_values.astype(BF16)

    @pl.when((step < steps) & (lax.rem(step, 2 * slots) == 2 * slots - 1))
    def pair_done():
        pair = head // 2
        rows = pl.ds(pl.multiple_of(pair * pair_rows, pair_rows), pair_rows)
        sums = dg(n_ref[0], dproj_ref[0, rows, :], NT)
        for j in range(1, slots):
            sums = sums + dg(n_ref[j], dproj_ref[j, rows, :], NT)
        for half in range(2):
            at = slice(half * model // 2, (half + 1) * model // 2)
            pair_refs[pair, half, :, 0:pair_rows] = sums[at].astype(BF16)

    @pl.when(step == 2 * slots - 1)
    def narrow_done():
        gates = 0.0
        for j in range(slots):
            logit = jnp.concatenate([dlogit_ref[j], jnp.zeros_like(dlogit_ref[j])], axis=0).astype(BF16)
            gates = gates + dg(n_ref[j], logit, NT)[:, :heads]
        tile = narrow_tile([narrow_ref[:, : heads + 2], gates, dg2_ref[...]], model)
        for half in range(2):
            at = slice(half * model // 2, (half + 1) * model // 2)
            pair_refs[0, half, :, pair_rows:] = tile[at].astype(BF16)
            for i in range(1, pairs):
                pair_refs[i, half, :, pair_rows:] = jnp.zeros_like(tile[at]).astype(BF16)
        for pair in range(pairs):
            for part in range(3):
                to = pair * pair_rows + part * 2 * size
                source = part * inner + pair * 2 * size
                wp_turned_ref[:, to : to + 2 * size] = wp_ref[:, source : source + 2 * size]

    def message(index):
        j, i = index // blocks, lax.rem(index, blocks)
        source = grad_buf.at[index]
        target = grad_out.at[batch_count * j + my_batch]
        return i, source, target

    @pl.when(step >= steps)
    def rows_done():
        index = step - steps
        j, i = index // blocks, lax.rem(index, blocks)
        at = pl.ds(pl.multiple_of(i * BLOCK, BLOCK), BLOCK)
        logit = logit_block_ref[0].astype(BF16)
        d_normed = dg(wp_turned_ref[...], dproj_ref[j, :, at], NN) + dg(wgt_ref[...], logit, TN)
        d_rows, _ = norm_backward(x_ref[0].astype(F32).T, column(g1_ref), d_normed)
        grad_buf[index] = (dmid_ref[0] + d_rows).T.astype(BF16)
        i, source, target = message(index)

        @pl.when(i == my_batch)
        def keep():
            pltpu.make_async_copy(source, target, local_sem.at[pair_at + pairs]).start()

        @pl.when(i != my_batch)
        def give():
            send(source, target, grad_sems.at[0], grad_sems.at[1], my_band, i)

    @pl.when(step == last)
    def finish():
        for index in sorted(plan):
            if index >= tail:
                for action in plan[index]:
                    action()
        await_bytes(grad_buf.at[pl.ds(0, slots)], local_sem.at[pair_at + pairs])
        others = grad_buf.at[pl.ds(0, slots * (batch_count - 1))]
        await_bytes(others, grad_sems.at[0])
        await_bytes(others, grad_sems.at[1])


def time_attention_backward(
    p, q, k, v, datt, minus, dlogit, n, x, dmid, cos, sin, g1, wp, wgt, narrow, dg2, parts, ffn_sums, batch_count
):
    slots, inner, frames = q.shape
    heads = minus.shape[1]
    size = inner // heads
    model = n.shape[1]
    pairs = heads // 2
    steps = heads * slots
    blocks = frames // BLOCK

    def clamp(t):
        return jnp.minimum(t, steps - 1)

    def tail(t):
        return jnp.maximum(t - steps, 0)

    def per_head(rows, columns):
        return pl.BlockSpec((1, rows, columns), lambda t: (lax.rem(clamp(t), slots), clamp(t) // slots, 0))

    consts = (n, dlogit, cos, sin, g1, wp, wgt, narrow, dg2)
    anywhere = pl.BlockSpec(memory_space=pl.ANY)
    dma = pltpu.SemaphoreType.DMA
    widths = [a.shape[2] for a in ffn_sums]
    pair_width = 8 * size

    def recv_buffers(width, *lead):
        rows = model // 2
        shapes = [(rows, width), (rows // 2, width), (rows // 4, width), (Z_COUNT - 1, rows // 4, width // Z_COUNT)]
        return [pltpu.VMEM(lead + shape, BF16) for shape in shapes]

    return pl.pallas_call(
        lambda *refs: time_attention_backward_kernel(heads, slots, batch_count, *refs),
        grid=(steps + slots * blocks,),
        out_shape=(
            jax.ShapeDtypeStruct((batch_count * slots, BLOCK, model), BF16),
            [jax.ShapeDtypeStruct((model, a.shape[1]), BF16) for a in parts],
            [jax.ShapeDtypeStruct((model, width), BF16) for width in widths],
            jax.ShapeDtypeStruct((pairs, model, pair_width), BF16),
        ),
        in_specs=[
            pl.BlockSpec((1, 1, frames, frames), lambda t: (lax.rem(clamp(t), slots), clamp(t) // slots, 0, 0)),
            per_head(size, frames),
            per_head(size, frames),
            per_head(size, frames),
            per_head(size, frames),
            pl.BlockSpec((1, heads, frames), lambda t: (lax.rem(clamp(t), slots), 0, 0)),
            pl.BlockSpec((1, BLOCK, model), lambda t: (tail(t) // blocks, lax.rem(tail(t), blocks), 0)),
            pl.BlockSpec((1, model, BLOCK), lambda t: (tail(t) // blocks, 0, lax.rem(tail(t), blocks))),
            pl.BlockSpec((1, heads, BLOCK), lambda t: (tail(t) // blocks, 0, lax.rem(tail(t), blocks))),
        ]
        + [whole_spec(c) for c in consts]
        + [[whole_spec(a) for a in parts], [anywhere] * len(ffn_sums)],
        out_specs=(anywhere, [anywhere] * len(parts), [anywhere] * len(ffn_sums), anywhere),
        scratch_shapes=[
            pltpu.VMEM((slots, 3 * inner, frames), BF16),
            pltpu.VMEM((model, 3 * inner), BF16),
            pltpu.VMEM((slots * blocks, BLOCK, model), BF16),
            [pltpu.VMEM(a.shape, BF16) for a in parts],
            [pltpu.VMEM((Z_COUNT - 1, a.shape[0], a.shape[1] // Z_COUNT), BF16) for a in parts[BAND_EARLY:]],
            [pltpu.VMEM((model // 2, width), BF16) for width in widths],
            [recv_buffers(width) for width in widths],
            pltpu.VMEM((pairs, 2, model // 2, pair_width), BF16),
            recv_buffers(pair_width, pairs),
            pltpu.VMEM((PAIR_ORDERS.count(None), 4 * Z_COUNT - 1, model // 8, pair_width // Z_COUNT), BF16),
            [dma((len(parts), TOTAL_STEPS))] * 2,
            [dma((len(widths), TOTAL_STEPS))] * 2,
            [dma((pairs, TOTAL_STEPS)), dma((pairs, TOTAL_STEPS))],
            dma((2,)),
            dma((len(parts) + 2 * len(widths) + pairs + 1,)),
        ],
        compiler_params=pltpu.CompilerParams(
            vmem_limit_bytes=VMEM_BYTES, collective_id=3, has_side_effects=True
        ),
        cost_estimate=cost(20.0e6 * slots * frames, 0, 60e6),
        name="time_attention_backward",
    )(p, q, k, v, datt, minus, x, dmid, dlogit, *consts, list(parts), list(ffn_sums))


def finish_kernel(
    heads,
    grad_ref,
    bwp_ref,
    bw1_ref,
    bw2t_ref,
    bwot_ref,
    w1_ref,
    wot_ref,
    w2t_ref,
    pair_ref,
    first_pair_ref,
    wp_ref,
    wgt_ref,
    g1_ref,
    y_ref,
    y_out,
    grad_out,
    dg1_out,
    dwp_out,
    dwg_out,
    dwo_out,
    dg2_out,
    dw1_out,
    dw2_out,
    bg1_out,
    bwp_out,
    bwg_out,
    bwo_out,
    bg2_out,
    bw1_out,
    bw2_out,
    scaled_ref,
):
    pair = pl.program_id(0)
    inner = wp_ref.shape[1] // 3
    width = inner // pl.num_programs(0)
    pairs, bands, parts, rows, model = y_ref.shape
    split = y_ref[...].astype(F32).reshape(pairs, bands, parts, 2, rows // 2, model)
    for j in range(2):
        values = split[:, :, :, j].reshape(pairs, bands * parts * rows // 2, model)
        for i in range(pairs):
            y_out[2 * i + j] = values[i].astype(BF16)
    grad_out[...] = grad_ref[...].astype(F32)
    bwp_out[...] = bwp_ref[...].astype(F32)
    bw1_out[...] = bw1_ref[...].astype(F32)
    bw2_out[...] = bw2t_ref[...].astype(F32).T
    bwo_out[...] = bwot_ref[...].astype(F32).T
    dw1_out[...] = w1_ref[...].astype(F32)
    dw2_out[...] = w2t_ref[...].astype(F32).T
    dwo_out[...] = wot_ref[...].astype(F32).T

    @pl.when(pair == 0)
    def clear():
        scaled_ref[...] = jnp.zeros_like(scaled_ref)

    for part in range(3):
        at = pl.ds(pl.multiple_of(part * inner + pair * width, 128), width)
        values = pair_ref[0, :, part * width : (part + 1) * width].astype(F32)
        dwp_out[:, at] = values
        scaled_ref[...] += values * wp_ref[:, at].astype(F32)

    @pl.when(pair == pl.num_programs(0) - 1)
    def narrow():
        tile = first_pair_ref[0, :, 3 * width :].astype(F32)
        rows = tile.T
        bwg_out[...] = rows[:heads]
        bg1_out[...] = rows[heads]
        bg2_out[...] = rows[heads + 1]
        gates = tile[:, heads + 2 : 2 * heads + 2]
        dwg_out[...] = rows[heads + 2 : 2 * heads + 2]
        dg2_out[...] = rows[2 * heads + 2]
        sums = jnp.sum(scaled_ref[...], axis=1, keepdims=True)
        sums = sums + jnp.sum(gates * wgt_ref[...].astype(F32).T, axis=1, keepdims=True)
        dg1_out[...] = jnp.broadcast_to(sums, (sums.shape[0], 128)).T[0] / g1_ref[...].astype(F32)


def finish_sums(grads, y, band_sums, ffn_sums, pair_sums, g1, params):
    wp, wgt, wo, w1, w2 = params
    model, hidden = w1.shape
    inner, heads = wo.shape[0], wgt.shape[0]
    pairs = pair_sums.shape[0]
    split = hidden // pairs
    out_split = inner // pairs
    slot_dev, frame_dev, _ = grads.shape

    def lanes(width):
        return pl.BlockSpec((model, width), lambda i: (0, i))

    def whole(*shape):
        return pl.BlockSpec(shape, lambda i: (0,) * len(shape))

    def cut_rows(rows):
        return pl.BlockSpec((rows, model), lambda i: (i, 0))

    band_wp, band_w1, band_w2t, band_wot = band_sums
    time_w2t, time_w1, time_wot = ffn_sums
    grad_block = pl.BlockSpec((slot_dev // pairs, frame_dev, model), lambda i: (i, 0, 0))
    narrow = [((model,), whole(model)), ((heads, model), whole(heads, model))]
    per_layer = [
        narrow[0],
        ((model, 3 * inner), None),
        narrow[1],
        ((inner, model), cut_rows(out_split)),
        narrow[0],
        ((model, hidden), lanes(split)),
        ((hidden, model), cut_rows(split)),
    ]
    shapes, specs = [jax.ShapeDtypeStruct(grads.shape, BF16), jax.ShapeDtypeStruct(grads.shape, F32)], [grad_block] * 2
    y_block = pl.BlockSpec((y.shape[0] // pairs,) + y.shape[1:], lambda i: (i, 0, 0, 0, 0))
    for layer in range(2):
        for shape, spec in per_layer:
            shapes.append(jax.ShapeDtypeStruct(shape, F32))
            if spec is None:
                spec = whole(*shape) if layer == 0 else lanes(3 * inner // pairs)
            specs.append(spec)
    return pl.pallas_call(
        lambda *refs: finish_kernel(heads, *refs),
        grid=(pairs,),
        out_shape=shapes,
        in_specs=[
            grad_block,
            lanes(3 * inner // pairs),
            lanes(split),
            lanes(split),
            lanes(out_split),
            lanes(split),
            lanes(out_split),
            lanes(split),
            pl.BlockSpec((1, model, pair_sums.shape[2]), lambda i: (i, 0, 0)),
            pl.BlockSpec((1, model, pair_sums.shape[2]), lambda i: (0, 0, 0)),
            whole_spec(wp),
            whole_spec(wgt),
            whole_spec(g1),
            y_block,
        ],
        out_specs=specs,
        scratch_shapes=[pltpu.VMEM((model, inner // pairs), F32)],
        compiler_params=pltpu.CompilerParams(vmem_limit_bytes=VMEM_BYTES),
        name="finish_sums",
    )(
        grads,
        band_wp,
        band_w1,
        band_w2t,
        band_wot,
        time_w1,
        time_wot,
        time_w2t,
        pair_sums,
        pair_sums,
        wp,
        wgt,
        g1,
        y,
    )


def band_kernel(
    heads,
    batch_count,
    band_count,
    x_ref,
    cot_ref,
    count_ref,
    slots_ref,
    g1_ref,
    g2_ref,
    wgt_ref,
    wpt_ref,
    wot_ref,
    w1t_ref,
    w2t_ref,
    wp_ref,
    wo_ref,
    w1_ref,
    w2_ref,
    y_out,
    dx_out,
    half_outs,
    narrow_out,
    q_ref,
    k_ref,
    v_ref,
    p_ref,
    turned_ref,
    gate_ref,
    linv_ref,
    att_ref,
    mixed_ref,
    act_ref,
    slope_ref,
    hidden_ref,
    dmixed_ref,
    dlogit_ref,
    dproj_ref,
    dwp_ref,
    dw1_ref,
    dw2t_ref,
    dwot_ref,
    dwg_ref,
    dg1_ref,
    dg2_ref,
    xs_ref,
    cots_ref,
    ys_ref,
    dxs_ref,
    y_buf,
    dx_buf,
    y_send,
    y_recv,
    dx_send,
    dx_recv,
    local_sem,
    bias_ref,
    cos_ref,
    sin_ref,
    valid_ref,
    halves,
    core_recvs,
    core_sems,
    half_sem,
):
    step = pl.program_id(0)
    slot_count, part_frames, model = x_ref.shape
    inner, tokens = q_ref.shape
    size = inner // heads
    groups = tokens // BLOCK
    taken = tokens // slot_count
    per_part = part_frames // taken
    part = step // per_part
    first = lax.rem(step, per_part) * taken
    my_band, my_batch = lax.axis_index("band"), lax.axis_index("batch")
    slot_dev = slot_count // band_count
    slots = slot_dev // batch_count
    own_chunk = my_batch * band_count + my_band
    chunks = band_count * batch_count

    columns = [slice(at, at + 128) for at in range(0, model, 128)]

    def tokens_of(ref):
        return jnp.concatenate(
            [
                jnp.concatenate(
                    [ref[c, pl.ds(first + i, slot_count, stride=part_frames), :] for i in range(taken)], axis=0
                ).T
                for c in range(len(columns))
            ],
            axis=0,
        )

    def put_tokens(ref, values, start, stride):
        for c, at in enumerate(columns):
            turned = values[at].T
            for i in range(taken):
                ref[c, pl.ds(start + i, slot_count, stride=stride), :] = turned[
                    i * slot_count : (i + 1) * slot_count
                ]

    @pl.when(step == 0)
    def enter():
        greet_all(band_count, batch_count)
        bands = slots_ref[...].reshape(1, slot_count)
        cos, sin = rotary_rows(jnp.maximum(bands, 0).astype(F32), size // 2)
        cos_ref[...] = jnp.concatenate([cos] * taken, axis=1)
        sin_ref[...] = jnp.concatenate([sin] * taken, axis=1)
        valid = jnp.concatenate([jnp.where(bands >= 0, 1.0, 0.0)] * taken, axis=1)
        valid_ref[...] = valid
        keys = jnp.broadcast_to(valid[:, :BLOCK], (8, BLOCK)).T[:, :1]
        row = lax.broadcasted_iota(jnp.int32, (BLOCK, BLOCK), 0) // slot_count
        column_index = lax.broadcasted_iota(jnp.int32, (BLOCK, BLOCK), 1) // slot_count
        bias_ref[...] = jnp.where((row == column_index) & (keys > 0.5), 0.0, NEG_FILL)

    @pl.when(lax.rem(step, per_part) == 0)
    def unpack():
        for c, at in enumerate(columns):
            xs_ref[c] = x_ref[:, :, at].astype(F32).reshape(xs_ref.shape[1:])
            cots_ref[c] = cot_ref[:, :, at].astype(F32).reshape(cots_ref.shape[1:])

    place = Place()
    totals = [
        Total(place, order, core_sems.at[0, i], core_sems.at[1, i]) for i, order in enumerate(BAND_ORDERS)
    ]
    gain1, gain2 = column(g1_ref), column(g2_ref)
    piece = part_frames * (pl.num_programs(0) // per_part)
    own_start = (my_batch * band_count + my_band) * piece

    @pl.when(step == 0)
    def clear():
        for ref in (dwp_ref, dw1_ref, dw2t_ref, dwot_ref, dwg_ref, dg1_ref, dg2_ref):
            ref[...] = jnp.zeros_like(ref)

    rows = tokens_of(xs_ref)
    normed = norm_forward(rows, gain1)
    q_ref[...], k_ref[...], v_ref[...] = project_block(
        normed, wpt_ref, cos_ref[...], sin_ref[...], inner, LOG2E * size**-0.5
    )
    gate_ref[...] = dg(wgt_ref[...], normed, NN)
    ones = extra_rows([jnp.ones((1, BLOCK), F32)], BLOCK)
    nothing = jnp.zeros((size, BLOCK), BF16)

    def apart(first, second):
        return jnp.concatenate(
            [jnp.concatenate([first, nothing], axis=1), jnp.concatenate([nothing, second], axis=1)], axis=0
        )

    turned_ref[...] = k_ref[...].T
    bias = jnp.concatenate([bias_ref[...]] * 2, axis=1)

    def attend(pair, carry):
        both = pl.ds(pl.multiple_of(2 * pair * size, 2 * size), 2 * size)
        at = [pl.ds(pl.multiple_of((2 * pair + i) * size, size), size) for i in range(2)]
        for group in range(groups):
            lanes = slice(group * BLOCK, (group + 1) * BLOCK)
            scores = dg(turned_ref[lanes, both], apart(*(q_ref[one, lanes] for one in at)), NN) + bias
            weights = jnp.exp2(scores - jnp.max(scores, axis=0, keepdims=True)).astype(BF16)
            p_ref[pair * groups + group] = weights
            for i, one in enumerate(at):
                row = pl.ds(2 * pair + i, 1)
                own = weights[:, i * BLOCK : (i + 1) * BLOCK]
                sums = dg(jnp.concatenate([v_ref[one, lanes], ones], axis=0), own, NN)
                inverse = 1.0 / sums[size : size + 1]
                attended = sums[:size] * inverse
                linv_ref[row, lanes] = inverse
                att_ref[one, lanes] = attended
                gate = jax.nn.sigmoid(gate_ref[row, lanes])
                mixed_ref[one, lanes] = (attended * gate).astype(BF16)
        return carry

    lax.fori_loop(0, heads // 2, attend, 0, unroll=4)
    middle = rows + dg(wot_ref[...], mixed_ref[...], NN)
    normed_ffn = norm_forward(middle, gain2)

    result = feed_forward(middle, normed_ffn, w1t_ref, w2t_ref, act_ref, slope_ref)
    frame = own_start + step * taken + lax.broadcasted_iota(jnp.int32, (1, tokens), 1) // slot_count
    mask = jnp.where(frame < count_ref[0], valid_ref[...], 0.0)
    result = result * mask
    put_tokens(ys_ref, result, 0, taken)

    couples = slot_dev // 2
    for c, at in enumerate(columns):
        y_buf[step, :, :, at] = ys_ref[c].reshape(slot_count // 2, 2 * taken, 128).astype(BF16)

    def give_row(i, carry):
        other = lax.rem(my_band + i, band_count)
        send(
            y_buf.at[step, pl.ds(other * couples, couples)],
            y_out.at[:, my_band, step],
            y_send,
            y_recv,
            other,
            my_batch,
        )
        return carry

    lax.fori_loop(1, band_count, give_row, 0)
    pltpu.make_async_copy(
        y_buf.at[step, pl.ds(my_band * couples, couples)], y_out.at[:, my_band, step], local_sem.at[0]
    ).start()

    grad = tokens_of(cots_ref) * mask
    d_middle, ffn_branch, d_hidden = ffn_backward(grad, slope_ref[...], middle, gain2, w1_ref, w2_ref, dg2_ref)
    hidden_ref[...] = d_hidden
    branch = d_middle.astype(BF16)
    dmixed_ref[...] = dg(wo_ref[...], branch, NN)

    turned_ref[...] = v_ref[...].T
    def attend_back(pair, carry):
        both = pl.ds(pl.multiple_of(2 * pair * size, 2 * size), 2 * size)
        starts = [pl.multiple_of((2 * pair + i) * size, size) for i in range(2)]
        at = [pl.ds(start, size) for start in starts]
        d_atts, minuses = [], []
        for i, one in enumerate(at):
            row = pl.ds(2 * pair + i, 1)
            d_att, minus, d_logit = head_backward(
                dmixed_ref[one, :], att_ref[one, :], gate_ref[row, :], linv_ref[row, :]
            )
            dlogit_ref[row, :] = d_logit
            d_atts.append(d_att)
            minuses.append(minus)
        for group in range(groups):
            lanes = slice(group * BLOCK, (group + 1) * BLOCK)
            weights = p_ref[pair * groups + group]
            d_weights = dg(turned_ref[lanes, both], apart(*(d_att[:, lanes] for d_att in d_atts)), NN)
            minus = jnp.concatenate([minus[:, lanes] for minus in minuses], axis=1)
            d_scores = (weights.astype(F32) * (d_weights + minus)).astype(BF16)
            cos, sin = cos_ref[:, lanes], -sin_ref[:, lanes]
            for i, one in enumerate(at):
                own = slice(i * BLOCK, (i + 1) * BLOCK)
                d_queries = dg(k_ref[one, lanes], d_scores[:, own], NN) * size**-0.5
                d_keys = dg(q_ref[one, lanes], d_scores[:, own], NT) * (1.0 / LOG2E)
                d_values = dg(d_atts[i][:, lanes], weights[:, own], NT)
                dproj_ref[one, lanes] = turn(d_queries, cos, sin).astype(BF16)
                dproj_ref[pl.ds(inner + starts[i], size), lanes] = turn(d_keys, cos, sin).astype(BF16)
                dproj_ref[pl.ds(2 * inner + starts[i], size), lanes] = d_values.astype(BF16)
        return carry

    lax.fori_loop(0, heads // 2, attend_back, 0, unroll=4)
    d_logit = jnp.concatenate([dlogit_ref[...], jnp.zeros_like(dlogit_ref)], axis=0).astype(BF16)
    d_normed = dg(wp_ref[...], dproj_ref[...], NN) + dg(wgt_ref[...], dlogit_ref[...].astype(BF16), TN)
    d_rows, terms = norm_backward(rows, gain1, d_normed)
    dg1_ref[...] += jnp.sum(terms, axis=1, keepdims=True)
    put_tokens(dxs_ref, d_middle + d_rows, 0, taken)
    for c, at in enumerate(columns):
        grouped = dxs_ref[c].reshape(band_count, slots, batch_count, taken, 128)
        grouped = jnp.concatenate([grouped[:, j][:, :, None] for j in range(slots)], axis=2)
        dx_buf[step, :, :, at] = grouped.reshape(chunks, slots * taken, 128).astype(BF16)

    def give_grad(i, carry):
        other = lax.rem(my_band * batch_count + my_batch + i, chunks)
        send(
            dx_buf.at[step, other],
            dx_out.at[own_chunk, step],
            dx_send,
            dx_recv,
            other // batch_count,
            lax.rem(other, batch_count),
        )
        return carry

    lax.fori_loop(1, chunks, give_grad, 0)
    pltpu.make_async_copy(
        dx_buf.at[step, my_band * batch_count + my_batch], dx_out.at[own_chunk, step], local_sem.at[1]
    ).start()

    dwp_ref[...] += dg(normed, dproj_ref[...], NT)
    dwg_ref[...] += dg(normed, d_logit, NT)[:, :heads]
    dwot_ref[...] += dg(branch, mixed_ref[...], NT)
    add_ffn_sums(dw1_ref, dw2t_ref, ffn_branch, act_ref[...], normed_ffn, hidden_ref[...])

    @pl.when(step == pl.num_programs(0) - 1)
    def finish():
        narrow_out[...] = narrow_tile([dwg_ref[...], dg1_ref[...], dg2_ref[...]], model)
        core = place.bits["core"]
        for i, ref in enumerate((dwp_ref, dw1_ref, dw2t_ref, dwot_ref)):
            lay_halves(halves[i], ref)
            totals[i].start_core(halves[i], core_recvs[i])
        for i, total in enumerate(totals):
            total.end_core(halves[i].at[core], core_recvs[i])
            pltpu.make_async_copy(halves[i].at[core], half_outs[i], half_sem.at[i]).start()
        for i in range(len(totals)):
            pltpu.make_async_copy(halves[i].at[core], half_outs[i], half_sem.at[i]).wait()
        await_bytes(y_out.at[:, 0], local_sem.at[0])
        await_bytes(dx_out.at[0], local_sem.at[1])
        for sem in (y_send, y_recv):
            await_bytes(y_out.at[:, pl.ds(0, band_count - 1)], sem)
        for sem in (dx_send, dx_recv):
            await_bytes(dx_out.at[pl.ds(0, chunks - 1)], sem)


def band_layer(rows, cot, counts, slot_bands, g1, g2, params, flips, band_count, batch_count):
    project, gating, output_weight, expand, shrink = params
    slot_count, piece, model = rows.shape
    tokens = 2 * BLOCK
    steps = slot_count * piece // tokens
    heads, inner, hidden = gating.shape[0], output_weight.shape[0], expand.shape[1]
    groups = tokens // BLOCK
    taken = tokens // slot_count
    part_frames = 16
    per_part = part_frames // taken
    slots = slot_count // (band_count * batch_count)
    slot_dev = slot_count // band_count
    consts = (slot_bands, g1, g2, gating) + flips + (project, output_weight, expand, shrink)
    widths = (3 * inner, hidden, hidden, inner)
    chunks = band_count * batch_count
    blocks = pl.BlockSpec((slot_count, part_frames, model), lambda i: (0, i // per_part, 0))
    anywhere = pl.BlockSpec(memory_space=pl.ANY)
    dma = pltpu.SemaphoreType.DMA
    return pl.pallas_call(
        lambda *refs: band_kernel(heads, batch_count, band_count, *refs),
        grid=(steps,),
        out_shape=(
            jax.ShapeDtypeStruct((slot_dev // 2, band_count, steps, 2 * taken, model), BF16),
            jax.ShapeDtypeStruct((chunks, steps, slots * taken, model), BF16),
            [jax.ShapeDtypeStruct((model // 2, width), BF16) for width in widths],
            jax.ShapeDtypeStruct((model, 128), F32),
        ),
        in_specs=[blocks, blocks, pl.BlockSpec(memory_space=pltpu.SMEM)] + [whole_spec(c) for c in consts],
        out_specs=(
            anywhere,
            anywhere,
            [anywhere for _ in widths],
            pl.BlockSpec((model, 128), lambda i: (0, 0)),
        ),
        scratch_shapes=[
            pltpu.VMEM((inner, tokens), BF16),
            pltpu.VMEM((inner, tokens), BF16),
            pltpu.VMEM((inner, tokens), BF16),
            pltpu.VMEM((heads // 2 * groups, BLOCK, 2 * BLOCK), BF16),
            pltpu.VMEM((tokens, inner), BF16),
            pltpu.VMEM((heads, tokens), F32),
            pltpu.VMEM((heads, tokens), F32),
            pltpu.VMEM((inner, tokens), F32),
            pltpu.VMEM((inner, tokens), BF16),
            pltpu.VMEM((hidden, tokens), BF16),
            pltpu.VMEM((hidden, tokens), BF16),
            pltpu.VMEM((hidden, tokens), BF16),
            pltpu.VMEM((inner, tokens), F32),
            pltpu.VMEM((heads, tokens), F32),
            pltpu.VMEM((3 * inner, tokens), BF16),
            pltpu.VMEM((model, 3 * inner), F32),
            pltpu.VMEM((model, hidden), F32),
            pltpu.VMEM((model, hidden), F32),
            pltpu.VMEM((model, inner), F32),
            pltpu.VMEM((model, heads), F32),
            pltpu.VMEM((model, 1), F32),
            pltpu.VMEM((model, 1), F32),
            pltpu.VMEM((model // 128, slot_count * part_frames, 128), F32),
            pltpu.VMEM((model // 128, slot_count * part_frames, 128), F32),
            pltpu.VMEM((model // 128, tokens, 128), F32),
            pltpu.VMEM((model // 128, tokens, 128), F32),
            pltpu.VMEM((steps, slot_count // 2, 2 * taken, model), BF16),
            pltpu.VMEM((steps, chunks, slots * taken, model), BF16),
            dma,
            dma,
            dma,
            dma,
            dma((2,)),
            pltpu.VMEM((BLOCK, BLOCK), F32),
            pltpu.VMEM((inner // heads // 2, tokens), F32),
            pltpu.VMEM((inner // heads // 2, tokens), F32),
            pltpu.VMEM((1, tokens), F32),
            [pltpu.VMEM((2, model // 2, width), BF16) for width in widths],
            [pltpu.VMEM((model // 2, width), BF16) for width in widths],
            dma((2, len(widths), TOTAL_STEPS)),
            dma((len(widths),)),
        ],
        compiler_params=pltpu.CompilerParams(
            vmem_limit_bytes=VMEM_BYTES, collective_id=1, has_side_effects=True
        ),
        cost_estimate=cost(30.0e6 * slot_count * piece, 0, 60e6),
        name="band_layer",
    )(rows, cot, counts, *consts)


def slot_shards(activations, cotangent, frame_counts, slot_bands, *weights):
    slot_dev, _, frame_dev, model = activations.shape
    batch, band = lax.axis_size("batch"), lax.axis_size("band")
    g1, wp, wg, wo, g2, w1, w2 = weights[:7]
    band_g1, band_wp, band_wg, band_wo, band_g2, band_w1, band_w2 = weights[7:]
    heads = wg.shape[1]
    time_params = (wp, wg.T, wo, w1, w2)
    band_params = (band_wp, band_wg.T, band_wo, band_w1, band_w2)
    band_rows, band_cot, rows, n, q, k, v, p, linv, gate, att, mixed, mid, nf, act, slope, *turned = time_forward(
        activations.reshape(slot_dev, frame_dev, model),
        cotangent.reshape(slot_dev, frame_dev, model),
        frame_counts,
        g1,
        g2,
        time_params,
        band_params,
        band,
        batch,
    )
    cos, sin = turned[-2:]
    y, slot_grad, band_halves, band_narrow = band_layer(
        band_rows,
        band_cot,
        frame_counts,
        slot_bands,
        band_g1,
        band_g2,
        band_params,
        tuple(turned[:-2]),
        band,
        batch,
    )
    dmid, datt, minus, dlogit, ffn_halves, dg2, band_parts = time_ffn_backward(
        slot_grad, act, slope, nf, mid, mixed, att, gate, linv, g2, w1, w2, wo, band_halves
    )
    input_grad, band_sums, ffn_sums, pair_sums = time_attention_backward(
        p,
        q,
        k,
        v,
        datt,
        minus,
        dlogit,
        n,
        rows,
        dmid,
        cos,
        sin,
        g1,
        wp,
        time_params[1],
        band_narrow,
        dg2,
        band_parts,
        ffn_halves,
        batch,
    )
    layer_output, input_grad, *grads = finish_sums(
        input_grad, y, band_sums, ffn_sums, pair_sums, g1, time_params
    )
    grads = [g.T if g.shape[0] == heads else g for g in grads]
    return (layer_output.reshape(activations.shape), input_grad.reshape(activations.shape), *grads)


def shards(activations, cotangent, frame_counts, slot_bands, *weights):
    slot_dev, clips, frame_dev, _ = activations.shape
    batch, band = lax.axis_size("batch"), lax.axis_size("band")
    fits = (
        clips == 1
        and batch == 4
        and band == 2 * Z_COUNT
        and slot_dev % batch == 0
        and frame_dev == BLOCK
        and frame_dev == 32 * band
        and slot_bands.shape[0] == 64 == slot_dev * band
        and slot_dev == 2 * batch
        and activations.shape[-1] % 128 == 0
        and (frame_dev // band * slot_bands.shape[0]) % (2 * BLOCK) == 0
        and weights[2].shape[1] == 8
    )
    form = slot_shards if fits else generic_shards
    return form(activations, cotangent, frame_counts, slot_bands, *weights)


def solution(mesh):
    return jax.shard_map(
        shards,
        mesh=mesh,
        in_specs=(
            P("band", None, "batch", None),
            P("band", None, "batch", None),
            P(),
            P(),
            P(),
            P(),
            P(),
            P(),
            P(),
            P(),
            P(),
            P(),
            P(),
            P(),
            P(),
            P(),
            P(),
            P(),
        ),
        out_specs=(
            P("band", None, "batch", None),
            P("band", None, "batch", None),
            P(),
            P(),
            P(),
            P(),
            P(),
            P(),
            P(),
            P(),
            P(),
            P(),
            P(),
            P(),
            P(),
            P(),
        ),
        check_vma=False,
    )
```

```python
import math

import jax
import jax.numpy as jnp
from jax import lax
from jax.experimental import pallas as pl
from jax.experimental.pallas import tpu as pltpu
from jax.sharding import PartitionSpec as P

EPSILON = 1e-05
NEG_FILL = -1000000000.0
TIME_LAYOUT = ("bqhe", "bkhe")
BAND_LAYOUT = ("qbhe", "kbhe")


def rms_scale(residual, gain):
    return (
        residual * lax.rsqrt(jnp.mean(residual * residual, axis=-1, keepdims=True) + EPSILON) * gain
    )


def gelu_exact(values):
    return jax.nn.gelu(values, approximate=False)


def rotary_tables(positions, head_size):
    half_size = head_size // 2
    rates = jnp.exp(-math.log(10000.0) * jnp.arange(half_size, dtype=jnp.float32) / half_size)
    angles = positions[:, None] * rates[None, :]
    return (jnp.cos(angles), jnp.sin(angles))


def rotate(vectors, cos_table, sin_table):
    half_size = vectors.shape[-1] // 2
    first = vectors[..., :half_size]
    second = vectors[..., half_size:]
    return jnp.concatenate(
        [first * cos_table - second * sin_table, first * sin_table + second * cos_table], axis=-1
    )


def token_sum(left, right):
    return lax.dot_general(
        left.reshape(-1, left.shape[-1]),
        right.reshape(-1, right.shape[-1]),
        (((0,), (0,)), ((), ())),
        preferred_element_type=jnp.float32,
    )


def back_dot(gradient, weight):
    return lax.dot_general(
        gradient,
        weight,
        (((gradient.ndim - 1,), (1,)), ((), ())),
        preferred_element_type=jnp.float32,
    )


def block_forward(queries, key_rows, value_rows, key_valid, layout):
    query_form, key_form = layout
    scores = (
        jnp.einsum(
            query_form + "," + key_form + "->bhqk",
            queries,
            key_rows,
            preferred_element_type=jnp.float32,
        )
        * 0.125
    )
    scores = jnp.where(key_valid[:, None, None, :], scores, NEG_FILL)
    highest = jnp.max(scores, axis=-1, keepdims=True)
    exponents = jnp.exp(scores - highest)
    totals = jnp.sum(exponents, axis=-1, keepdims=True)
    soft_weights = (exponents / totals).astype(jnp.bfloat16)
    output = jnp.einsum(
        "bhqk," + key_form + "->" + query_form,
        soft_weights,
        value_rows,
        preferred_element_type=jnp.float32,
    )
    return (output, highest + jnp.log(totals))


def block_backward(queries, key_rows, value_rows, key_valid, log_totals, out_grad, layout):
    query_form, key_form = layout
    scores = (
        jnp.einsum(
            query_form + "," + key_form + "->bhqk",
            queries,
            key_rows,
            preferred_element_type=jnp.float32,
        )
        * 0.125
    )
    soft_weights = jnp.where(key_valid[:, None, None, :], jnp.exp(scores - log_totals), 0.0)
    weight_grad = jnp.einsum(
        query_form + "," + key_form + "->bhqk",
        out_grad,
        value_rows,
        preferred_element_type=jnp.float32,
    )
    score_grad = (
        soft_weights * (weight_grad - jnp.sum(soft_weights * weight_grad, axis=-1, keepdims=True))
    ).astype(jnp.bfloat16)
    query_grad = (
        jnp.einsum(
            "bhqk," + key_form + "->" + query_form,
            score_grad,
            key_rows,
            preferred_element_type=jnp.float32,
        )
        * 0.125
    )
    key_grad = (
        jnp.einsum(
            "bhqk," + query_form + "->" + key_form,
            score_grad,
            queries,
            preferred_element_type=jnp.float32,
        )
        * 0.125
    )
    value_grad = jnp.einsum(
        "bhqk," + query_form + "->" + key_form,
        soft_weights.astype(jnp.bfloat16),
        out_grad,
        preferred_element_type=jnp.float32,
    )
    return (query_grad, key_grad, value_grad)


def time_attend(queries, key_rows, value_rows, key_valid):
    keys_full, values_full = (
        lax.all_gather(key_rows, "batch", axis=1, tiled=True),
        lax.all_gather(value_rows, "batch", axis=1, tiled=True),
    )
    output, log_totals = block_forward(queries, keys_full, values_full, key_valid, TIME_LAYOUT)
    return (output, (log_totals, keys_full, values_full))


def time_attend_back(queries, key_rows, value_rows, key_valid, attn_kept, out_grad):
    log_totals, keys_full, values_full = attn_kept
    query_grad, key_full_grad, value_full_grad = block_backward(
        queries, keys_full, values_full, key_valid, log_totals, out_grad, TIME_LAYOUT
    )
    key_grad, value_grad = (
        lax.psum_scatter(
            key_full_grad.astype(jnp.bfloat16), "batch", scatter_dimension=1, tiled=True
        ).astype(jnp.float32),
        lax.psum_scatter(
            value_full_grad.astype(jnp.bfloat16), "batch", scatter_dimension=1, tiled=True
        ).astype(jnp.float32),
    )
    return (query_grad, key_grad, value_grad)


def band_attend(queries, key_rows, value_rows, key_valid):
    return block_forward(queries, key_rows, value_rows, key_valid, BAND_LAYOUT)


def band_attend_back(queries, key_rows, value_rows, key_valid, attn_kept, out_grad):
    return block_backward(
        queries, key_rows, value_rows, key_valid, attn_kept, out_grad, BAND_LAYOUT
    )


def layer_forward(residual, params, tables, key_valid, attend):
    prenorm, project, gating, output_weight, midnorm, expand, shrink = params
    cos_table, sin_table = tables
    normed = rms_scale(residual, prenorm.astype(jnp.float32)).astype(jnp.bfloat16)
    projected = jnp.dot(normed, project, preferred_element_type=jnp.float32)
    gate_logits = jnp.dot(normed, gating, preferred_element_type=jnp.float32)
    inner_width = output_weight.shape[0]
    head_count = gating.shape[1]
    head_shape = residual.shape[:-1] + (head_count, inner_width // head_count)
    queries = rotate(projected[..., :inner_width].reshape(head_shape), cos_table, sin_table).astype(
        jnp.bfloat16
    )
    key_rows = rotate(
        projected[..., inner_width : 2 * inner_width].reshape(head_shape), cos_table, sin_table
    ).astype(jnp.bfloat16)
    value_rows = projected[..., 2 * inner_width :].reshape(head_shape).astype(jnp.bfloat16)
    attended, attn_kept = attend(queries, key_rows, value_rows, key_valid)
    gate_values = jax.nn.sigmoid(gate_logits)
    mixed_heads = (
        (attended * gate_values[..., None])
        .reshape(residual.shape[:-1] + (inner_width,))
        .astype(jnp.bfloat16)
    )
    middle = residual + jnp.dot(mixed_heads, output_weight, preferred_element_type=jnp.float32)
    normed_ffn = rms_scale(middle, midnorm.astype(jnp.float32)).astype(jnp.bfloat16)
    hidden = jnp.dot(normed_ffn, expand, preferred_element_type=jnp.float32)
    active = gelu_exact(hidden).astype(jnp.bfloat16)
    result = middle + jnp.dot(active, shrink, preferred_element_type=jnp.float32)
    kept_values = (
        residual,
        normed,
        gate_logits,
        queries,
        key_rows,
        value_rows,
        attn_kept,
        attended,
        mixed_heads,
        middle,
        normed_ffn,
        hidden,
        active,
    )
    return (result, kept_values)


def layer_backward(result_grad, params, kept_values, tables, key_valid, attend_back):
    prenorm, project, gating, output_weight, midnorm, expand, shrink = params
    (
        residual,
        normed,
        gate_logits,
        queries,
        key_rows,
        value_rows,
        attn_kept,
        attended,
        mixed_heads,
        middle,
        normed_ffn,
        hidden,
        active,
    ) = kept_values
    cos_table, sin_table = tables
    branch_grad = result_grad.astype(jnp.bfloat16)
    shrink_grad = token_sum(active, branch_grad)
    active_grad = back_dot(branch_grad, shrink)
    hidden_grad = jax.vjp(gelu_exact, hidden)[1](active_grad)[0].astype(jnp.bfloat16)
    expand_grad = token_sum(normed_ffn, hidden_grad)
    normed_ffn_grad = back_dot(hidden_grad, expand)
    middle_norm_grad, midnorm_grad = jax.vjp(rms_scale, middle, midnorm.astype(jnp.float32))[1](
        normed_ffn_grad
    )
    middle_grad = result_grad + middle_norm_grad
    attn_branch = middle_grad.astype(jnp.bfloat16)
    output_grad = token_sum(mixed_heads, attn_branch)
    mixed_grad = back_dot(attn_branch, output_weight).reshape(attended.shape)
    gate_values = jax.nn.sigmoid(gate_logits)
    attended_grad = (mixed_grad * gate_values[..., None]).astype(jnp.bfloat16)
    logit_grad = (
        jnp.sum(mixed_grad * attended, axis=-1) * gate_values * (1.0 - gate_values)
    ).astype(jnp.bfloat16)
    query_grad, key_grad, value_grad = attend_back(
        queries, key_rows, value_rows, key_valid, attn_kept, attended_grad
    )
    flat_shape = residual.shape[:-1] + (-1,)
    projected_grad = jnp.concatenate(
        [
            rotate(query_grad, cos_table, -sin_table).reshape(flat_shape),
            rotate(key_grad, cos_table, -sin_table).reshape(flat_shape),
            value_grad.reshape(flat_shape),
        ],
        axis=-1,
    ).astype(jnp.bfloat16)
    project_grad = token_sum(normed, projected_grad)
    gating_grad = token_sum(normed, logit_grad)
    normed_grad = back_dot(projected_grad, project) + back_dot(logit_grad, gating)
    residual_norm_grad, prenorm_grad = jax.vjp(rms_scale, residual, prenorm.astype(jnp.float32))[1](
        normed_grad
    )
    return (
        middle_grad + residual_norm_grad,
        (
            prenorm_grad,
            project_grad,
            gating_grad,
            output_grad,
            midnorm_grad,
            expand_grad,
            shrink_grad,
        ),
    )


def generic_shards(
    activations,
    cotangent,
    frame_counts,
    slot_bands,
    time_prenorm,
    time_project,
    time_gating,
    time_output,
    time_midnorm,
    time_expand,
    time_shrink,
    band_prenorm,
    band_project,
    band_gating,
    band_output,
    band_midnorm,
    band_expand,
    band_shrink,
):
    slot_dev, clip_count, frame_dev, model_width = activations.shape
    slot_count = slot_bands.shape[0]
    frames_all = frame_dev * lax.axis_size("batch")
    head_size = time_output.shape[0] // time_gating.shape[1]
    time_params = (
        time_prenorm,
        time_project,
        time_gating,
        time_output,
        time_midnorm,
        time_expand,
        time_shrink,
    )
    band_params = (
        band_prenorm,
        band_project,
        band_gating,
        band_output,
        band_midnorm,
        band_expand,
        band_shrink,
    )
    own_bands = lax.dynamic_slice_in_dim(slot_bands, lax.axis_index("band") * slot_dev, slot_dev)
    frame_start = lax.axis_index("batch") * frame_dev
    own_frames = frame_start + jnp.arange(frame_dev, dtype=jnp.int32)
    frame_valid = own_frames[None, :] < frame_counts[:, None]
    row_valid = (own_bands >= 0)[:, None, None] & frame_valid[None]
    full_valid = jnp.arange(frames_all, dtype=jnp.int32)[None, :] < frame_counts[:, None]
    time_valid = jnp.broadcast_to(full_valid[None], (slot_dev, clip_count, frames_all)).reshape(
        slot_dev * clip_count, frames_all
    )
    time_cos, time_sin = rotary_tables(own_frames.astype(jnp.float32), head_size)
    time_tables = (time_cos[None, :, None, :], time_sin[None, :, None, :])
    band_cos, band_sin = rotary_tables(jnp.maximum(slot_bands, 0).astype(jnp.float32), head_size)
    band_tables = (band_cos[:, None, None, :], band_sin[:, None, None, :])
    residual = activations.astype(jnp.float32).reshape(
        slot_dev * clip_count, frame_dev, model_width
    )
    time_result, time_kept = layer_forward(
        residual, time_params, time_tables, time_valid, time_attend
    )
    masked_cot = jnp.where(row_valid[..., None], cotangent, jnp.zeros((), jnp.bfloat16)).reshape(
        slot_dev, clip_count * frame_dev, model_width
    )
    frame_rows = lax.all_to_all(
        time_result.astype(jnp.bfloat16), "band", split_axis=1, concat_axis=0, tiled=True
    ).astype(time_result.dtype)
    band_valid = jnp.broadcast_to((slot_bands >= 0)[None, :], (frame_rows.shape[1], slot_count))
    band_result, band_kept = layer_forward(
        frame_rows, band_params, band_tables, band_valid, band_attend
    )
    back_rows = lax.all_to_all(
        band_result.astype(jnp.bfloat16), "band", split_axis=0, concat_axis=1, tiled=True
    ).astype(band_result.dtype)
    layer_output = jnp.where(
        row_valid[..., None], back_rows.reshape(activations.shape), 0.0
    ).astype(jnp.bfloat16)
    frame_cot = lax.all_to_all(masked_cot, "band", split_axis=1, concat_axis=0, tiled=True)
    frame_grad, band_grads = layer_backward(
        frame_cot.astype(jnp.float32),
        band_params,
        band_kept,
        band_tables,
        band_valid,
        band_attend_back,
    )
    slot_grad = lax.all_to_all(
        frame_grad.astype(jnp.bfloat16), "band", split_axis=0, concat_axis=1, tiled=True
    ).astype(frame_grad.dtype)
    input_grad, time_grads = layer_backward(
        slot_grad, time_params, time_kept, time_tables, time_valid, time_attend_back
    )
    input_grad = input_grad.reshape(activations.shape)
    all_grads = lax.psum(
        (
            time_grads[0],
            time_grads[1],
            time_grads[2],
            time_grads[3],
            time_grads[4],
            time_grads[5],
            time_grads[6],
            band_grads[0],
            band_grads[1],
            band_grads[2],
            band_grads[3],
            band_grads[4],
            band_grads[5],
            band_grads[6],
        ),
        ("band", "batch"),
    )
    return (
        layer_output,
        input_grad,
        all_grads[0],
        all_grads[1],
        all_grads[2],
        all_grads[3],
        all_grads[4],
        all_grads[5],
        all_grads[6],
        all_grads[7],
        all_grads[8],
        all_grads[9],
        all_grads[10],
        all_grads[11],
        all_grads[12],
        all_grads[13],
    )


BLOCK = 256
LOG2E = 1.4426950408889634
F32 = jnp.float32
BF16 = jnp.bfloat16
NN = (((1,), (0,)), ((), ()))
NT = (((1,), (1,)), ((), ()))
TN = (((0,), (0,)), ((), ()))
VMEM_BYTES = 60 * 2**20


def dg(left, right, dims):
    return lax.dot_general(left, right, dims, preferred_element_type=F32)


def norm_forward(rows, gain):
    scale = lax.rsqrt(jnp.mean(rows * rows, axis=0, keepdims=True) + EPSILON)
    return (rows * scale * gain).astype(BF16)


def norm_backward(rows, gain, grad):
    scale = lax.rsqrt(jnp.mean(rows * rows, axis=0, keepdims=True) + EPSILON)
    unit = rows * scale
    scaled = grad * gain
    inner = jnp.mean(scaled * unit, axis=0, keepdims=True)
    return scale * (scaled - unit * inner), grad * unit


def gelu_pair(values):
    size = jnp.abs(values)
    denominator = 1.0 + (0.3275911 * math.sqrt(0.5)) * size
    t = pl.reciprocal(denominator, approx=True)
    t = t * (2.0 - denominator * t)
    bell = jnp.exp2(values * values * (-0.5 * LOG2E))
    poly = 0.5 * 1.061405429
    for coefficient in (-1.453152027, 1.421413741, -0.284496736, 0.254829592):
        poly = poly * t + 0.5 * coefficient
    tail = poly * t * bell
    upper = jnp.where(values < 0.0, tail, 1.0 - tail)
    slope = upper + values * bell * (1.0 / math.sqrt(2.0 * math.pi))
    return values * upper, slope


def feed_forward(middle, normed, w1t_ref, w2t_ref, act_ref, slope_ref):
    part = w1t_ref.shape[0] // 3
    result = middle
    hidden = dg(w1t_ref[0:part, :], normed, NN)
    for i in range(3):
        rows = slice(i * part, (i + 1) * part)
        later = None
        if i < 2:
            later = dg(w1t_ref[(i + 1) * part : (i + 2) * part, :], normed, NN)
        active, slope = gelu_pair(hidden)
        active = active.astype(BF16)
        act_ref[rows, :] = active
        slope_ref[rows, :] = slope.astype(BF16)
        result = result + dg(w2t_ref[:, rows], active, NN)
        hidden = later
    return result


def turn(vectors, cos, sin):
    half = cos.shape[0]
    split = vectors.reshape(-1, 2 * half, vectors.shape[-1])
    first = split[:, :half]
    second = split[:, half:]
    turned = jnp.concatenate([first * cos - second * sin, first * sin + second * cos], axis=1)
    return turned.reshape(vectors.shape)


def three_parts(values):
    top = values.astype(BF16).astype(F32)
    rest = values - top
    middle = rest.astype(BF16).astype(F32)
    return top, middle, rest - middle


def extra_rows(rows, width):
    tile = jnp.concatenate(rows + [jnp.zeros((8 - len(rows), width), F32)], axis=0)
    return jnp.concatenate([tile, jnp.zeros((8, width), F32)], axis=0).astype(BF16)


def project_block(normed, wpt_ref, cos, sin, inner, scale):
    queries = turn(dg(wpt_ref[0:inner, :], normed, NN), cos, sin) * scale
    keys = turn(dg(wpt_ref[inner : 2 * inner, :], normed, NN), cos, sin)
    values = dg(wpt_ref[2 * inner : 3 * inner, :], normed, NN)
    return queries.astype(BF16), keys.astype(BF16), values.astype(BF16)


def column(gain_ref):
    row = gain_ref[...].astype(F32).reshape(1, gain_ref.shape[0])
    return jnp.broadcast_to(row, (8, row.shape[1])).T[:, :1]


def rotary_rows(positions, half):
    rank = lax.broadcasted_iota(jnp.int32, (half, positions.shape[1]), 0).astype(F32)
    angles = positions * jnp.exp(-math.log(10000.0) * rank / half)
    return jnp.cos(angles), jnp.sin(angles)


def flipped(ref):
    return ref[...].astype(F32).T.astype(BF16)


def greet_all(band_count, batch_count):
    count = band_count * batch_count
    me = lax.axis_index("band") * batch_count + lax.axis_index("batch")
    barrier = pltpu.get_barrier_semaphore()

    def signal(i, carry):
        other = lax.rem(me + i, count)
        pl.semaphore_signal(
            barrier,
            inc=1,
            device_id=(other // batch_count, lax.rem(other, batch_count)),
            device_id_type=pl.DeviceIdType.MESH,
        )
        return carry

    lax.fori_loop(1, count, signal, 0)
    pl.semaphore_wait(barrier, count - 1)


def send(source, target, send_sem, recv_sem, band, batch):
    pltpu.make_async_remote_copy(
        src_ref=source,
        dst_ref=target,
        send_sem=send_sem,
        recv_sem=recv_sem,
        device_id=(band, batch),
        device_id_type=pl.DeviceIdType.MESH,
    ).start()


def await_bytes(ref, sem):
    pltpu.make_async_copy(ref, ref, sem).wait()


def by_rows(rows, action):
    def block(i, carry):
        action(pl.multiple_of(i * 16, 16))
        return carry

    lax.fori_loop(0, rows // 16, block, 0)


class Place:
    def __init__(self):
        self.band, self.batch = lax.axis_index("band"), lax.axis_index("batch")
        self.bits = {
            "core": lax.rem(self.batch, 2),
            "x": self.batch // 2,
            "y": lax.rem(self.band, 2),
        }
        self.z = self.band // 2

    def across(self, axis):
        bit = self.bits[axis]
        if axis == "core":
            return self.band, self.batch + 1 - 2 * bit
        if axis == "x":
            return self.band, self.batch + 2 - 4 * bit
        return self.band + 1 - 2 * bit, self.batch

    def along_z(self, step):
        other = lax.rem(self.z + step, Z_COUNT)
        return other, (other * 2 + self.bits["y"], self.batch)


Z_COUNT = 4


def greet(others):
    barrier = pltpu.get_barrier_semaphore()
    for other in others:
        pl.semaphore_signal(barrier, inc=1, device_id=other, device_id_type=pl.DeviceIdType.MESH)
    pl.semaphore_wait(barrier, len(others))


class Total:
    def __init__(self, place, order, sends, recvs):
        self.place = place
        self.order = order
        self.sends, self.recvs = sends, recvs
        self.core = place.bits["core"]
        if order is not None:
            self.first, self.second = (place.bits[axis] for axis in order)

    def give(self, step, source, target, other):
        send(source, target, self.sends.at[step], self.recvs.at[step], *other)

    def took(self, step, ref):
        await_bytes(ref, self.recvs.at[step])
        await_bytes(ref, self.sends.at[step])

    def add(self, ref, start, part):
        def some(i):
            at, own = pl.ds(pl.multiple_of(start + i, 16), 16), pl.ds(i, 16)
            ref[at] = (ref[at].astype(F32) + part[own].astype(F32)).astype(BF16)

        by_rows(part.shape[0], some)

    def start_core(self, source, recv):
        self.give(0, source.at[1 - self.core], recv, self.place.across("core"))

    def end_core(self, held, recv):
        self.took(0, recv)
        self.add(held, 0, recv)

    def half_rows(self, held, level):
        rows = held.shape[0] // 2
        base = 0
        if level == 2:
            base, rows = self.first * rows, rows // 2
        bit = self.first if level == 1 else self.second
        keep = pl.ds(pl.multiple_of(base + bit * rows, rows), rows)
        away = pl.ds(pl.multiple_of(base + (1 - bit) * rows, rows), rows)
        return keep, away

    def start_half(self, level, held, recv):
        away = self.half_rows(held, level)[1]
        self.give(level, held.at[away], recv, self.place.across(self.order[level - 1]))

    def end_half(self, level, held, recv):
        self.took(level, recv)
        self.add(held, self.half_rows(held, level)[0].start, recv)

    def start_z(self, piece, recv):
        width = recv.shape[2]
        for step in range(1, Z_COUNT):
            index, other = self.place.along_z(step)
            lanes = pl.ds(pl.multiple_of(index * width, 128), width)
            self.give(3, piece.at[:, lanes], recv.at[step - 1], other)

    def z_lanes(self, width):
        return pl.ds(pl.multiple_of(self.place.z * width, 128), width)

    def end_z(self, piece, recv):
        self.took(3, recv)
        lanes = self.z_lanes(recv.shape[2])
        sums = piece[:, lanes].astype(F32)
        for step in range(Z_COUNT - 1):
            sums = sums + recv[step].astype(F32)
        piece[:, lanes] = sums.astype(BF16)

    def own_copy(self, piece, target, width, sem):
        lanes = self.z_lanes(width)
        return pltpu.make_async_copy(piece.at[:, lanes], target.at[:, lanes], sem)

    def start_z_back(self, piece, target, width, sem):
        lanes = self.z_lanes(width)
        for step in range(1, Z_COUNT):
            _, other = self.place.along_z(step)
            self.give(4, piece.at[:, lanes], target.at[:, lanes], other)
        self.own_copy(piece, target, width, sem).start()

    def end_z_back(self, piece, target, width, sem):
        self.took(4, target.at[:, pl.ds(0, (Z_COUNT - 1) * width)])
        self.own_copy(piece, target, width, sem).wait()

    def chip(self, step):
        x = lax.rem(self.place.bits["x"] + lax.rem(step // 2, 2), 2)
        y = lax.rem(self.place.bits["y"] + lax.rem(step, 2), 2)
        z = lax.rem(self.place.z + step // 4, Z_COUNT)
        return 2 * x + y, z, (2 * z + y, 2 * x + self.core)

    def around(self, action):
        def one(step, carry):
            action(step, *self.chip(step))
            return carry

        lax.fori_loop(1, 4 * Z_COUNT, one, 0)

    def tile(self, ref, base, quarter, z, shape):
        rows = pl.ds(pl.multiple_of(base + quarter * shape[0], shape[0]), shape[0])
        return ref.at[rows, pl.ds(pl.multiple_of(z * shape[1], 128), shape[1])]

    def start_around(self, held, recv):
        def one(step, quarter, z, other):
            self.give(1, self.tile(held, 0, quarter, z, recv.shape[1:]), recv.at[step - 1], other)

        self.around(one)

    def own_tile(self, ref, base, shape):
        return self.tile(ref, base, 2 * self.place.bits["x"] + self.place.bits["y"], self.place.z, shape)

    def end_around(self, held, recv):
        self.took(1, recv)
        own = self.own_tile(held, 0, recv.shape[1:])
        sums = own[...].astype(F32)
        for i in range(recv.shape[0]):
            sums = sums + recv[i].astype(F32)
        own[...] = sums.astype(BF16)

    def start_around_back(self, held, recv, out, sem):
        shape = recv.shape[1:]
        own = self.own_tile(held, 0, shape)
        target = self.own_tile(out, self.core * (out.shape[0] // 2), shape)
        self.around(lambda step, quarter, z, other: self.give(2, own, target, other))
        pltpu.make_async_copy(own, target, sem).start()

    def end_around_back(self, held, recv, out, sem):
        shape = recv.shape[1:]
        self.took(2, recv)
        target = self.own_tile(out, self.core * (out.shape[0] // 2), shape)
        pltpu.make_async_copy(self.own_tile(held, 0, shape), target, sem).wait()

    def back_rows(self, out, level):
        rows = out.shape[0] // 2
        base = self.core * rows
        if level >= 1:
            rows = rows // 2
            base = base + self.first * rows
        if level >= 2:
            rows = rows // 2
            base = base + self.second * rows
        return pl.ds(pl.multiple_of(base, rows), rows)

    def start_back(self, level, out, source=None):
        rows = self.back_rows(out, level)
        axis = "core" if level == 0 else self.order[level - 1]
        self.give(7 - level, out.at[rows] if source is None else source, out.at[rows], self.place.across(axis))

    def end_back(self, level, out):
        self.took(7 - level, out.at[self.back_rows(out, level)])


TOTAL_STEPS = 8


def time_forward_kernel(
    heads,
    batch_count,
    band_count,
    act_in,
    cot_in,
    count_ref,
    g1_ref,
    g2_ref,
    wgt_ref,
    wp_ref,
    wo_ref,
    w1_ref,
    w2_ref,
    band_wp_ref,
    band_wo_ref,
    band_w1_ref,
    band_w2_ref,
    band_rows,
    band_cot,
    rows_ref,
    n_ref,
    q_ref,
    k_ref,
    v_ref,
    p_ref,
    linv_ref,
    gate_ref,
    att_ref,
    mixed_ref,
    mid_ref,
    nf_ref,
    act_ref,
    slope_ref,
    band_wpt_ref,
    band_wot_ref,
    band_w1t_ref,
    band_w2t_ref,
    cos_ref,
    sin_ref,
    xt_ref,
    x_ref,
    result_ref,
    wpt_ref,
    wot_ref,
    w1t_ref,
    w2t_ref,
    row_send,
    row_recv,
    cot_send,
    cot_recv,
    result_send,
    result_recv,
    local_sem,
):
    slot, head = pl.program_id(0), pl.program_id(1)
    slots = pl.num_programs(0)
    slot_dev = cot_in.shape[0]
    frames, model = rows_ref.shape[1:]
    inner = q_ref.shape[1]
    size = inner // heads
    my_band, my_batch = lax.axis_index("band"), lax.axis_index("batch")
    frame_dev = frames // batch_count
    piece = frame_dev // band_count
    own_rows = pl.ds(pl.multiple_of(my_batch * frame_dev, frame_dev), frame_dev)
    held = x_ref.shape[0]
    frame_index = lax.broadcasted_iota(jnp.int32, (1, frames), 1)

    def neighbour(i):
        core, x = lax.rem(my_batch, 2), my_batch // 2
        return lax.rem(x + i // 2, 2) * 2 + lax.rem(core + lax.rem(i, 2), 2)

    def own_row_copy(j):
        return pltpu.make_async_copy(
            act_in.at[batch_count * j + my_batch], x_ref.at[j, own_rows], local_sem.at[j]
        )

    def own_cot_copy():
        return pltpu.make_async_copy(
            cot_in.at[:, pl.ds(pl.multiple_of(my_band * piece, piece), piece)],
            band_cot.at[pl.ds(my_band * slot_dev, slot_dev)],
            local_sem.at[held],
        )

    @pl.when((slot == 0) & (head == 0))
    def start():
        greet_all(band_count, batch_count)
        for j in range(held):
            for i in range(1, batch_count):
                other = neighbour(i)
                send(
                    act_in.at[batch_count * j + other],
                    x_ref.at[j, own_rows],
                    row_send,
                    row_recv.at[j, i],
                    my_band,
                    other,
                )
            own_row_copy(j).start()

        def send_cot(i, carry):
            other = lax.rem(my_band + i, band_count)
            send(
                cot_in.at[:, pl.ds(pl.multiple_of(other * piece, piece), piece)],
                band_cot.at[pl.ds(my_band * slot_dev, slot_dev)],
                cot_send,
                cot_recv,
                other,
                my_batch,
            )
            return carry

        lax.fori_loop(1, band_count, send_cot, 0)
        own_cot_copy().start()
        cos_ref[...], sin_ref[...] = rotary_rows(frame_index.astype(F32), size // 2)
        wpt_ref[...] = flipped(wp_ref)
        wot_ref[...] = flipped(wo_ref)
        w1t_ref[...] = flipped(w1_ref)
        w2t_ref[...] = flipped(w2_ref)
        band_wpt_ref[...] = flipped(band_wp_ref)
        band_wot_ref[...] = flipped(band_wo_ref)
        band_w1t_ref[...] = flipped(band_w1_ref)
        band_w2t_ref[...] = flipped(band_w2_ref)

    @pl.when(head == 0)
    def before():
        gain = column(g1_ref)

        def block(i, carry):
            at = pl.ds(pl.multiple_of(neighbour(i) * BLOCK, BLOCK), BLOCK)

            @pl.when(i == 0)
            def own():
                for j in range(held):

                    @pl.when(slot == j)
                    def kept():
                        own_row_copy(j).wait()

            @pl.when(i > 0)
            def arrived():
                await_bytes(x_ref.at[slot, at], row_recv.at[slot, i])

            held_rows = x_ref[slot, at, :]
            rows_ref[0, at, :] = held_rows
            rows = held_rows.astype(F32).T
            xt_ref[:, at] = rows
            normed = norm_forward(rows, gain)
            n_ref[0, :, at] = normed
            queries, keys, values = project_block(
                normed, wpt_ref, cos_ref[:, at], sin_ref[:, at], inner, LOG2E * size**-0.5
            )
            q_ref[0, :, at] = queries
            k_ref[0, :, at] = keys
            v_ref[0, :, at] = values
            gate_ref[0, :, at] = dg(wgt_ref[...], normed, NN)
            return carry

        lax.fori_loop(0, frames // BLOCK, block, 0, unroll=1)

    at_head = pl.ds(pl.multiple_of(head * size, size), size)
    ones = jnp.ones((1, frames), F32)
    queries = jnp.concatenate([q_ref[0, at_head, :], extra_rows([ones], frames)], axis=0)
    keys = jnp.concatenate([k_ref[0, at_head, :], extra_rows([jnp.where(frame_index < count_ref[0], 0.0, NEG_FILL)], frames)], axis=0)
    values = jnp.concatenate([v_ref[0, at_head, :], extra_rows([ones], frames)], axis=0)
    scores = dg(keys, queries, TN)
    weights = jnp.exp2(scores - jnp.max(scores, axis=0, keepdims=True)).astype(BF16)
    p_ref[0, 0] = weights
    sums = dg(values, weights, NN)
    inverse = 1.0 / sums[size : size + 1]
    attended = sums[:size] * inverse
    linv_ref[0, pl.ds(head, 1), :] = inverse
    att_ref[0, at_head, :] = attended
    gate = jax.nn.sigmoid(gate_ref[0, pl.ds(head, 1), :])
    mixed_ref[0, at_head, :] = (attended * gate).astype(BF16)

    @pl.when(head == heads - 1)
    def after():
        gain = column(g2_ref)
        to_slot = my_band * slot_dev + batch_count * slot + my_batch

        def block(i, carry):
            at = pl.ds(pl.multiple_of(i * BLOCK, BLOCK), BLOCK)
            middle = xt_ref[:, at] + dg(wot_ref[...], mixed_ref[0, :, at], NN)
            mid_ref[0, :, at] = middle
            normed = norm_forward(middle, gain)
            nf_ref[0, :, at] = normed
            result = feed_forward(
                middle, normed, w1t_ref, w2t_ref, act_ref.at[0, :, at], slope_ref.at[0, :, at]
            )
            result_ref[slot, at, :] = result.T.astype(BF16)

            def send_result(j, carry):
                other = lax.rem(my_band + j, band_count)
                source = result_ref.at[slot, pl.ds(pl.multiple_of(i * frame_dev + other * piece, piece), piece)]
                mine = (other == my_band) & (i == my_batch)

                @pl.when(mine)
                def keep():
                    pltpu.make_async_copy(source, band_rows.at[to_slot], local_sem.at[held + 1]).start()

                @pl.when(jnp.logical_not(mine))
                def give():
                    send(source, band_rows.at[to_slot], result_send, result_recv, other, i)

                return carry

            lax.fori_loop(1, band_count + 1, send_result, 0)
            return carry

        lax.fori_loop(0, frames // BLOCK, block, 0, unroll=1)

    @pl.when((slot == slots - 1) & (head == heads - 1))
    def finish():
        others = held * (band_count * batch_count - 1)
        others_cot = (band_count - 1) * slot_dev
        others_rows = (batch_count - 1) * frame_dev
        await_bytes(band_cot.at[pl.ds(0, others_cot)], cot_recv)
        await_bytes(band_cot.at[pl.ds(0, others_cot)], cot_send)
        own_cot_copy().wait()
        await_bytes(x_ref.at[:, pl.ds(0, others_rows)], row_send)
        await_bytes(band_rows.at[pl.ds(0, others)], result_send)
        await_bytes(band_rows.at[pl.ds(0, held)], local_sem.at[held + 1])
        await_bytes(band_rows.at[pl.ds(0, others)], result_recv)


def cost(flops, exps=0, moved=0):
    return pl.CostEstimate(flops=int(flops), bytes_accessed=int(moved), transcendentals=int(exps))


def whole_spec(array):
    nd = array.ndim
    return pl.BlockSpec(array.shape, lambda *ids: (0,) * nd, pipeline_mode=pl.Buffered(1))


def time_forward(activations, cotangent, counts, g1, g2, params, band_params, band_count, batch_count):
    wp, wgt, wo, w1, w2 = params
    bwp, _, bwo, bw1, bw2 = band_params
    slot_dev, frame_dev, model = activations.shape
    slots, frames = slot_dev // batch_count, frame_dev * batch_count
    heads, inner, hidden = wgt.shape[0], wo.shape[0], w1.shape[1]
    piece = frame_dev // band_count

    def per_slot(*shape):
        return pl.BlockSpec((1,) + shape, lambda s, h: (s,) + (0,) * len(shape))

    outs = [
        ((frames, model), BF16),
        ((model, frames), BF16),
        ((inner, frames), BF16),
        ((inner, frames), BF16),
        ((inner, frames), BF16),
        None,
        ((heads, frames), F32),
        ((heads, frames), F32),
        ((inner, frames), F32),
        ((inner, frames), BF16),
        ((model, frames), F32),
        ((model, frames), BF16),
        ((hidden, frames), BF16),
        ((hidden, frames), BF16),
    ]
    flips = [(w.shape[1], w.shape[0]) for w in (bwp, bwo, bw1, bw2)]
    own_flips = [(w.shape[1], w.shape[0]) for w in (wp, wo, w1, w2)]
    exchanged = jax.ShapeDtypeStruct((slot_dev * band_count, piece, model), BF16)
    anywhere = pl.BlockSpec(memory_space=pl.ANY)
    shapes, specs = [exchanged, exchanged], [anywhere, anywhere]
    for entry in outs:
        if entry is None:
            shapes.append(jax.ShapeDtypeStruct((slots, heads, frames, frames), BF16))
            specs.append(pl.BlockSpec((1, 1, frames, frames), lambda s, h: (s, h, 0, 0)))
        else:
            shapes.append(jax.ShapeDtypeStruct((slots,) + entry[0], entry[1]))
            specs.append(per_slot(*entry[0]))
    for shape in flips:
        shapes.append(jax.ShapeDtypeStruct(shape, BF16))
        specs.append(pl.BlockSpec(shape, lambda s, h: (0, 0), pipeline_mode=pl.Buffered(1)))
    consts = (g1, g2, wgt, wp, wo, w1, w2, bwp, bwo, bw1, bw2)
    half = inner // heads // 2
    for _ in range(2):
        shapes.append(jax.ShapeDtypeStruct((half, frames), F32))
        specs.append(pl.BlockSpec((half, frames), lambda s, h: (0, 0)))
    dma = pltpu.SemaphoreType.DMA
    return pl.pallas_call(
        lambda *refs: time_forward_kernel(heads, batch_count, band_count, *refs),
        grid=(slots, heads),
        out_shape=shapes,
        in_specs=[anywhere, anywhere, pl.BlockSpec(memory_space=pltpu.SMEM)] + [whole_spec(c) for c in consts],
        out_specs=specs,
        scratch_shapes=[
            pltpu.VMEM((model, frames), F32),
            pltpu.VMEM((slots, frames, model), BF16),
            pltpu.VMEM((slots, frames, model), BF16),
        ]
        + [pltpu.VMEM(shape, BF16) for shape in own_flips]
        + [dma, dma((slots, batch_count)), dma, dma, dma, dma, dma((slots + 2,))],
        compiler_params=pltpu.CompilerParams(
            vmem_limit_bytes=VMEM_BYTES, collective_id=0, has_side_effects=True
        ),
        cost_estimate=cost(2.0e6 * 4 * slots * frames, 2 * slots * heads * frames * frames, 60e6),
        name="time_forward",
    )(activations, cotangent, counts, *consts)


def ffn_backward(grad, slope, middle, gain, w1_ref, w2_ref, dg2_ref):
    branch = grad.astype(BF16)
    d_hidden = (dg(w2_ref[...], branch, NN) * slope.astype(F32)).astype(BF16)
    d_normed = dg(w1_ref[...], d_hidden, NN)
    d_rows, terms = norm_backward(middle, gain, d_normed)
    dg2_ref[...] += jnp.sum(terms, axis=1, keepdims=True)
    return grad + d_rows, branch, d_hidden


def add_ffn_sums(dw1_ref, dw2t_ref, branch, act, normed, d_hidden):
    dw2t_ref[...] += dg(branch, act, NT)
    dw1_ref[...] += dg(normed, d_hidden, NT)


def head_backward(d_mixed, attended, gate_logit, inverse):
    gate = jax.nn.sigmoid(gate_logit)
    d_logit = jnp.sum(d_mixed * attended, axis=0, keepdims=True) * gate * (1.0 - gate)
    d_att = (d_mixed * (gate * inverse)).astype(BF16)
    minus = -jnp.sum(d_att.astype(F32) * attended, axis=0, keepdims=True)
    return d_att, minus, d_logit


def scores_backward(queries, keys, values, weights, d_att, minus, cos, sin, scale):
    width = queries.shape[1]
    ones = jnp.ones((1, width), F32)
    d_weights = dg(
        jnp.concatenate([values, extra_rows([ones, ones, ones], width)], axis=0),
        jnp.concatenate([d_att, extra_rows(list(three_parts(minus)), width)], axis=0),
        TN,
    )
    d_scores = (weights.astype(F32) * d_weights).astype(BF16)
    d_values = dg(d_att, weights, NT)
    d_queries = dg(keys, d_scores, NN) * scale
    d_keys = dg(queries, d_scores, NT) * (1.0 / LOG2E)
    return turn(d_queries, cos, -sin), turn(d_keys, cos, -sin), d_values


def time_ffn_backward_kernel(
    heads,
    grad_ref,
    act_ref,
    slope_ref,
    nf_ref,
    mid_ref,
    mixed_ref,
    att_ref,
    gate_ref,
    linv_ref,
    g2_ref,
    w1_ref,
    w2_ref,
    wo_ref,
    half_refs,
    dmid_ref,
    datt_ref,
    minus_ref,
    dlogit_ref,
    sums_refs,
    dg2_out,
    part_refs,
    dw1_ref,
    dw2t_ref,
    dwot_ref,
    dg2_ref,
    held_refs,
    half_recvs,
    z_recvs,
    sends,
    recvs,
    local_sem,
):
    place = Place()
    totals = [Total(place, order, sends.at[i], recvs.at[i]) for i, order in enumerate(BAND_ORDERS)]
    early = len(z_recvs)
    work = list(zip(totals, half_refs, held_refs, half_recvs))

    def half_copy(i):
        return pltpu.make_async_copy(half_refs[i], held_refs[i], local_sem.at[i])

    def part_copy(i):
        rows = totals[i].half_rows(held_refs[i], 2)[0]
        return pltpu.make_async_copy(held_refs[i].at[rows], part_refs[i], local_sem.at[len(totals) + i])

    step = pl.program_id(0) * pl.num_programs(1) + pl.program_id(1)
    last = pl.num_programs(0) * pl.num_programs(1) - 1
    size = wo_ref.shape[0] // heads

    @pl.when(step == 0)
    def clear():
        for ref in (dw1_ref, dw2t_ref, dwot_ref, dg2_ref):
            ref[...] = jnp.zeros_like(ref)
        greet([place.across("x"), place.across("y")] + [place.along_z(i)[1] for i in range(1, Z_COUNT)])
        for i, (total, halves, held, recv) in enumerate(work):
            half_copy(i).start()
            total.start_half(1, halves, recv[0])

    def eighth(i):
        return held_refs[i].at[totals[i].half_rows(held_refs[i], 2)[0]]

    @pl.when(step == last - 1)
    def first_half():
        for i, (total, halves, held, recv) in list(enumerate(work))[:early]:
            half_copy(i).wait()
            total.end_half(1, held, recv[0])
            total.start_half(2, held, recv[1])

    @pl.when(step == last)
    def second_half():
        for i, (total, halves, held, recv) in list(enumerate(work))[early:]:
            half_copy(i).wait()
            total.end_half(1, held, recv[0])
            total.start_half(2, held, recv[1])
        for i, (total, halves, held, recv) in list(enumerate(work))[:early]:
            total.end_half(2, held, recv[1])
            total.start_z(eighth(i), z_recvs[i])

    slot = pl.program_id(0)
    chunks, parts, rows, model = grad_ref.shape
    slots = pl.num_programs(0)
    taken = rows // slots
    both = grad_ref[...].astype(F32).reshape(chunks * parts, slots, taken, model)
    grad = both[:, 0]
    for j in range(1, slots):
        grad = jnp.where(slot == j, both[:, j], grad)
    grad = grad.reshape(chunks * parts * taken, model).T
    d_middle, branch, d_hidden = ffn_backward(
        grad, slope_ref[0], mid_ref[0], column(g2_ref), w1_ref, w2_ref, dg2_ref
    )
    add_ffn_sums(dw1_ref, dw2t_ref, branch, act_ref[0], nf_ref[0], d_hidden)
    dmid_ref[0] = d_middle
    branch = d_middle.astype(BF16)
    dwot_ref[...] += dg(branch, mixed_ref[0], NT)
    d_mixed = dg(wo_ref[...], branch, NN)
    logits, minuses = [], []
    for head in range(heads):
        at = slice(head * size, (head + 1) * size)
        d_att, minus, d_logit = head_backward(
            d_mixed[at], att_ref[0, at], gate_ref[0, head : head + 1], linv_ref[0, head : head + 1]
        )
        datt_ref[0, at] = d_att
        minuses.append(minus)
        logits.append(d_logit)
    minus_ref[0] = jnp.concatenate(minuses, axis=0)
    dlogit_ref[0] = jnp.concatenate(logits, axis=0)

    @pl.when(step == last)
    def finish():
        for sums, ref in zip(sums_refs, (dw2t_ref, dw1_ref, dwot_ref)):
            lay_halves(sums, ref)
        dg2_out[...] = dg2_ref[...]
        for i, (total, halves, held, recv) in list(enumerate(work))[early:]:
            total.end_half(2, held, recv[1])
            part_copy(i).start()
        for i, (total, halves, held, recv) in list(enumerate(work))[:early]:
            total.end_z(eighth(i), z_recvs[i])
            part_copy(i).start()
        for i in range(len(work)):
            part_copy(i).wait()


def narrow_tile(parts, rows):
    used = sum(part.shape[1] for part in parts)
    return jnp.concatenate(list(parts) + [jnp.zeros((rows, 128 - used), F32)], axis=1)


def lay_halves(target, ref):
    half_rows = ref.shape[0] // 2
    for half in range(2):

        def some(i, half=half):
            target[half, pl.ds(i, 16), :] = ref[pl.ds(half * half_rows + i, 16), :].astype(BF16)

        by_rows(half_rows, some)


XY, YX = ("x", "y"), ("y", "x")
BAND_ORDERS = (YX, XY, YX, XY)
BAND_EARLY = 2
FFN_ORDERS = (YX, XY, YX)
PAIR_ORDERS = (YX, YX, None, None)


def time_ffn_backward(grad, act, slope, nf, mid, mixed, att, gate, linv, g2, w1, w2, wo, halves_in):
    slots, model, frames = mid.shape
    heads = gate.shape[1]
    inner, hidden = wo.shape[0], w1.shape[1]
    chunks, parts, _, _ = grad.shape
    tokens = frames // 2

    def cut(rows):
        return pl.BlockSpec((1, rows, tokens), lambda s, c: (s, 0, c))

    def whole(*shape):
        return pl.BlockSpec(shape, lambda s, c: (0,) * len(shape))

    consts = (g2, w1, w2, wo)
    anywhere = pl.BlockSpec(memory_space=pl.ANY)
    halves = [(2, model // 2, width) for width in (hidden, hidden, inner)]
    widths = [a.shape[1] for a in halves_in]
    dma = pltpu.SemaphoreType.DMA
    return pl.pallas_call(
        lambda *refs: time_ffn_backward_kernel(heads, *refs),
        grid=(slots, frames // tokens),
        out_shape=(
            jax.ShapeDtypeStruct((slots, model, frames), F32),
            jax.ShapeDtypeStruct((slots, inner, frames), BF16),
            jax.ShapeDtypeStruct((slots, heads, frames), F32),
            jax.ShapeDtypeStruct((slots, heads, frames), F32),
            [jax.ShapeDtypeStruct(shape, BF16) for shape in halves],
            jax.ShapeDtypeStruct((model, 1), F32),
            [jax.ShapeDtypeStruct((model // 8, width), BF16) for width in widths],
        ),
        in_specs=[pl.BlockSpec((chunks // 2,) + grad.shape[1:], lambda s, c: (c, 0, 0, 0))]
        + [cut(a.shape[1]) for a in (act, slope, nf, mid, mixed, att, gate, linv)]
        + [whole_spec(c) for c in consts]
        + [[anywhere for _ in widths]],
        out_specs=(
            cut(model),
            cut(inner),
            cut(heads),
            cut(heads),
            [whole(*shape) for shape in halves],
            whole(model, 1),
            [anywhere for _ in widths],
        ),
        scratch_shapes=[
            pltpu.VMEM((model, hidden), F32),
            pltpu.VMEM((model, hidden), F32),
            pltpu.VMEM((model, inner), F32),
            pltpu.VMEM((model, 1), F32),
            [pltpu.VMEM((model // 2, width), BF16) for width in widths],
            [
                [pltpu.VMEM((rows, width), BF16) for rows in (model // 4, model // 8)]
                for width in widths
            ],
            [pltpu.VMEM((Z_COUNT - 1, model // 8, width // Z_COUNT), BF16) for width in widths[:BAND_EARLY]],
            dma((len(widths), TOTAL_STEPS)),
            dma((len(widths), TOTAL_STEPS)),
            dma((2 * len(widths),)),
        ],
        compiler_params=pltpu.CompilerParams(
            vmem_limit_bytes=VMEM_BYTES, collective_id=2, has_side_effects=True
        ),
        cost_estimate=cost(8.0e6 * slots * frames, 0, 30e6),
        name="time_ffn_backward",
    )(grad, act, slope, nf, mid, mixed, att, gate, linv, *consts, list(halves_in))


BAND_PLACES = ((0, 2, 5, 9, 10), (0, 3, 6, 9, 10), (0, 4, 6, 10, 13, 14), (0, 5, 7, 10, 12, 13))
FFN_PLACES = ((0, 1, 4, 6, 8, 11, 13, 16, 18), (0, 1, 4, 7, 9, 12, 14, 18, 20), (0, 2, 5, 7, 10, 12, 14, 19, 20))
PAIR_PLACES = ((4, 5, 10, 12, 14, 16, 18, 23, 24), (8, 9, 11, 14, 16, 18, 24, 25, 26), (12, 13, 18, 24, 25), (16, 18, 22, 24, 25))


def time_attention_backward_kernel(
    heads,
    slots,
    batch_count,
    p_ref,
    q_ref,
    k_ref,
    v_ref,
    datt_ref,
    minus_ref,
    x_ref,
    dmid_ref,
    logit_block_ref,
    n_ref,
    dlogit_ref,
    cos_ref,
    sin_ref,
    g1_ref,
    wp_ref,
    wgt_ref,
    narrow_ref,
    dg2_ref,
    part_refs,
    ffn_refs,
    grad_out,
    band_outs,
    ffn_outs,
    pair_outs,
    dproj_ref,
    wp_turned_ref,
    grad_buf,
    piece_refs,
    band_recvs,
    held_refs,
    ffn_recvs,
    pair_refs,
    pair_recvs,
    around_recv,
    band_sems,
    ffn_sems,
    pair_sems,
    grad_sems,
    local_sem,
):
    place = Place()
    step = pl.program_id(0)
    steps = heads * slots
    head, slot = step // slots, lax.rem(step, slots)
    size, frames = q_ref.shape[1:]
    model = n_ref.shape[1]
    inner = heads * size
    pairs = heads // 2
    pair_rows = 6 * size
    blocks = frames // BLOCK
    last = pl.num_programs(0) - 1
    my_band, my_batch = place.band, place.batch

    bands = [Total(place, order, band_sems[0].at[i], band_sems[1].at[i]) for i, order in enumerate(BAND_ORDERS)]
    ffns = [Total(place, order, ffn_sems[0].at[i], ffn_sems[1].at[i]) for i, order in enumerate(FFN_ORDERS)]
    own = [
        Total(place, PAIR_ORDERS[i], pair_sems[0].at[i], pair_sems[1].at[i]) for i in range(pairs)
    ]

    def half_copy(i):
        return pltpu.make_async_copy(ffn_refs[i].at[place.bits["core"]], held_refs[i], local_sem.at[len(bands) + i])

    def eighth(total, held):
        return held.at[total.half_rows(held, 2)[0]]

    def all_steps(total, source, held, recvs, out, sem):
        width = recvs[3].shape[2]

        def back_region():
            return out.at[total.back_rows(out, 2)]

        def s0():
            total.start_core(source, recvs[0])

        def s1():
            total.end_core(held, recvs[0])
            total.start_half(1, held, recvs[1])

        def s2():
            total.end_half(1, held, recvs[1])
            total.start_half(2, held, recvs[2])

        def s3():
            total.end_half(2, held, recvs[2])
            total.start_z(eighth(total, held), recvs[3])

        def s4():
            total.end_z(eighth(total, held), recvs[3])
            total.start_z_back(eighth(total, held), back_region(), width, sem)

        def s5():
            total.end_z_back(eighth(total, held), back_region(), width, sem)
            total.start_back(2, out)

        def s6():
            total.end_back(2, out)
            total.start_back(1, out)

        def s7():
            total.end_back(1, out)
            total.start_back(0, out)

        def s8():
            total.end_back(0, out)

        return [s0, s1, s2, s3, s4, s5, s6, s7, s8]

    plan = {}

    def at_step(index, action):
        plan.setdefault(index, []).append(action)

    def enter():
        other_x = place.across("x")[1] // 2
        diagonal = (my_band, 2 * other_x + 1 - place.bits["core"])
        barrier = pltpu.get_barrier_semaphore()

        def call(other):
            pl.semaphore_signal(barrier, inc=1, device_id=other, device_id_type=pl.DeviceIdType.MESH)

        own[-1].around(lambda step, quarter, z, other: call(other))
        call(place.across("core"))
        call(diagonal)
        pl.semaphore_wait(barrier, 4 * Z_COUNT + 1)
        for i in range(len(ffns)):
            half_copy(i).start()

    tail = steps + slots * blocks
    at_step(0, enter)

    def schedule(actions, places):
        for at, action in zip(places, actions):
            at_step(at, action)

    for i in range(len(bands)):
        out = band_outs[i]
        region = out.at[bands[i].back_rows(out, 2)]
        quarter = band_outs[i].shape[1] // Z_COUNT

        def z_begin(i=i):
            piece_refs[i][...] = part_refs[i][...]
            if i >= BAND_EARLY:
                bands[i].start_z(piece_refs[i], band_recvs[i - BAND_EARLY])

        def z_turn(i=i, region=region, quarter=quarter):
            if i >= BAND_EARLY:
                bands[i].end_z(piece_refs[i], band_recvs[i - BAND_EARLY])
            bands[i].start_z_back(piece_refs[i], region, quarter, local_sem.at[i])

        def z_end(i=i, region=region, quarter=quarter, out=out):
            bands[i].end_z_back(piece_refs[i], region, quarter, local_sem.at[i])
            bands[i].start_back(2, out)

        def back_two(i=i, out=out):
            bands[i].end_back(2, out)
            bands[i].start_back(1, out)

        def back_one(i=i, out=out):
            bands[i].end_back(1, out)
            bands[i].start_back(0, out)

        actions = [z_begin, z_turn, z_end, back_two, back_one, lambda i=i, out=out: bands[i].end_back(0, out)]
        if i < BAND_EARLY:
            at_step(0, z_begin)
            actions = actions[1:]
        schedule(actions, BAND_PLACES[i])
    ffn_at = len(bands) + len(ffns)
    for i in range(len(ffns)):
        sem = local_sem.at[ffn_at + i]
        actions = all_steps(ffns[i], ffn_refs[i], held_refs[i], ffn_recvs[i], ffn_outs[i], sem)
        at_step(FFN_PLACES[i][1], lambda i=i: half_copy(i).wait())
        schedule(actions, FFN_PLACES[i])
    pair_at = ffn_at + len(ffns)

    def around_steps(total, source, held, recv, out, sem):
        def s0():
            total.start_core(source, recv[0])

        def s1():
            total.end_core(held, recv[0])
            total.start_around(held, recv[1])

        def s2():
            total.end_around(held, recv[1])
            total.start_around_back(held, recv[1], out, sem)

        def s3():
            total.end_around_back(held, recv[1], out, sem)
            total.start_back(0, out)

        def s4():
            total.end_back(0, out)

        return [s0, s1, s2, s3, s4]

    for i in range(pairs):
        source, held = pair_refs.at[i], pair_refs.at[i, place.bits["core"]]
        out, sem = pair_outs.at[i], local_sem.at[pair_at + i]
        recv = [ref.at[i] for ref in pair_recvs]
        if PAIR_ORDERS[i] is None:
            actions = around_steps(own[i], source, held, [recv[0], around_recv.at[PAIR_ORDERS[:i].count(None)]], out, sem)
        else:
            actions = all_steps(own[i], source, held, recv, out, sem)
        schedule(actions, PAIR_PLACES[i])

    for index in sorted(plan):
        if index < tail:

            @pl.when(step == index)
            def work(index=index):
                for action in plan[index]:
                    action()

    @pl.when(step < steps)
    def attention():
        d_queries, d_keys, d_values = scores_backward(
            q_ref[0],
            k_ref[0],
            v_ref[0],
            p_ref[0, 0],
            datt_ref[0],
            minus_ref[0, pl.ds(head, 1), :],
            cos_ref[...],
            sin_ref[...],
            size**-0.5,
        )
        start = pl.multiple_of((head // 2) * pair_rows + lax.rem(head, 2) * size, size)
        dproj_ref[slot, pl.ds(start, size), :] = d_queries.astype(BF16)
        dproj_ref[slot, pl.ds(start + 2 * size, size), :] = d_keys.astype(BF16)
        dproj_ref[slot, pl.ds(start + 4 * size, size), :] = d_values.astype(BF16)

    @pl.when((step < steps) & (lax.rem(step, 2 * slots) == 2 * slots - 1))
    def pair_done():
        pair = head // 2
        rows = pl.ds(pl.multiple_of(pair * pair_rows, pair_rows), pair_rows)
        sums = dg(n_ref[0], dproj_ref[0, rows, :], NT)
        for j in range(1, slots):
            sums = sums + dg(n_ref[j], dproj_ref[j, rows, :], NT)
        for half in range(2):
            at = slice(half * model // 2, (half + 1) * model // 2)
            pair_refs[pair, half, :, 0:pair_rows] = sums[at].astype(BF16)

    @pl.when(step == 2 * slots - 1)
    def narrow_done():
        gates = 0.0
        for j in range(slots):
            logit = jnp.concatenate([dlogit_ref[j], jnp.zeros_like(dlogit_ref[j])], axis=0).astype(BF16)
            gates = gates + dg(n_ref[j], logit, NT)[:, :heads]
        tile = narrow_tile([narrow_ref[:, : heads + 2], gates, dg2_ref[...]], model)
        for half in range(2):
            at = slice(half * model // 2, (half + 1) * model // 2)
            pair_refs[0, half, :, pair_rows:] = tile[at].astype(BF16)
            for i in range(1, pairs):
                pair_refs[i, half, :, pair_rows:] = jnp.zeros_like(tile[at]).astype(BF16)
        for pair in range(pairs):
            for part in range(3):
                to = pair * pair_rows + part * 2 * size
                source = part * inner + pair * 2 * size
                wp_turned_ref[:, to : to + 2 * size] = wp_ref[:, source : source + 2 * size]

    def message(index):
        j, i = index // blocks, lax.rem(index, blocks)
        source = grad_buf.at[index]
        target = grad_out.at[batch_count * j + my_batch]
        return i, source, target

    @pl.when(step >= steps)
    def rows_done():
        index = step - steps
        j, i = index // blocks, lax.rem(index, blocks)
        at = pl.ds(pl.multiple_of(i * BLOCK, BLOCK), BLOCK)
        logit = logit_block_ref[0].astype(BF16)
        d_normed = dg(wp_turned_ref[...], dproj_ref[j, :, at], NN) + dg(wgt_ref[...], logit, TN)
        d_rows, _ = norm_backward(x_ref[0].astype(F32).T, column(g1_ref), d_normed)
        grad_buf[index] = (dmid_ref[0] + d_rows).T.astype(BF16)
        i, source, target = message(index)

        @pl.when(i == my_batch)
        def keep():
            pltpu.make_async_copy(source, target, local_sem.at[pair_at + pairs]).start()

        @pl.when(i != my_batch)
        def give():
            send(source, target, grad_sems.at[0], grad_sems.at[1], my_band, i)

    @pl.when(step == last)
    def finish():
        for index in sorted(plan):
            if index >= tail:
                for action in plan[index]:
                    action()
        await_bytes(grad_buf.at[pl.ds(0, slots)], local_sem.at[pair_at + pairs])
        others = grad_buf.at[pl.ds(0, slots * (batch_count - 1))]
        await_bytes(others, grad_sems.at[0])
        await_bytes(others, grad_sems.at[1])


def time_attention_backward(
    p, q, k, v, datt, minus, dlogit, n, x, dmid, cos, sin, g1, wp, wgt, narrow, dg2, parts, ffn_sums, batch_count
):
    slots, inner, frames = q.shape
    heads = minus.shape[1]
    size = inner // heads
    model = n.shape[1]
    pairs = heads // 2
    steps = heads * slots
    blocks = frames // BLOCK

    def clamp(t):
        return jnp.minimum(t, steps - 1)

    def tail(t):
        return jnp.maximum(t - steps, 0)

    def per_head(rows, columns):
        return pl.BlockSpec((1, rows, columns), lambda t: (lax.rem(clamp(t), slots), clamp(t) // slots, 0))

    consts = (n, dlogit, cos, sin, g1, wp, wgt, narrow, dg2)
    anywhere = pl.BlockSpec(memory_space=pl.ANY)
    dma = pltpu.SemaphoreType.DMA
    widths = [a.shape[2] for a in ffn_sums]
    pair_width = 8 * size

    def recv_buffers(width, *lead):
        rows = model // 2
        shapes = [(rows, width), (rows // 2, width), (rows // 4, width), (Z_COUNT - 1, rows // 4, width // Z_COUNT)]
        return [pltpu.VMEM(lead + shape, BF16) for shape in shapes]

    return pl.pallas_call(
        lambda *refs: time_attention_backward_kernel(heads, slots, batch_count, *refs),
        grid=(steps + slots * blocks,),
        out_shape=(
            jax.ShapeDtypeStruct((batch_count * slots, BLOCK, model), BF16),
            [jax.ShapeDtypeStruct((model, a.shape[1]), BF16) for a in parts],
            [jax.ShapeDtypeStruct((model, width), BF16) for width in widths],
            jax.ShapeDtypeStruct((pairs, model, pair_width), BF16),
        ),
        in_specs=[
            pl.BlockSpec((1, 1, frames, frames), lambda t: (lax.rem(clamp(t), slots), clamp(t) // slots, 0, 0)),
            per_head(size, frames),
            per_head(size, frames),
            per_head(size, frames),
            per_head(size, frames),
            pl.BlockSpec((1, heads, frames), lambda t: (lax.rem(clamp(t), slots), 0, 0)),
            pl.BlockSpec((1, BLOCK, model), lambda t: (tail(t) // blocks, lax.rem(tail(t), blocks), 0)),
            pl.BlockSpec((1, model, BLOCK), lambda t: (tail(t) // blocks, 0, lax.rem(tail(t), blocks))),
            pl.BlockSpec((1, heads, BLOCK), lambda t: (tail(t) // blocks, 0, lax.rem(tail(t), blocks))),
        ]
        + [whole_spec(c) for c in consts]
        + [[whole_spec(a) for a in parts], [anywhere] * len(ffn_sums)],
        out_specs=(anywhere, [anywhere] * len(parts), [anywhere] * len(ffn_sums), anywhere),
        scratch_shapes=[
            pltpu.VMEM((slots, 3 * inner, frames), BF16),
            pltpu.VMEM((model, 3 * inner), BF16),
            pltpu.VMEM((slots * blocks, BLOCK, model), BF16),
            [pltpu.VMEM(a.shape, BF16) for a in parts],
            [pltpu.VMEM((Z_COUNT - 1, a.shape[0], a.shape[1] // Z_COUNT), BF16) for a in parts[BAND_EARLY:]],
            [pltpu.VMEM((model // 2, width), BF16) for width in widths],
            [recv_buffers(width) for width in widths],
            pltpu.VMEM((pairs, 2, model // 2, pair_width), BF16),
            recv_buffers(pair_width, pairs),
            pltpu.VMEM((PAIR_ORDERS.count(None), 4 * Z_COUNT - 1, model // 8, pair_width // Z_COUNT), BF16),
            [dma((len(parts), TOTAL_STEPS))] * 2,
            [dma((len(widths), TOTAL_STEPS))] * 2,
            [dma((pairs, TOTAL_STEPS)), dma((pairs, TOTAL_STEPS))],
            dma((2,)),
            dma((len(parts) + 2 * len(widths) + pairs + 1,)),
        ],
        compiler_params=pltpu.CompilerParams(
            vmem_limit_bytes=VMEM_BYTES, collective_id=3, has_side_effects=True
        ),
        cost_estimate=cost(20.0e6 * slots * frames, 0, 60e6),
        name="time_attention_backward",
    )(p, q, k, v, datt, minus, x, dmid, dlogit, *consts, list(parts), list(ffn_sums))


def finish_kernel(
    heads,
    grad_ref,
    bwp_ref,
    bw1_ref,
    bw2t_ref,
    bwot_ref,
    w1_ref,
    wot_ref,
    w2t_ref,
    pair_ref,
    first_pair_ref,
    wp_ref,
    wgt_ref,
    g1_ref,
    y_ref,
    y_out,
    grad_out,
    dg1_out,
    dwp_out,
    dwg_out,
    dwo_out,
    dg2_out,
    dw1_out,
    dw2_out,
    bg1_out,
    bwp_out,
    bwg_out,
    bwo_out,
    bg2_out,
    bw1_out,
    bw2_out,
    scaled_ref,
):
    pair = pl.program_id(0)
    inner = wp_ref.shape[1] // 3
    width = inner // pl.num_programs(0)
    pairs, bands, parts, rows, model = y_ref.shape
    split = y_ref[...].astype(F32).reshape(pairs, bands, parts, 2, rows // 2, model)
    for j in range(2):
        values = split[:, :, :, j].reshape(pairs, bands * parts * rows // 2, model)
        for i in range(pairs):
            y_out[2 * i + j] = values[i].astype(BF16)
    grad_out[...] = grad_ref[...].astype(F32)
    bwp_out[...] = bwp_ref[...].astype(F32)
    bw1_out[...] = bw1_ref[...].astype(F32)
    bw2_out[...] = bw2t_ref[...].astype(F32).T
    bwo_out[...] = bwot_ref[...].astype(F32).T
    dw1_out[...] = w1_ref[...].astype(F32)
    dw2_out[...] = w2t_ref[...].astype(F32).T
    dwo_out[...] = wot_ref[...].astype(F32).T

    @pl.when(pair == 0)
    def clear():
        scaled_ref[...] = jnp.zeros_like(scaled_ref)

    for part in range(3):
        at = pl.ds(pl.multiple_of(part * inner + pair * width, 128), width)
        values = pair_ref[0, :, part * width : (part + 1) * width].astype(F32)
        dwp_out[:, at] = values
        scaled_ref[...] += values * wp_ref[:, at].astype(F32)

    @pl.when(pair == pl.num_programs(0) - 1)
    def narrow():
        tile = first_pair_ref[0, :, 3 * width :].astype(F32)
        rows = tile.T
        bwg_out[...] = rows[:heads]
        bg1_out[...] = rows[heads]
        bg2_out[...] = rows[heads + 1]
        gates = tile[:, heads + 2 : 2 * heads + 2]
        dwg_out[...] = rows[heads + 2 : 2 * heads + 2]
        dg2_out[...] = rows[2 * heads + 2]
        sums = jnp.sum(scaled_ref[...], axis=1, keepdims=True)
        sums = sums + jnp.sum(gates * wgt_ref[...].astype(F32).T, axis=1, keepdims=True)
        dg1_out[...] = jnp.broadcast_to(sums, (sums.shape[0], 128)).T[0] / g1_ref[...].astype(F32)


def finish_sums(grads, y, band_sums, ffn_sums, pair_sums, g1, params):
    wp, wgt, wo, w1, w2 = params
    model, hidden = w1.shape
    inner, heads = wo.shape[0], wgt.shape[0]
    pairs = pair_sums.shape[0]
    split = hidden // pairs
    out_split = inner // pairs
    slot_dev, frame_dev, _ = grads.shape

    def lanes(width):
        return pl.BlockSpec((model, width), lambda i: (0, i))

    def whole(*shape):
        return pl.BlockSpec(shape, lambda i: (0,) * len(shape))

    def cut_rows(rows):
        return pl.BlockSpec((rows, model), lambda i: (i, 0))

    band_wp, band_w1, band_w2t, band_wot = band_sums
    time_w2t, time_w1, time_wot = ffn_sums
    grad_block = pl.BlockSpec((slot_dev // pairs, frame_dev, model), lambda i: (i, 0, 0))
    narrow = [((model,), whole(model)), ((heads, model), whole(heads, model))]
    per_layer = [
        narrow[0],
        ((model, 3 * inner), None),
        narrow[1],
        ((inner, model), cut_rows(out_split)),
        narrow[0],
        ((model, hidden), lanes(split)),
        ((hidden, model), cut_rows(split)),
    ]
    shapes, specs = [jax.ShapeDtypeStruct(grads.shape, BF16), jax.ShapeDtypeStruct(grads.shape, F32)], [grad_block] * 2
    y_block = pl.BlockSpec((y.shape[0] // pairs,) + y.shape[1:], lambda i: (i, 0, 0, 0, 0))
    for layer in range(2):
        for shape, spec in per_layer:
            shapes.append(jax.ShapeDtypeStruct(shape, F32))
            if spec is None:
                spec = whole(*shape) if layer == 0 else lanes(3 * inner // pairs)
            specs.append(spec)
    return pl.pallas_call(
        lambda *refs: finish_kernel(heads, *refs),
        grid=(pairs,),
        out_shape=shapes,
        in_specs=[
            grad_block,
            lanes(3 * inner // pairs),
            lanes(split),
            lanes(split),
            lanes(out_split),
            lanes(split),
            lanes(out_split),
            lanes(split),
            pl.BlockSpec((1, model, pair_sums.shape[2]), lambda i: (i, 0, 0)),
            pl.BlockSpec((1, model, pair_sums.shape[2]), lambda i: (0, 0, 0)),
            whole_spec(wp),
            whole_spec(wgt),
            whole_spec(g1),
            y_block,
        ],
        out_specs=specs,
        scratch_shapes=[pltpu.VMEM((model, inner // pairs), F32)],
        compiler_params=pltpu.CompilerParams(vmem_limit_bytes=VMEM_BYTES),
        name="finish_sums",
    )(
        grads,
        band_wp,
        band_w1,
        band_w2t,
        band_wot,
        time_w1,
        time_wot,
        time_w2t,
        pair_sums,
        pair_sums,
        wp,
        wgt,
        g1,
        y,
    )


def band_kernel(
    heads,
    batch_count,
    band_count,
    x_ref,
    cot_ref,
    count_ref,
    slots_ref,
    g1_ref,
    g2_ref,
    wgt_ref,
    wpt_ref,
    wot_ref,
    w1t_ref,
    w2t_ref,
    wp_ref,
    wo_ref,
    w1_ref,
    w2_ref,
    y_out,
    dx_out,
    half_outs,
    narrow_out,
    q_ref,
    k_ref,
    v_ref,
    p_ref,
    turned_ref,
    gate_ref,
    linv_ref,
    att_ref,
    mixed_ref,
    act_ref,
    slope_ref,
    hidden_ref,
    dmixed_ref,
    dlogit_ref,
    dproj_ref,
    dwp_ref,
    dw1_ref,
    dw2t_ref,
    dwot_ref,
    dwg_ref,
    dg1_ref,
    dg2_ref,
    xs_ref,
    cots_ref,
    ys_ref,
    dxs_ref,
    y_buf,
    dx_buf,
    y_send,
    y_recv,
    dx_send,
    dx_recv,
    local_sem,
    bias_ref,
    cos_ref,
    sin_ref,
    valid_ref,
    halves,
    core_recvs,
    core_sems,
    half_sem,
):
    step = pl.program_id(0)
    slot_count, part_frames, model = x_ref.shape
    inner, tokens = q_ref.shape
    size = inner // heads
    groups = tokens // BLOCK
    taken = tokens // slot_count
    per_part = part_frames // taken
    part = step // per_part
    first = lax.rem(step, per_part) * taken
    my_band, my_batch = lax.axis_index("band"), lax.axis_index("batch")
    slot_dev = slot_count // band_count
    slots = slot_dev // batch_count
    own_chunk = my_batch * band_count + my_band
    chunks = band_count * batch_count

    columns = [slice(at, at + 128) for at in range(0, model, 128)]

    def tokens_of(ref):
        return jnp.concatenate(
            [
                jnp.concatenate(
                    [ref[c, pl.ds(first + i, slot_count, stride=part_frames), :] for i in range(taken)], axis=0
                ).T
                for c in range(len(columns))
            ],
            axis=0,
        )

    def put_tokens(ref, values, start, stride):
        for c, at in enumerate(columns):
            turned = values[at].T
            for i in range(taken):
                ref[c, pl.ds(start + i, slot_count, stride=stride), :] = turned[
                    i * slot_count : (i + 1) * slot_count
                ]

    @pl.when(step == 0)
    def enter():
        greet_all(band_count, batch_count)
        bands = slots_ref[...].reshape(1, slot_count)
        cos, sin = rotary_rows(jnp.maximum(bands, 0).astype(F32), size // 2)
        cos_ref[...] = jnp.concatenate([cos] * taken, axis=1)
        sin_ref[...] = jnp.concatenate([sin] * taken, axis=1)
        valid = jnp.concatenate([jnp.where(bands >= 0, 1.0, 0.0)] * taken, axis=1)
        valid_ref[...] = valid
        keys = jnp.broadcast_to(valid[:, :BLOCK], (8, BLOCK)).T[:, :1]
        row = lax.broadcasted_iota(jnp.int32, (BLOCK, BLOCK), 0) // slot_count
        column_index = lax.broadcasted_iota(jnp.int32, (BLOCK, BLOCK), 1) // slot_count
        bias_ref[...] = jnp.where((row == column_index) & (keys > 0.5), 0.0, NEG_FILL)

    @pl.when(lax.rem(step, per_part) == 0)
    def unpack():
        held = slot_count * part_frames
        for c, at in enumerate(columns):
            xs_ref[c, pl.ds(0, held)] = x_ref[:, :, at].astype(F32).reshape(held, 128)
            cots_ref[c, pl.ds(0, held)] = cot_ref[:, :, at].astype(F32).reshape(held, 128)

    place = Place()
    totals = [
        Total(place, order, core_sems.at[0, i], core_sems.at[1, i]) for i, order in enumerate(BAND_ORDERS)
    ]
    gain1, gain2 = column(g1_ref), column(g2_ref)
    piece = part_frames * (pl.num_programs(0) // per_part)
    own_start = (my_batch * band_count + my_band) * piece

    @pl.when(step == 0)
    def clear():
        for ref in (dwp_ref, dw1_ref, dw2t_ref, dwot_ref, dwg_ref, dg1_ref, dg2_ref):
            ref[...] = jnp.zeros_like(ref)

    rows = tokens_of(xs_ref)
    normed = norm_forward(rows, gain1)
    q_ref[...], k_ref[...], v_ref[...] = project_block(
        normed, wpt_ref, cos_ref[...], sin_ref[...], inner, LOG2E * size**-0.5
    )
    gate_ref[...] = dg(wgt_ref[...], normed, NN)
    ones = extra_rows([jnp.ones((1, BLOCK), F32)], BLOCK)
    nothing = jnp.zeros((size, BLOCK), BF16)

    def apart(first, second):
        return jnp.concatenate(
            [jnp.concatenate([first, nothing], axis=1), jnp.concatenate([nothing, second], axis=1)], axis=0
        )

    turned_ref[...] = k_ref[...].T
    bias = jnp.concatenate([bias_ref[...]] * 2, axis=1)

    def attend(pair, carry):
        both = pl.ds(pl.multiple_of(2 * pair * size, 2 * size), 2 * size)
        at = [pl.ds(pl.multiple_of((2 * pair + i) * size, size), size) for i in range(2)]
        for group in range(groups):
            lanes = slice(group * BLOCK, (group + 1) * BLOCK)
            scores = dg(turned_ref[lanes, both], apart(*(q_ref[one, lanes] for one in at)), NN) + bias
            weights = jnp.exp2(scores - jnp.max(scores, axis=0, keepdims=True)).astype(BF16)
            p_ref[pair * groups + group] = weights
            for i, one in enumerate(at):
                row = pl.ds(2 * pair + i, 1)
                own = weights[:, i * BLOCK : (i + 1) * BLOCK]
                sums = dg(jnp.concatenate([v_ref[one, lanes], ones], axis=0), own, NN)
                inverse = 1.0 / sums[size : size + 1]
                attended = sums[:size] * inverse
                linv_ref[row, lanes] = inverse
                att_ref[one, lanes] = attended
                gate = jax.nn.sigmoid(gate_ref[row, lanes])
                mixed_ref[one, lanes] = (attended * gate).astype(BF16)
        return carry

    lax.fori_loop(0, heads // 2, attend, 0, unroll=4)
    middle = rows + dg(wot_ref[...], mixed_ref[...], NN)
    normed_ffn = norm_forward(middle, gain2)

    result = feed_forward(middle, normed_ffn, w1t_ref, w2t_ref, act_ref, slope_ref)
    frame = own_start + step * taken + lax.broadcasted_iota(jnp.int32, (1, tokens), 1) // slot_count
    mask = jnp.where(frame < count_ref[0], valid_ref[...], 0.0)
    result = result * mask
    put_tokens(ys_ref, result, 0, taken)

    couples = slot_dev // 2
    for c, at in enumerate(columns):
        y_buf[step, :, :, at] = ys_ref[c, pl.ds(0, tokens)].reshape(slot_count // 2, 2 * taken, 128).astype(BF16)

    def give_row(i, carry):
        other = lax.rem(my_band + i, band_count)
        send(
            y_buf.at[step, pl.ds(other * couples, couples)],
            y_out.at[:, my_band, step],
            y_send,
            y_recv,
            other,
            my_batch,
        )
        return carry

    lax.fori_loop(1, band_count, give_row, 0)
    pltpu.make_async_copy(
        y_buf.at[step, pl.ds(my_band * couples, couples)], y_out.at[:, my_band, step], local_sem.at[0]
    ).start()

    grad = tokens_of(cots_ref) * mask
    d_middle, ffn_branch, d_hidden = ffn_backward(grad, slope_ref[...], middle, gain2, w1_ref, w2_ref, dg2_ref)
    hidden_ref[...] = d_hidden
    branch = d_middle.astype(BF16)
    dmixed_ref[...] = dg(wo_ref[...], branch, NN)

    turned_ref[...] = v_ref[...].T
    def attend_back(pair, carry):
        both = pl.ds(pl.multiple_of(2 * pair * size, 2 * size), 2 * size)
        starts = [pl.multiple_of((2 * pair + i) * size, size) for i in range(2)]
        at = [pl.ds(start, size) for start in starts]
        d_atts, minuses = [], []
        for i, one in enumerate(at):
            row = pl.ds(2 * pair + i, 1)
            d_att, minus, d_logit = head_backward(
                dmixed_ref[one, :], att_ref[one, :], gate_ref[row, :], linv_ref[row, :]
            )
            dlogit_ref[row, :] = d_logit
            d_atts.append(d_att)
            minuses.append(minus)
        for group in range(groups):
            lanes = slice(group * BLOCK, (group + 1) * BLOCK)
            weights = p_ref[pair * groups + group]
            d_weights = dg(turned_ref[lanes, both], apart(*(d_att[:, lanes] for d_att in d_atts)), NN)
            minus = jnp.concatenate([minus[:, lanes] for minus in minuses], axis=1)
            d_scores = (weights.astype(F32) * (d_weights + minus)).astype(BF16)
            cos, sin = cos_ref[:, lanes], -sin_ref[:, lanes]
            for i, one in enumerate(at):
                own = slice(i * BLOCK, (i + 1) * BLOCK)
                d_queries = dg(k_ref[one, lanes], d_scores[:, own], NN) * size**-0.5
                d_keys = dg(q_ref[one, lanes], d_scores[:, own], NT) * (1.0 / LOG2E)
                d_values = dg(d_atts[i][:, lanes], weights[:, own], NT)
                dproj_ref[one, lanes] = turn(d_queries, cos, sin).astype(BF16)
                dproj_ref[pl.ds(inner + starts[i], size), lanes] = turn(d_keys, cos, sin).astype(BF16)
                dproj_ref[pl.ds(2 * inner + starts[i], size), lanes] = d_values.astype(BF16)
        return carry

    lax.fori_loop(0, heads // 2, attend_back, 0, unroll=4)
    d_logit = jnp.concatenate([dlogit_ref[...], jnp.zeros_like(dlogit_ref)], axis=0).astype(BF16)
    d_normed = dg(wp_ref[...], dproj_ref[...], NN) + dg(wgt_ref[...], dlogit_ref[...].astype(BF16), TN)
    d_rows, terms = norm_backward(rows, gain1, d_normed)
    dg1_ref[...] += jnp.sum(terms, axis=1, keepdims=True)
    put_tokens(dxs_ref, d_middle + d_rows, 0, taken)
    for c, at in enumerate(columns):
        grouped = dxs_ref[c, pl.ds(0, tokens)].reshape(band_count, slots, batch_count, taken, 128)
        grouped = jnp.concatenate([grouped[:, j][:, :, None] for j in range(slots)], axis=2)
        dx_buf[step, :, :, at] = grouped.reshape(chunks, slots * taken, 128).astype(BF16)

    def give_grad(i, carry):
        other = lax.rem(my_band * batch_count + my_batch + i, chunks)
        send(
            dx_buf.at[step, other],
            dx_out.at[own_chunk, step],
            dx_send,
            dx_recv,
            other // batch_count,
            lax.rem(other, batch_count),
        )
        return carry

    lax.fori_loop(1, chunks, give_grad, 0)
    pltpu.make_async_copy(
        dx_buf.at[step, my_band * batch_count + my_batch], dx_out.at[own_chunk, step], local_sem.at[1]
    ).start()

    dwp_ref[...] += dg(normed, dproj_ref[...], NT)
    dwg_ref[...] += dg(normed, d_logit, NT)[:, :heads]
    dwot_ref[...] += dg(branch, mixed_ref[...], NT)
    add_ffn_sums(dw1_ref, dw2t_ref, ffn_branch, act_ref[...], normed_ffn, hidden_ref[...])

    @pl.when(step == pl.num_programs(0) - 1)
    def finish():
        narrow_out[...] = narrow_tile([dwg_ref[...], dg1_ref[...], dg2_ref[...]], model)
        core = place.bits["core"]
        for i, ref in enumerate((dwp_ref, dw1_ref, dw2t_ref, dwot_ref)):
            lay_halves(halves[i], ref)
            totals[i].start_core(halves[i], core_recvs[i])
        for i, total in enumerate(totals):
            total.end_core(halves[i].at[core], core_recvs[i])
            pltpu.make_async_copy(halves[i].at[core], half_outs[i], half_sem.at[i]).start()
        for i in range(len(totals)):
            pltpu.make_async_copy(halves[i].at[core], half_outs[i], half_sem.at[i]).wait()
        await_bytes(y_out.at[:, 0], local_sem.at[0])
        await_bytes(dx_out.at[0], local_sem.at[1])
        for sem in (y_send, y_recv):
            await_bytes(y_out.at[:, pl.ds(0, band_count - 1)], sem)
        for sem in (dx_send, dx_recv):
            await_bytes(dx_out.at[pl.ds(0, chunks - 1)], sem)


def band_layer(rows, cot, counts, slot_bands, g1, g2, params, flips, band_count, batch_count):
    project, gating, output_weight, expand, shrink = params
    slot_count, piece, model = rows.shape
    tokens = 2 * BLOCK
    steps = slot_count * piece // tokens
    heads, inner, hidden = gating.shape[0], output_weight.shape[0], expand.shape[1]
    groups = tokens // BLOCK
    taken = tokens // slot_count
    part_frames = 16
    per_part = part_frames // taken
    slots = slot_count // (band_count * batch_count)
    slot_dev = slot_count // band_count
    consts = (slot_bands, g1, g2, gating) + flips + (project, output_weight, expand, shrink)
    widths = (3 * inner, hidden, hidden, inner)
    chunks = band_count * batch_count
    blocks = pl.BlockSpec((slot_count, part_frames, model), lambda i: (0, i // per_part, 0))
    anywhere = pl.BlockSpec(memory_space=pl.ANY)
    dma = pltpu.SemaphoreType.DMA
    return pl.pallas_call(
        lambda *refs: band_kernel(heads, batch_count, band_count, *refs),
        grid=(steps,),
        out_shape=(
            jax.ShapeDtypeStruct((slot_dev // 2, band_count, steps, 2 * taken, model), BF16),
            jax.ShapeDtypeStruct((chunks, steps, slots * taken, model), BF16),
            [jax.ShapeDtypeStruct((model // 2, width), BF16) for width in widths],
            jax.ShapeDtypeStruct((model, 128), F32),
        ),
        in_specs=[blocks, blocks, pl.BlockSpec(memory_space=pltpu.SMEM)] + [whole_spec(c) for c in consts],
        out_specs=(
            anywhere,
            anywhere,
            [anywhere for _ in widths],
            pl.BlockSpec((model, 128), lambda i: (0, 0)),
        ),
        scratch_shapes=[
            pltpu.VMEM((inner, tokens), BF16),
            pltpu.VMEM((inner, tokens), BF16),
            pltpu.VMEM((inner, tokens), BF16),
            pltpu.VMEM((heads // 2 * groups, BLOCK, 2 * BLOCK), BF16),
            pltpu.VMEM((tokens, inner), BF16),
            pltpu.VMEM((heads, tokens), F32),
            pltpu.VMEM((heads, tokens), F32),
            pltpu.VMEM((inner, tokens), F32),
            pltpu.VMEM((inner, tokens), BF16),
            pltpu.VMEM((hidden, tokens), BF16),
            pltpu.VMEM((hidden, tokens), BF16),
            pltpu.VMEM((hidden, tokens), BF16),
            pltpu.VMEM((inner, tokens), F32),
            pltpu.VMEM((heads, tokens), F32),
            pltpu.VMEM((3 * inner, tokens), BF16),
            pltpu.VMEM((model, 3 * inner), F32),
            pltpu.VMEM((model, hidden), F32),
            pltpu.VMEM((model, hidden), F32),
            pltpu.VMEM((model, inner), F32),
            pltpu.VMEM((model, heads), F32),
            pltpu.VMEM((model, 1), F32),
            pltpu.VMEM((model, 1), F32),
            pltpu.VMEM((model // 128, (slot_count + 1) * part_frames, 128), F32),
            pltpu.VMEM((model // 128, (slot_count + 1) * part_frames, 128), F32),
            pltpu.VMEM((model // 128, tokens + taken, 128), F32),
            pltpu.VMEM((model // 128, tokens + taken, 128), F32),
            pltpu.VMEM((steps, slot_count // 2, 2 * taken, model), BF16),
            pltpu.VMEM((steps, chunks, slots * taken, model), BF16),
            dma,
            dma,
            dma,
            dma,
            dma((2,)),
            pltpu.VMEM((BLOCK, BLOCK), F32),
            pltpu.VMEM((inner // heads // 2, tokens), F32),
            pltpu.VMEM((inner // heads // 2, tokens), F32),
            pltpu.VMEM((1, tokens), F32),
            [pltpu.VMEM((2, model // 2, width), BF16) for width in widths],
            [pltpu.VMEM((model // 2, width), BF16) for width in widths],
            dma((2, len(widths), TOTAL_STEPS)),
            dma((len(widths),)),
        ],
        compiler_params=pltpu.CompilerParams(
            vmem_limit_bytes=VMEM_BYTES, collective_id=1, has_side_effects=True
        ),
        cost_estimate=cost(30.0e6 * slot_count * piece, 0, 60e6),
        name="band_layer",
    )(rows, cot, counts, *consts)


def slot_shards(activations, cotangent, frame_counts, slot_bands, *weights):
    slot_dev, _, frame_dev, model = activations.shape
    batch, band = lax.axis_size("batch"), lax.axis_size("band")
    g1, wp, wg, wo, g2, w1, w2 = weights[:7]
    band_g1, band_wp, band_wg, band_wo, band_g2, band_w1, band_w2 = weights[7:]
    heads = wg.shape[1]
    time_params = (wp, wg.T, wo, w1, w2)
    band_params = (band_wp, band_wg.T, band_wo, band_w1, band_w2)
    band_rows, band_cot, rows, n, q, k, v, p, linv, gate, att, mixed, mid, nf, act, slope, *turned = time_forward(
        activations.reshape(slot_dev, frame_dev, model),
        cotangent.reshape(slot_dev, frame_dev, model),
        frame_counts,
        g1,
        g2,
        time_params,
        band_params,
        band,
        batch,
    )
    cos, sin = turned[-2:]
    y, slot_grad, band_halves, band_narrow = band_layer(
        band_rows,
        band_cot,
        frame_counts,
        slot_bands,
        band_g1,
        band_g2,
        band_params,
        tuple(turned[:-2]),
        band,
        batch,
    )
    dmid, datt, minus, dlogit, ffn_halves, dg2, band_parts = time_ffn_backward(
        slot_grad, act, slope, nf, mid, mixed, att, gate, linv, g2, w1, w2, wo, band_halves
    )
    input_grad, band_sums, ffn_sums, pair_sums = time_attention_backward(
        p,
        q,
        k,
        v,
        datt,
        minus,
        dlogit,
        n,
        rows,
        dmid,
        cos,
        sin,
        g1,
        wp,
        time_params[1],
        band_narrow,
        dg2,
        band_parts,
        ffn_halves,
        batch,
    )
    layer_output, input_grad, *grads = finish_sums(
        input_grad, y, band_sums, ffn_sums, pair_sums, g1, time_params
    )
    grads = [g.T if g.shape[0] == heads else g for g in grads]
    return (layer_output.reshape(activations.shape), input_grad.reshape(activations.shape), *grads)


def shards(activations, cotangent, frame_counts, slot_bands, *weights):
    slot_dev, clips, frame_dev, _ = activations.shape
    batch, band = lax.axis_size("batch"), lax.axis_size("band")
    fits = (
        clips == 1
        and batch == 4
        and band == 2 * Z_COUNT
        and slot_dev % batch == 0
        and frame_dev == BLOCK
        and frame_dev == 32 * band
        and slot_bands.shape[0] == 64 == slot_dev * band
        and slot_dev == 2 * batch
        and activations.shape[-1] % 128 == 0
        and (frame_dev // band * slot_bands.shape[0]) % (2 * BLOCK) == 0
        and weights[2].shape[1] == 8
    )
    form = slot_shards if fits else generic_shards
    return form(activations, cotangent, frame_counts, slot_bands, *weights)


def solution(mesh):
    return jax.shard_map(
        shards,
        mesh=mesh,
        in_specs=(
            P("band", None, "batch", None),
            P("band", None, "batch", None),
            P(),
            P(),
            P(),
            P(),
            P(),
            P(),
            P(),
            P(),
            P(),
            P(),
            P(),
            P(),
            P(),
            P(),
            P(),
            P(),
        ),
        out_specs=(
            P("band", None, "batch", None),
            P("band", None, "batch", None),
            P(),
            P(),
            P(),
            P(),
            P(),
            P(),
            P(),
            P(),
            P(),
            P(),
            P(),
            P(),
            P(),
            P(),
        ),
        check_vma=False,
    )
```
